32 devices in a mesh: req: 8 (over z, y), tp: 4 (over x, core).
Axes of the slice: x: 2, y: 2, z: 4, core: 2. Of those that a mesh axis runs over, the one named last changes fastest.
Arguments:
- query: bfloat16 [32, 2048], P('req', 'tp'), may hold values from -8 to 8
- key_new: bfloat16 [32, 2048], P('req', 'tp'), may hold values from -4 to 4
- value_new: bfloat16 [32, 2048], P('req', 'tp'), may hold values from -4 to 4
- resid: bfloat16 [32, 2048], P('req', 'tp'), may hold values from -6 to 6
- lengths: int32 [32], replicated, may hold values from 1 to 512, as said below
- owner: int32 [32], replicated, may hold values from 0 to 7, as said below
- page_table: int32 [32, 16], replicated, may hold values from 0 to 21, as said below
- kv_pool: bfloat16 [2, 176, 32, 2048], P(None, 'req', None, 'tp'), may hold values from -4 to 4
- out_weight: bfloat16 [2048, 2048], P('tp'), may hold values from -0.125 to 0.125
- out_bias: bfloat16 [2048], P('tp'), may hold values from -3 to 3
- norm_gain: bfloat16 [2048], P('tp'), may hold values from 0.099609375 to 1.8984375
- norm_bias: bfloat16 [2048], P('tp'), may hold values from -3 to 3
- up_weight_t: bfloat16 [8192, 2048], P('req', 'tp'), may hold values from -0.125 to 0.125
- up_bias: bfloat16 [8192], P('req'), may hold values from -3 to 3
- down_weight: bfloat16 [8192, 2048], P('req', 'tp'), may hold values from -0.0625 to 0.0625
- down_bias: bfloat16 [2048], P('tp'), may hold values from -3 to 3
- order: int32 [32], replicated, may hold values from 0 to 31, each once
Outputs:
- layer_out: bfloat16 [32, 2048], P('req', 'tp')
The draws below stay inside these ranges and needn't reach their ends.
Inputs may be any that keep to these rules, and one draw needn't show every extreme that they name: `lengths`: one request in 32 (at least one) is long, with a length from 256 to 512; the others have at most 63 positions. `owner`: every index of req owns exactly 4 requests, at most one of them long, and no two of them among the 4 rows that one index of req holds. `page_table`: entry j of request r for j < ceil(lengths[r] / 32) names a page of the owner's pool that no other entry of that owner's requests below that bound names; later entries are arbitrary pages.
All inputs are finite; a program needn't handle non-finite values.
Results may differ from the reference program's by a relative error of at most 0.015.
Values may be sent and summed in bfloat16 or wider, within the bound.
No kernel may reach another device: no remote copies, remote signals or barrier semaphores. Data moves between devices by JAX's collectives and lax.ppermute only.
A program may use at most 64 MiB of HBM per device.

```python
import math
import jax
import jax.numpy as jnp
from jax import lax

D = 2048
HEADS = 16
HEAD_DIM = 128
FF = 8192
REQ_DEV = 4
PAGE = 32
LONG = 512
REQS = 32
MAXP = 16
POOL = 22
SHORT = 63
N_REQ = 8


def plan(key):
    base_key = jax.random.fold_in(key, 11)
    key_dev, key_off, key_col, key_short, key_long, key_pool = jax.random.split(base_key, 6)
    long_count = max(REQS // 32, 1)
    dev_perm = jax.random.permutation(key_dev, N_REQ).astype(jnp.int32)
    dev_inverse = jnp.zeros((N_REQ,), jnp.int32).at[dev_perm].set(jnp.arange(N_REQ, dtype=jnp.int32))
    offsets = jax.random.permutation(key_off, N_REQ).astype(jnp.int32)[:REQ_DEV]
    col_perm = jax.vmap(lambda sub: jax.random.permutation(sub, REQ_DEV).astype(jnp.int32))(jax.random.split(key_col, N_REQ))
    slots = jnp.arange(REQS, dtype=jnp.int32)
    slot_dev = slots // REQ_DEV
    slot_rank = slots % REQ_DEV
    source = (dev_inverse[slot_dev] - offsets[slot_rank]) % N_REQ
    slot_req = (source * REQ_DEV + col_perm[source, slot_rank]).astype(jnp.int32)
    owner = jnp.zeros((REQS,), jnp.int32).at[slot_req].set(slot_dev)
    long_ids = slot_req.reshape(N_REQ, REQ_DEV)[dev_perm[:long_count], 0]
    is_long = jnp.zeros((REQS,), jnp.int32).at[long_ids].set(1)
    short_len = jax.random.randint(key_short, (REQS,), 1, SHORT + 1).astype(jnp.int32)
    long_len = jax.random.randint(key_long, (REQS,), LONG // 2, LONG + 1).astype(jnp.int32)
    lengths = jnp.where(is_long == 1, long_len, short_len)
    lengths = lengths.at[long_ids[0]].set(LONG)
    slot_len = lengths[slot_req]
    grid_pages = ((slot_len + PAGE - 1) // PAGE).reshape(N_REQ, REQ_DEV)
    offset = jnp.cumsum(grid_pages, axis=1) - grid_pages
    used_total = jnp.sum(grid_pages, axis=1, keepdims=True)
    unused = MAXP - grid_pages
    unused_offset = jnp.cumsum(unused, axis=1) - unused
    entry = jnp.arange(MAXP, dtype=jnp.int32)[None, None, :]
    used_place = offset[:, :, None] + entry
    spare_place = used_total[:, :, None] + unused_offset[:, :, None] + (entry - grid_pages[:, :, None])
    place = jnp.where(entry < grid_pages[:, :, None], used_place, spare_place) % POOL
    pool_perm = jax.vmap(lambda sub: jax.random.permutation(sub, POOL).astype(jnp.int32))(jax.random.split(key_pool, N_REQ))
    page_ids = jnp.take_along_axis(pool_perm, place.reshape(N_REQ, REQ_DEV * MAXP), axis=1)
    table = jnp.zeros((REQS, MAXP), jnp.int32).at[slot_req].set(page_ids.reshape(REQS, MAXP))
    return (lengths, owner, table)


def draw_lengths(key, part):
    return plan(key)[0]


def draw_owner(key, part):
    return plan(key)[1]


def draw_page_table(key, part):
    return plan(key)[2]


def draw_query(key, part):
    fresh = jax.random.fold_in(key, 31)
    shape = (REQS, HEADS * HEAD_DIM)
    return jnp.clip(jax.random.normal(fresh, shape, jnp.float32), -6.0, 6.0).astype(jnp.bfloat16)


def draw_kv_pool(key, part):
    fresh = jax.random.fold_in(key, 41)
    shape = (2, N_REQ * POOL, PAGE, HEADS * HEAD_DIM)
    return jnp.clip(jax.random.normal(fresh, shape, jnp.float32), -4.0, 4.0).astype(jnp.bfloat16)


def block_levels(stream_key, extent, cuts, smallest, high):
    def one(position, shards_of):
        steps = jax.random.uniform(jax.random.fold_in(jax.random.fold_in(stream_key, 6), position), (shards_of,), jnp.float32, smallest / len(cuts), high / len(cuts))
        return jnp.repeat(jnp.exp(steps), extent[position] // shards_of).reshape((-1,) + (1,) * (len(extent) - position - 1))

    level = one(*cuts[0])
    for cut in cuts[1:]:
        level = level * one(*cut)
    return level


def bell_draw(own_key, dims, width, bound, cuts=(), kind=jnp.bfloat16):
    values = jax.random.normal(own_key, dims, jnp.float32) * width
    if len(cuts) > 0:
        values = block_levels(own_key, dims, cuts, -0.22, 0.18) * values
    return jnp.clip(values, min=-bound, max=bound).astype(kind)


def setup_inputs(seed: int = 0) -> dict:
    splits = jax.random.split(jax.random.key(seed), 18)
    return {
        "query": draw_query(jax.random.fold_in(splits[17], 71), 0),
        "key_new": bell_draw(splits[1], (REQS, HEADS * HEAD_DIM), 1.0, 4.0, ((0, 8), (1, 4))),
        "value_new": bell_draw(splits[2], (REQS, HEADS * HEAD_DIM), 1.0, 4.0, ((0, 8), (1, 4))),
        "resid": bell_draw(splits[3], (REQS, D), 1.0, 6.0, ((0, 8), (1, 4))),
        "lengths": draw_lengths(jax.random.fold_in(splits[17], 71), 0),
        "owner": draw_owner(jax.random.fold_in(splits[17], 71), 0),
        "page_table": draw_page_table(jax.random.fold_in(splits[17], 71), 0),
        "kv_pool": draw_kv_pool(jax.random.fold_in(splits[17], 71), 0),
        "out_weight": bell_draw(splits[8], (HEADS * HEAD_DIM, D), D ** -0.5, 0.125, ((0, 4),)),
        "out_bias": bell_draw(splits[9], (D,), 0.5, 3.0, ((0, 4),)),
        "norm_gain": jnp.clip(1.0 + 0.18 * jax.random.normal(splits[10], (D,), jnp.float32), 0.099609375, 1.8984375).astype(jnp.bfloat16),
        "norm_bias": bell_draw(splits[11], (D,), 0.5, 3.0, ((0, 4),)),
        "up_weight_t": bell_draw(splits[12], (FF, D), D ** -0.5, 0.125, ((0, 8), (1, 4))),
        "up_bias": bell_draw(splits[13], (FF,), 0.5, 3.0, ((0, 8),)),
        "down_weight": bell_draw(splits[14], (FF, D), FF ** -0.5, 0.0625, ((0, 8), (1, 4))),
        "down_bias": bell_draw(splits[15], (D,), 0.5, 3.0, ((0, 4),)),
        "order": jax.random.permutation(splits[16], REQS).astype(jnp.int32),
    }


def reference(query, key_new, value_new, resid, lengths, owner, page_table, kv_pool, out_weight, out_bias, norm_gain, norm_bias, up_weight_t, up_bias, down_weight, down_bias, order):
    score_scale = 1.0 / math.sqrt(HEAD_DIM)
    span = MAXP * PAGE
    highest = lax.Precision.HIGHEST

    def attend(request):
        pages = (owner[request] * POOL + page_table[request]).astype(jnp.int32)
        page_keys = kv_pool[0, pages].reshape(span, HEADS, HEAD_DIM).astype(jnp.float32)
        page_values = kv_pool[1, pages].reshape(span, HEADS, HEAD_DIM).astype(jnp.float32)
        query_row = query[request].reshape(HEADS, HEAD_DIM).astype(jnp.float32)
        key_row = key_new[request].reshape(HEADS, HEAD_DIM).astype(jnp.float32)
        value_row = value_new[request].reshape(HEADS, HEAD_DIM).astype(jnp.float32)
        scores = jnp.einsum('hd,shd->hs', query_row, page_keys, precision=highest) * score_scale
        position_ok = (jnp.arange(span, dtype=jnp.int32) < lengths[request])[None, :]
        scores = jnp.where(position_ok, scores, -jnp.inf)
        self_score = lax.optimization_barrier(jnp.sum(query_row * key_row, axis=-1)) * score_scale
        top = jnp.maximum(lax.optimization_barrier(jnp.max(scores, axis=1)), self_score)
        weights = jnp.where(position_ok, jnp.exp(scores - top[:, None]), 0.0)
        self_weight = jnp.exp(self_score - top)
        denom = lax.optimization_barrier(jnp.sum(weights, axis=1)) + self_weight
        packed = weights.astype(jnp.bfloat16).astype(jnp.float32)
        numer = jnp.einsum('hs,shd->hd', packed, page_values, precision=highest)
        numer = numer + self_weight.astype(jnp.bfloat16).astype(jnp.float32)[:, None] * value_row
        return (numer / denom[:, None]).reshape(-1).astype(jnp.bfloat16)
    attn = lax.map(attend, jnp.arange(REQS, dtype=jnp.int32))
    projected = jnp.dot(attn, out_weight, preferred_element_type=jnp.float32)
    stream = (resid.astype(jnp.float32) + projected + out_bias.astype(jnp.float32)[None, :]).astype(jnp.bfloat16)
    stream_f = stream.astype(jnp.float32)
    mean = lax.optimization_barrier(jnp.mean(stream_f, axis=1, keepdims=True))
    var = lax.optimization_barrier(jnp.mean((stream_f - mean) ** 2, axis=1, keepdims=True))
    normed = ((stream_f - mean) * lax.rsqrt(var + 1e-05) * norm_gain.astype(jnp.float32)[None, :] + norm_bias.astype(jnp.float32)[None, :]).astype(jnp.bfloat16)
    hidden_in = jnp.dot(normed, up_weight_t.T, preferred_element_type=jnp.float32) + up_bias.astype(jnp.float32)[None, :]
    activated = jax.nn.gelu(hidden_in, approximate=False).astype(jnp.bfloat16)
    feed = jnp.dot(activated, down_weight, preferred_element_type=jnp.float32) + down_bias.astype(jnp.float32)[None, :]
    combined = stream_f + feed
    return combined[order].astype(jnp.bfloat16)
```

```python
import math

import jax
import jax.numpy as jnp
from jax import lax
from jax.sharding import PartitionSpec as P

HEAD_DIM = 128
NORM_EPS = 1e-05
DIRECT = 16


def swap(x, axis, n, step):
    if step == 0:
        return x
    return lax.ppermute(x, axis, [(i, i ^ step) for i in range(n)])


def trade(blocks, axis, n):
    if n <= DIRECT:
        return [swap(blocks[s], axis, n, s) for s in range(n)]
    me = lax.axis_index(axis)
    pos = jnp.arange(n, dtype=jnp.int32) ^ me
    stacked = jnp.stack(blocks)[pos]
    moved = lax.all_to_all(stacked, axis, 0, 0, tiled=True)
    moved = moved[pos]
    return [moved[s] for s in range(n)]


def spread(x, axis, n):
    if n <= DIRECT:
        return [swap(x, axis, n, s) for s in range(n)]
    me = lax.axis_index(axis)
    pos = jnp.arange(n, dtype=jnp.int32) ^ me
    whole = lax.all_gather(x, axis, axis=0)[pos]
    return [whole[s] for s in range(n)]


def per_device(
    query,
    key_new,
    value_new,
    resid,
    lengths,
    owner,
    page_table,
    kv_pool,
    out_weight,
    out_bias,
    norm_gain,
    norm_bias,
    up_weight_t,
    up_bias,
    down_weight,
    down_bias,
    order,
):
    f32, bf16, i32 = jnp.float32, jnp.bfloat16, jnp.int32
    n_req = lax.axis_size("req")
    n_tp = lax.axis_size("tp")
    me = lax.axis_index("req")
    me_tp = lax.axis_index("tp")
    rows, cols = query.shape
    width = cols * n_tp
    heads = cols // HEAD_DIM
    pool_pages, page_len = kv_pool.shape[1], kv_pool.shape[2]
    positions = pool_pages * page_len
    scale = 1.0 / math.sqrt(HEAD_DIM)

    steps = jnp.arange(n_req, dtype=i32)
    my_owner = lax.dynamic_slice_in_dim(owner, me * rows, rows)
    send_hot = (my_owner[None, :] == (steps ^ me)[:, None]).astype(bf16)
    packed = jnp.concatenate([query, key_new, value_new, resid], axis=1)
    outgoing = jnp.dot(send_hot, packed, preferred_element_type=f32).astype(bf16)
    arrived = jnp.concatenate(
        trade([outgoing[s : s + 1] for s in range(n_req)], "req", n_req), axis=0
    )

    owner2 = owner.reshape(n_req, rows)
    same = owner[:, None] == owner[None, :]
    ids = jnp.arange(owner.shape[0], dtype=i32)
    rank = jnp.sum((same & (ids[None, :] < ids[:, None])).astype(i32), axis=1)
    slots = jnp.arange(rows, dtype=i32)
    mine = (owner == me)[None, :] & (rank[None, :] == slots[:, None])
    mine_i = mine.astype(i32)
    own_len = jnp.sum(mine_i * lengths[None, :], axis=1)
    own_table = jnp.sum(mine_i[:, :, None] * page_table[None], axis=1)
    own_src = jnp.sum(mine_i * (ids // rows)[None, :], axis=1)
    take_hot = (own_src[:, None] == (steps ^ me)[None, :]).astype(bf16)
    own = jnp.dot(take_hot, arrived, preferred_element_type=f32).astype(bf16)
    query_own, key_own, value_own, resid_own = (own[:, i * cols : (i + 1) * cols] for i in range(4))

    pos = jnp.arange(positions, dtype=i32)
    page, within = pos // page_len, pos % page_len
    entry = jnp.arange(page_table.shape[1], dtype=i32)
    start = entry * page_len
    hit = (own_table[:, :, None] == page[None, None, :]) & (
        start[None, :, None] + within[None, None, :] < own_len[:, None, None]
    )
    valid = jnp.any(hit, axis=1)

    keys = kv_pool[0].reshape(positions, cols)
    values = kv_pool[1].reshape(positions, cols)
    head_of = jnp.arange(cols, dtype=i32) // HEAD_DIM
    head_mask = head_of[None, :] == jnp.arange(heads, dtype=i32)[:, None]
    spread_q = jnp.where(head_mask[:, None, :], query_own[None], 0).reshape(heads * rows, cols)
    scores = (
        lax.dot_general(spread_q, keys, (((1,), (1,)), ((), ())), preferred_element_type=f32) * scale
    ).reshape(heads, rows, positions)
    scores = jnp.where(valid[None], scores, -jnp.inf)
    self_score = (
        jnp.sum(
            (query_own.astype(f32) * key_own.astype(f32)).reshape(rows, heads, HEAD_DIM), axis=-1
        ).T
        * scale
    )
    top = jnp.maximum(jnp.max(scores, axis=2), self_score)
    weights = jnp.exp(scores - top[:, :, None])
    self_weight = jnp.exp(self_score - top)
    total = jnp.sum(weights, axis=2) + self_weight
    numer = jnp.dot(
        weights.astype(bf16).reshape(heads * rows, positions), values, preferred_element_type=f32
    ).reshape(heads, rows, cols)
    numer = numer + self_weight.astype(bf16).astype(f32)[:, :, None] * value_own.astype(f32)[None]
    attn = jnp.sum(
        jnp.where(head_mask[:, None, :], numer / total[:, :, None], 0.0), axis=0
    ).astype(bf16)

    extra = resid_own.astype(f32) + out_bias.astype(f32)[None, :]
    partial = jnp.dot(attn, out_weight, preferred_element_type=f32)
    place = (jnp.arange(n_tp, dtype=i32) == me_tp)[None, :, None]
    partial = (
        partial.reshape(rows, n_tp, cols) + jnp.where(place, extra[:, None, :], 0.0)
    ).reshape(rows, width)
    stream = sum(spread(partial, "tp", n_tp)).astype(bf16)
    stream_f = stream.astype(f32)
    mean = jnp.mean(stream_f, axis=1, keepdims=True)
    var = jnp.mean((stream_f - mean) ** 2, axis=1, keepdims=True)
    inverse = lax.rsqrt(var + NORM_EPS)
    stream_own = lax.dynamic_slice_in_dim(stream, me_tp * cols, cols, axis=1)
    normed = (
        (stream_own.astype(f32) - mean) * inverse * norm_gain.astype(f32)[None, :]
        + norm_bias.astype(f32)[None, :]
    ).astype(bf16)

    normed_all = jnp.concatenate(spread(normed, "req", n_req), axis=0)
    order_rel = order.reshape(n_req, rows)[steps ^ me].reshape(-1)
    slot_rel = (owner ^ me) * rows + rank
    place_hot = (slot_rel[order_rel][:, None] == ids[None, :]).astype(bf16)
    normed_out = jnp.dot(place_hot, normed_all, preferred_element_type=f32).astype(bf16)
    hidden = lax.dot_general(
        normed_out, up_weight_t, (((1,), (1,)), ((), ())), preferred_element_type=f32
    ).astype(bf16)
    summed = sum(h.astype(f32) for h in spread(hidden, "tp", n_tp))
    activated = jax.nn.gelu(summed + up_bias.astype(f32)[None, :], approximate=False).astype(bf16)
    feed = jnp.dot(activated, down_weight, preferred_element_type=f32)
    feed = feed + jnp.dot(place_hot[:, :rows], stream_own, preferred_element_type=f32)
    pieces = trade([feed[s * rows : (s + 1) * rows] for s in range(n_req)], "req", n_req)
    return (sum(pieces) + down_bias.astype(f32)[None, :]).astype(bf16)


def solution(mesh):
    in_specs = (
        P("req", "tp"),
        P("req", "tp"),
        P("req", "tp"),
        P("req", "tp"),
        P(),
        P(),
        P(),
        P(None, "req", None, "tp"),
        P("tp", None),
        P("tp"),
        P("tp"),
        P("tp"),
        P("req", "tp"),
        P("req"),
        P("req", "tp"),
        P("tp"),
        P(),
    )
    out_specs = P("req", "tp")
    return jax.shard_map(
        per_device, mesh=mesh, in_specs=in_specs, out_specs=out_specs, check_vma=False
    )
```

```python
import math

import jax
import jax.numpy as jnp
from jax import lax
from jax.sharding import PartitionSpec as P

HEAD_DIM = 128
NORM_EPS = 1e-05


def trade(blocks, axis):
    return lax.all_to_all(blocks, axis, 0, 0, tiled=True)


def spread(x, axis):
    return trade(jnp.broadcast_to(x[None], (lax.axis_size(axis),) + x.shape), axis)


def per_device(
    query,
    key_new,
    value_new,
    resid,
    lengths,
    owner,
    page_table,
    kv_pool,
    out_weight,
    out_bias,
    norm_gain,
    norm_bias,
    up_weight_t,
    up_bias,
    down_weight,
    down_bias,
    order,
):
    f32, bf16, i32 = jnp.float32, jnp.bfloat16, jnp.int32
    n_req = lax.axis_size("req")
    n_tp = lax.axis_size("tp")
    me = lax.axis_index("req")
    me_tp = lax.axis_index("tp")
    rows, cols = query.shape
    width = cols * n_tp
    heads = cols // HEAD_DIM
    pool_pages, page_len = kv_pool.shape[1], kv_pool.shape[2]
    positions = pool_pages * page_len
    scale = 1.0 / math.sqrt(HEAD_DIM)

    steps = jnp.arange(n_req, dtype=i32)
    my_owner = lax.dynamic_slice_in_dim(owner, me * rows, rows)
    send_hot = (my_owner[None, :] == steps[:, None]).astype(bf16)
    packed = jnp.concatenate([query, key_new, value_new, resid], axis=1)
    outgoing = jnp.dot(send_hot, packed, preferred_element_type=f32).astype(bf16)
    arrived = trade(outgoing[:, None], "req")[:, 0]

    same = owner[:, None] == owner[None, :]
    ids = jnp.arange(owner.shape[0], dtype=i32)
    rank = jnp.sum((same & (ids[None, :] < ids[:, None])).astype(i32), axis=1)
    slots = jnp.arange(rows, dtype=i32)
    mine = (owner == me)[None, :] & (rank[None, :] == slots[:, None])
    mine_i = mine.astype(i32)
    own_len = jnp.sum(mine_i * lengths[None, :], axis=1)
    own_table = jnp.sum(mine_i[:, :, None] * page_table[None], axis=1)
    own_src = jnp.sum(mine_i * (ids // rows)[None, :], axis=1)
    take_hot = (own_src[:, None] == steps[None, :]).astype(bf16)
    own = jnp.dot(take_hot, arrived, preferred_element_type=f32).astype(bf16)
    query_own, key_own, value_own, resid_own = (own[:, i * cols : (i + 1) * cols] for i in range(4))

    pos = jnp.arange(positions, dtype=i32)
    page, within = pos // page_len, pos % page_len
    entry = jnp.arange(page_table.shape[1], dtype=i32)
    start = entry * page_len
    hit = (own_table[:, :, None] == page[None, None, :]) & (
        start[None, :, None] + within[None, None, :] < own_len[:, None, None]
    )
    valid = jnp.any(hit, axis=1)

    keys = kv_pool[0].reshape(positions, cols)
    values = kv_pool[1].reshape(positions, cols)
    head_of = jnp.arange(cols, dtype=i32) // HEAD_DIM
    head_mask = head_of[None, :] == jnp.arange(heads, dtype=i32)[:, None]
    spread_q = jnp.where(head_mask[:, None, :], query_own[None], 0).reshape(heads * rows, cols)
    scores = (
        lax.dot_general(spread_q, keys, (((1,), (1,)), ((), ())), preferred_element_type=f32) * scale
    ).reshape(heads, rows, positions)
    scores = jnp.where(valid[None], scores, -jnp.inf)
    self_score = (
        jnp.sum(
            (query_own.astype(f32) * key_own.astype(f32)).reshape(rows, heads, HEAD_DIM), axis=-1
        ).T
        * scale
    )
    top = jnp.maximum(jnp.max(scores, axis=2), self_score)
    weights = jnp.exp(scores - top[:, :, None])
    self_weight = jnp.exp(self_score - top)
    total = jnp.sum(weights, axis=2) + self_weight
    numer = jnp.dot(
        weights.astype(bf16).reshape(heads * rows, positions), values, preferred_element_type=f32
    ).reshape(heads, rows, cols)
    numer = numer + self_weight.astype(bf16).astype(f32)[:, :, None] * value_own.astype(f32)[None]
    attn = jnp.sum(
        jnp.where(head_mask[:, None, :], numer / total[:, :, None], 0.0), axis=0
    ).astype(bf16)

    extra = resid_own.astype(f32) + out_bias.astype(f32)[None, :]
    partial = jnp.dot(attn, out_weight, preferred_element_type=f32)
    place = (jnp.arange(n_tp, dtype=i32) == me_tp)[None, :, None]
    partial = (
        partial.reshape(rows, n_tp, cols) + jnp.where(place, extra[:, None, :], 0.0)
    ).reshape(rows, width)
    stream = jnp.sum(spread(partial, "tp"), axis=0).astype(bf16)
    stream_f = stream.astype(f32)
    mean = jnp.mean(stream_f, axis=1, keepdims=True)
    var = jnp.mean((stream_f - mean) ** 2, axis=1, keepdims=True)
    inverse = lax.rsqrt(var + NORM_EPS)
    stream_own = lax.dynamic_slice_in_dim(stream, me_tp * cols, cols, axis=1)
    normed = (
        (stream_own.astype(f32) - mean) * inverse * norm_gain.astype(f32)[None, :]
        + norm_bias.astype(f32)[None, :]
    ).astype(bf16)

    normed_all = spread(normed, "req").reshape(-1, cols)
    slot_of = owner * rows + rank
    place_hot = (slot_of[order][:, None] == ids[None, :]).astype(bf16)
    mine_hot = (slot_of[order][:, None] == (me * rows + slots)[None, :]).astype(bf16)
    normed_out = jnp.dot(place_hot, normed_all, preferred_element_type=f32).astype(bf16)
    hidden = lax.dot_general(
        normed_out, up_weight_t, (((1,), (1,)), ((), ())), preferred_element_type=f32
    ).astype(bf16)
    summed = jnp.sum(spread(hidden, "tp").astype(f32), axis=0)
    activated = jax.nn.gelu(summed + up_bias.astype(f32)[None, :], approximate=False).astype(bf16)
    feed = jnp.dot(activated, down_weight, preferred_element_type=f32)
    feed = feed + jnp.dot(mine_hot, stream_own, preferred_element_type=f32)
    pieces = trade(feed.reshape(n_req, rows, cols), "req")
    return (jnp.sum(pieces, axis=0) + down_bias.astype(f32)[None, :]).astype(bf16)


def solution(mesh):
    in_specs = (
        P("req", "tp"),
        P("req", "tp"),
        P("req", "tp"),
        P("req", "tp"),
        P(),
        P(),
        P(),
        P(None, "req", None, "tp"),
        P("tp", None),
        P("tp"),
        P("tp"),
        P("tp"),
        P("req", "tp"),
        P("req"),
        P("req", "tp"),
        P("tp"),
        P(),
    )
    out_specs = P("req", "tp")
    return jax.shard_map(
        per_device, mesh=mesh, in_specs=in_specs, out_specs=out_specs, check_vma=False
    )
```

```python
import math

import jax
import jax.numpy as jnp
from jax import lax
from jax.sharding import PartitionSpec as P

HEAD_DIM = 128
NORM_EPS = 1e-05
PAIRWISE = 16


def swap(x, axis, step):
    n = lax.axis_size(axis)
    return lax.ppermute(x, axis, [(i, i ^ step) for i in range(n)])


def origins(axis):
    n, me = lax.axis_size(axis), lax.axis_index(axis)
    if n > PAIRWISE:
        return jnp.arange(n, dtype=jnp.int32)
    offsets = [0]
    step = n // 2
    while step:
        offsets = offsets + [o ^ step for o in offsets]
        step //= 2
    return jnp.array(offsets, dtype=jnp.int32) ^ me


def gather_rows(x, axis):
    n = lax.axis_size(axis)
    if n > PAIRWISE:
        return lax.all_gather(x, axis, axis=0, tiled=True)
    step = n // 2
    while step:
        x = jnp.concatenate([x, swap(x, axis, step)], axis=0)
        step //= 2
    return x


def fold_rows(x, axis):
    n = lax.axis_size(axis)
    if n > PAIRWISE:
        return lax.psum_scatter(x, axis, scatter_dimension=0, tiled=True)
    step = 1
    while step < n:
        half = x.shape[0] // 2
        x = x[:half] + swap(x[half:], axis, step)
        step *= 2
    return x


def sum_pairs(x, axis):
    n = lax.axis_size(axis)
    step = 1
    while step < n:
        x = (x.astype(jnp.float32) + swap(x, axis, step).astype(jnp.float32)).astype(x.dtype)
        step *= 2
    return x


def per_device(
    query,
    key_new,
    value_new,
    resid,
    lengths,
    owner,
    page_table,
    kv_pool,
    out_weight,
    out_bias,
    norm_gain,
    norm_bias,
    up_weight_t,
    up_bias,
    down_weight,
    down_bias,
    order,
):
    f32, bf16, i32 = jnp.float32, jnp.bfloat16, jnp.int32
    n_req = lax.axis_size("req")
    n_tp = lax.axis_size("tp")
    me = lax.axis_index("req")
    me_tp = lax.axis_index("tp")
    rows, cols = query.shape
    width = cols * n_tp
    heads = cols // HEAD_DIM
    pool_pages, page_len = kv_pool.shape[1], kv_pool.shape[2]
    positions = pool_pages * page_len
    scale = 1.0 / math.sqrt(HEAD_DIM)

    origin = origins("req")
    packed = jnp.concatenate([query, key_new, value_new, resid], axis=1)
    arrived = gather_rows(packed, "req")

    same = owner[:, None] == owner[None, :]
    ids = jnp.arange(owner.shape[0], dtype=i32)
    rank = jnp.sum((same & (ids[None, :] < ids[:, None])).astype(i32), axis=1)
    slots = jnp.arange(rows, dtype=i32)
    mine = (owner == me)[None, :] & (rank[None, :] == slots[:, None])
    mine_i = mine.astype(i32)
    own_len = jnp.sum(mine_i * lengths[None, :], axis=1)
    own_table = jnp.sum(mine_i[:, :, None] * page_table[None], axis=1)
    origin_ids = (origin[:, None] * rows + slots[None, :]).reshape(-1)
    own_id = jnp.sum(mine_i * ids[None, :], axis=1)
    take_hot = (own_id[:, None] == origin_ids[None, :]).astype(bf16)
    own = jnp.dot(take_hot, arrived, preferred_element_type=f32).astype(bf16)
    query_own, key_own, value_own, resid_own = (own[:, i * cols : (i + 1) * cols] for i in range(4))

    pos = jnp.arange(positions, dtype=i32)
    page, within = pos // page_len, pos % page_len
    entry = jnp.arange(page_table.shape[1], dtype=i32)
    start = entry * page_len
    hit = (own_table[:, :, None] == page[None, None, :]) & (
        start[None, :, None] + within[None, None, :] < own_len[:, None, None]
    )
    valid = jnp.any(hit, axis=1)

    keys = kv_pool[0].reshape(positions, cols)
    values = kv_pool[1].reshape(positions, cols)
    head_of = jnp.arange(cols, dtype=i32) // HEAD_DIM
    head_mask = head_of[None, :] == jnp.arange(heads, dtype=i32)[:, None]
    spread_q = jnp.where(head_mask[:, None, :], query_own[None], 0).reshape(heads * rows, cols)
    scores = (
        lax.dot_general(spread_q, keys, (((1,), (1,)), ((), ())), preferred_element_type=f32) * scale
    ).reshape(heads, rows, positions)
    scores = jnp.where(valid[None], scores, -jnp.inf)
    self_score = (
        jnp.sum(
            (query_own.astype(f32) * key_own.astype(f32)).reshape(rows, heads, HEAD_DIM), axis=-1
        ).T
        * scale
    )
    top = jnp.maximum(jnp.max(scores, axis=2), self_score)
    weights = jnp.exp(scores - top[:, :, None])
    self_weight = jnp.exp(self_score - top)
    total = jnp.sum(weights, axis=2) + self_weight
    numer = jnp.dot(
        weights.astype(bf16).reshape(heads * rows, positions), values, preferred_element_type=f32
    ).reshape(heads, rows, cols)
    numer = numer + self_weight.astype(bf16).astype(f32)[:, :, None] * value_own.astype(f32)[None]
    attn = jnp.sum(
        jnp.where(head_mask[:, None, :], numer / total[:, :, None], 0.0), axis=0
    ).astype(bf16)

    extra = resid_own.astype(f32) + out_bias.astype(f32)[None, :]
    partial = jnp.dot(attn, out_weight, preferred_element_type=f32)
    place = (jnp.arange(n_tp, dtype=i32) == me_tp)[None, :, None]
    partial = (
        partial.reshape(rows, n_tp, cols) + jnp.where(place, extra[:, None, :], 0.0)
    ).reshape(rows, width)
    stream = sum_pairs(partial, "tp").astype(bf16)
    stream_f = stream.astype(f32)
    mean = jnp.mean(stream_f, axis=1, keepdims=True)
    var = jnp.mean((stream_f - mean) ** 2, axis=1, keepdims=True)
    inverse = lax.rsqrt(var + NORM_EPS)
    stream_own = lax.dynamic_slice_in_dim(stream, me_tp * cols, cols, axis=1)
    normed = (
        (stream_own.astype(f32) - mean) * inverse * norm_gain.astype(f32)[None, :]
        + norm_bias.astype(f32)[None, :]
    ).astype(bf16)

    normed_all = gather_rows(normed, "req")
    slot_of = owner * rows + rank
    wanted = slot_of[order[origin_ids]]
    place_hot = (wanted[:, None] == origin_ids[None, :]).astype(bf16)
    mine_hot = (wanted[:, None] == (me * rows + slots)[None, :]).astype(bf16)
    normed_out = jnp.dot(place_hot, normed_all, preferred_element_type=f32).astype(bf16)
    hidden = lax.dot_general(
        normed_out, up_weight_t, (((1,), (1,)), ((), ())), preferred_element_type=f32
    ).astype(bf16)
    summed = sum_pairs(hidden, "tp").astype(f32)
    activated = jax.nn.gelu(summed + up_bias.astype(f32)[None, :], approximate=False).astype(bf16)
    feed = jnp.dot(activated, down_weight, preferred_element_type=f32)
    feed = feed + jnp.dot(mine_hot, stream_own, preferred_element_type=f32)
    mixed = fold_rows(feed, "req")
    return (mixed + down_bias.astype(f32)[None, :]).astype(bf16)


def solution(mesh):
    in_specs = (
        P("req", "tp"),
        P("req", "tp"),
        P("req", "tp"),
        P("req", "tp"),
        P(),
        P(),
        P(),
        P(None, "req", None, "tp"),
        P("tp", None),
        P("tp"),
        P("tp"),
        P("tp"),
        P("req", "tp"),
        P("req"),
        P("req", "tp"),
        P("tp"),
        P(),
    )
    out_specs = P("req", "tp")
    return jax.shard_map(
        per_device, mesh=mesh, in_specs=in_specs, out_specs=out_specs, check_vma=False
    )
```

```python
import functools
import math

import jax
import jax.numpy as jnp
from jax import lax
from jax.experimental import pallas as pl
from jax.experimental.pallas import tpu as pltpu
from jax.sharding import PartitionSpec as P

HEAD_DIM = 128
NORM_EPS = 1e-05
PAIRWISE = 16

REQ, TP = 8, 4
Z_STEPS = (0, 2, 4, 6)
Y_STEPS = (0, 1)
F32, BF16, I32 = jnp.float32, jnp.bfloat16, jnp.int32
VMEM = pl.BlockSpec(memory_space=pltpu.VMEM)
SMEM = pl.BlockSpec(memory_space=pltpu.SMEM)


def send(x, from_odd, req_step, tp_step):
    pairs = [
        (q * TP + t, (q ^ req_step) * TP + (t ^ tp_step))
        for q in range(REQ)
        for t in range(TP)
        if t % 2 == from_odd
    ]
    return lax.ppermute(x, ("req", "tp"), pairs)


def iota(shape, dim):
    return lax.broadcasted_iota(I32, shape, dim)


def onto_mxu(a, b):
    return jnp.dot(a, b, preferred_element_type=F32)


def nt_dot(a, b):
    return lax.dot_general(a, b, (((1,), (1,)), ((), ())), preferred_element_type=F32)


def hot(condition):
    return jnp.where(condition, 1.0, 0.0).astype(BF16)


def pack_kernel(query, key, value, resid, out):
    rows = query.shape[0]
    for i, ref in enumerate((query, key, value, resid)):
        out[i * rows : (i + 1) * rows, :] = ref[...]


def index_kernel(place, owner, order, lengths, table, pick1, pick2, valid, arrange, *, page_len):
    me = place[0]
    count = owner.shape[1]
    rows = count // REQ
    square = (count, count)
    down, across = iota(square, 0), iota(square, 1)
    same_place = down == across
    owner_row = owner[...]
    owner_col = jnp.sum(jnp.where(same_place, owner_row, 0), axis=1, keepdims=True)
    same_owner = owner_col == owner_row
    rank_row = jnp.sum(jnp.where(same_owner & (down < across), 1, 0), axis=0, keepdims=True)
    rank_col = jnp.sum(jnp.where(same_owner & (across < down), 1, 0), axis=1, keepdims=True)

    source = me ^ (across // (4 * rows))
    here = hot((down // rows == source) & (down % rows == across % rows))
    owner_there = onto_mxu(owner_row.astype(F32).astype(BF16), here).astype(I32)
    target = me ^ (2 * (down // (2 * rows)))
    pick1[...] = hot(
        ((down // rows) % 2 == across // (4 * rows))
        & (down % rows == (across // rows) % rows)
        & (owner_there == target)
    )

    half = (4 * rows, count)
    down_h, across_h = iota(half, 0), iota(half, 1)
    mine = hot((owner_row == me) & (rank_row == down_h % rows))
    came_from = me ^ (2 * (across // (2 * rows))) ^ ((across // rows) % 2)
    from_there = onto_mxu(mine, hot(down // rows == came_from))
    pick2[...] = hot((from_there > 0.5) & (down_h // rows == across_h % rows))

    shape = valid.shape
    slot = iota((shape[0], count), 0) % rows
    mine_v = hot((owner_row == me) & (rank_row == slot))
    table_v = onto_mxu(mine_v, table[...].astype(F32).astype(BF16)).astype(I32)
    length_v = jnp.sum(jnp.where(mine_v > 0.5, lengths[...], 0), axis=1, keepdims=True)
    position = iota(shape, 1)
    page, within = position // page_len, position % page_len
    seen = jnp.zeros(shape, F32)
    for j in range(table.shape[1]):
        inside = (table_v[:, j : j + 1] == page) & (within + j * page_len < length_v)
        seen = jnp.where(inside, 1.0, seen)
    valid[...] = seen

    row_at = me ^ (down // (4 * rows)) ^ (2 * ((down // rows) % 4))
    there = (across // rows == row_at) & (across % rows == down % rows)
    wanted = jnp.sum(jnp.where(there, order[...], 0), axis=1, keepdims=True)
    owner_at = me ^ (2 * (across // (2 * rows))) ^ ((across // rows) % 2)
    holds = (owner_col == owner_at) & (rank_col == across % rows)
    arrange[...] = onto_mxu(hot(wanted == across), hot(holds)).astype(BF16)


def route_kernel(place, pick, own, sibling, far_even, far_odd, *outs):
    @pl.when(place[1] == 1)
    def _():
        near = jnp.concatenate([sibling[...], own[...]], axis=1)
        far = jnp.concatenate([far_even[...], far_odd[...]], axis=1)
        moved = onto_mxu(pick[...], jnp.concatenate([near, far], axis=0)).astype(BF16)
        each = moved.shape[0] // len(outs)
        for i, out in enumerate(outs):
            out[...] = moved[i * each : (i + 1) * each]


def collect_kernel(place, pick, first, second, third, fourth, gain, bias, kept, passed):
    @pl.when(place[1] == 0)
    def _():
        rows = jnp.concatenate([first[...], second[...], third[...], fourth[...]], axis=0)
        own = onto_mxu(pick[...], rows).astype(BF16)
        half = kept.shape[1]
        used = own.shape[0]
        kept[...] = own[:, :half]
        passed[:used, :] = own[:, half:]
        passed[used : used + 1, :] = gain[...]
        passed[used + 1 : used + 2, :] = bias[...]


def attention_kernel(place, kept, passed, valid, pool, weight, out_bias, partial, *, rows):
    cols = kept.shape[1]
    heads = cols // HEAD_DIM
    used = 4 * rows
    scale = 1.0 / math.sqrt(HEAD_DIM)
    own = jnp.where(place[1] == 0, kept[...].astype(F32), passed[:used, :].astype(F32))
    query, key, value, resid = (own[i * rows : (i + 1) * rows] for i in range(4))

    def tile(x):
        return jnp.concatenate([x] * heads, axis=0)

    shape = (heads * rows, cols)
    in_head = iota(shape, 0) // rows == iota(shape, 1) // HEAD_DIM
    wide = jnp.where(in_head, tile(query), 0.0)
    positions = valid.shape[1]
    keys = pool[0].reshape(positions, cols)
    values = pool[1].reshape(positions, cols)
    scores = nt_dot(wide.astype(BF16), keys) * scale
    scores = jnp.where(valid[...] > 0.5, scores, -jnp.inf)
    self_score = jnp.sum(wide * tile(key), axis=1, keepdims=True) * scale
    top = jnp.maximum(jnp.max(scores, axis=1, keepdims=True), self_score)
    weights = jnp.exp(scores - top)
    self_weight = jnp.exp(self_score - top)
    total = jnp.sum(weights, axis=1, keepdims=True) + self_weight
    numer = onto_mxu(weights.astype(BF16), values)
    numer = numer + self_weight.astype(BF16).astype(F32) * tile(value)
    numer = jnp.where(in_head, numer / total, 0.0)
    attn = sum(numer[i * rows : (i + 1) * rows] for i in range(heads))
    attn = jnp.concatenate([attn, jnp.zeros_like(attn)], axis=0).astype(BF16)
    partial[...] = onto_mxu(attn, weight[...])[:rows]
    mine = pl.ds(pl.multiple_of(place[2] * cols, cols), cols)
    partial[:, mine] += resid + out_bias[...].astype(F32)


def norm_kernel(place, own, sibling, far_even, far_odd, passed, gain, bias, out, *, used):
    @pl.when(place[1] == 1)
    def _():
        whole = (sibling[...] + own[...]) + (far_even[...] + far_odd[...])
        stream = whole.astype(BF16).astype(F32)
        rows, width = stream.shape
        mean = jnp.sum(stream, axis=1, keepdims=True) / width
        var = jnp.sum((stream - mean) ** 2, axis=1, keepdims=True) / width
        mine = jnp.where(place[2] // 2 == 0, stream[:, : width // 2], stream[:, width // 2 :])
        gains = jnp.concatenate([passed[used : used + 1, :], gain[...]], axis=1).astype(F32)
        biases = jnp.concatenate([passed[used + 1 : used + 2, :], bias[...]], axis=1).astype(F32)
        normed = (mine - mean) * lax.rsqrt(var + NORM_EPS) * gains + biases
        out[...] = jnp.concatenate([normed, mine], axis=0).astype(BF16)


def up_kernel(place, arrange, first, second, third, fourth, moved, weight, out):
    @pl.when(place[1] == 1)
    def _():
        rows = jnp.concatenate([first[...], second[...], third[...], fourth[...]], axis=0)
        ordered = onto_mxu(arrange[...], rows).astype(BF16)
        half = moved.shape[1]
        hidden = nt_dot(ordered[:, :half], moved[...]) + nt_dot(ordered[:, half:], weight[...])
        out[...] = hidden.astype(BF16)


def down_kernel(place, arrange, near, far, up_bias, stream, weight, moved, first, second, *, rows):
    @pl.when(place[1] == 0)
    def _():
        hidden = near[...].astype(F32) + far[...].astype(F32) + up_bias[...].astype(F32)
        activated = (0.5 * hidden * (1.0 + lax.erf(hidden * math.sqrt(0.5)))).astype(BF16)
        kept = onto_mxu(arrange[:, :rows], stream[rows:, :])
        feed = jnp.concatenate(
            [onto_mxu(activated, weight[...]), onto_mxu(activated, moved[...])], axis=1
        )
        feed = feed + kept
        half = feed.shape[0] // 2
        first[...] = feed[:half]
        second[...] = feed[half:]


def call(kernel, shapes, args, smem, flops=0, **fixed):
    moved = sum(a.size * a.dtype.itemsize for a in args)
    return pl.pallas_call(
        functools.partial(kernel, **fixed) if fixed else kernel,
        out_shape=shapes,
        in_specs=[SMEM] * smem + [VMEM] * (len(args) - smem),
        out_specs=[VMEM] * len(shapes),
        compiler_params=pltpu.CompilerParams(vmem_limit_bytes=24 * 2**20),
        cost_estimate=pl.CostEstimate(flops=flops, bytes_accessed=moved, transcendentals=0),
    )(*args)


def on_pairs(
    query,
    key_new,
    value_new,
    resid,
    lengths,
    owner,
    page_table,
    kv_pool,
    out_weight,
    out_bias,
    norm_gain,
    norm_bias,
    up_weight_t,
    up_bias,
    down_weight,
    down_bias,
    order,
):
    rows, cols = query.shape
    width = cols * TP
    pool_pages, page_len = kv_pool.shape[1], kv_pool.shape[2]
    positions = pool_pages * page_len
    heads = cols // HEAD_DIM
    count = owner.shape[0]
    hidden = up_bias.shape[0]
    used = 4 * rows

    def arr(shape, dtype=BF16):
        return jax.ShapeDtypeStruct(shape, dtype)

    me, me_tp = lax.axis_index("req").astype(I32), lax.axis_index("tp").astype(I32)
    place = jnp.stack([me, me_tp % 2, me_tp])
    gain, bias = norm_gain[None, :], norm_bias[None, :]

    (packed,) = call(pack_kernel, [arr((used, cols))], [query, key_new, value_new, resid], 0)
    from_sibling = send(packed, 0, 0, 1)
    from_far_even = send(packed, 0, 1, 1)
    from_far_odd = send(packed, 1, 1, 0)
    up_moved = send(up_weight_t, 0, 0, 1)
    down_moved = send(down_weight, 1, 0, 1)
    pick1, pick2, valid, arrange = call(
        functools.partial(index_kernel, page_len=page_len),
        [
            arr((count, count)),
            arr((used, count)),
            arr((heads * rows, positions), F32),
            arr((count, count)),
        ],
        [place, owner[None, :], order[None, :], lengths[None, :], page_table],
        1,
    )
    outgoing = call(
        route_kernel,
        [arr((2 * rows, 2 * cols))] * len(Z_STEPS),
        [place, pick1, packed, from_sibling, from_far_even, from_far_odd],
        1,
    )
    arrived = [send(x, 1, step, 1) for x, step in zip(outgoing, Z_STEPS)]
    kept, passed = call(
        collect_kernel,
        [arr((used, cols)), arr((2 * used, cols))],
        [place, pick2, *arrived, gain, bias],
        1,
    )
    passed = send(passed, 0, 0, 1)

    (partial,) = call(
        attention_kernel,
        [arr((rows, width), F32)],
        [place, kept, passed, valid, kv_pool, out_weight, out_bias[None, :]],
        1,
        rows=rows,
    )
    (normed,) = call(
        norm_kernel,
        [arr((2 * rows, 2 * cols))],
        [
            place,
            partial,
            send(partial, 0, 0, 1),
            send(partial, 0, 0, 3),
            send(partial, 1, 0, 2),
            passed,
            gain,
            bias,
        ],
        1,
        used=used,
    )

    along_y = [send(normed, 1, step, 1) for step in Y_STEPS]
    two = jnp.concatenate([x[:rows] for x in along_y], axis=0)
    along_z = [send(two, 0, step, 1) for step in Z_STEPS]
    (partial_hidden,) = call(
        up_kernel,
        [arr((count, hidden))],
        [place, arrange, *along_z, up_moved, up_weight_t],
        1,
    )
    near = send(partial_hidden, 1, 0, 1)
    far = send(partial_hidden, 1, 0, 3)
    feeds = call(
        down_kernel,
        [arr((count // 2, 2 * cols), F32)] * 2,
        [place, arrange, near, far, up_bias[None, :], along_y[0], down_weight, down_moved],
        1,
        rows=rows,
    )

    halves = [send(x, 0, step, 1) for x, step in zip(feeds, Y_STEPS)]
    summed = halves[0] + halves[1]
    blocks = [
        send(summed[i * rows : (i + 1) * rows], 1, step, 1) for i, step in enumerate(Z_STEPS)
    ]
    final = (blocks[0] + blocks[1]) + (blocks[2] + blocks[3])
    other = send(final[:, cols:], 0, 0, 1)
    mine = jnp.where(place[1] == 0, final[:, :cols], other)
    return (mine + down_bias.astype(F32)[None, :]).astype(BF16)


def swap(x, axis, step):
    n = lax.axis_size(axis)
    return lax.ppermute(x, axis, [(i, i ^ step) for i in range(n)])


def origins(axis):
    n, me = lax.axis_size(axis), lax.axis_index(axis)
    if n > PAIRWISE:
        return jnp.arange(n, dtype=jnp.int32)
    offsets = [0]
    step = n // 2
    while step:
        offsets = offsets + [o ^ step for o in offsets]
        step //= 2
    return jnp.array(offsets, dtype=jnp.int32) ^ me


def gather_rows(x, axis):
    n = lax.axis_size(axis)
    if n > PAIRWISE:
        return lax.all_gather(x, axis, axis=0, tiled=True)
    step = n // 2
    while step:
        x = jnp.concatenate([x, swap(x, axis, step)], axis=0)
        step //= 2
    return x


def fold_rows(x, axis):
    n = lax.axis_size(axis)
    if n > PAIRWISE:
        return lax.psum_scatter(x, axis, scatter_dimension=0, tiled=True)
    step = 1
    while step < n:
        half = x.shape[0] // 2
        x = x[:half] + swap(x[half:], axis, step)
        step *= 2
    return x


def sum_pairs(x, axis):
    n = lax.axis_size(axis)
    step = 1
    while step < n:
        x = (x.astype(jnp.float32) + swap(x, axis, step).astype(jnp.float32)).astype(x.dtype)
        step *= 2
    return x


def on_any_mesh(
    query,
    key_new,
    value_new,
    resid,
    lengths,
    owner,
    page_table,
    kv_pool,
    out_weight,
    out_bias,
    norm_gain,
    norm_bias,
    up_weight_t,
    up_bias,
    down_weight,
    down_bias,
    order,
):
    f32, bf16, i32 = jnp.float32, jnp.bfloat16, jnp.int32
    n_req = lax.axis_size("req")
    n_tp = lax.axis_size("tp")
    me = lax.axis_index("req")
    me_tp = lax.axis_index("tp")
    rows, cols = query.shape
    width = cols * n_tp
    heads = cols // HEAD_DIM
    pool_pages, page_len = kv_pool.shape[1], kv_pool.shape[2]
    positions = pool_pages * page_len
    scale = 1.0 / math.sqrt(HEAD_DIM)

    origin = origins("req")
    packed = jnp.concatenate([query, key_new, value_new, resid], axis=1)
    arrived = gather_rows(packed, "req")

    same = owner[:, None] == owner[None, :]
    ids = jnp.arange(owner.shape[0], dtype=i32)
    rank = jnp.sum((same & (ids[None, :] < ids[:, None])).astype(i32), axis=1)
    slots = jnp.arange(rows, dtype=i32)
    mine = (owner == me)[None, :] & (rank[None, :] == slots[:, None])
    mine_i = mine.astype(i32)
    own_len = jnp.sum(mine_i * lengths[None, :], axis=1)
    own_table = jnp.sum(mine_i[:, :, None] * page_table[None], axis=1)
    origin_ids = (origin[:, None] * rows + slots[None, :]).reshape(-1)
    own_id = jnp.sum(mine_i * ids[None, :], axis=1)
    take_hot = (own_id[:, None] == origin_ids[None, :]).astype(bf16)
    own = jnp.dot(take_hot, arrived, preferred_element_type=f32).astype(bf16)
    query_own, key_own, value_own, resid_own = (own[:, i * cols : (i + 1) * cols] for i in range(4))

    pos = jnp.arange(positions, dtype=i32)
    page, within = pos // page_len, pos % page_len
    entry = jnp.arange(page_table.shape[1], dtype=i32)
    start = entry * page_len
    hit = (own_table[:, :, None] == page[None, None, :]) & (
        start[None, :, None] + within[None, None, :] < own_len[:, None, None]
    )
    valid = jnp.any(hit, axis=1)

    keys = kv_pool[0].reshape(positions, cols)
    values = kv_pool[1].reshape(positions, cols)
    head_of = jnp.arange(cols, dtype=i32) // HEAD_DIM
    head_mask = head_of[None, :] == jnp.arange(heads, dtype=i32)[:, None]
    spread_q = jnp.where(head_mask[:, None, :], query_own[None], 0).reshape(heads * rows, cols)
    scores = (
        lax.dot_general(spread_q, keys, (((1,), (1,)), ((), ())), preferred_element_type=f32) * scale
    ).reshape(heads, rows, positions)
    scores = jnp.where(valid[None], scores, -jnp.inf)
    self_score = (
        jnp.sum(
            (query_own.astype(f32) * key_own.astype(f32)).reshape(rows, heads, HEAD_DIM), axis=-1
        ).T
        * scale
    )
    top = jnp.maximum(jnp.max(scores, axis=2), self_score)
    weights = jnp.exp(scores - top[:, :, None])
    self_weight = jnp.exp(self_score - top)
    total = jnp.sum(weights, axis=2) + self_weight
    numer = jnp.dot(
        weights.astype(bf16).reshape(heads * rows, positions), values, preferred_element_type=f32
    ).reshape(heads, rows, cols)
    numer = numer + self_weight.astype(bf16).astype(f32)[:, :, None] * value_own.astype(f32)[None]
    attn = jnp.sum(
        jnp.where(head_mask[:, None, :], numer / total[:, :, None], 0.0), axis=0
    ).astype(bf16)

    extra = resid_own.astype(f32) + out_bias.astype(f32)[None, :]
    partial = jnp.dot(attn, out_weight, preferred_element_type=f32)
    place = (jnp.arange(n_tp, dtype=i32) == me_tp)[None, :, None]
    partial = (
        partial.reshape(rows, n_tp, cols) + jnp.where(place, extra[:, None, :], 0.0)
    ).reshape(rows, width)
    stream = sum_pairs(partial, "tp").astype(bf16)
    stream_f = stream.astype(f32)
    mean = jnp.mean(stream_f, axis=1, keepdims=True)
    var = jnp.mean((stream_f - mean) ** 2, axis=1, keepdims=True)
    inverse = lax.rsqrt(var + NORM_EPS)
    stream_own = lax.dynamic_slice_in_dim(stream, me_tp * cols, cols, axis=1)
    normed = (
        (stream_own.astype(f32) - mean) * inverse * norm_gain.astype(f32)[None, :]
        + norm_bias.astype(f32)[None, :]
    ).astype(bf16)

    normed_all = gather_rows(normed, "req")
    slot_of = owner * rows + rank
    wanted = slot_of[order[origin_ids]]
    place_hot = (wanted[:, None] == origin_ids[None, :]).astype(bf16)
    mine_hot = (wanted[:, None] == (me * rows + slots)[None, :]).astype(bf16)
    normed_out = jnp.dot(place_hot, normed_all, preferred_element_type=f32).astype(bf16)
    hidden = lax.dot_general(
        normed_out, up_weight_t, (((1,), (1,)), ((), ())), preferred_element_type=f32
    ).astype(bf16)
    summed = sum_pairs(hidden, "tp").astype(f32)
    activated = jax.nn.gelu(summed + up_bias.astype(f32)[None, :], approximate=False).astype(bf16)
    feed = jnp.dot(activated, down_weight, preferred_element_type=f32)
    feed = feed + jnp.dot(mine_hot, stream_own, preferred_element_type=f32)
    mixed = fold_rows(feed, "req")
    return (mixed + down_bias.astype(f32)[None, :]).astype(bf16)


def solution(mesh):
    pairs = mesh.shape["req"] == REQ and mesh.shape["tp"] == TP
    per_device = on_pairs if pairs else on_any_mesh
    in_specs = (
        P("req", "tp"),
        P("req", "tp"),
        P("req", "tp"),
        P("req", "tp"),
        P(),
        P(),
        P(),
        P(None, "req", None, "tp"),
        P("tp", None),
        P("tp"),
        P("tp"),
        P("tp"),
        P("req", "tp"),
        P("req"),
        P("req", "tp"),
        P("tp"),
        P(),
    )
    out_specs = P("req", "tp")
    return jax.shard_map(
        per_device, mesh=mesh, in_specs=in_specs, out_specs=out_specs, check_vma=False
    )
```

```python
import math

import jax
import jax.numpy as jnp
from jax import lax
from jax.sharding import PartitionSpec as P

HEAD_DIM = 128
NORM_EPS = 1e-05
PAIRWISE = 16


def swap(x, axis, step):
    n = lax.axis_size(axis)
    return lax.ppermute(x, axis, [(i, i ^ step) for i in range(n)])


def origins(axis):
    n, me = lax.axis_size(axis), lax.axis_index(axis)
    if n > PAIRWISE:
        return jnp.arange(n, dtype=jnp.int32)
    offsets = [0]
    step = n // 2
    while step:
        offsets = offsets + [o ^ step for o in offsets]
        step //= 2
    return jnp.array(offsets, dtype=jnp.int32) ^ me


def gather_rows(x, axis):
    n = lax.axis_size(axis)
    if n > PAIRWISE:
        return lax.all_gather(x, axis, axis=0, tiled=True)
    step = n // 2
    while step:
        x = jnp.concatenate([x, swap(x, axis, step)], axis=0)
        step //= 2
    return x


def fold_rows(x, axis):
    n = lax.axis_size(axis)
    if n > PAIRWISE:
        return lax.psum_scatter(x, axis, scatter_dimension=0, tiled=True)
    step = 1
    while step < n:
        half = x.shape[0] // 2
        x = x[:half] + swap(x[half:], axis, step)
        step *= 2
    return x


def sum_pairs(x, axis):
    n = lax.axis_size(axis)
    step = 1
    while step < n:
        x = (x.astype(jnp.float32) + swap(x, axis, 2 * step - 1).astype(jnp.float32)).astype(x.dtype)
        step *= 2
    return x


def gather_by_odd(x, even_cols):
    n_req, n_tp = lax.axis_size("req"), lax.axis_size("tp")
    odd = lax.axis_index("tp") % 2 == 1
    step = n_req // 2
    while step:
        pairs = [
            (q * n_tp + t, (q ^ step if t % 2 else q) * n_tp + t)
            for q in range(n_req)
            for t in range(n_tp)
        ]
        x = jnp.concatenate([x, lax.ppermute(x, ("req", "tp"), pairs)], axis=0)
        step //= 2
    passed = swap(x[:, :even_cols], "tp", 1)
    return jnp.where(odd, x[:, even_cols:], passed)


def per_device(
    query,
    key_new,
    value_new,
    resid,
    lengths,
    owner,
    page_table,
    kv_pool,
    out_weight,
    out_bias,
    norm_gain,
    norm_bias,
    up_weight_t,
    up_bias,
    down_weight,
    down_bias,
    order,
):
    f32, bf16, i32 = jnp.float32, jnp.bfloat16, jnp.int32
    n_req = lax.axis_size("req")
    n_tp = lax.axis_size("tp")
    me = lax.axis_index("req")
    me_tp = lax.axis_index("tp")
    rows, cols = query.shape
    width = cols * n_tp
    heads = cols // HEAD_DIM
    pool_pages, page_len = kv_pool.shape[1], kv_pool.shape[2]
    positions = pool_pages * page_len
    scale = 1.0 / math.sqrt(HEAD_DIM)

    origin = origins("req")
    packed = jnp.concatenate([query, key_new, value_new, resid], axis=1)
    arrived = gather_rows(packed, "req")

    same = owner[:, None] == owner[None, :]
    ids = jnp.arange(owner.shape[0], dtype=i32)
    rank = jnp.sum((same & (ids[None, :] < ids[:, None])).astype(i32), axis=1)
    slots = jnp.arange(rows, dtype=i32)
    mine = (owner == me)[None, :] & (rank[None, :] == slots[:, None])
    mine_i = mine.astype(i32)
    own_len = jnp.sum(mine_i * lengths[None, :], axis=1)
    own_table = jnp.sum(mine_i[:, :, None] * page_table[None], axis=1)
    origin_ids = (origin[:, None] * rows + slots[None, :]).reshape(-1)
    own_id = jnp.sum(mine_i * ids[None, :], axis=1)
    take_hot = (own_id[:, None] == origin_ids[None, :]).astype(bf16)
    own = jnp.dot(take_hot, arrived, preferred_element_type=f32).astype(bf16)
    query_own, key_own, value_own, resid_own = (own[:, i * cols : (i + 1) * cols] for i in range(4))

    pos = jnp.arange(positions, dtype=i32)
    page, within = pos // page_len, pos % page_len
    entry = jnp.arange(page_table.shape[1], dtype=i32)
    start = entry * page_len
    hit = (own_table[:, :, None] == page[None, None, :]) & (
        start[None, :, None] + within[None, None, :] < own_len[:, None, None]
    )
    valid = jnp.any(hit, axis=1)

    keys = kv_pool[0].reshape(positions, cols)
    values = kv_pool[1].reshape(positions, cols)
    head_of = jnp.arange(cols, dtype=i32) // HEAD_DIM
    head_mask = head_of[None, :] == jnp.arange(heads, dtype=i32)[:, None]
    spread_q = jnp.where(head_mask[:, None, :], query_own[None], 0).reshape(heads * rows, cols)
    scores = (
        lax.dot_general(spread_q, keys, (((1,), (1,)), ((), ())), preferred_element_type=f32) * scale
    ).reshape(heads, rows, positions)
    scores = jnp.where(valid[None], scores, -jnp.inf)
    self_score = (
        jnp.sum(
            (query_own.astype(f32) * key_own.astype(f32)).reshape(rows, heads, HEAD_DIM), axis=-1
        ).T
        * scale
    )
    top = jnp.maximum(jnp.max(scores, axis=2), self_score)
    weights = jnp.exp(scores - top[:, :, None])
    self_weight = jnp.exp(self_score - top)
    total = jnp.sum(weights, axis=2) + self_weight
    numer = jnp.dot(
        weights.astype(bf16).reshape(heads * rows, positions), values, preferred_element_type=f32
    ).reshape(heads, rows, cols)
    numer = numer + self_weight.astype(bf16).astype(f32)[:, :, None] * value_own.astype(f32)[None]
    attn = jnp.sum(
        jnp.where(head_mask[:, None, :], numer / total[:, :, None], 0.0), axis=0
    ).astype(bf16)

    extra = resid_own.astype(f32) + out_bias.astype(f32)[None, :]
    partial = jnp.dot(attn, out_weight, preferred_element_type=f32)
    place = (jnp.arange(n_tp, dtype=i32) == me_tp)[None, :, None]
    partial = (
        partial.reshape(rows, n_tp, cols) + jnp.where(place, extra[:, None, :], 0.0)
    ).reshape(rows, width)
    stream = sum_pairs(partial, "tp").astype(bf16)
    stream_f = stream.astype(f32)
    mean = jnp.mean(stream_f, axis=1, keepdims=True)
    var = jnp.mean((stream_f - mean) ** 2, axis=1, keepdims=True)
    inverse = lax.rsqrt(var + NORM_EPS)
    stream_own = lax.dynamic_slice_in_dim(stream, me_tp * cols, cols, axis=1)
    stream_pair = lax.dynamic_slice_in_dim(stream, (me_tp // 2) * 2 * cols, 2 * cols, axis=1)
    gain_pair, bias_pair = (
        jnp.concatenate([jnp.where(me_tp % 2 == 0, v, w), jnp.where(me_tp % 2 == 0, w, v)])
        for v, w in ((v, swap(v, "tp", 1)) for v in (norm_gain, norm_bias))
    )
    normed = (
        (stream_pair.astype(f32) - mean) * inverse * gain_pair.astype(f32)[None, :]
        + bias_pair.astype(f32)[None, :]
    ).astype(bf16)

    if n_req > PAIRWISE:
        own = lax.dynamic_slice_in_dim(normed, (me_tp % 2) * cols, cols, axis=1)
        normed_all = gather_rows(own, "req")
    else:
        normed_all = gather_by_odd(normed, cols)
    slot_of = owner * rows + rank
    wanted = slot_of[order[origin_ids]]
    place_hot = (wanted[:, None] == origin_ids[None, :]).astype(bf16)
    mine_hot = (wanted[:, None] == (me * rows + slots)[None, :]).astype(bf16)
    normed_out = jnp.dot(place_hot, normed_all, preferred_element_type=f32).astype(bf16)
    hidden = lax.dot_general(
        normed_out, up_weight_t, (((1,), (1,)), ((), ())), preferred_element_type=f32
    ).astype(bf16)
    summed = sum_pairs(hidden, "tp").astype(f32)
    activated = jax.nn.gelu(summed + up_bias.astype(f32)[None, :], approximate=False).astype(bf16)
    feed = jnp.dot(activated, down_weight, preferred_element_type=f32)
    feed = feed + jnp.dot(mine_hot, stream_own, preferred_element_type=f32)
    mixed = fold_rows(feed, "req")
    return (mixed + down_bias.astype(f32)[None, :]).astype(bf16)


def solution(mesh):
    in_specs = (
        P("req", "tp"),
        P("req", "tp"),
        P("req", "tp"),
        P("req", "tp"),
        P(),
        P(),
        P(),
        P(None, "req", None, "tp"),
        P("tp", None),
        P("tp"),
        P("tp"),
        P("tp"),
        P("req", "tp"),
        P("req"),
        P("req", "tp"),
        P("tp"),
        P(),
    )
    out_specs = P("req", "tp")
    return jax.shard_map(
        per_device, mesh=mesh, in_specs=in_specs, out_specs=out_specs, check_vma=False
    )
```

```python
import functools
import math

import jax
import jax.numpy as jnp
from jax import lax
from jax.experimental import pallas as pl
from jax.experimental.pallas import tpu as pltpu
from jax.sharding import PartitionSpec as P

HEAD_DIM = 128
NORM_EPS = 1e-05
PAIRWISE = 16
REQ, TP = 8, 4
F32, BF16, I32 = jnp.float32, jnp.bfloat16, jnp.int32
VMEM = pl.BlockSpec(memory_space=pltpu.VMEM)
SMEM = pl.BlockSpec(memory_space=pltpu.SMEM)
HBM = pl.BlockSpec(memory_space=pltpu.HBM)


def iota(shape, dim):
    return lax.broadcasted_iota(I32, shape, dim)


def onto_mxu(a, b):
    return jnp.dot(a, b, preferred_element_type=F32)


def nt_dot(a, b):
    return lax.dot_general(a, b, (((1,), (1,)), ((), ())), preferred_element_type=F32)


def hot(condition):
    return jnp.where(condition, 1.0, 0.0).astype(BF16)


def pile(parts):
    height = sum(p.shape[0] for p in parts)
    at, piled = 0, 0
    for p in parts:
        around = ((at, height - at - p.shape[0]),) + ((0, 0),) * (p.ndim - 1)
        piled += jnp.pad(p, around)
        at += p.shape[0]
    return piled


def row(vectors, i, cols):
    return vectors[i * cols : (i + 1) * cols][None, :]


def pack_kernel(place, numbers, fields_in, out):
    count = numbers.shape[1]
    rows = count // REQ
    fields = 4
    cols = fields_in.shape[1]
    shape = (REQ * fields, fields * rows)
    down, across = iota(shape, 0), iota(shape, 1)
    here = (count, fields * rows)
    of_mine = hot(iota(here, 0) == place[0] * rows + iota(here, 1) % rows)
    owner_of = onto_mxu(numbers[0:1, :].astype(F32).astype(BF16), of_mine).astype(I32)
    pick = hot((down % fields == across // rows) & (owner_of == down // fields))
    blocks = onto_mxu(pick, fields_in[...].astype(BF16)).astype(BF16)
    for d in range(REQ):
        block = blocks[d * fields : (d + 1) * fields]
        out[d, :fields, :] = block[:, : cols // 2]
        out[d, fields:, :] = block[:, cols // 2 :]


def index_kernel(
    place, numbers, pool, pick, valid, arrange, arrange_own, *, page_len
):
    del pool
    owner, order, lengths = (numbers[i : i + 1, :] for i in range(3))
    table = numbers[8:, :]
    me = place[0]
    count = owner.shape[1]
    rows = count // REQ
    square = (count, count)
    down, across = iota(square, 0), iota(square, 1)
    owner_row = owner
    same_place = down == across
    owner_col = jnp.sum(jnp.where(same_place, owner_row, 0), axis=1, keepdims=True)
    order_col = jnp.sum(jnp.where(same_place, order, 0), axis=1, keepdims=True)
    same_owner = owner_col == owner_row
    rank_row = jnp.sum(jnp.where(same_owner & (down < across), 1, 0), axis=0, keepdims=True)
    rank_col = jnp.sum(jnp.where(same_owner & (across < down), 1, 0), axis=1, keepdims=True)

    shape = pick.shape
    down_p, across_p = iota(shape, 0), iota(shape, 1)
    down_i = iota((shape[0], count), 0)
    mine = hot((owner_row == me) & (rank_row == down_i % rows))
    came = hot(iota((count, shape[1]), 0) // rows == iota((count, shape[1]), 1) // (2 * rows))
    from_there = onto_mxu(mine, came)
    pick[...] = hot((from_there > 0.5) & (down_p // rows == across_p % rows))

    shape = valid.shape
    slot = iota((shape[0], count), 0) % rows
    mine_v = hot((owner_row == me) & (rank_row == slot))
    table_v = nt_dot(mine_v, table.astype(F32).astype(BF16)).astype(I32)
    length_v = jnp.sum(jnp.where(mine_v > 0.5, lengths, 0), axis=1, keepdims=True)
    position = iota(shape, 1)
    page, within = position // page_len, position % page_len
    seen = jnp.zeros(shape, F32)
    for j in range(table.shape[0]):
        inside = (table_v[:, j : j + 1] == page) & (within + j * page_len < length_v)
        seen = jnp.where(inside, 1.0, seen)
    valid[...] = seen

    ordered = hot(order_col == across)
    shape = arrange.shape
    across_a = iota(shape, 1)
    holds = hot((owner_col == across_a // (2 * rows)) & (rank_col == across_a % rows))
    arrange[...] = onto_mxu(ordered, holds).astype(BF16)
    here = hot((owner_col == me) & (rank_col == iota(arrange_own.shape, 1)))
    arrange_own[...] = onto_mxu(ordered, here).astype(BF16)


def attention_kernel(place, arrived, pick, valid, vectors, pool, weight, partial, *, rows):
    half = arrived.shape[2]
    cols = 2 * half
    heads = cols // HEAD_DIM
    scale = 1.0 / math.sqrt(HEAD_DIM)
    came = arrived[...].reshape(-1, half)
    which = (iota(pick.shape, 1) // rows) % 2
    chosen = pick[...].astype(F32)
    own = jnp.concatenate(
        [onto_mxu(jnp.where(which == i, chosen, 0.0).astype(BF16), came) for i in range(2)], axis=1
    )
    query, key, value, resid = (own[i * rows : (i + 1) * rows] for i in range(4))

    def tile(x):
        return jnp.concatenate([x] * heads, axis=0)

    shape = (heads * rows, cols)
    in_head = iota(shape, 0) // rows == iota(shape, 1) // HEAD_DIM
    wide = jnp.where(in_head, tile(query), 0.0)
    positions = valid.shape[1]
    self_score = jnp.sum(wide * tile(key), axis=1, keepdims=True) * scale
    scores = nt_dot(wide.astype(BF16), pool[0].reshape(positions, cols)) * scale
    scores = jnp.where(valid[...] > 0.5, scores, -jnp.inf)
    top = jnp.maximum(jnp.max(scores, axis=1, keepdims=True), self_score)
    weights = jnp.exp(scores - top)
    self_weight = jnp.exp(self_score - top)
    total = jnp.sum(weights, axis=1, keepdims=True) + self_weight
    numer = onto_mxu(weights.astype(BF16), pool[1].reshape(positions, cols))
    numer = numer + self_weight.astype(BF16).astype(F32) * tile(value)
    numer = jnp.where(in_head, numer / total, 0.0)
    attn = sum(numer[i * rows : (i + 1) * rows] for i in range(heads))
    attn = jnp.concatenate([attn, jnp.zeros_like(attn)], axis=0).astype(BF16)
    partial[...] = onto_mxu(attn, weight[...])[:rows]
    mine = pl.ds(pl.multiple_of(place[1] * cols, cols), cols)
    partial[:, mine] += resid + row(vectors, 0, cols)


def norm_kernel(place, near, far, vectors, other, blocks, stream_own):
    stream = (near[...] + far[...]).astype(BF16).astype(F32)
    rows, width = stream.shape
    cols = width // TP
    mean = jnp.sum(stream, axis=1, keepdims=True) / width
    var = jnp.sum((stream - mean) ** 2, axis=1, keepdims=True) / width
    inverse = lax.rsqrt(var + NORM_EPS)
    core, chip = place[1] % 2, place[1] // 2
    parts = []
    for x in range(2):
        even, odd = (stream[:, (2 * x + c) * cols : (2 * x + c + 1) * cols] for c in range(2))
        part = jnp.where(core == 0, even, odd)
        gain, bias = (jnp.where(chip == x, row(vectors, i, cols), row(other, i, cols)) for i in (1, 2))
        parts.append((part, (part - mean) * inverse * gain + bias))
    stream_own[...] = jnp.where(chip == 0, parts[0][0], parts[1][0]).astype(BF16)
    block = jnp.concatenate([parts[0][1], parts[1][1]], axis=0).astype(BF16)
    for d in range(REQ):
        blocks[d] = block


def up_kernel(place, rows_in, arrange, weight, moved, out, *, rows):
    came = rows_in[...].reshape(-1, rows_in.shape[2])
    which = (iota(arrange.shape, 1) // rows) % 2
    chosen = arrange[...].astype(F32)
    chip = place[1] // 2

    def ordered(x):
        return onto_mxu(jnp.where(which == x, chosen, 0.0).astype(BF16), came).astype(BF16)

    hidden = nt_dot(ordered(chip), weight[...]) + nt_dot(ordered(1 - chip), moved[...])
    out[...] = hidden.astype(BF16)


def down_kernel(near, far, vectors, weight, arrange_own, stream_own, out):
    hidden = near[...].astype(F32) + far[...].astype(F32)
    hidden = hidden + vectors[vectors.shape[0] - hidden.shape[1] :][None, :]
    activated = (0.5 * hidden * (1.0 + lax.erf(hidden * math.sqrt(0.5)))).astype(BF16)
    feed = onto_mxu(activated, weight[...]) + onto_mxu(arrange_own[...], stream_own[...])
    rows = out.shape[1]
    for d in range(REQ):
        out[d] = feed[d * rows : (d + 1) * rows]


def call(kernel, shapes, specs, args, scratch=(), room=16, **fixed):
    moved = sum(a.size * a.dtype.itemsize for a in args)
    return pl.pallas_call(
        functools.partial(kernel, **fixed) if fixed else kernel,
        out_shape=shapes,
        in_specs=specs,
        out_specs=[VMEM] * len(shapes),
        scratch_shapes=scratch,
        compiler_params=pltpu.CompilerParams(vmem_limit_bytes=room * 2**20),
        cost_estimate=pl.CostEstimate(flops=0, bytes_accessed=moved, transcendentals=0),
    )(*args)


def trade(blocks):
    return lax.all_to_all(blocks, "req", 0, 0, tiled=True)


def on_pairs(
    query,
    key_new,
    value_new,
    resid,
    lengths,
    owner,
    page_table,
    kv_pool,
    out_weight,
    out_bias,
    norm_gain,
    norm_bias,
    up_weight_t,
    up_bias,
    down_weight,
    down_bias,
    order,
):
    rows, cols = query.shape
    width = cols * TP
    pool_pages, page_len = kv_pool.shape[1], kv_pool.shape[2]
    positions = pool_pages * page_len
    heads = cols // HEAD_DIM
    count = owner.shape[0]
    hidden = up_bias.shape[0]

    def arr(shape, dtype=BF16):
        return jax.ShapeDtypeStruct(shape, dtype)

    me, me_tp = lax.axis_index("req").astype(I32), lax.axis_index("tp").astype(I32)
    place = jnp.stack([me, me_tp])

    numbers = pile(
        [owner[None, :], order[None, :], lengths[None, :], jnp.zeros((5, count), I32), page_table.T]
    )
    fields = pile([x.astype(F32) for x in (query, key_new, value_new, resid)])
    (packed,) = call(
        pack_kernel,
        [arr((REQ, 8, cols // 2))],
        [SMEM, VMEM, VMEM],
        [place, numbers, fields],
    )
    up_moved = swap(up_weight_t, "tp", 2)
    arrived = trade(packed)
    vectors = pile([x.astype(F32) for x in (out_bias, norm_gain, norm_bias, down_bias, up_bias)])
    pick, valid, arrange, arrange_own = call(
        index_kernel,
        [
            arr((4 * rows, 2 * count)),
            arr((heads * rows, positions), F32),
            arr((count, 2 * count)),
            arr((count, rows)),
        ],
        [SMEM, VMEM, HBM],
        [place, numbers, kv_pool],
        page_len=page_len,
    )
    other = swap(vectors, "tp", 2)

    (partial,) = call(
        attention_kernel,
        [arr((rows, width), F32)],
        [SMEM] + [VMEM] * 6,
        [place, arrived, pick, valid, vectors, kv_pool, out_weight],
        rows=rows,
    )
    pair = partial + swap(partial, "tp", 1)
    blocks, stream_own = call(
        norm_kernel,
        [arr((REQ, 2 * rows, cols)), arr((rows, cols))],
        [SMEM] + [VMEM] * 4,
        [place, pair, swap(pair, "tp", 3), vectors, other],
    )

    (part,) = call(
        up_kernel,
        [arr((count, hidden))],
        [SMEM] + [VMEM] * 4,
        [place, trade(blocks), arrange, up_weight_t, up_moved],
        rows=rows,
    )
    (feed,) = call(
        down_kernel,
        [arr((REQ, rows, cols), F32)],
        [VMEM] * 6,
        [part, swap(part, "tp", 1), vectors, down_weight, arrange_own, stream_own],
    )
    return (jnp.sum(trade(feed), axis=0) + down_bias.astype(F32)[None, :]).astype(BF16)


def swap(x, axis, step):
    n = lax.axis_size(axis)
    return lax.ppermute(x, axis, [(i, i ^ step) for i in range(n)])


def origins(axis):
    n, me = lax.axis_size(axis), lax.axis_index(axis)
    if n > PAIRWISE:
        return jnp.arange(n, dtype=jnp.int32)
    offsets = [0]
    step = n // 2
    while step:
        offsets = offsets + [o ^ step for o in offsets]
        step //= 2
    return jnp.array(offsets, dtype=jnp.int32) ^ me


def gather_rows(x, axis):
    n = lax.axis_size(axis)
    if n > PAIRWISE:
        return lax.all_gather(x, axis, axis=0, tiled=True)
    step = n // 2
    while step:
        x = jnp.concatenate([x, swap(x, axis, step)], axis=0)
        step //= 2
    return x


def fold_rows(x, axis):
    n = lax.axis_size(axis)
    if n > PAIRWISE:
        return lax.psum_scatter(x, axis, scatter_dimension=0, tiled=True)
    step = 1
    while step < n:
        half = x.shape[0] // 2
        x = x[:half] + swap(x[half:], axis, step)
        step *= 2
    return x


def sum_pairs(x, axis):
    n = lax.axis_size(axis)
    step = 1
    while step < n:
        x = (x.astype(jnp.float32) + swap(x, axis, step).astype(jnp.float32)).astype(x.dtype)
        step *= 2
    return x


def on_any_mesh(
    query,
    key_new,
    value_new,
    resid,
    lengths,
    owner,
    page_table,
    kv_pool,
    out_weight,
    out_bias,
    norm_gain,
    norm_bias,
    up_weight_t,
    up_bias,
    down_weight,
    down_bias,
    order,
):
    f32, bf16, i32 = jnp.float32, jnp.bfloat16, jnp.int32
    n_req = lax.axis_size("req")
    n_tp = lax.axis_size("tp")
    me = lax.axis_index("req")
    me_tp = lax.axis_index("tp")
    rows, cols = query.shape
    width = cols * n_tp
    heads = cols // HEAD_DIM
    pool_pages, page_len = kv_pool.shape[1], kv_pool.shape[2]
    positions = pool_pages * page_len
    scale = 1.0 / math.sqrt(HEAD_DIM)

    origin = origins("req")
    packed = jnp.concatenate([query, key_new, value_new, resid], axis=1)
    arrived = gather_rows(packed, "req")

    same = owner[:, None] == owner[None, :]
    ids = jnp.arange(owner.shape[0], dtype=i32)
    rank = jnp.sum((same & (ids[None, :] < ids[:, None])).astype(i32), axis=1)
    slots = jnp.arange(rows, dtype=i32)
    mine = (owner == me)[None, :] & (rank[None, :] == slots[:, None])
    mine_i = mine.astype(i32)
    own_len = jnp.sum(mine_i * lengths[None, :], axis=1)
    own_table = jnp.sum(mine_i[:, :, None] * page_table[None], axis=1)
    origin_ids = (origin[:, None] * rows + slots[None, :]).reshape(-1)
    own_id = jnp.sum(mine_i * ids[None, :], axis=1)
    take_hot = (own_id[:, None] == origin_ids[None, :]).astype(bf16)
    own = jnp.dot(take_hot, arrived, preferred_element_type=f32).astype(bf16)
    query_own, key_own, value_own, resid_own = (own[:, i * cols : (i + 1) * cols] for i in range(4))

    pos = jnp.arange(positions, dtype=i32)
    page, within = pos // page_len, pos % page_len
    entry = jnp.arange(page_table.shape[1], dtype=i32)
    start = entry * page_len
    hit = (own_table[:, :, None] == page[None, None, :]) & (
        start[None, :, None] + within[None, None, :] < own_len[:, None, None]
    )
    valid = jnp.any(hit, axis=1)

    keys = kv_pool[0].reshape(positions, cols)
    values = kv_pool[1].reshape(positions, cols)
    head_of = jnp.arange(cols, dtype=i32) // HEAD_DIM
    head_mask = head_of[None, :] == jnp.arange(heads, dtype=i32)[:, None]
    spread_q = jnp.where(head_mask[:, None, :], query_own[None], 0).reshape(heads * rows, cols)
    scores = (
        lax.dot_general(spread_q, keys, (((1,), (1,)), ((), ())), preferred_element_type=f32) * scale
    ).reshape(heads, rows, positions)
    scores = jnp.where(valid[None], scores, -jnp.inf)
    self_score = (
        jnp.sum(
            (query_own.astype(f32) * key_own.astype(f32)).reshape(rows, heads, HEAD_DIM), axis=-1
        ).T
        * scale
    )
    top = jnp.maximum(jnp.max(scores, axis=2), self_score)
    weights = jnp.exp(scores - top[:, :, None])
    self_weight = jnp.exp(self_score - top)
    total = jnp.sum(weights, axis=2) + self_weight
    numer = jnp.dot(
        weights.astype(bf16).reshape(heads * rows, positions), values, preferred_element_type=f32
    ).reshape(heads, rows, cols)
    numer = numer + self_weight.astype(bf16).astype(f32)[:, :, None] * value_own.astype(f32)[None]
    attn = jnp.sum(
        jnp.where(head_mask[:, None, :], numer / total[:, :, None], 0.0), axis=0
    ).astype(bf16)

    extra = resid_own.astype(f32) + out_bias.astype(f32)[None, :]
    partial = jnp.dot(attn, out_weight, preferred_element_type=f32)
    place = (jnp.arange(n_tp, dtype=i32) == me_tp)[None, :, None]
    partial = (
        partial.reshape(rows, n_tp, cols) + jnp.where(place, extra[:, None, :], 0.0)
    ).reshape(rows, width)
    stream = sum_pairs(partial, "tp").astype(bf16)
    stream_f = stream.astype(f32)
    mean = jnp.mean(stream_f, axis=1, keepdims=True)
    var = jnp.mean((stream_f - mean) ** 2, axis=1, keepdims=True)
    inverse = lax.rsqrt(var + NORM_EPS)
    stream_own = lax.dynamic_slice_in_dim(stream, me_tp * cols, cols, axis=1)
    normed = (
        (stream_own.astype(f32) - mean) * inverse * norm_gain.astype(f32)[None, :]
        + norm_bias.astype(f32)[None, :]
    ).astype(bf16)

    normed_all = gather_rows(normed, "req")
    slot_of = owner * rows + rank
    wanted = slot_of[order[origin_ids]]
    place_hot = (wanted[:, None] == origin_ids[None, :]).astype(bf16)
    mine_hot = (wanted[:, None] == (me * rows + slots)[None, :]).astype(bf16)
    normed_out = jnp.dot(place_hot, normed_all, preferred_element_type=f32).astype(bf16)
    hidden = lax.dot_general(
        normed_out, up_weight_t, (((1,), (1,)), ((), ())), preferred_element_type=f32
    ).astype(bf16)
    summed = sum_pairs(hidden, "tp").astype(f32)
    activated = jax.nn.gelu(summed + up_bias.astype(f32)[None, :], approximate=False).astype(bf16)
    feed = jnp.dot(activated, down_weight, preferred_element_type=f32)
    feed = feed + jnp.dot(mine_hot, stream_own, preferred_element_type=f32)
    mixed = fold_rows(feed, "req")
    return (mixed + down_bias.astype(f32)[None, :]).astype(bf16)


def solution(mesh):
    pairs = mesh.shape["req"] == REQ and mesh.shape["tp"] == TP
    per_device = on_pairs if pairs else on_any_mesh
    in_specs = (
        P("req", "tp"),
        P("req", "tp"),
        P("req", "tp"),
        P("req", "tp"),
        P(),
        P(),
        P(),
        P(None, "req", None, "tp"),
        P("tp", None),
        P("tp"),
        P("tp"),
        P("tp"),
        P("req", "tp"),
        P("req"),
        P("req", "tp"),
        P("tp"),
        P(),
    )
    out_specs = P("req", "tp")
    return jax.shard_map(
        per_device, mesh=mesh, in_specs=in_specs, out_specs=out_specs, check_vma=False
    )
```

```python
import functools
import math

import jax
import jax.numpy as jnp
from jax import lax
from jax.experimental import pallas as pl
from jax.experimental.pallas import tpu as pltpu
from jax.sharding import PartitionSpec as P

HEAD_DIM = 128
NORM_EPS = 1e-05
PAIRWISE = 16
REQ, TP = 8, 4
F32, BF16, I32 = jnp.float32, jnp.bfloat16, jnp.int32
VMEM = pl.BlockSpec(memory_space=pltpu.VMEM)
HBM = pl.BlockSpec(memory_space=pltpu.HBM)


def iota(shape, dim):
    return lax.broadcasted_iota(I32, shape, dim)


def onto_mxu(a, b):
    return jnp.dot(a, b, preferred_element_type=F32)


def nt_dot(a, b):
    return lax.dot_general(a, b, (((1,), (1,)), ((), ())), preferred_element_type=F32)


def hot(condition):
    return jnp.where(condition, 1.0, 0.0).astype(BF16)


def pile(parts):
    height = sum(p.shape[0] for p in parts)
    at, piled = 0, 0
    for p in parts:
        around = ((at, height - at - p.shape[0]),) + ((0, 0),) * (p.ndim - 1)
        piled += jnp.pad(p, around)
        at += p.shape[0]
    return piled


def row(vectors, i, cols):
    return vectors[i * cols : (i + 1) * cols][None, :]


def pack_kernel(place, fields_in, out):
    fields = 4
    used = fields_in.shape[0] - 1
    rows = used // fields
    count = REQ * rows
    cols = fields_in.shape[1]
    shape = (REQ * fields, used)
    down, across = iota(shape, 0), iota(shape, 1)
    here = (count, used)
    of_mine = hot(iota(here, 0) == place[0:1, 0:1] * rows + iota(here, 1) % rows)
    owner = fields_in[used : used + 1, :count].astype(BF16)
    owner_of = onto_mxu(owner, of_mine).astype(I32)
    pick = hot((down % fields == across // rows) & (owner_of == down // fields))
    blocks = onto_mxu(pick, fields_in[:used, :].astype(BF16)).astype(BF16)
    for d in range(REQ):
        block = blocks[d * fields : (d + 1) * fields]
        out[d, :fields, :] = block[:, : cols // 2]
        out[d, fields:, :] = block[:, cols // 2 :]


def index_kernel(
    place, numbers, pool, out_weight, pick, valid, arrange, arrange_own, *, page_len
):
    del pool, out_weight
    owner, order, lengths = (numbers[i : i + 1, :] for i in range(3))
    table = numbers[8:, :]
    me = place[0:1, 0:1]
    count = owner.shape[1]
    rows = count // REQ
    square = (count, count)
    down, across = iota(square, 0), iota(square, 1)
    owner_row = owner
    same_place = down == across
    owner_col = jnp.sum(jnp.where(same_place, owner_row, 0), axis=1, keepdims=True)
    order_col = jnp.sum(jnp.where(same_place, order, 0), axis=1, keepdims=True)
    same_owner = owner_col == owner_row
    rank_row = jnp.sum(jnp.where(same_owner & (down < across), 1, 0), axis=0, keepdims=True)
    rank_col = jnp.sum(jnp.where(same_owner & (across < down), 1, 0), axis=1, keepdims=True)

    shape = pick.shape
    down_p, across_p = iota(shape, 0), iota(shape, 1)
    down_i = iota((shape[0], count), 0)
    mine = hot((owner_row == me) & (rank_row == down_i % rows))
    came = hot(iota((count, shape[1]), 0) // rows == iota((count, shape[1]), 1) // (2 * rows))
    from_there = onto_mxu(mine, came)
    pick[...] = hot((from_there > 0.5) & (down_p // rows == across_p % rows))

    shape = valid.shape
    slot = iota((shape[0], count), 0) % rows
    mine_v = hot((owner_row == me) & (rank_row == slot))
    table_v = nt_dot(mine_v, table.astype(F32).astype(BF16)).astype(I32)
    length_v = jnp.sum(jnp.where(mine_v > 0.5, lengths, 0), axis=1, keepdims=True)
    position = iota(shape, 1)
    page, within = position // page_len, position % page_len
    seen = jnp.zeros(shape, F32)
    for j in range(table.shape[0]):
        inside = (table_v[:, j : j + 1] == page) & (within + j * page_len < length_v)
        seen = jnp.where(inside, 1.0, seen)
    valid[...] = seen

    ordered = hot(order_col == across)
    holds = hot((owner_col == across // rows) & (rank_col == across % rows))
    arrange[...] = onto_mxu(ordered, holds).astype(BF16)
    here = hot((owner_col == me) & (rank_col == iota(arrange_own.shape, 1)))
    arrange_own[...] = onto_mxu(ordered, here).astype(BF16)


def attention_kernel(place, arrived, pick, valid, vectors, pool, weight, partial, *, rows):
    half = arrived.shape[2]
    cols = 2 * half
    heads = cols // HEAD_DIM
    scale = 1.0 / math.sqrt(HEAD_DIM)
    came = arrived[...].reshape(-1, half)
    which = (iota(pick.shape, 1) // rows) % 2
    chosen = pick[...].astype(F32)
    own = jnp.concatenate(
        [onto_mxu(jnp.where(which == i, chosen, 0.0).astype(BF16), came) for i in range(2)], axis=1
    )
    query, key, value, resid = (own[i * rows : (i + 1) * rows] for i in range(4))

    def tile(x):
        return jnp.concatenate([x] * heads, axis=0)

    shape = (heads * rows, cols)
    in_head = iota(shape, 0) // rows == iota(shape, 1) // HEAD_DIM
    wide = jnp.where(in_head, tile(query), 0.0)
    positions = valid.shape[1]
    self_score = jnp.sum(wide * tile(key), axis=1, keepdims=True) * scale
    scores = nt_dot(wide.astype(BF16), pool[0].reshape(positions, cols)) * scale
    scores = jnp.where(valid[...] > 0.5, scores, -jnp.inf)
    top = jnp.maximum(jnp.max(scores, axis=1, keepdims=True), self_score)
    weights = jnp.exp(scores - top)
    self_weight = jnp.exp(self_score - top)
    total = jnp.sum(weights, axis=1, keepdims=True) + self_weight
    numer = onto_mxu(weights.astype(BF16), pool[1].reshape(positions, cols))
    numer = numer + self_weight.astype(BF16).astype(F32) * tile(value)
    numer = jnp.where(in_head, numer / total, 0.0)
    attn = sum(numer[i * rows : (i + 1) * rows] for i in range(heads))
    attn = jnp.concatenate([attn, jnp.zeros_like(attn)], axis=0).astype(BF16)
    projected = onto_mxu(attn, weight[...])[:rows]
    extra = resid + row(vectors, 0, cols)
    for t in range(TP):
        mine = jnp.where(place[1:2, 0:1] == t, extra, 0.0)
        partial[:, t * cols : (t + 1) * cols] = projected[:, t * cols : (t + 1) * cols] + mine


def norm_kernel(place, near, far, vectors, blocks, stream_own):
    stream = (near[...] + far[...]).astype(BF16).astype(F32)
    width = stream.shape[1]
    cols = width // TP
    mean = jnp.sum(stream, axis=1, keepdims=True) / width
    var = jnp.sum((stream - mean) ** 2, axis=1, keepdims=True) / width
    own = stream[:, :cols]
    for t in range(1, TP):
        own = jnp.where(place[1:2, 0:1] == t, stream[:, t * cols : (t + 1) * cols], own)
    stream_own[...] = own.astype(BF16)
    gain, bias = row(vectors, 1, cols), row(vectors, 2, cols)
    block = ((own - mean) * lax.rsqrt(var + NORM_EPS) * gain + bias).astype(BF16)
    for d in range(REQ):
        blocks[d] = block


def up_kernel(rows_in, arrange, weight, out):
    came = rows_in[...].reshape(-1, rows_in.shape[2])
    ordered = onto_mxu(arrange[...], came).astype(BF16)
    out[...] = nt_dot(ordered, weight[...]).astype(BF16)


def down_kernel(near, far, vectors, weight, arrange_own, stream_own, out):
    hidden = near[...].astype(F32) + far[...].astype(F32)
    hidden = hidden + vectors[vectors.shape[0] - hidden.shape[1] :][None, :]
    activated = (0.5 * hidden * (1.0 + lax.erf(hidden * math.sqrt(0.5)))).astype(BF16)
    feed = onto_mxu(activated, weight[...]) + onto_mxu(arrange_own[...], stream_own[...])
    rows = out.shape[1]
    for d in range(REQ):
        out[d] = feed[d * rows : (d + 1) * rows]


def call(kernel, shapes, specs, args, scratch=(), room=16, **fixed):
    moved = sum(a.size * a.dtype.itemsize for a in args)
    return pl.pallas_call(
        functools.partial(kernel, **fixed) if fixed else kernel,
        out_shape=shapes,
        in_specs=specs,
        out_specs=[VMEM] * len(shapes),
        scratch_shapes=scratch,
        compiler_params=pltpu.CompilerParams(vmem_limit_bytes=room * 2**20),
        cost_estimate=pl.CostEstimate(flops=0, bytes_accessed=moved, transcendentals=0),
    )(*args)


def trade(blocks):
    return lax.all_to_all(blocks, "req", 0, 0, tiled=True)


def on_pairs(
    query,
    key_new,
    value_new,
    resid,
    lengths,
    owner,
    page_table,
    kv_pool,
    out_weight,
    out_bias,
    norm_gain,
    norm_bias,
    up_weight_t,
    up_bias,
    down_weight,
    down_bias,
    order,
):
    rows, cols = query.shape
    width = cols * TP
    pool_pages, page_len = kv_pool.shape[1], kv_pool.shape[2]
    positions = pool_pages * page_len
    heads = cols // HEAD_DIM
    count = owner.shape[0]
    hidden = up_bias.shape[0]

    def arr(shape, dtype=BF16):
        return jax.ShapeDtypeStruct(shape, dtype)

    position = jnp.stack([lax.axis_index("req"), lax.axis_index("tp")]).astype(I32)
    place = jnp.broadcast_to(position[:, None], (2, HEAD_DIM))

    owner_f = jnp.pad(owner.astype(F32)[None, :], ((0, 0), (0, cols - count)))
    fields = pile([x.astype(F32) for x in (query, key_new, value_new, resid)] + [owner_f])
    (packed,) = call(pack_kernel, [arr((REQ, 8, cols // 2))], [VMEM] * 2, [place, fields])
    arrived = trade(packed)
    numbers = pile(
        [owner[None, :], order[None, :], lengths[None, :], jnp.zeros((5, count), I32), page_table.T]
    )
    vectors = pile([x.astype(F32) for x in (out_bias, norm_gain, norm_bias, down_bias, up_bias)])
    pick, valid, arrange, arrange_own = call(
        index_kernel,
        [
            arr((4 * rows, 2 * count)),
            arr((heads * rows, positions), F32),
            arr((count, count)),
            arr((count, rows)),
        ],
        [VMEM, VMEM, HBM, HBM],
        [place, numbers, kv_pool, out_weight],
        page_len=page_len,
    )

    (partial,) = call(
        attention_kernel,
        [arr((rows, width), F32)],
        [VMEM] * 7,
        [place, arrived, pick, valid, vectors, kv_pool, out_weight],
        rows=rows,
    )
    pair = partial + swap(partial, "tp", 1)
    blocks, stream_own = call(
        norm_kernel,
        [arr((REQ, rows, cols)), arr((rows, cols))],
        [VMEM] * 4,
        [place, pair, swap(pair, "tp", 3), vectors],
    )

    (part,) = call(
        up_kernel,
        [arr((count, hidden))],
        [VMEM] * 3,
        [trade(blocks), arrange, up_weight_t],
    )
    part = (part.astype(F32) + swap(part, "tp", 1).astype(F32)).astype(BF16)
    (feed,) = call(
        down_kernel,
        [arr((REQ, rows, cols), F32)],
        [VMEM] * 6,
        [part, swap(part, "tp", 3), vectors, down_weight, arrange_own, stream_own],
    )
    return (jnp.sum(trade(feed), axis=0) + row(vectors, 3, cols)).astype(BF16)


def swap(x, axis, step):
    n = lax.axis_size(axis)
    return lax.ppermute(x, axis, [(i, i ^ step) for i in range(n)])


def origins(axis):
    n, me = lax.axis_size(axis), lax.axis_index(axis)
    if n > PAIRWISE:
        return jnp.arange(n, dtype=jnp.int32)
    offsets = [0]
    step = n // 2
    while step:
        offsets = offsets + [o ^ step for o in offsets]
        step //= 2
    return jnp.array(offsets, dtype=jnp.int32) ^ me


def gather_rows(x, axis):
    n = lax.axis_size(axis)
    if n > PAIRWISE:
        return lax.all_gather(x, axis, axis=0, tiled=True)
    step = n // 2
    while step:
        x = jnp.concatenate([x, swap(x, axis, step)], axis=0)
        step //= 2
    return x


def fold_rows(x, axis):
    n = lax.axis_size(axis)
    if n > PAIRWISE:
        return lax.psum_scatter(x, axis, scatter_dimension=0, tiled=True)
    step = 1
    while step < n:
        half = x.shape[0] // 2
        x = x[:half] + swap(x[half:], axis, step)
        step *= 2
    return x


def sum_pairs(x, axis):
    n = lax.axis_size(axis)
    step = 1
    while step < n:
        x = (x.astype(jnp.float32) + swap(x, axis, step).astype(jnp.float32)).astype(x.dtype)
        step *= 2
    return x


def on_any_mesh(
    query,
    key_new,
    value_new,
    resid,
    lengths,
    owner,
    page_table,
    kv_pool,
    out_weight,
    out_bias,
    norm_gain,
    norm_bias,
    up_weight_t,
    up_bias,
    down_weight,
    down_bias,
    order,
):
    f32, bf16, i32 = jnp.float32, jnp.bfloat16, jnp.int32
    n_req = lax.axis_size("req")
    n_tp = lax.axis_size("tp")
    me = lax.axis_index("req")
    me_tp = lax.axis_index("tp")
    rows, cols = query.shape
    width = cols * n_tp
    heads = cols // HEAD_DIM
    pool_pages, page_len = kv_pool.shape[1], kv_pool.shape[2]
    positions = pool_pages * page_len
    scale = 1.0 / math.sqrt(HEAD_DIM)

    origin = origins("req")
    packed = jnp.concatenate([query, key_new, value_new, resid], axis=1)
    arrived = gather_rows(packed, "req")

    same = owner[:, None] == owner[None, :]
    ids = jnp.arange(owner.shape[0], dtype=i32)
    rank = jnp.sum((same & (ids[None, :] < ids[:, None])).astype(i32), axis=1)
    slots = jnp.arange(rows, dtype=i32)
    mine = (owner == me)[None, :] & (rank[None, :] == slots[:, None])
    mine_i = mine.astype(i32)
    own_len = jnp.sum(mine_i * lengths[None, :], axis=1)
    own_table = jnp.sum(mine_i[:, :, None] * page_table[None], axis=1)
    origin_ids = (origin[:, None] * rows + slots[None, :]).reshape(-1)
    own_id = jnp.sum(mine_i * ids[None, :], axis=1)
    take_hot = (own_id[:, None] == origin_ids[None, :]).astype(bf16)
    own = jnp.dot(take_hot, arrived, preferred_element_type=f32).astype(bf16)
    query_own, key_own, value_own, resid_own = (own[:, i * cols : (i + 1) * cols] for i in range(4))

    pos = jnp.arange(positions, dtype=i32)
    page, within = pos // page_len, pos % page_len
    entry = jnp.arange(page_table.shape[1], dtype=i32)
    start = entry * page_len
    hit = (own_table[:, :, None] == page[None, None, :]) & (
        start[None, :, None] + within[None, None, :] < own_len[:, None, None]
    )
    valid = jnp.any(hit, axis=1)

    keys = kv_pool[0].reshape(positions, cols)
    values = kv_pool[1].reshape(positions, cols)
    head_of = jnp.arange(cols, dtype=i32) // HEAD_DIM
    head_mask = head_of[None, :] == jnp.arange(heads, dtype=i32)[:, None]
    spread_q = jnp.where(head_mask[:, None, :], query_own[None], 0).reshape(heads * rows, cols)
    scores = (
        lax.dot_general(spread_q, keys, (((1,), (1,)), ((), ())), preferred_element_type=f32) * scale
    ).reshape(heads, rows, positions)
    scores = jnp.where(valid[None], scores, -jnp.inf)
    self_score = (
        jnp.sum(
            (query_own.astype(f32) * key_own.astype(f32)).reshape(rows, heads, HEAD_DIM), axis=-1
        ).T
        * scale
    )
    top = jnp.maximum(jnp.max(scores, axis=2), self_score)
    weights = jnp.exp(scores - top[:, :, None])
    self_weight = jnp.exp(self_score - top)
    total = jnp.sum(weights, axis=2) + self_weight
    numer = jnp.dot(
        weights.astype(bf16).reshape(heads * rows, positions), values, preferred_element_type=f32
    ).reshape(heads, rows, cols)
    numer = numer + self_weight.astype(bf16).astype(f32)[:, :, None] * value_own.astype(f32)[None]
    attn = jnp.sum(
        jnp.where(head_mask[:, None, :], numer / total[:, :, None], 0.0), axis=0
    ).astype(bf16)

    extra = resid_own.astype(f32) + out_bias.astype(f32)[None, :]
    partial = jnp.dot(attn, out_weight, preferred_element_type=f32)
    place = (jnp.arange(n_tp, dtype=i32) == me_tp)[None, :, None]
    partial = (
        partial.reshape(rows, n_tp, cols) + jnp.where(place, extra[:, None, :], 0.0)
    ).reshape(rows, width)
    stream = sum_pairs(partial, "tp").astype(bf16)
    stream_f = stream.astype(f32)
    mean = jnp.mean(stream_f, axis=1, keepdims=True)
    var = jnp.mean((stream_f - mean) ** 2, axis=1, keepdims=True)
    inverse = lax.rsqrt(var + NORM_EPS)
    stream_own = lax.dynamic_slice_in_dim(stream, me_tp * cols, cols, axis=1)
    normed = (
        (stream_own.astype(f32) - mean) * inverse * norm_gain.astype(f32)[None, :]
        + norm_bias.astype(f32)[None, :]
    ).astype(bf16)

    normed_all = gather_rows(normed, "req")
    slot_of = owner * rows + rank
    wanted = slot_of[order[origin_ids]]
    place_hot = (wanted[:, None] == origin_ids[None, :]).astype(bf16)
    mine_hot = (wanted[:, None] == (me * rows + slots)[None, :]).astype(bf16)
    normed_out = jnp.dot(place_hot, normed_all, preferred_element_type=f32).astype(bf16)
    hidden = lax.dot_general(
        normed_out, up_weight_t, (((1,), (1,)), ((), ())), preferred_element_type=f32
    ).astype(bf16)
    summed = sum_pairs(hidden, "tp").astype(f32)
    activated = jax.nn.gelu(summed + up_bias.astype(f32)[None, :], approximate=False).astype(bf16)
    feed = jnp.dot(activated, down_weight, preferred_element_type=f32)
    feed = feed + jnp.dot(mine_hot, stream_own, preferred_element_type=f32)
    mixed = fold_rows(feed, "req")
    return (mixed + down_bias.astype(f32)[None, :]).astype(bf16)


def solution(mesh):
    pairs = mesh.shape["req"] == REQ and mesh.shape["tp"] == TP
    per_device = on_pairs if pairs else on_any_mesh
    in_specs = (
        P("req", "tp"),
        P("req", "tp"),
        P("req", "tp"),
        P("req", "tp"),
        P(),
        P(),
        P(),
        P(None, "req", None, "tp"),
        P("tp", None),
        P("tp"),
        P("tp"),
        P("tp"),
        P("req", "tp"),
        P("req"),
        P("req", "tp"),
        P("tp"),
        P(),
    )
    out_specs = P("req", "tp")
    return jax.shard_map(
        per_device, mesh=mesh, in_specs=in_specs, out_specs=out_specs, check_vma=False
    )
```

```python
import functools
import math

import jax
import jax.numpy as jnp
from jax import lax
from jax.experimental import pallas as pl
from jax.experimental.pallas import tpu as pltpu
from jax.sharding import PartitionSpec as P

HEAD_DIM = 128
NORM_EPS = 1e-05
PAIRWISE = 16
REQ, TP = 8, 4
WEIGHT_PARTS = 4
ATTENTION_ROOM = 63.3
F32, BF16, I32 = jnp.float32, jnp.bfloat16, jnp.int32
VMEM = pl.BlockSpec(memory_space=pltpu.VMEM)
HBM = pl.BlockSpec(memory_space=pltpu.HBM)


def iota(shape, dim):
    return lax.broadcasted_iota(I32, shape, dim)


def onto_mxu(a, b):
    return jnp.dot(a, b, preferred_element_type=F32)


def nt_dot(a, b):
    return lax.dot_general(a, b, (((1,), (1,)), ((), ())), preferred_element_type=F32)


def hot(condition):
    return jnp.where(condition, 1.0, 0.0).astype(BF16)


def pile(parts):
    height = sum(p.shape[0] for p in parts)
    at, piled = 0, 0
    for p in parts:
        around = ((at, height - at - p.shape[0]),) + ((0, 0),) * (p.ndim - 1)
        piled += jnp.pad(p, around)
        at += p.shape[0]
    return piled


def row(vectors, i, cols):
    return vectors[i * cols : (i + 1) * cols][None, :]


def pack_kernel(place, fields_in, out):
    fields = 4
    used = fields_in.shape[0] - 1
    rows = used // fields
    count = REQ * rows
    cols = fields_in.shape[1]
    shape = (REQ * fields, used)
    down, across = iota(shape, 0), iota(shape, 1)
    here = (count, used)
    of_mine = hot(iota(here, 0) == place[0:1, 0:1] * rows + iota(here, 1) % rows)
    owner = fields_in[used : used + 1, :count].astype(BF16)
    owner_of = onto_mxu(owner, of_mine).astype(I32)
    pick = hot((down % fields == across // rows) & (owner_of == down // fields))
    blocks = onto_mxu(pick, fields_in[:used, :].astype(BF16)).astype(BF16)
    for d in range(REQ):
        block = blocks[d * fields : (d + 1) * fields]
        out[d, :fields, :] = block[:, : cols // 2]
        out[d, fields:, :] = block[:, cols // 2 :]


def index_kernel(place, numbers, pick, valid, arrange, arrange_own, *, page_len):
    owner, order, lengths = (numbers[i : i + 1, :] for i in range(3))
    table = numbers[8:, :]
    me = place[0:1, 0:1]
    count = owner.shape[1]
    rows = count // REQ
    square = (count, count)
    down, across = iota(square, 0), iota(square, 1)
    owner_row = owner
    same_place = down == across
    owner_col = jnp.sum(jnp.where(same_place, owner_row, 0), axis=1, keepdims=True)
    order_col = jnp.sum(jnp.where(same_place, order, 0), axis=1, keepdims=True)
    same_owner = owner_col == owner_row
    rank_row = jnp.sum(jnp.where(same_owner & (down < across), 1, 0), axis=0, keepdims=True)
    rank_col = jnp.sum(jnp.where(same_owner & (across < down), 1, 0), axis=1, keepdims=True)

    shape = pick.shape
    down_p, across_p = iota(shape, 0), iota(shape, 1)
    down_i = iota((shape[0], count), 0)
    mine = hot((owner_row == me) & (rank_row == down_i % rows))
    came = hot(iota((count, shape[1]), 0) // rows == iota((count, shape[1]), 1) // (2 * rows))
    from_there = onto_mxu(mine, came)
    pick[...] = hot((from_there > 0.5) & (down_p // rows == across_p % rows))

    shape = valid.shape
    slot = iota((shape[0], count), 0) % rows
    mine_v = hot((owner_row == me) & (rank_row == slot))
    table_v = nt_dot(mine_v, table.astype(F32).astype(BF16)).astype(I32)
    length_v = jnp.sum(jnp.where(mine_v > 0.5, lengths, 0), axis=1, keepdims=True)
    position = iota(shape, 1)
    page, within = position // page_len, position % page_len
    seen = jnp.zeros(shape, F32)
    for j in range(table.shape[0]):
        inside = (table_v[:, j : j + 1] == page) & (within + j * page_len < length_v)
        seen = jnp.where(inside, 1.0, seen)
    valid[...] = seen

    ordered = hot(order_col == across)
    holds = hot((owner_col == across // rows) & (rank_col == across % rows))
    arrange[...] = onto_mxu(ordered, holds).astype(BF16)
    here = hot((owner_col == me) & (rank_col == iota(arrange_own.shape, 1)))
    arrange_own[...] = onto_mxu(ordered, here).astype(BF16)


def attention_kernel(
    place, arrived, pick, valid, vectors, pool_in, weight_in, partial, pool, weight, sems, *, rows
):
    deep = weight.shape[0] // WEIGHT_PARTS
    copies = [pltpu.make_async_copy(pool_in.at[i], pool.at[i], sems.at[i]) for i in range(2)]
    for i in range(WEIGHT_PARTS):
        part = pl.ds(i * deep, deep)
        copies.append(
            pltpu.make_async_copy(weight_in.at[part], weight.at[part], sems.at[2 + i])
        )
    for copy in copies:
        copy.start()
    half = arrived.shape[2]
    cols = 2 * half
    heads = cols // HEAD_DIM
    scale = 1.0 / math.sqrt(HEAD_DIM)
    came = arrived[...].reshape(-1, half)
    which = (iota(pick.shape, 1) // rows) % 2
    chosen = pick[...].astype(F32)
    own = jnp.concatenate(
        [onto_mxu(jnp.where(which == i, chosen, 0.0).astype(BF16), came) for i in range(2)], axis=1
    )
    query, key, value, resid = (own[i * rows : (i + 1) * rows] for i in range(4))

    def tile(x):
        return jnp.concatenate([x] * heads, axis=0)

    shape = (heads * rows, cols)
    in_head = iota(shape, 0) // rows == iota(shape, 1) // HEAD_DIM
    wide = jnp.where(in_head, tile(query), 0.0)
    positions = valid.shape[1]
    self_score = jnp.sum(wide * tile(key), axis=1, keepdims=True) * scale
    copies[0].wait()
    scores = nt_dot(wide.astype(BF16), pool[0].reshape(positions, cols)) * scale
    scores = jnp.where(valid[...] > 0.5, scores, -jnp.inf)
    top = jnp.maximum(jnp.max(scores, axis=1, keepdims=True), self_score)
    weights = jnp.exp(scores - top)
    self_weight = jnp.exp(self_score - top)
    total = jnp.sum(weights, axis=1, keepdims=True) + self_weight
    copies[1].wait()
    numer = onto_mxu(weights.astype(BF16), pool[1].reshape(positions, cols))
    numer = numer + self_weight.astype(BF16).astype(F32) * tile(value)
    numer = jnp.where(in_head, numer / total, 0.0)
    attn = sum(numer[i * rows : (i + 1) * rows] for i in range(heads))
    attn = jnp.concatenate([attn, jnp.zeros_like(attn)], axis=0).astype(BF16)
    for copy in copies[2:]:
        copy.wait()
    projected = onto_mxu(attn, weight[...])[:rows]
    extra = resid + row(vectors, 0, cols)
    for t in range(TP):
        mine = jnp.where(place[1:2, 0:1] == t, extra, 0.0)
        partial[:, t * cols : (t + 1) * cols] = projected[:, t * cols : (t + 1) * cols] + mine


def norm_kernel(place, near, far, vectors, blocks, stream_own):
    stream = (near[...] + far[...]).astype(BF16).astype(F32)
    width = stream.shape[1]
    cols = width // TP
    mean = jnp.sum(stream, axis=1, keepdims=True) / width
    var = jnp.sum((stream - mean) ** 2, axis=1, keepdims=True) / width
    own = stream[:, :cols]
    for t in range(1, TP):
        own = jnp.where(place[1:2, 0:1] == t, stream[:, t * cols : (t + 1) * cols], own)
    stream_own[...] = own.astype(BF16)
    gain, bias = row(vectors, 1, cols), row(vectors, 2, cols)
    block = ((own - mean) * lax.rsqrt(var + NORM_EPS) * gain + bias).astype(BF16)
    for d in range(REQ):
        blocks[d] = block


def up_kernel(rows_in, arrange, weight, out):
    came = rows_in[...].reshape(-1, rows_in.shape[2])
    ordered = onto_mxu(arrange[...], came).astype(BF16)
    out[...] = nt_dot(ordered, weight[...]).astype(BF16)


def down_kernel(near, far, vectors, weight, arrange_own, stream_own, out):
    hidden = near[...].astype(F32) + far[...].astype(F32)
    hidden = hidden + vectors[vectors.shape[0] - hidden.shape[1] :][None, :]
    activated = (0.5 * hidden * (1.0 + lax.erf(hidden * math.sqrt(0.5)))).astype(BF16)
    feed = onto_mxu(activated, weight[...]) + onto_mxu(arrange_own[...], stream_own[...])
    rows = out.shape[1]
    for d in range(REQ):
        out[d] = feed[d * rows : (d + 1) * rows]


def finish_kernel(pieces, vectors, out):
    cols = out.shape[1]
    out[...] = (jnp.sum(pieces[...], axis=0) + row(vectors, 3, cols)).astype(BF16)


def call(kernel, shapes, specs, args, scratch=(), room=16, **fixed):
    moved = sum(a.size * a.dtype.itemsize for a in args)
    return pl.pallas_call(
        functools.partial(kernel, **fixed) if fixed else kernel,
        out_shape=shapes,
        in_specs=specs,
        out_specs=[VMEM] * len(shapes),
        scratch_shapes=scratch,
        compiler_params=pltpu.CompilerParams(vmem_limit_bytes=int(room * 2**20)),
        cost_estimate=pl.CostEstimate(flops=0, bytes_accessed=moved, transcendentals=0),
    )(*args)


def trade(blocks):
    return lax.all_to_all(blocks, "req", 0, 0, tiled=True)


def on_pairs(
    query,
    key_new,
    value_new,
    resid,
    lengths,
    owner,
    page_table,
    kv_pool,
    out_weight,
    out_bias,
    norm_gain,
    norm_bias,
    up_weight_t,
    up_bias,
    down_weight,
    down_bias,
    order,
):
    rows, cols = query.shape
    width = cols * TP
    pool_pages, page_len = kv_pool.shape[1], kv_pool.shape[2]
    positions = pool_pages * page_len
    heads = cols // HEAD_DIM
    count = owner.shape[0]
    hidden = up_bias.shape[0]

    def arr(shape, dtype=BF16):
        return jax.ShapeDtypeStruct(shape, dtype)

    position = jnp.stack([lax.axis_index("req"), lax.axis_index("tp")]).astype(I32)
    place = jnp.broadcast_to(position[:, None], (2, HEAD_DIM))

    owner_f = jnp.pad(owner.astype(F32)[None, :], ((0, 0), (0, cols - count)))
    fields = pile([x.astype(F32) for x in (query, key_new, value_new, resid)] + [owner_f])
    (packed,) = call(pack_kernel, [arr((REQ, 8, cols // 2))], [VMEM] * 2, [place, fields])
    arrived = trade(packed)
    numbers = pile(
        [owner[None, :], order[None, :], lengths[None, :], jnp.zeros((5, count), I32), page_table.T]
    )
    vectors = pile([x.astype(F32) for x in (out_bias, norm_gain, norm_bias, down_bias, up_bias)])
    pick, valid, arrange, arrange_own = call(
        index_kernel,
        [
            arr((4 * rows, 2 * count)),
            arr((heads * rows, positions), F32),
            arr((count, count)),
            arr((count, rows)),
        ],
        [VMEM, VMEM],
        [place, numbers],
        page_len=page_len,
    )

    (partial,) = call(
        attention_kernel,
        [arr((rows, width), F32)],
        [VMEM] * 5 + [HBM] * 2,
        [place, arrived, pick, valid, vectors, kv_pool, out_weight],
        [
            pltpu.VMEM(kv_pool.shape, BF16),
            pltpu.VMEM(out_weight.shape, BF16),
            pltpu.SemaphoreType.DMA((2 + WEIGHT_PARTS,)),
        ],
        room=ATTENTION_ROOM,
        rows=rows,
    )
    pair = partial + swap(partial, "tp", 1)
    blocks, stream_own = call(
        norm_kernel,
        [arr((REQ, rows, cols)), arr((rows, cols))],
        [VMEM] * 4,
        [place, pair, swap(pair, "tp", 3), vectors],
    )

    (part,) = call(
        up_kernel,
        [arr((count, hidden))],
        [VMEM] * 3,
        [trade(blocks), arrange, up_weight_t],
    )
    part = (part.astype(F32) + swap(part, "tp", 1).astype(F32)).astype(BF16)
    (feed,) = call(
        down_kernel,
        [arr((REQ, rows, cols), F32)],
        [VMEM] * 6,
        [part, swap(part, "tp", 3), vectors, down_weight, arrange_own, stream_own],
    )
    (out,) = call(finish_kernel, [arr((rows, cols))], [VMEM] * 2, [trade(feed), vectors])
    return out


def swap(x, axis, step):
    n = lax.axis_size(axis)
    return lax.ppermute(x, axis, [(i, i ^ step) for i in range(n)])


def origins(axis):
    n, me = lax.axis_size(axis), lax.axis_index(axis)
    if n > PAIRWISE:
        return jnp.arange(n, dtype=jnp.int32)
    offsets = [0]
    step = n // 2
    while step:
        offsets = offsets + [o ^ step for o in offsets]
        step //= 2
    return jnp.array(offsets, dtype=jnp.int32) ^ me


def gather_rows(x, axis):
    n = lax.axis_size(axis)
    if n > PAIRWISE:
        return lax.all_gather(x, axis, axis=0, tiled=True)
    step = n // 2
    while step:
        x = jnp.concatenate([x, swap(x, axis, step)], axis=0)
        step //= 2
    return x


def fold_rows(x, axis):
    n = lax.axis_size(axis)
    if n > PAIRWISE:
        return lax.psum_scatter(x, axis, scatter_dimension=0, tiled=True)
    step = 1
    while step < n:
        half = x.shape[0] // 2
        x = x[:half] + swap(x[half:], axis, step)
        step *= 2
    return x


def sum_pairs(x, axis):
    n = lax.axis_size(axis)
    step = 1
    while step < n:
        x = (x.astype(jnp.float32) + swap(x, axis, step).astype(jnp.float32)).astype(x.dtype)
        step *= 2
    return x


def on_any_mesh(
    query,
    key_new,
    value_new,
    resid,
    lengths,
    owner,
    page_table,
    kv_pool,
    out_weight,
    out_bias,
    norm_gain,
    norm_bias,
    up_weight_t,
    up_bias,
    down_weight,
    down_bias,
    order,
):
    f32, bf16, i32 = jnp.float32, jnp.bfloat16, jnp.int32
    n_req = lax.axis_size("req")
    n_tp = lax.axis_size("tp")
    me = lax.axis_index("req")
    me_tp = lax.axis_index("tp")
    rows, cols = query.shape
    width = cols * n_tp
    heads = cols // HEAD_DIM
    pool_pages, page_len = kv_pool.shape[1], kv_pool.shape[2]
    positions = pool_pages * page_len
    scale = 1.0 / math.sqrt(HEAD_DIM)

    origin = origins("req")
    packed = jnp.concatenate([query, key_new, value_new, resid], axis=1)
    arrived = gather_rows(packed, "req")

    same = owner[:, None] == owner[None, :]
    ids = jnp.arange(owner.shape[0], dtype=i32)
    rank = jnp.sum((same & (ids[None, :] < ids[:, None])).astype(i32), axis=1)
    slots = jnp.arange(rows, dtype=i32)
    mine = (owner == me)[None, :] & (rank[None, :] == slots[:, None])
    mine_i = mine.astype(i32)
    own_len = jnp.sum(mine_i * lengths[None, :], axis=1)
    own_table = jnp.sum(mine_i[:, :, None] * page_table[None], axis=1)
    origin_ids = (origin[:, None] * rows + slots[None, :]).reshape(-1)
    own_id = jnp.sum(mine_i * ids[None, :], axis=1)
    take_hot = (own_id[:, None] == origin_ids[None, :]).astype(bf16)
    own = jnp.dot(take_hot, arrived, preferred_element_type=f32).astype(bf16)
    query_own, key_own, value_own, resid_own = (own[:, i * cols : (i + 1) * cols] for i in range(4))

    pos = jnp.arange(positions, dtype=i32)
    page, within = pos // page_len, pos % page_len
    entry = jnp.arange(page_table.shape[1], dtype=i32)
    start = entry * page_len
    hit = (own_table[:, :, None] == page[None, None, :]) & (
        start[None, :, None] + within[None, None, :] < own_len[:, None, None]
    )
    valid = jnp.any(hit, axis=1)

    keys = kv_pool[0].reshape(positions, cols)
    values = kv_pool[1].reshape(positions, cols)
    head_of = jnp.arange(cols, dtype=i32) // HEAD_DIM
    head_mask = head_of[None, :] == jnp.arange(heads, dtype=i32)[:, None]
    spread_q = jnp.where(head_mask[:, None, :], query_own[None], 0).reshape(heads * rows, cols)
    scores = (
        lax.dot_general(spread_q, keys, (((1,), (1,)), ((), ())), preferred_element_type=f32) * scale
    ).reshape(heads, rows, positions)
    scores = jnp.where(valid[None], scores, -jnp.inf)
    self_score = (
        jnp.sum(
            (query_own.astype(f32) * key_own.astype(f32)).reshape(rows, heads, HEAD_DIM), axis=-1
        ).T
        * scale
    )
    top = jnp.maximum(jnp.max(scores, axis=2), self_score)
    weights = jnp.exp(scores - top[:, :, None])
    self_weight = jnp.exp(self_score - top)
    total = jnp.sum(weights, axis=2) + self_weight
    numer = jnp.dot(
        weights.astype(bf16).reshape(heads * rows, positions), values, preferred_element_type=f32
    ).reshape(heads, rows, cols)
    numer = numer + self_weight.astype(bf16).astype(f32)[:, :, None] * value_own.astype(f32)[None]
    attn = jnp.sum(
        jnp.where(head_mask[:, None, :], numer / total[:, :, None], 0.0), axis=0
    ).astype(bf16)

    extra = resid_own.astype(f32) + out_bias.astype(f32)[None, :]
    partial = jnp.dot(attn, out_weight, preferred_element_type=f32)
    place = (jnp.arange(n_tp, dtype=i32) == me_tp)[None, :, None]
    partial = (
        partial.reshape(rows, n_tp, cols) + jnp.where(place, extra[:, None, :], 0.0)
    ).reshape(rows, width)
    stream = sum_pairs(partial, "tp").astype(bf16)
    stream_f = stream.astype(f32)
    mean = jnp.mean(stream_f, axis=1, keepdims=True)
    var = jnp.mean((stream_f - mean) ** 2, axis=1, keepdims=True)
    inverse = lax.rsqrt(var + NORM_EPS)
    stream_own = lax.dynamic_slice_in_dim(stream, me_tp * cols, cols, axis=1)
    normed = (
        (stream_own.astype(f32) - mean) * inverse * norm_gain.astype(f32)[None, :]
        + norm_bias.astype(f32)[None, :]
    ).astype(bf16)

    normed_all = gather_rows(normed, "req")
    slot_of = owner * rows + rank
    wanted = slot_of[order[origin_ids]]
    place_hot = (wanted[:, None] == origin_ids[None, :]).astype(bf16)
    mine_hot = (wanted[:, None] == (me * rows + slots)[None, :]).astype(bf16)
    normed_out = jnp.dot(place_hot, normed_all, preferred_element_type=f32).astype(bf16)
    hidden = lax.dot_general(
        normed_out, up_weight_t, (((1,), (1,)), ((), ())), preferred_element_type=f32
    ).astype(bf16)
    summed = sum_pairs(hidden, "tp").astype(f32)
    activated = jax.nn.gelu(summed + up_bias.astype(f32)[None, :], approximate=False).astype(bf16)
    feed = jnp.dot(activated, down_weight, preferred_element_type=f32)
    feed = feed + jnp.dot(mine_hot, stream_own, preferred_element_type=f32)
    mixed = fold_rows(feed, "req")
    return (mixed + down_bias.astype(f32)[None, :]).astype(bf16)


def solution(mesh):
    pairs = mesh.shape["req"] == REQ and mesh.shape["tp"] == TP
    per_device = on_pairs if pairs else on_any_mesh
    in_specs = (
        P("req", "tp"),
        P("req", "tp"),
        P("req", "tp"),
        P("req", "tp"),
        P(),
        P(),
        P(),
        P(None, "req", None, "tp"),
        P("tp", None),
        P("tp"),
        P("tp"),
        P("tp"),
        P("req", "tp"),
        P("req"),
        P("req", "tp"),
        P("tp"),
        P(),
    )
    out_specs = P("req", "tp")
    return jax.shard_map(
        per_device, mesh=mesh, in_specs=in_specs, out_specs=out_specs, check_vma=False
    )
```

```python
import functools
import math

import jax
import jax.numpy as jnp
from jax import lax
from jax.experimental import pallas as pl
from jax.experimental.pallas import tpu as pltpu
from jax.sharding import PartitionSpec as P

HEAD_DIM = 128
NORM_EPS = 1e-05
PAIRWISE = 16
REQ, TP = 8, 4
WEIGHT_PARTS = 4
ATTENTION_ROOM = 53.2
ALL_ROOM = 58
F32, BF16, I32 = jnp.float32, jnp.bfloat16, jnp.int32
VMEM = pl.BlockSpec(memory_space=pltpu.VMEM)
HBM = pl.BlockSpec(memory_space=pltpu.HBM)


def iota(shape, dim):
    return lax.broadcasted_iota(I32, shape, dim)


def onto_mxu(a, b):
    return jnp.dot(a, b, preferred_element_type=F32)


def nt_dot(a, b):
    return lax.dot_general(a, b, (((1,), (1,)), ((), ())), preferred_element_type=F32)


def hot(condition):
    return jnp.where(condition, 1.0, 0.0).astype(BF16)


def pile(parts):
    height = sum(p.shape[0] for p in parts)
    at, piled = 0, 0
    for p in parts:
        around = ((at, height - at - p.shape[0]),) + ((0, 0),) * (p.ndim - 1)
        piled += jnp.pad(p, around)
        at += p.shape[0]
    return piled


def row(vectors, i, cols):
    return vectors[i * cols : (i + 1) * cols][None, :]


def pack_kernel(owner_in, query, key, value, resid, out, owner, q, k, v, r, sems):
    parts = ((owner_in, owner), (query, q), (key, k), (value, v), (resid, r))
    copies = [pltpu.make_async_copy(x, y, sems.at[i]) for i, (x, y) in enumerate(parts)]
    for copy in copies:
        copy.start()
    rows, cols = q.shape
    fields = 4
    count = REQ * rows
    shape = (REQ * fields, fields * rows)
    down, across = iota(shape, 0), iota(shape, 1)
    here = (count, fields * rows)
    of_mine = hot(iota(here, 0) == lax.axis_index("req") * rows + iota(here, 1) % rows)
    copies[0].wait()
    owner_of = onto_mxu(owner[...].astype(F32).astype(BF16), of_mine).astype(I32)
    pick = hot((down % fields == across // rows) & (owner_of == down // fields))
    for copy in copies[1:]:
        copy.wait()
    all_rows = jnp.concatenate([q[...], k[...], v[...], r[...]], axis=0)
    blocks = onto_mxu(pick, all_rows).astype(BF16)
    for d in range(REQ):
        block = blocks[d * fields : (d + 1) * fields]
        out[d, :fields, :] = block[:, : cols // 2]
        out[d, fields:, :] = block[:, cols // 2 :]


def index_kernel(place, numbers, pick, valid, arrange, arrange_own, *, page_len):
    owner, order, lengths = (numbers[i : i + 1, :] for i in range(3))
    table = numbers[8:, :]
    me = place[0:1, 0:1]
    count = owner.shape[1]
    rows = count // REQ
    square = (count, count)
    down, across = iota(square, 0), iota(square, 1)
    owner_row = owner
    same_place = down == across
    owner_col = jnp.sum(jnp.where(same_place, owner_row, 0), axis=1, keepdims=True)
    order_col = jnp.sum(jnp.where(same_place, order, 0), axis=1, keepdims=True)
    same_owner = owner_col == owner_row
    rank_row = jnp.sum(jnp.where(same_owner & (down < across), 1, 0), axis=0, keepdims=True)
    rank_col = jnp.sum(jnp.where(same_owner & (across < down), 1, 0), axis=1, keepdims=True)

    shape = pick.shape
    down_p, across_p = iota(shape, 0), iota(shape, 1)
    down_i = iota((shape[0], count), 0)
    mine = hot((owner_row == me) & (rank_row == down_i % rows))
    came = hot(iota((count, shape[1]), 0) // rows == iota((count, shape[1]), 1) // (2 * rows))
    from_there = onto_mxu(mine, came)
    pick[...] = hot((from_there > 0.5) & (down_p // rows == across_p % rows))

    shape = valid.shape
    slot = iota((shape[0], count), 0) % rows
    mine_v = hot((owner_row == me) & (rank_row == slot))
    table_v = nt_dot(mine_v, table.astype(F32).astype(BF16)).astype(I32)
    length_v = jnp.sum(jnp.where(mine_v > 0.5, lengths, 0), axis=1, keepdims=True)
    position = iota(shape, 1)
    page, within = position // page_len, position % page_len
    seen = jnp.zeros(shape, F32)
    for j in range(table.shape[0]):
        inside = (table_v[:, j : j + 1] == page) & (within + j * page_len < length_v)
        seen = jnp.where(inside, 1.0, seen)
    valid[...] = seen

    ordered = hot(order_col == across)
    holds = hot((owner_col == across // rows) & (rank_col == across % rows))
    arrange[...] = onto_mxu(ordered, holds).astype(BF16)
    here = hot((owner_col == me) & (rank_col == iota(arrange_own.shape, 1)))
    arrange_own[...] = onto_mxu(ordered, here).astype(BF16)


def attention_kernel(
    place, arrived, pick, valid, vectors, pool_in, weight_in, partial, pool, weight, sems, *, rows
):
    deep = weight.shape[0] // WEIGHT_PARTS
    copies = [pltpu.make_async_copy(pool_in.at[i], pool.at[i], sems.at[i]) for i in range(2)]
    for i in range(WEIGHT_PARTS):
        part = pl.ds(i * deep, deep)
        copies.append(
            pltpu.make_async_copy(weight_in.at[part], weight.at[part], sems.at[2 + i])
        )
    for copy in copies:
        copy.start()
    half = arrived.shape[2]
    cols = 2 * half
    heads = cols // HEAD_DIM
    scale = 1.0 / math.sqrt(HEAD_DIM)
    came = arrived[...].reshape(-1, half)
    which = (iota(pick.shape, 1) // rows) % 2
    chosen = pick[...].astype(F32)
    own = jnp.concatenate(
        [onto_mxu(jnp.where(which == i, chosen, 0.0).astype(BF16), came) for i in range(2)], axis=1
    )
    query, key, value, resid = (own[i * rows : (i + 1) * rows] for i in range(4))

    def tile(x):
        return jnp.concatenate([x] * heads, axis=0)

    shape = (heads * rows, cols)
    in_head = iota(shape, 0) // rows == iota(shape, 1) // HEAD_DIM
    wide = jnp.where(in_head, tile(query), 0.0)
    positions = valid.shape[1]
    self_score = jnp.sum(wide * tile(key), axis=1, keepdims=True) * scale
    copies[0].wait()
    scores = nt_dot(wide.astype(BF16), pool[0].reshape(positions, cols)) * scale
    scores = jnp.where(valid[...] > 0.5, scores, -jnp.inf)
    top = jnp.maximum(jnp.max(scores, axis=1, keepdims=True), self_score)
    weights = jnp.exp(scores - top)
    self_weight = jnp.exp(self_score - top)
    total = jnp.sum(weights, axis=1, keepdims=True) + self_weight
    copies[1].wait()
    numer = onto_mxu(weights.astype(BF16), pool[1].reshape(positions, cols))
    numer = numer + self_weight.astype(BF16).astype(F32) * tile(value)
    numer = jnp.where(in_head, numer / total, 0.0)
    attn = sum(numer[i * rows : (i + 1) * rows] for i in range(heads))
    attn = jnp.concatenate([attn, jnp.zeros_like(attn)], axis=0).astype(BF16)
    for copy in copies[2:]:
        copy.wait()
    projected = onto_mxu(attn, weight[...])[:rows]
    extra = resid + row(vectors, 0, cols)
    for t in range(TP):
        mine = jnp.where(place[1:2, 0:1] == t, extra, 0.0)
        partial[:, t * cols : (t + 1) * cols] = projected[:, t * cols : (t + 1) * cols] + mine


def norm_kernel(place, near, far, vectors, blocks, stream_own):
    stream = (near[...] + far[...]).astype(BF16).astype(F32)
    width = stream.shape[1]
    cols = width // TP
    mean = jnp.sum(stream, axis=1, keepdims=True) / width
    var = jnp.sum((stream - mean) ** 2, axis=1, keepdims=True) / width
    own = stream[:, :cols]
    for t in range(1, TP):
        own = jnp.where(place[1:2, 0:1] == t, stream[:, t * cols : (t + 1) * cols], own)
    stream_own[...] = own.astype(BF16)
    gain, bias = row(vectors, 1, cols), row(vectors, 2, cols)
    block = ((own - mean) * lax.rsqrt(var + NORM_EPS) * gain + bias).astype(BF16)
    for d in range(REQ):
        blocks[d] = block


def up_kernel(rows_in, arrange, weight, out):
    came = rows_in[...].reshape(-1, rows_in.shape[2])
    ordered = onto_mxu(arrange[...], came).astype(BF16)
    out[...] = nt_dot(ordered, weight[...]).astype(BF16)


def down_kernel(near, far, vectors, weight, arrange_own, stream_own, out):
    hidden = near[...].astype(F32) + far[...].astype(F32)
    hidden = hidden + vectors[vectors.shape[0] - hidden.shape[1] :][None, :]
    activated = (0.5 * hidden * (1.0 + lax.erf(hidden * math.sqrt(0.5)))).astype(BF16)
    feed = onto_mxu(activated, weight[...]) + onto_mxu(arrange_own[...], stream_own[...])
    rows = out.shape[1]
    for d in range(REQ):
        out[d] = feed[d * rows : (d + 1) * rows]


def finish_kernel(pieces, vectors, out):
    cols = out.shape[1]
    out[...] = (jnp.sum(pieces[...], axis=0) + row(vectors, 3, cols)).astype(BF16)


def call(kernel, shapes, specs, args, scratch=(), room=16, **fixed):
    moved = sum(a.size * a.dtype.itemsize for a in args)
    return pl.pallas_call(
        functools.partial(kernel, **fixed) if fixed else kernel,
        out_shape=shapes,
        in_specs=specs,
        out_specs=[VMEM] * len(shapes),
        scratch_shapes=scratch,
        compiler_params=pltpu.CompilerParams(vmem_limit_bytes=int(room * 2**20)),
        cost_estimate=pl.CostEstimate(flops=0, bytes_accessed=moved, transcendentals=0),
    )(*args)


def trade(blocks):
    return lax.all_to_all(blocks, "req", 0, 0, tiled=True)


def on_pairs(
    query,
    key_new,
    value_new,
    resid,
    lengths,
    owner,
    page_table,
    kv_pool,
    out_weight,
    out_bias,
    norm_gain,
    norm_bias,
    up_weight_t,
    up_bias,
    down_weight,
    down_bias,
    order,
):
    rows, cols = query.shape
    width = cols * TP
    pool_pages, page_len = kv_pool.shape[1], kv_pool.shape[2]
    positions = pool_pages * page_len
    heads = cols // HEAD_DIM
    count = owner.shape[0]
    hidden = up_bias.shape[0]

    def arr(shape, dtype=BF16):
        return jax.ShapeDtypeStruct(shape, dtype)

    position = jnp.stack([lax.axis_index("req"), lax.axis_index("tp")]).astype(I32)
    place = jnp.broadcast_to(position[:, None], (2, HEAD_DIM))

    (packed,) = call(
        pack_kernel,
        [arr((REQ, 8, cols // 2))],
        [HBM] * 5,
        [owner[None, :], query, key_new, value_new, resid],
        [pltpu.VMEM((1, count), I32)]
        + [pltpu.VMEM((rows, cols), BF16)] * 4
        + [pltpu.SemaphoreType.DMA((5,))],
        room=ALL_ROOM,
    )
    arrived = trade(packed)
    numbers = pile(
        [owner[None, :], order[None, :], lengths[None, :], jnp.zeros((5, count), I32), page_table.T]
    )
    vectors = pile([x.astype(F32) for x in (out_bias, norm_gain, norm_bias, down_bias, up_bias)])
    pick, valid, arrange, arrange_own = call(
        index_kernel,
        [
            arr((4 * rows, 2 * count)),
            arr((heads * rows, positions), F32),
            arr((count, count)),
            arr((count, rows)),
        ],
        [VMEM, VMEM],
        [place, numbers],
        page_len=page_len,
    )

    (partial,) = call(
        attention_kernel,
        [arr((rows, width), F32)],
        [VMEM] * 5 + [HBM] * 2,
        [place, arrived, pick, valid, vectors, kv_pool, out_weight],
        [
            pltpu.VMEM(kv_pool.shape, BF16),
            pltpu.VMEM(out_weight.shape, BF16),
            pltpu.SemaphoreType.DMA((2 + WEIGHT_PARTS,)),
        ],
        room=ATTENTION_ROOM,
        rows=rows,
    )
    pair = partial + swap(partial, "tp", 1)
    blocks, stream_own = call(
        norm_kernel,
        [arr((REQ, rows, cols)), arr((rows, cols))],
        [VMEM] * 4,
        [place, pair, swap(pair, "tp", 3), vectors],
    )

    (part,) = call(
        up_kernel,
        [arr((count, hidden))],
        [VMEM] * 3,
        [trade(blocks), arrange, up_weight_t],
    )
    part = (part.astype(F32) + swap(part, "tp", 1).astype(F32)).astype(BF16)
    (feed,) = call(
        down_kernel,
        [arr((REQ, rows, cols), F32)],
        [VMEM] * 6,
        [part, swap(part, "tp", 3), vectors, down_weight, arrange_own, stream_own],
    )
    (out,) = call(finish_kernel, [arr((rows, cols))], [VMEM] * 2, [trade(feed), vectors])
    return out


def swap(x, axis, step):
    n = lax.axis_size(axis)
    return lax.ppermute(x, axis, [(i, i ^ step) for i in range(n)])


def origins(axis):
    n, me = lax.axis_size(axis), lax.axis_index(axis)
    if n > PAIRWISE:
        return jnp.arange(n, dtype=jnp.int32)
    offsets = [0]
    step = n // 2
    while step:
        offsets = offsets + [o ^ step for o in offsets]
        step //= 2
    return jnp.array(offsets, dtype=jnp.int32) ^ me


def gather_rows(x, axis):
    n = lax.axis_size(axis)
    if n > PAIRWISE:
        return lax.all_gather(x, axis, axis=0, tiled=True)
    step = n // 2
    while step:
        x = jnp.concatenate([x, swap(x, axis, step)], axis=0)
        step //= 2
    return x


def fold_rows(x, axis):
    n = lax.axis_size(axis)
    if n > PAIRWISE:
        return lax.psum_scatter(x, axis, scatter_dimension=0, tiled=True)
    step = 1
    while step < n:
        half = x.shape[0] // 2
        x = x[:half] + swap(x[half:], axis, step)
        step *= 2
    return x


def sum_pairs(x, axis):
    n = lax.axis_size(axis)
    step = 1
    while step < n:
        x = (x.astype(jnp.float32) + swap(x, axis, step).astype(jnp.float32)).astype(x.dtype)
        step *= 2
    return x


def on_any_mesh(
    query,
    key_new,
    value_new,
    resid,
    lengths,
    owner,
    page_table,
    kv_pool,
    out_weight,
    out_bias,
    norm_gain,
    norm_bias,
    up_weight_t,
    up_bias,
    down_weight,
    down_bias,
    order,
):
    f32, bf16, i32 = jnp.float32, jnp.bfloat16, jnp.int32
    n_req = lax.axis_size("req")
    n_tp = lax.axis_size("tp")
    me = lax.axis_index("req")
    me_tp = lax.axis_index("tp")
    rows, cols = query.shape
    width = cols * n_tp
    heads = cols // HEAD_DIM
    pool_pages, page_len = kv_pool.shape[1], kv_pool.shape[2]
    positions = pool_pages * page_len
    scale = 1.0 / math.sqrt(HEAD_DIM)

    origin = origins("req")
    packed = jnp.concatenate([query, key_new, value_new, resid], axis=1)
    arrived = gather_rows(packed, "req")

    same = owner[:, None] == owner[None, :]
    ids = jnp.arange(owner.shape[0], dtype=i32)
    rank = jnp.sum((same & (ids[None, :] < ids[:, None])).astype(i32), axis=1)
    slots = jnp.arange(rows, dtype=i32)
    mine = (owner == me)[None, :] & (rank[None, :] == slots[:, None])
    mine_i = mine.astype(i32)
    own_len = jnp.sum(mine_i * lengths[None, :], axis=1)
    own_table = jnp.sum(mine_i[:, :, None] * page_table[None], axis=1)
    origin_ids = (origin[:, None] * rows + slots[None, :]).reshape(-1)
    own_id = jnp.sum(mine_i * ids[None, :], axis=1)
    take_hot = (own_id[:, None] == origin_ids[None, :]).astype(bf16)
    own = jnp.dot(take_hot, arrived, preferred_element_type=f32).astype(bf16)
    query_own, key_own, value_own, resid_own = (own[:, i * cols : (i + 1) * cols] for i in range(4))

    pos = jnp.arange(positions, dtype=i32)
    page, within = pos // page_len, pos % page_len
    entry = jnp.arange(page_table.shape[1], dtype=i32)
    start = entry * page_len
    hit = (own_table[:, :, None] == page[None, None, :]) & (
        start[None, :, None] + within[None, None, :] < own_len[:, None, None]
    )
    valid = jnp.any(hit, axis=1)

    keys = kv_pool[0].reshape(positions, cols)
    values = kv_pool[1].reshape(positions, cols)
    head_of = jnp.arange(cols, dtype=i32) // HEAD_DIM
    head_mask = head_of[None, :] == jnp.arange(heads, dtype=i32)[:, None]
    spread_q = jnp.where(head_mask[:, None, :], query_own[None], 0).reshape(heads * rows, cols)
    scores = (
        lax.dot_general(spread_q, keys, (((1,), (1,)), ((), ())), preferred_element_type=f32) * scale
    ).reshape(heads, rows, positions)
    scores = jnp.where(valid[None], scores, -jnp.inf)
    self_score = (
        jnp.sum(
            (query_own.astype(f32) * key_own.astype(f32)).reshape(rows, heads, HEAD_DIM), axis=-1
        ).T
        * scale
    )
    top = jnp.maximum(jnp.max(scores, axis=2), self_score)
    weights = jnp.exp(scores - top[:, :, None])
    self_weight = jnp.exp(self_score - top)
    total = jnp.sum(weights, axis=2) + self_weight
    numer = jnp.dot(
        weights.astype(bf16).reshape(heads * rows, positions), values, preferred_element_type=f32
    ).reshape(heads, rows, cols)
    numer = numer + self_weight.astype(bf16).astype(f32)[:, :, None] * value_own.astype(f32)[None]
    attn = jnp.sum(
        jnp.where(head_mask[:, None, :], numer / total[:, :, None], 0.0), axis=0
    ).astype(bf16)

    extra = resid_own.astype(f32) + out_bias.astype(f32)[None, :]
    partial = jnp.dot(attn, out_weight, preferred_element_type=f32)
    place = (jnp.arange(n_tp, dtype=i32) == me_tp)[None, :, None]
    partial = (
        partial.reshape(rows, n_tp, cols) + jnp.where(place, extra[:, None, :], 0.0)
    ).reshape(rows, width)
    stream = sum_pairs(partial, "tp").astype(bf16)
    stream_f = stream.astype(f32)
    mean = jnp.mean(stream_f, axis=1, keepdims=True)
    var = jnp.mean((stream_f - mean) ** 2, axis=1, keepdims=True)
    inverse = lax.rsqrt(var + NORM_EPS)
    stream_own = lax.dynamic_slice_in_dim(stream, me_tp * cols, cols, axis=1)
    normed = (
        (stream_own.astype(f32) - mean) * inverse * norm_gain.astype(f32)[None, :]
        + norm_bias.astype(f32)[None, :]
    ).astype(bf16)

    normed_all = gather_rows(normed, "req")
    slot_of = owner * rows + rank
    wanted = slot_of[order[origin_ids]]
    place_hot = (wanted[:, None] == origin_ids[None, :]).astype(bf16)
    mine_hot = (wanted[:, None] == (me * rows + slots)[None, :]).astype(bf16)
    normed_out = jnp.dot(place_hot, normed_all, preferred_element_type=f32).astype(bf16)
    hidden = lax.dot_general(
        normed_out, up_weight_t, (((1,), (1,)), ((), ())), preferred_element_type=f32
    ).astype(bf16)
    summed = sum_pairs(hidden, "tp").astype(f32)
    activated = jax.nn.gelu(summed + up_bias.astype(f32)[None, :], approximate=False).astype(bf16)
    feed = jnp.dot(activated, down_weight, preferred_element_type=f32)
    feed = feed + jnp.dot(mine_hot, stream_own, preferred_element_type=f32)
    mixed = fold_rows(feed, "req")
    return (mixed + down_bias.astype(f32)[None, :]).astype(bf16)


def solution(mesh):
    pairs = mesh.shape["req"] == REQ and mesh.shape["tp"] == TP
    per_device = on_pairs if pairs else on_any_mesh
    in_specs = (
        P("req", "tp"),
        P("req", "tp"),
        P("req", "tp"),
        P("req", "tp"),
        P(),
        P(),
        P(),
        P(None, "req", None, "tp"),
        P("tp", None),
        P("tp"),
        P("tp"),
        P("tp"),
        P("req", "tp"),
        P("req"),
        P("req", "tp"),
        P("tp"),
        P(),
    )
    out_specs = P("req", "tp")
    return jax.shard_map(
        per_device, mesh=mesh, in_specs=in_specs, out_specs=out_specs, check_vma=False
    )
```

```python
import functools
import math

import jax
import jax.numpy as jnp
from jax import lax
from jax.experimental import pallas as pl
from jax.experimental.pallas import tpu as pltpu
from jax.sharding import PartitionSpec as P

HEAD_DIM = 128
NORM_EPS = 1e-05
PAIRWISE = 16
REQ, TP = 8, 4
ALL_ROOM = 58
F32, BF16, I32 = jnp.float32, jnp.bfloat16, jnp.int32
VMEM = pl.BlockSpec(memory_space=pltpu.VMEM)
HBM = pl.BlockSpec(memory_space=pltpu.HBM)


def iota(shape, dim):
    return lax.broadcasted_iota(I32, shape, dim)


def onto_mxu(a, b):
    return jnp.dot(a, b, preferred_element_type=F32)


def nt_dot(a, b):
    return lax.dot_general(a, b, (((1,), (1,)), ((), ())), preferred_element_type=F32)


def hot(condition):
    return jnp.where(condition, 1.0, 0.0).astype(BF16)


def pile(parts):
    height = sum(p.shape[0] for p in parts)
    at, piled = 0, 0
    for p in parts:
        around = ((at, height - at - p.shape[0]),) + ((0, 0),) * (p.ndim - 1)
        piled += jnp.pad(p, around)
        at += p.shape[0]
    return piled


def row(vectors, i, cols):
    return vectors[i * cols : (i + 1) * cols][None, :]


def pack_kernel(owner_in, query, key, value, resid, out, owner, q, k, v, r, sems):
    parts = ((owner_in, owner), (query, q), (key, k), (value, v), (resid, r))
    copies = [pltpu.make_async_copy(x, y, sems.at[i]) for i, (x, y) in enumerate(parts)]
    for copy in copies:
        copy.start()
    rows, cols = q.shape
    fields = 4
    count = REQ * rows
    shape = (REQ * fields, fields * rows)
    down, across = iota(shape, 0), iota(shape, 1)
    here = (count, fields * rows)
    of_mine = hot(iota(here, 0) == lax.axis_index("req") * rows + iota(here, 1) % rows)
    copies[0].wait()
    owner_of = onto_mxu(owner[...].astype(F32).astype(BF16), of_mine).astype(I32)
    pick = hot((down % fields == across // rows) & (owner_of == down // fields))
    for copy in copies[1:]:
        copy.wait()
    all_rows = jnp.concatenate([q[...], k[...], v[...], r[...]], axis=0)
    blocks = onto_mxu(pick, all_rows).astype(BF16)
    for d in range(REQ):
        block = blocks[d * fields : (d + 1) * fields]
        out[d, :fields, :] = block[:, : cols // 2]
        out[d, fields:, :] = block[:, cols // 2 :]


def index_kernel(place, numbers, pick, valid, arrange, arrange_own, *, page_len):
    owner, order, lengths = (numbers[i : i + 1, :] for i in range(3))
    table = numbers[8:, :]
    me = place[0:1, 0:1]
    count = owner.shape[1]
    rows = count // REQ
    square = (count, count)
    down, across = iota(square, 0), iota(square, 1)
    owner_row = owner
    same_place = down == across
    owner_col = jnp.sum(jnp.where(same_place, owner_row, 0), axis=1, keepdims=True)
    order_col = jnp.sum(jnp.where(same_place, order, 0), axis=1, keepdims=True)
    same_owner = owner_col == owner_row
    rank_row = jnp.sum(jnp.where(same_owner & (down < across), 1, 0), axis=0, keepdims=True)
    rank_col = jnp.sum(jnp.where(same_owner & (across < down), 1, 0), axis=1, keepdims=True)

    shape = pick.shape
    down_p, across_p = iota(shape, 0), iota(shape, 1)
    down_i = iota((shape[0], count), 0)
    mine = hot((owner_row == me) & (rank_row == down_i % rows))
    came = hot(iota((count, shape[1]), 0) // rows == iota((count, shape[1]), 1) // (2 * rows))
    from_there = onto_mxu(mine, came)
    pick[...] = hot((from_there > 0.5) & (down_p // rows == across_p % rows))

    shape = valid.shape
    slot = iota((shape[0], count), 0) % rows
    mine_v = hot((owner_row == me) & (rank_row == slot))
    table_v = nt_dot(mine_v, table.astype(F32).astype(BF16)).astype(I32)
    length_v = jnp.sum(jnp.where(mine_v > 0.5, lengths, 0), axis=1, keepdims=True)
    position = iota(shape, 1)
    page, within = position // page_len, position % page_len
    seen = jnp.zeros(shape, F32)
    for j in range(table.shape[0]):
        inside = (table_v[:, j : j + 1] == page) & (within + j * page_len < length_v)
        seen = jnp.where(inside, 1.0, seen)
    valid[...] = seen

    ordered = hot(order_col == across)
    holds = hot((owner_col == across // rows) & (rank_col == across % rows))
    arrange[...] = onto_mxu(ordered, holds).astype(BF16)
    here = hot((owner_col == me) & (rank_col == iota(arrange_own.shape, 1)))
    arrange_own[...] = onto_mxu(ordered, here).astype(BF16)


def attention_kernel(place, arrived, pick, valid, vectors, pool, weight, partial, *, rows):
    half = arrived.shape[2]
    cols = 2 * half
    heads = cols // HEAD_DIM
    scale = 1.0 / math.sqrt(HEAD_DIM)
    came = arrived[...].reshape(-1, half)
    which = (iota(pick.shape, 1) // rows) % 2
    chosen = pick[...].astype(F32)
    own = jnp.concatenate(
        [onto_mxu(jnp.where(which == i, chosen, 0.0).astype(BF16), came) for i in range(2)], axis=1
    )
    query, key, value, resid = (own[i * rows : (i + 1) * rows] for i in range(4))

    def tile(x):
        return jnp.concatenate([x] * heads, axis=0)

    shape = (heads * rows, cols)
    in_head = iota(shape, 0) // rows == iota(shape, 1) // HEAD_DIM
    wide = jnp.where(in_head, tile(query), 0.0)
    positions = valid.shape[1]
    self_score = jnp.sum(wide * tile(key), axis=1, keepdims=True) * scale
    scores = nt_dot(wide.astype(BF16), pool[0].reshape(positions, cols)) * scale
    scores = jnp.where(valid[...] > 0.5, scores, -jnp.inf)
    top = jnp.maximum(jnp.max(scores, axis=1, keepdims=True), self_score)
    weights = jnp.exp(scores - top)
    self_weight = jnp.exp(self_score - top)
    total = jnp.sum(weights, axis=1, keepdims=True) + self_weight
    numer = onto_mxu(weights.astype(BF16), pool[1].reshape(positions, cols))
    numer = numer + self_weight.astype(BF16).astype(F32) * tile(value)
    numer = jnp.where(in_head, numer / total, 0.0)
    attn = sum(numer[i * rows : (i + 1) * rows] for i in range(heads))
    attn = jnp.concatenate([attn, jnp.zeros_like(attn)], axis=0).astype(BF16)
    projected = onto_mxu(attn, weight[...])[:rows]
    extra = resid + row(vectors, 0, cols)
    for t in range(TP):
        mine = jnp.where(place[1:2, 0:1] == t, extra, 0.0)
        partial[:, t * cols : (t + 1) * cols] = projected[:, t * cols : (t + 1) * cols] + mine


def norm_kernel(place, near, far, vectors, blocks, stream_own):
    mine = near[...].astype(BF16).astype(F32)
    stream = (mine + far[...].astype(F32)).astype(BF16).astype(F32)
    width = stream.shape[1]
    cols = width // TP
    mean = jnp.sum(stream, axis=1, keepdims=True) / width
    var = jnp.sum((stream - mean) ** 2, axis=1, keepdims=True) / width
    own = stream[:, :cols]
    for t in range(1, TP):
        own = jnp.where(place[1:2, 0:1] == t, stream[:, t * cols : (t + 1) * cols], own)
    stream_own[...] = own.astype(BF16)
    gain, bias = row(vectors, 1, cols), row(vectors, 2, cols)
    block = ((own - mean) * lax.rsqrt(var + NORM_EPS) * gain + bias).astype(BF16)
    for d in range(REQ):
        blocks[d] = block


def up_kernel(rows_in, arrange, weight, out):
    came = rows_in[...].reshape(-1, rows_in.shape[2])
    ordered = onto_mxu(arrange[...], came).astype(BF16)
    out[...] = nt_dot(ordered, weight[...]).astype(BF16)


def down_kernel(near, far, vectors, weight, arrange_own, stream_own, out):
    hidden = near[...].astype(F32) + far[...].astype(F32)
    hidden = hidden + vectors[vectors.shape[0] - hidden.shape[1] :][None, :]
    activated = (0.5 * hidden * (1.0 + lax.erf(hidden * math.sqrt(0.5)))).astype(BF16)
    feed = onto_mxu(activated, weight[...]) + onto_mxu(arrange_own[...], stream_own[...])
    rows = out.shape[1]
    for d in range(REQ):
        out[d] = feed[d * rows : (d + 1) * rows]


def finish_kernel(pieces, vectors, out):
    cols = out.shape[1]
    out[...] = (jnp.sum(pieces[...], axis=0) + row(vectors, 3, cols)).astype(BF16)


def call(kernel, shapes, specs, args, scratch=(), room=16, **fixed):
    moved = sum(a.size * a.dtype.itemsize for a in args)
    return pl.pallas_call(
        functools.partial(kernel, **fixed) if fixed else kernel,
        out_shape=shapes,
        in_specs=specs,
        out_specs=[VMEM] * len(shapes),
        scratch_shapes=scratch,
        compiler_params=pltpu.CompilerParams(vmem_limit_bytes=int(room * 2**20)),
        cost_estimate=pl.CostEstimate(flops=0, bytes_accessed=moved, transcendentals=0),
    )(*args)


def trade(blocks):
    return lax.all_to_all(blocks, "req", 0, 0, tiled=True)


def on_pairs(
    query,
    key_new,
    value_new,
    resid,
    lengths,
    owner,
    page_table,
    kv_pool,
    out_weight,
    out_bias,
    norm_gain,
    norm_bias,
    up_weight_t,
    up_bias,
    down_weight,
    down_bias,
    order,
):
    rows, cols = query.shape
    width = cols * TP
    pool_pages, page_len = kv_pool.shape[1], kv_pool.shape[2]
    positions = pool_pages * page_len
    heads = cols // HEAD_DIM
    count = owner.shape[0]
    hidden = up_bias.shape[0]

    def arr(shape, dtype=BF16):
        return jax.ShapeDtypeStruct(shape, dtype)

    position = jnp.stack([lax.axis_index("req"), lax.axis_index("tp")]).astype(I32)
    place = jnp.broadcast_to(position[:, None], (2, HEAD_DIM))

    (packed,) = call(
        pack_kernel,
        [arr((REQ, 8, cols // 2))],
        [HBM] * 5,
        [owner[None, :], query, key_new, value_new, resid],
        [pltpu.VMEM((1, count), I32)]
        + [pltpu.VMEM((rows, cols), BF16)] * 4
        + [pltpu.SemaphoreType.DMA((5,))],
        room=ALL_ROOM,
    )
    arrived = trade(packed)
    numbers = pile(
        [owner[None, :], order[None, :], lengths[None, :], jnp.zeros((5, count), I32), page_table.T]
    )
    vectors = pile([x.astype(F32) for x in (out_bias, norm_gain, norm_bias, down_bias, up_bias)])
    pick, valid, arrange, arrange_own = call(
        index_kernel,
        [
            arr((4 * rows, 2 * count)),
            arr((heads * rows, positions), F32),
            arr((count, count)),
            arr((count, rows)),
        ],
        [VMEM, VMEM],
        [place, numbers],
        page_len=page_len,
    )

    here = position[0] >= 0
    pool = jnp.where(here, kv_pool, jnp.zeros_like(kv_pool))
    weight = jnp.where(here, out_weight, jnp.zeros_like(out_weight))

    (partial,) = call(
        attention_kernel,
        [arr((rows, width), F32)],
        [VMEM] * 7,
        [place, arrived, pick, valid, vectors, pool, weight],
        rows=rows,
    )
    pair = partial + swap(partial, "tp", 1)
    blocks, stream_own = call(
        norm_kernel,
        [arr((REQ, rows, cols)), arr((rows, cols))],
        [VMEM] * 4,
        [place, pair, swap(pair.astype(BF16), "tp", 3), vectors],
    )

    (part,) = call(
        up_kernel,
        [arr((count, hidden))],
        [VMEM] * 3,
        [trade(blocks), arrange, up_weight_t],
    )
    part = (part.astype(F32) + swap(part, "tp", 1).astype(F32)).astype(BF16)
    (feed,) = call(
        down_kernel,
        [arr((REQ, rows, cols), F32)],
        [VMEM] * 6,
        [part, swap(part, "tp", 3), vectors, down_weight, arrange_own, stream_own],
    )
    (out,) = call(finish_kernel, [arr((rows, cols))], [VMEM] * 2, [trade(feed), vectors])
    return out


def swap(x, axis, step):
    n = lax.axis_size(axis)
    return lax.ppermute(x, axis, [(i, i ^ step) for i in range(n)])


def origins(axis):
    n, me = lax.axis_size(axis), lax.axis_index(axis)
    if n > PAIRWISE:
        return jnp.arange(n, dtype=jnp.int32)
    offsets = [0]
    step = n // 2
    while step:
        offsets = offsets + [o ^ step for o in offsets]
        step //= 2
    return jnp.array(offsets, dtype=jnp.int32) ^ me


def gather_rows(x, axis):
    n = lax.axis_size(axis)
    if n > PAIRWISE:
        return lax.all_gather(x, axis, axis=0, tiled=True)
    step = n // 2
    while step:
        x = jnp.concatenate([x, swap(x, axis, step)], axis=0)
        step //= 2
    return x


def fold_rows(x, axis):
    n = lax.axis_size(axis)
    if n > PAIRWISE:
        return lax.psum_scatter(x, axis, scatter_dimension=0, tiled=True)
    step = 1
    while step < n:
        half = x.shape[0] // 2
        x = x[:half] + swap(x[half:], axis, step)
        step *= 2
    return x


def sum_pairs(x, axis):
    n = lax.axis_size(axis)
    step = 1
    while step < n:
        x = (x.astype(jnp.float32) + swap(x, axis, step).astype(jnp.float32)).astype(x.dtype)
        step *= 2
    return x


def on_any_mesh(
    query,
    key_new,
    value_new,
    resid,
    lengths,
    owner,
    page_table,
    kv_pool,
    out_weight,
    out_bias,
    norm_gain,
    norm_bias,
    up_weight_t,
    up_bias,
    down_weight,
    down_bias,
    order,
):
    f32, bf16, i32 = jnp.float32, jnp.bfloat16, jnp.int32
    n_req = lax.axis_size("req")
    n_tp = lax.axis_size("tp")
    me = lax.axis_index("req")
    me_tp = lax.axis_index("tp")
    rows, cols = query.shape
    width = cols * n_tp
    heads = cols // HEAD_DIM
    pool_pages, page_len = kv_pool.shape[1], kv_pool.shape[2]
    positions = pool_pages * page_len
    scale = 1.0 / math.sqrt(HEAD_DIM)

    origin = origins("req")
    packed = jnp.concatenate([query, key_new, value_new, resid], axis=1)
    arrived = gather_rows(packed, "req")

    same = owner[:, None] == owner[None, :]
    ids = jnp.arange(owner.shape[0], dtype=i32)
    rank = jnp.sum((same & (ids[None, :] < ids[:, None])).astype(i32), axis=1)
    slots = jnp.arange(rows, dtype=i32)
    mine = (owner == me)[None, :] & (rank[None, :] == slots[:, None])
    mine_i = mine.astype(i32)
    own_len = jnp.sum(mine_i * lengths[None, :], axis=1)
    own_table = jnp.sum(mine_i[:, :, None] * page_table[None], axis=1)
    origin_ids = (origin[:, None] * rows + slots[None, :]).reshape(-1)
    own_id = jnp.sum(mine_i * ids[None, :], axis=1)
    take_hot = (own_id[:, None] == origin_ids[None, :]).astype(bf16)
    own = jnp.dot(take_hot, arrived, preferred_element_type=f32).astype(bf16)
    query_own, key_own, value_own, resid_own = (own[:, i * cols : (i + 1) * cols] for i in range(4))

    pos = jnp.arange(positions, dtype=i32)
    page, within = pos // page_len, pos % page_len
    entry = jnp.arange(page_table.shape[1], dtype=i32)
    start = entry * page_len
    hit = (own_table[:, :, None] == page[None, None, :]) & (
        start[None, :, None] + within[None, None, :] < own_len[:, None, None]
    )
    valid = jnp.any(hit, axis=1)

    keys = kv_pool[0].reshape(positions, cols)
    values = kv_pool[1].reshape(positions, cols)
    head_of = jnp.arange(cols, dtype=i32) // HEAD_DIM
    head_mask = head_of[None, :] == jnp.arange(heads, dtype=i32)[:, None]
    spread_q = jnp.where(head_mask[:, None, :], query_own[None], 0).reshape(heads * rows, cols)
    scores = (
        lax.dot_general(spread_q, keys, (((1,), (1,)), ((), ())), preferred_element_type=f32) * scale
    ).reshape(heads, rows, positions)
    scores = jnp.where(valid[None], scores, -jnp.inf)
    self_score = (
        jnp.sum(
            (query_own.astype(f32) * key_own.astype(f32)).reshape(rows, heads, HEAD_DIM), axis=-1
        ).T
        * scale
    )
    top = jnp.maximum(jnp.max(scores, axis=2), self_score)
    weights = jnp.exp(scores - top[:, :, None])
    self_weight = jnp.exp(self_score - top)
    total = jnp.sum(weights, axis=2) + self_weight
    numer = jnp.dot(
        weights.astype(bf16).reshape(heads * rows, positions), values, preferred_element_type=f32
    ).reshape(heads, rows, cols)
    numer = numer + self_weight.astype(bf16).astype(f32)[:, :, None] * value_own.astype(f32)[None]
    attn = jnp.sum(
        jnp.where(head_mask[:, None, :], numer / total[:, :, None], 0.0), axis=0
    ).astype(bf16)

    extra = resid_own.astype(f32) + out_bias.astype(f32)[None, :]
    partial = jnp.dot(attn, out_weight, preferred_element_type=f32)
    place = (jnp.arange(n_tp, dtype=i32) == me_tp)[None, :, None]
    partial = (
        partial.reshape(rows, n_tp, cols) + jnp.where(place, extra[:, None, :], 0.0)
    ).reshape(rows, width)
    stream = sum_pairs(partial, "tp").astype(bf16)
    stream_f = stream.astype(f32)
    mean = jnp.mean(stream_f, axis=1, keepdims=True)
    var = jnp.mean((stream_f - mean) ** 2, axis=1, keepdims=True)
    inverse = lax.rsqrt(var + NORM_EPS)
    stream_own = lax.dynamic_slice_in_dim(stream, me_tp * cols, cols, axis=1)
    normed = (
        (stream_own.astype(f32) - mean) * inverse * norm_gain.astype(f32)[None, :]
        + norm_bias.astype(f32)[None, :]
    ).astype(bf16)

    normed_all = gather_rows(normed, "req")
    slot_of = owner * rows + rank
    wanted = slot_of[order[origin_ids]]
    place_hot = (wanted[:, None] == origin_ids[None, :]).astype(bf16)
    mine_hot = (wanted[:, None] == (me * rows + slots)[None, :]).astype(bf16)
    normed_out = jnp.dot(place_hot, normed_all, preferred_element_type=f32).astype(bf16)
    hidden = lax.dot_general(
        normed_out, up_weight_t, (((1,), (1,)), ((), ())), preferred_element_type=f32
    ).astype(bf16)
    summed = sum_pairs(hidden, "tp").astype(f32)
    activated = jax.nn.gelu(summed + up_bias.astype(f32)[None, :], approximate=False).astype(bf16)
    feed = jnp.dot(activated, down_weight, preferred_element_type=f32)
    feed = feed + jnp.dot(mine_hot, stream_own, preferred_element_type=f32)
    mixed = fold_rows(feed, "req")
    return (mixed + down_bias.astype(f32)[None, :]).astype(bf16)


def solution(mesh):
    pairs = mesh.shape["req"] == REQ and mesh.shape["tp"] == TP
    per_device = on_pairs if pairs else on_any_mesh
    in_specs = (
        P("req", "tp"),
        P("req", "tp"),
        P("req", "tp"),
        P("req", "tp"),
        P(),
        P(),
        P(),
        P(None, "req", None, "tp"),
        P("tp", None),
        P("tp"),
        P("tp"),
        P("tp"),
        P("req", "tp"),
        P("req"),
        P("req", "tp"),
        P("tp"),
        P(),
    )
    out_specs = P("req", "tp")
    return jax.shard_map(
        per_device, mesh=mesh, in_specs=in_specs, out_specs=out_specs, check_vma=False
    )
```

```python
import functools
import math

import jax
import jax.numpy as jnp
from jax import lax
from jax.experimental import pallas as pl
from jax.experimental.pallas import tpu as pltpu
from jax.sharding import PartitionSpec as P

HEAD_DIM = 128
NORM_EPS = 1e-05
PAIRWISE = 16
REQ, TP = 8, 4
WEIGHT_PARTS = 4
ATTENTION_ROOM = 53.2
ALL_ROOM = 58
F32, BF16, I32 = jnp.float32, jnp.bfloat16, jnp.int32
VMEM = pl.BlockSpec(memory_space=pltpu.VMEM)
HBM = pl.BlockSpec(memory_space=pltpu.HBM)


def iota(shape, dim):
    return lax.broadcasted_iota(I32, shape, dim)


def onto_mxu(a, b):
    return jnp.dot(a, b, preferred_element_type=F32)


def nt_dot(a, b):
    return lax.dot_general(a, b, (((1,), (1,)), ((), ())), preferred_element_type=F32)


def hot(condition):
    return jnp.where(condition, 1.0, 0.0).astype(BF16)


def pile(parts):
    height = sum(p.shape[0] for p in parts)
    at, piled = 0, 0
    for p in parts:
        around = ((at, height - at - p.shape[0]),) + ((0, 0),) * (p.ndim - 1)
        piled += jnp.pad(p, around)
        at += p.shape[0]
    return piled


def row(vectors, i, cols):
    return vectors[i * cols : (i + 1) * cols][None, :]


def pack_kernel(owner_in, query, key, value, resid, out, owner, q, k, v, r, sems):
    parts = ((owner_in, owner), (query, q), (key, k), (value, v), (resid, r))
    copies = [pltpu.make_async_copy(x, y, sems.at[i]) for i, (x, y) in enumerate(parts)]
    for copy in copies:
        copy.start()
    rows, cols = q.shape
    fields = 4
    count = REQ * rows
    shape = (REQ * fields, fields * rows)
    down, across = iota(shape, 0), iota(shape, 1)
    here = (count, fields * rows)
    of_mine = hot(iota(here, 0) == lax.axis_index("req") * rows + iota(here, 1) % rows)
    copies[0].wait()
    owner_of = onto_mxu(owner[...].astype(F32).astype(BF16), of_mine).astype(I32)
    pick = hot((down % fields == across // rows) & (owner_of == down // fields))
    for copy in copies[1:]:
        copy.wait()
    all_rows = jnp.concatenate([q[...], k[...], v[...], r[...]], axis=0)
    blocks = onto_mxu(pick, all_rows).astype(BF16)
    for d in range(REQ):
        block = blocks[d * fields : (d + 1) * fields]
        out[d, :fields, :] = block[:, : cols // 2]
        out[d, fields:, :] = block[:, cols // 2 :]


def index_kernel(place, numbers, pick, valid, arrange, arrange_own, *, page_len):
    owner, order, lengths = (numbers[i : i + 1, :] for i in range(3))
    table = numbers[8:, :]
    me = place[0:1, 0:1]
    count = owner.shape[1]
    rows = count // REQ
    square = (count, count)
    down, across = iota(square, 0), iota(square, 1)
    owner_row = owner
    same_place = down == across
    owner_col = jnp.sum(jnp.where(same_place, owner_row, 0), axis=1, keepdims=True)
    order_col = jnp.sum(jnp.where(same_place, order, 0), axis=1, keepdims=True)
    same_owner = owner_col == owner_row
    rank_row = jnp.sum(jnp.where(same_owner & (down < across), 1, 0), axis=0, keepdims=True)
    rank_col = jnp.sum(jnp.where(same_owner & (across < down), 1, 0), axis=1, keepdims=True)

    shape = pick.shape
    down_p, across_p = iota(shape, 0), iota(shape, 1)
    down_i = iota((shape[0], count), 0)
    mine = hot((owner_row == me) & (rank_row == down_i % rows))
    came = hot(iota((count, shape[1]), 0) // rows == iota((count, shape[1]), 1) // (2 * rows))
    from_there = onto_mxu(mine, came)
    pick[...] = hot((from_there > 0.5) & (down_p // rows == across_p % rows))

    shape = valid.shape
    slot = iota((shape[0], count), 0) % rows
    mine_v = hot((owner_row == me) & (rank_row == slot))
    table_v = nt_dot(mine_v, table.astype(F32).astype(BF16)).astype(I32)
    length_v = jnp.sum(jnp.where(mine_v > 0.5, lengths, 0), axis=1, keepdims=True)
    position = iota(shape, 1)
    page, within = position // page_len, position % page_len
    seen = jnp.zeros(shape, F32)
    for j in range(table.shape[0]):
        inside = (table_v[:, j : j + 1] == page) & (within + j * page_len < length_v)
        seen = jnp.where(inside, 1.0, seen)
    valid[...] = seen

    ordered = hot(order_col == across)
    holds = hot((owner_col == across // rows) & (rank_col == across % rows))
    arrange[...] = onto_mxu(ordered, holds).astype(BF16)
    here = hot((owner_col == me) & (rank_col == iota(arrange_own.shape, 1)))
    arrange_own[...] = onto_mxu(ordered, here).astype(BF16)


def attention_kernel(
    place, arrived, pick, valid, vectors, pool_in, weight_in, partial, pool, weight, sems, *, rows
):
    deep = weight.shape[0] // WEIGHT_PARTS
    copies = [pltpu.make_async_copy(pool_in.at[i], pool.at[i], sems.at[i]) for i in range(2)]
    for i in range(WEIGHT_PARTS):
        part = pl.ds(i * deep, deep)
        copies.append(
            pltpu.make_async_copy(weight_in.at[part], weight.at[part], sems.at[2 + i])
        )
    for copy in copies:
        copy.start()
    half = arrived.shape[2]
    cols = 2 * half
    heads = cols // HEAD_DIM
    scale = 1.0 / math.sqrt(HEAD_DIM)
    came = arrived[...].reshape(-1, half)
    which = (iota(pick.shape, 1) // rows) % 2
    chosen = pick[...].astype(F32)
    own = jnp.concatenate(
        [onto_mxu(jnp.where(which == i, chosen, 0.0).astype(BF16), came) for i in range(2)], axis=1
    )
    query, key, value, resid = (own[i * rows : (i + 1) * rows] for i in range(4))

    def tile(x):
        return jnp.concatenate([x] * heads, axis=0)

    shape = (heads * rows, cols)
    in_head = iota(shape, 0) // rows == iota(shape, 1) // HEAD_DIM
    wide = jnp.where(in_head, tile(query), 0.0)
    positions = valid.shape[1]
    self_score = jnp.sum(wide * tile(key), axis=1, keepdims=True) * scale
    copies[0].wait()
    scores = nt_dot(wide.astype(BF16), pool[0].reshape(positions, cols)) * scale
    scores = jnp.where(valid[...] > 0.5, scores, -jnp.inf)
    top = jnp.maximum(jnp.max(scores, axis=1, keepdims=True), self_score)
    weights = jnp.exp(scores - top)
    self_weight = jnp.exp(self_score - top)
    total = jnp.sum(weights, axis=1, keepdims=True) + self_weight
    copies[1].wait()
    numer = onto_mxu(weights.astype(BF16), pool[1].reshape(positions, cols))
    numer = numer + self_weight.astype(BF16).astype(F32) * tile(value)
    numer = jnp.where(in_head, numer / total, 0.0)
    attn = sum(numer[i * rows : (i + 1) * rows] for i in range(heads))
    attn = jnp.concatenate([attn, jnp.zeros_like(attn)], axis=0).astype(BF16)
    for copy in copies[2:]:
        copy.wait()
    projected = onto_mxu(attn, weight[...])[:rows]
    extra = resid + row(vectors, 0, cols)
    for t in range(TP):
        mine = jnp.where(place[1:2, 0:1] == t, extra, 0.0)
        partial[:, t * cols : (t + 1) * cols] = projected[:, t * cols : (t + 1) * cols] + mine


def norm_kernel(place, near, far, vectors, blocks, stream_own):
    mine = near[...].astype(BF16).astype(F32)
    stream = (mine + far[...].astype(F32)).astype(BF16).astype(F32)
    width = stream.shape[1]
    cols = width // TP
    mean = jnp.sum(stream, axis=1, keepdims=True) / width
    var = jnp.sum((stream - mean) ** 2, axis=1, keepdims=True) / width
    own = stream[:, :cols]
    for t in range(1, TP):
        own = jnp.where(place[1:2, 0:1] == t, stream[:, t * cols : (t + 1) * cols], own)
    stream_own[...] = own.astype(BF16)
    gain, bias = row(vectors, 1, cols), row(vectors, 2, cols)
    block = ((own - mean) * lax.rsqrt(var + NORM_EPS) * gain + bias).astype(BF16)
    for d in range(REQ):
        blocks[d] = block


def up_kernel(rows_in, arrange, weight, out):
    came = rows_in[...].reshape(-1, rows_in.shape[2])
    ordered = onto_mxu(arrange[...], came).astype(BF16)
    out[...] = nt_dot(ordered, weight[...]).astype(BF16)


def down_kernel(near, far, vectors, weight, arrange_own, stream_own, out):
    hidden = near[...].astype(F32) + far[...].astype(F32)
    hidden = hidden + vectors[vectors.shape[0] - hidden.shape[1] :][None, :]
    activated = (0.5 * hidden * (1.0 + lax.erf(hidden * math.sqrt(0.5)))).astype(BF16)
    feed = onto_mxu(activated, weight[...]) + onto_mxu(arrange_own[...], stream_own[...])
    rows = out.shape[1]
    for d in range(REQ):
        out[REQ - 1 - d] = feed[d * rows : (d + 1) * rows]


def finish_kernel(pieces, vectors, out):
    cols = out.shape[1]
    out[...] = (jnp.sum(pieces[...], axis=0) + row(vectors, 3, cols)).astype(BF16)


def call(kernel, shapes, specs, args, scratch=(), room=16, **fixed):
    moved = sum(a.size * a.dtype.itemsize for a in args)
    return pl.pallas_call(
        functools.partial(kernel, **fixed) if fixed else kernel,
        out_shape=shapes,
        in_specs=specs,
        out_specs=[VMEM] * len(shapes),
        scratch_shapes=scratch,
        compiler_params=pltpu.CompilerParams(vmem_limit_bytes=int(room * 2**20)),
        cost_estimate=pl.CostEstimate(flops=0, bytes_accessed=moved, transcendentals=0),
    )(*args)


def trade(blocks):
    return lax.all_to_all(blocks, "req", 0, 0, tiled=True)


def trade_back(blocks):
    group = [list(reversed(range(REQ)))]
    return lax.all_to_all(blocks, "req", 0, 0, tiled=True, axis_index_groups=group)


def on_pairs(
    query,
    key_new,
    value_new,
    resid,
    lengths,
    owner,
    page_table,
    kv_pool,
    out_weight,
    out_bias,
    norm_gain,
    norm_bias,
    up_weight_t,
    up_bias,
    down_weight,
    down_bias,
    order,
):
    rows, cols = query.shape
    width = cols * TP
    pool_pages, page_len = kv_pool.shape[1], kv_pool.shape[2]
    positions = pool_pages * page_len
    heads = cols // HEAD_DIM
    count = owner.shape[0]
    hidden = up_bias.shape[0]

    def arr(shape, dtype=BF16):
        return jax.ShapeDtypeStruct(shape, dtype)

    position = jnp.stack([lax.axis_index("req"), lax.axis_index("tp")]).astype(I32)
    place = jnp.broadcast_to(position[:, None], (2, HEAD_DIM))

    (packed,) = call(
        pack_kernel,
        [arr((REQ, 8, cols // 2))],
        [HBM] * 5,
        [owner[None, :], query, key_new, value_new, resid],
        [pltpu.VMEM((1, count), I32)]
        + [pltpu.VMEM((rows, cols), BF16)] * 4
        + [pltpu.SemaphoreType.DMA((5,))],
        room=ALL_ROOM,
    )
    arrived = trade(packed)
    numbers = pile(
        [owner[None, :], order[None, :], lengths[None, :], jnp.zeros((5, count), I32), page_table.T]
    )
    vectors = pile([x.astype(F32) for x in (out_bias, norm_gain, norm_bias, down_bias, up_bias)])
    pick, valid, arrange, arrange_own = call(
        index_kernel,
        [
            arr((4 * rows, 2 * count)),
            arr((heads * rows, positions), F32),
            arr((count, count)),
            arr((count, rows)),
        ],
        [VMEM, VMEM],
        [place, numbers],
        page_len=page_len,
    )

    (partial,) = call(
        attention_kernel,
        [arr((rows, width), F32)],
        [VMEM] * 5 + [HBM] * 2,
        [place, arrived, pick, valid, vectors, kv_pool, out_weight],
        [
            pltpu.VMEM(kv_pool.shape, BF16),
            pltpu.VMEM(out_weight.shape, BF16),
            pltpu.SemaphoreType.DMA((2 + WEIGHT_PARTS,)),
        ],
        room=ATTENTION_ROOM,
        rows=rows,
    )
    pair = partial + swap(partial, "tp", 1)
    blocks, stream_own = call(
        norm_kernel,
        [arr((REQ, rows, cols)), arr((rows, cols))],
        [VMEM] * 4,
        [place, pair, swap(pair.astype(BF16), "tp", 3), vectors],
    )

    (part,) = call(
        up_kernel,
        [arr((count, hidden))],
        [VMEM] * 3,
        [trade(blocks), arrange, up_weight_t],
    )
    part = (part.astype(F32) + swap(part, "tp", 1).astype(F32)).astype(BF16)
    (feed,) = call(
        down_kernel,
        [arr((REQ, rows, cols), F32)],
        [VMEM] * 6,
        [part, swap(part, "tp", 3), vectors, down_weight, arrange_own, stream_own],
    )
    (out,) = call(finish_kernel, [arr((rows, cols))], [VMEM] * 2, [trade_back(feed), vectors])
    return out


def swap(x, axis, step):
    n = lax.axis_size(axis)
    return lax.ppermute(x, axis, [(i, i ^ step) for i in range(n)])


def origins(axis):
    n, me = lax.axis_size(axis), lax.axis_index(axis)
    if n > PAIRWISE:
        return jnp.arange(n, dtype=jnp.int32)
    offsets = [0]
    step = n // 2
    while step:
        offsets = offsets + [o ^ step for o in offsets]
        step //= 2
    return jnp.array(offsets, dtype=jnp.int32) ^ me


def gather_rows(x, axis):
    n = lax.axis_size(axis)
    if n > PAIRWISE:
        return lax.all_gather(x, axis, axis=0, tiled=True)
    step = n // 2
    while step:
        x = jnp.concatenate([x, swap(x, axis, step)], axis=0)
        step //= 2
    return x


def fold_rows(x, axis):
    n = lax.axis_size(axis)
    if n > PAIRWISE:
        return lax.psum_scatter(x, axis, scatter_dimension=0, tiled=True)
    step = 1
    while step < n:
        half = x.shape[0] // 2
        x = x[:half] + swap(x[half:], axis, step)
        step *= 2
    return x


def sum_pairs(x, axis):
    n = lax.axis_size(axis)
    step = 1
    while step < n:
        x = (x.astype(jnp.float32) + swap(x, axis, step).astype(jnp.float32)).astype(x.dtype)
        step *= 2
    return x


def on_any_mesh(
    query,
    key_new,
    value_new,
    resid,
    lengths,
    owner,
    page_table,
    kv_pool,
    out_weight,
    out_bias,
    norm_gain,
    norm_bias,
    up_weight_t,
    up_bias,
    down_weight,
    down_bias,
    order,
):
    f32, bf16, i32 = jnp.float32, jnp.bfloat16, jnp.int32
    n_req = lax.axis_size("req")
    n_tp = lax.axis_size("tp")
    me = lax.axis_index("req")
    me_tp = lax.axis_index("tp")
    rows, cols = query.shape
    width = cols * n_tp
    heads = cols // HEAD_DIM
    pool_pages, page_len = kv_pool.shape[1], kv_pool.shape[2]
    positions = pool_pages * page_len
    scale = 1.0 / math.sqrt(HEAD_DIM)

    origin = origins("req")
    packed = jnp.concatenate([query, key_new, value_new, resid], axis=1)
    arrived = gather_rows(packed, "req")

    same = owner[:, None] == owner[None, :]
    ids = jnp.arange(owner.shape[0], dtype=i32)
    rank = jnp.sum((same & (ids[None, :] < ids[:, None])).astype(i32), axis=1)
    slots = jnp.arange(rows, dtype=i32)
    mine = (owner == me)[None, :] & (rank[None, :] == slots[:, None])
    mine_i = mine.astype(i32)
    own_len = jnp.sum(mine_i * lengths[None, :], axis=1)
    own_table = jnp.sum(mine_i[:, :, None] * page_table[None], axis=1)
    origin_ids = (origin[:, None] * rows + slots[None, :]).reshape(-1)
    own_id = jnp.sum(mine_i * ids[None, :], axis=1)
    take_hot = (own_id[:, None] == origin_ids[None, :]).astype(bf16)
    own = jnp.dot(take_hot, arrived, preferred_element_type=f32).astype(bf16)
    query_own, key_own, value_own, resid_own = (own[:, i * cols : (i + 1) * cols] for i in range(4))

    pos = jnp.arange(positions, dtype=i32)
    page, within = pos // page_len, pos % page_len
    entry = jnp.arange(page_table.shape[1], dtype=i32)
    start = entry * page_len
    hit = (own_table[:, :, None] == page[None, None, :]) & (
        start[None, :, None] + within[None, None, :] < own_len[:, None, None]
    )
    valid = jnp.any(hit, axis=1)

    keys = kv_pool[0].reshape(positions, cols)
    values = kv_pool[1].reshape(positions, cols)
    head_of = jnp.arange(cols, dtype=i32) // HEAD_DIM
    head_mask = head_of[None, :] == jnp.arange(heads, dtype=i32)[:, None]
    spread_q = jnp.where(head_mask[:, None, :], query_own[None], 0).reshape(heads * rows, cols)
    scores = (
        lax.dot_general(spread_q, keys, (((1,), (1,)), ((), ())), preferred_element_type=f32) * scale
    ).reshape(heads, rows, positions)
    scores = jnp.where(valid[None], scores, -jnp.inf)
    self_score = (
        jnp.sum(
            (query_own.astype(f32) * key_own.astype(f32)).reshape(rows, heads, HEAD_DIM), axis=-1
        ).T
        * scale
    )
    top = jnp.maximum(jnp.max(scores, axis=2), self_score)
    weights = jnp.exp(scores - top[:, :, None])
    self_weight = jnp.exp(self_score - top)
    total = jnp.sum(weights, axis=2) + self_weight
    numer = jnp.dot(
        weights.astype(bf16).reshape(heads * rows, positions), values, preferred_element_type=f32
    ).reshape(heads, rows, cols)
    numer = numer + self_weight.astype(bf16).astype(f32)[:, :, None] * value_own.astype(f32)[None]
    attn = jnp.sum(
        jnp.where(head_mask[:, None, :], numer / total[:, :, None], 0.0), axis=0
    ).astype(bf16)

    extra = resid_own.astype(f32) + out_bias.astype(f32)[None, :]
    partial = jnp.dot(attn, out_weight, preferred_element_type=f32)
    place = (jnp.arange(n_tp, dtype=i32) == me_tp)[None, :, None]
    partial = (
        partial.reshape(rows, n_tp, cols) + jnp.where(place, extra[:, None, :], 0.0)
    ).reshape(rows, width)
    stream = sum_pairs(partial, "tp").astype(bf16)
    stream_f = stream.astype(f32)
    mean = jnp.mean(stream_f, axis=1, keepdims=True)
    var = jnp.mean((stream_f - mean) ** 2, axis=1, keepdims=True)
    inverse = lax.rsqrt(var + NORM_EPS)
    stream_own = lax.dynamic_slice_in_dim(stream, me_tp * cols, cols, axis=1)
    normed = (
        (stream_own.astype(f32) - mean) * inverse * norm_gain.astype(f32)[None, :]
        + norm_bias.astype(f32)[None, :]
    ).astype(bf16)

    normed_all = gather_rows(normed, "req")
    slot_of = owner * rows + rank
    wanted = slot_of[order[origin_ids]]
    place_hot = (wanted[:, None] == origin_ids[None, :]).astype(bf16)
    mine_hot = (wanted[:, None] == (me * rows + slots)[None, :]).astype(bf16)
    normed_out = jnp.dot(place_hot, normed_all, preferred_element_type=f32).astype(bf16)
    hidden = lax.dot_general(
        normed_out, up_weight_t, (((1,), (1,)), ((), ())), preferred_element_type=f32
    ).astype(bf16)
    summed = sum_pairs(hidden, "tp").astype(f32)
    activated = jax.nn.gelu(summed + up_bias.astype(f32)[None, :], approximate=False).astype(bf16)
    feed = jnp.dot(activated, down_weight, preferred_element_type=f32)
    feed = feed + jnp.dot(mine_hot, stream_own, preferred_element_type=f32)
    mixed = fold_rows(feed, "req")
    return (mixed + down_bias.astype(f32)[None, :]).astype(bf16)


def solution(mesh):
    pairs = mesh.shape["req"] == REQ and mesh.shape["tp"] == TP
    per_device = on_pairs if pairs else on_any_mesh
    in_specs = (
        P("req", "tp"),
        P("req", "tp"),
        P("req", "tp"),
        P("req", "tp"),
        P(),
        P(),
        P(),
        P(None, "req", None, "tp"),
        P("tp", None),
        P("tp"),
        P("tp"),
        P("tp"),
        P("req", "tp"),
        P("req"),
        P("req", "tp"),
        P("tp"),
        P(),
    )
    out_specs = P("req", "tp")
    return jax.shard_map(
        per_device, mesh=mesh, in_specs=in_specs, out_specs=out_specs, check_vma=False
    )
```

```python
import functools
import math

import jax
import jax.numpy as jnp
from jax import lax
from jax.experimental import pallas as pl
from jax.experimental.pallas import tpu as pltpu
from jax.sharding import PartitionSpec as P

HEAD_DIM = 128
NORM_EPS = 1e-05
PAIRWISE = 16
REQ, TP = 8, 4
WEIGHT_PARTS = 4
ATTENTION_ROOM = 53.2
ALL_ROOM = 58
F32, BF16, I32 = jnp.float32, jnp.bfloat16, jnp.int32
VMEM = pl.BlockSpec(memory_space=pltpu.VMEM)
HBM = pl.BlockSpec(memory_space=pltpu.HBM)


def iota(shape, dim):
    return lax.broadcasted_iota(I32, shape, dim)


def onto_mxu(a, b):
    return jnp.dot(a, b, preferred_element_type=F32)


def nt_dot(a, b):
    return lax.dot_general(a, b, (((1,), (1,)), ((), ())), preferred_element_type=F32)


def hot(condition):
    return jnp.where(condition, 1.0, 0.0).astype(BF16)


def pile(parts):
    height = sum(p.shape[0] for p in parts)
    at, piled = 0, 0
    for p in parts:
        around = ((at, height - at - p.shape[0]),) + ((0, 0),) * (p.ndim - 1)
        piled += jnp.pad(p, around)
        at += p.shape[0]
    return piled


def row(vectors, i, cols):
    return vectors[i * cols : (i + 1) * cols][None, :]


def pack_kernel(owner_in, query, key, value, resid, out, owner, q, k, v, r, sems):
    parts = ((owner_in, owner), (query, q), (key, k), (value, v), (resid, r))
    copies = [pltpu.make_async_copy(x, y, sems.at[i]) for i, (x, y) in enumerate(parts)]
    for copy in copies:
        copy.start()
    rows, cols = q.shape
    fields = 4
    count = REQ * rows
    shape = (REQ * fields, fields * rows)
    down, across = iota(shape, 0), iota(shape, 1)
    here = (count, fields * rows)
    of_mine = hot(iota(here, 0) == lax.axis_index("req") * rows + iota(here, 1) % rows)
    copies[0].wait()
    owner_of = onto_mxu(owner[...].astype(F32).astype(BF16), of_mine).astype(I32)
    pick = hot((down % fields == across // rows) & (owner_of == down // fields))
    for copy in copies[1:]:
        copy.wait()
    all_rows = jnp.concatenate([q[...], k[...], v[...], r[...]], axis=0)
    blocks = onto_mxu(pick, all_rows).astype(BF16)
    for d in range(REQ):
        block = blocks[d * fields : (d + 1) * fields]
        out[REQ - 1 - d, :fields, :] = block[:, : cols // 2]
        out[REQ - 1 - d, fields:, :] = block[:, cols // 2 :]


def index_kernel(place, numbers, pick, valid, arrange, arrange_own, *, page_len):
    owner, order, lengths = (numbers[i : i + 1, :] for i in range(3))
    table = numbers[8:, :]
    me = place[0:1, 0:1]
    count = owner.shape[1]
    rows = count // REQ
    square = (count, count)
    down, across = iota(square, 0), iota(square, 1)
    owner_row = owner
    same_place = down == across
    owner_col = jnp.sum(jnp.where(same_place, owner_row, 0), axis=1, keepdims=True)
    order_col = jnp.sum(jnp.where(same_place, order, 0), axis=1, keepdims=True)
    same_owner = owner_col == owner_row
    rank_row = jnp.sum(jnp.where(same_owner & (down < across), 1, 0), axis=0, keepdims=True)
    rank_col = jnp.sum(jnp.where(same_owner & (across < down), 1, 0), axis=1, keepdims=True)

    shape = pick.shape
    down_p, across_p = iota(shape, 0), iota(shape, 1)
    down_i = iota((shape[0], count), 0)
    mine = hot((owner_row == me) & (rank_row == down_i % rows))
    source = REQ - 1 - iota((count, shape[1]), 1) // (2 * rows)
    came = hot(iota((count, shape[1]), 0) // rows == source)
    from_there = onto_mxu(mine, came)
    pick[...] = hot((from_there > 0.5) & (down_p // rows == across_p % rows))

    shape = valid.shape
    slot = iota((shape[0], count), 0) % rows
    mine_v = hot((owner_row == me) & (rank_row == slot))
    table_v = nt_dot(mine_v, table.astype(F32).astype(BF16)).astype(I32)
    length_v = jnp.sum(jnp.where(mine_v > 0.5, lengths, 0), axis=1, keepdims=True)
    position = iota(shape, 1)
    page, within = position // page_len, position % page_len
    seen = jnp.zeros(shape, F32)
    for j in range(table.shape[0]):
        inside = (table_v[:, j : j + 1] == page) & (within + j * page_len < length_v)
        seen = jnp.where(inside, 1.0, seen)
    valid[...] = seen

    ordered = hot(order_col == across)
    holds = hot((owner_col == REQ - 1 - across // rows) & (rank_col == across % rows))
    arrange[...] = onto_mxu(ordered, holds).astype(BF16)
    here = hot((owner_col == me) & (rank_col == iota(arrange_own.shape, 1)))
    arrange_own[...] = onto_mxu(ordered, here).astype(BF16)


def attention_kernel(
    place, arrived, pick, valid, vectors, pool_in, weight_in, partial, pool, weight, sems, *, rows
):
    deep = weight.shape[0] // WEIGHT_PARTS
    copies = [pltpu.make_async_copy(pool_in.at[i], pool.at[i], sems.at[i]) for i in range(2)]
    for i in range(WEIGHT_PARTS):
        part = pl.ds(i * deep, deep)
        copies.append(
            pltpu.make_async_copy(weight_in.at[part], weight.at[part], sems.at[2 + i])
        )
    for copy in copies:
        copy.start()
    half = arrived.shape[2]
    cols = 2 * half
    heads = cols // HEAD_DIM
    scale = 1.0 / math.sqrt(HEAD_DIM)
    came = arrived[...].reshape(-1, half)
    which = (iota(pick.shape, 1) // rows) % 2
    chosen = pick[...].astype(F32)
    own = jnp.concatenate(
        [onto_mxu(jnp.where(which == i, chosen, 0.0).astype(BF16), came) for i in range(2)], axis=1
    )
    query, key, value, resid = (own[i * rows : (i + 1) * rows] for i in range(4))

    def tile(x):
        return jnp.concatenate([x] * heads, axis=0)

    shape = (heads * rows, cols)
    in_head = iota(shape, 0) // rows == iota(shape, 1) // HEAD_DIM
    wide = jnp.where(in_head, tile(query), 0.0)
    positions = valid.shape[1]
    self_score = jnp.sum(wide * tile(key), axis=1, keepdims=True) * scale
    copies[0].wait()
    scores = nt_dot(wide.astype(BF16), pool[0].reshape(positions, cols)) * scale
    scores = jnp.where(valid[...] > 0.5, scores, -jnp.inf)
    top = jnp.maximum(jnp.max(scores, axis=1, keepdims=True), self_score)
    weights = jnp.exp(scores - top)
    self_weight = jnp.exp(self_score - top)
    total = jnp.sum(weights, axis=1, keepdims=True) + self_weight
    copies[1].wait()
    numer = onto_mxu(weights.astype(BF16), pool[1].reshape(positions, cols))
    numer = numer + self_weight.astype(BF16).astype(F32) * tile(value)
    numer = jnp.where(in_head, numer / total, 0.0)
    attn = sum(numer[i * rows : (i + 1) * rows] for i in range(heads))
    attn = jnp.concatenate([attn, jnp.zeros_like(attn)], axis=0).astype(BF16)
    for copy in copies[2:]:
        copy.wait()
    projected = onto_mxu(attn, weight[...])[:rows]
    extra = resid + row(vectors, 0, cols)
    for t in range(TP):
        mine = jnp.where(place[1:2, 0:1] == t, extra, 0.0)
        partial[:, t * cols : (t + 1) * cols] = projected[:, t * cols : (t + 1) * cols] + mine


def norm_kernel(place, near, far, vectors, blocks, stream_own):
    mine = near[...].astype(BF16).astype(F32)
    stream = (mine + far[...].astype(F32)).astype(BF16).astype(F32)
    width = stream.shape[1]
    cols = width // TP
    mean = jnp.sum(stream, axis=1, keepdims=True) / width
    var = jnp.sum((stream - mean) ** 2, axis=1, keepdims=True) / width
    own = stream[:, :cols]
    for t in range(1, TP):
        own = jnp.where(place[1:2, 0:1] == t, stream[:, t * cols : (t + 1) * cols], own)
    stream_own[...] = own.astype(BF16)
    gain, bias = row(vectors, 1, cols), row(vectors, 2, cols)
    block = ((own - mean) * lax.rsqrt(var + NORM_EPS) * gain + bias).astype(BF16)
    for d in range(REQ):
        blocks[d] = block


def up_kernel(rows_in, arrange, weight, out):
    came = rows_in[...].reshape(-1, rows_in.shape[2])
    ordered = onto_mxu(arrange[...], came).astype(BF16)
    out[...] = nt_dot(ordered, weight[...]).astype(BF16)


def down_kernel(near, far, vectors, weight, arrange_own, stream_own, out):
    hidden = near[...].astype(F32) + far[...].astype(F32)
    hidden = hidden + vectors[vectors.shape[0] - hidden.shape[1] :][None, :]
    activated = (0.5 * hidden * (1.0 + lax.erf(hidden * math.sqrt(0.5)))).astype(BF16)
    feed = onto_mxu(activated, weight[...]) + onto_mxu(arrange_own[...], stream_own[...])
    rows = out.shape[1]
    for d in range(REQ):
        out[REQ - 1 - d] = feed[d * rows : (d + 1) * rows]


def finish_kernel(pieces, vectors, out):
    cols = out.shape[1]
    out[...] = (jnp.sum(pieces[...], axis=0) + row(vectors, 3, cols)).astype(BF16)


def call(kernel, shapes, specs, args, scratch=(), room=16, **fixed):
    moved = sum(a.size * a.dtype.itemsize for a in args)
    return pl.pallas_call(
        functools.partial(kernel, **fixed) if fixed else kernel,
        out_shape=shapes,
        in_specs=specs,
        out_specs=[VMEM] * len(shapes),
        scratch_shapes=scratch,
        compiler_params=pltpu.CompilerParams(vmem_limit_bytes=int(room * 2**20)),
        cost_estimate=pl.CostEstimate(flops=0, bytes_accessed=moved, transcendentals=0),
    )(*args)


def trade(blocks):
    group = [list(reversed(range(REQ)))]
    return lax.all_to_all(blocks, "req", 0, 0, tiled=True, axis_index_groups=group)


def on_pairs(
    query,
    key_new,
    value_new,
    resid,
    lengths,
    owner,
    page_table,
    kv_pool,
    out_weight,
    out_bias,
    norm_gain,
    norm_bias,
    up_weight_t,
    up_bias,
    down_weight,
    down_bias,
    order,
):
    rows, cols = query.shape
    width = cols * TP
    pool_pages, page_len = kv_pool.shape[1], kv_pool.shape[2]
    positions = pool_pages * page_len
    heads = cols // HEAD_DIM
    count = owner.shape[0]
    hidden = up_bias.shape[0]

    def arr(shape, dtype=BF16):
        return jax.ShapeDtypeStruct(shape, dtype)

    position = jnp.stack([lax.axis_index("req"), lax.axis_index("tp")]).astype(I32)
    place = jnp.broadcast_to(position[:, None], (2, HEAD_DIM))

    (packed,) = call(
        pack_kernel,
        [arr((REQ, 8, cols // 2))],
        [HBM] * 5,
        [owner[None, :], query, key_new, value_new, resid],
        [pltpu.VMEM((1, count), I32)]
        + [pltpu.VMEM((rows, cols), BF16)] * 4
        + [pltpu.SemaphoreType.DMA((5,))],
        room=ALL_ROOM,
    )
    arrived = trade(packed)
    numbers = pile(
        [owner[None, :], order[None, :], lengths[None, :], jnp.zeros((5, count), I32), page_table.T]
    )
    vectors = pile([x.astype(F32) for x in (out_bias, norm_gain, norm_bias, down_bias, up_bias)])
    pick, valid, arrange, arrange_own = call(
        index_kernel,
        [
            arr((4 * rows, 2 * count)),
            arr((heads * rows, positions), F32),
            arr((count, count)),
            arr((count, rows)),
        ],
        [VMEM, VMEM],
        [place, numbers],
        page_len=page_len,
    )

    (partial,) = call(
        attention_kernel,
        [arr((rows, width), F32)],
        [VMEM] * 5 + [HBM] * 2,
        [place, arrived, pick, valid, vectors, kv_pool, out_weight],
        [
            pltpu.VMEM(kv_pool.shape, BF16),
            pltpu.VMEM(out_weight.shape, BF16),
            pltpu.SemaphoreType.DMA((2 + WEIGHT_PARTS,)),
        ],
        room=ATTENTION_ROOM,
        rows=rows,
    )
    pair = partial + swap(partial, "tp", 1)
    blocks, stream_own = call(
        norm_kernel,
        [arr((REQ, rows, cols)), arr((rows, cols))],
        [VMEM] * 4,
        [place, pair, swap(pair.astype(BF16), "tp", 3), vectors],
    )

    (part,) = call(
        up_kernel,
        [arr((count, hidden))],
        [VMEM] * 3,
        [trade(blocks), arrange, up_weight_t],
    )
    part = (part.astype(F32) + swap(part, "tp", 1).astype(F32)).astype(BF16)
    (feed,) = call(
        down_kernel,
        [arr((REQ, rows, cols), F32)],
        [VMEM] * 6,
        [part, swap(part, "tp", 3), vectors, down_weight, arrange_own, stream_own],
    )
    (out,) = call(finish_kernel, [arr((rows, cols))], [VMEM] * 2, [trade(feed), vectors])
    return out


def swap(x, axis, step):
    n = lax.axis_size(axis)
    return lax.ppermute(x, axis, [(i, i ^ step) for i in range(n)])


def origins(axis):
    n, me = lax.axis_size(axis), lax.axis_index(axis)
    if n > PAIRWISE:
        return jnp.arange(n, dtype=jnp.int32)
    offsets = [0]
    step = n // 2
    while step:
        offsets = offsets + [o ^ step for o in offsets]
        step //= 2
    return jnp.array(offsets, dtype=jnp.int32) ^ me


def gather_rows(x, axis):
    n = lax.axis_size(axis)
    if n > PAIRWISE:
        return lax.all_gather(x, axis, axis=0, tiled=True)
    step = n // 2
    while step:
        x = jnp.concatenate([x, swap(x, axis, step)], axis=0)
        step //= 2
    return x


def fold_rows(x, axis):
    n = lax.axis_size(axis)
    if n > PAIRWISE:
        return lax.psum_scatter(x, axis, scatter_dimension=0, tiled=True)
    step = 1
    while step < n:
        half = x.shape[0] // 2
        x = x[:half] + swap(x[half:], axis, step)
        step *= 2
    return x


def sum_pairs(x, axis):
    n = lax.axis_size(axis)
    step = 1
    while step < n:
        x = (x.astype(jnp.float32) + swap(x, axis, step).astype(jnp.float32)).astype(x.dtype)
        step *= 2
    return x


def on_any_mesh(
    query,
    key_new,
    value_new,
    resid,
    lengths,
    owner,
    page_table,
    kv_pool,
    out_weight,
    out_bias,
    norm_gain,
    norm_bias,
    up_weight_t,
    up_bias,
    down_weight,
    down_bias,
    order,
):
    f32, bf16, i32 = jnp.float32, jnp.bfloat16, jnp.int32
    n_req = lax.axis_size("req")
    n_tp = lax.axis_size("tp")
    me = lax.axis_index("req")
    me_tp = lax.axis_index("tp")
    rows, cols = query.shape
    width = cols * n_tp
    heads = cols // HEAD_DIM
    pool_pages, page_len = kv_pool.shape[1], kv_pool.shape[2]
    positions = pool_pages * page_len
    scale = 1.0 / math.sqrt(HEAD_DIM)

    origin = origins("req")
    packed = jnp.concatenate([query, key_new, value_new, resid], axis=1)
    arrived = gather_rows(packed, "req")

    same = owner[:, None] == owner[None, :]
    ids = jnp.arange(owner.shape[0], dtype=i32)
    rank = jnp.sum((same & (ids[None, :] < ids[:, None])).astype(i32), axis=1)
    slots = jnp.arange(rows, dtype=i32)
    mine = (owner == me)[None, :] & (rank[None, :] == slots[:, None])
    mine_i = mine.astype(i32)
    own_len = jnp.sum(mine_i * lengths[None, :], axis=1)
    own_table = jnp.sum(mine_i[:, :, None] * page_table[None], axis=1)
    origin_ids = (origin[:, None] * rows + slots[None, :]).reshape(-1)
    own_id = jnp.sum(mine_i * ids[None, :], axis=1)
    take_hot = (own_id[:, None] == origin_ids[None, :]).astype(bf16)
    own = jnp.dot(take_hot, arrived, preferred_element_type=f32).astype(bf16)
    query_own, key_own, value_own, resid_own = (own[:, i * cols : (i + 1) * cols] for i in range(4))

    pos = jnp.arange(positions, dtype=i32)
    page, within = pos // page_len, pos % page_len
    entry = jnp.arange(page_table.shape[1], dtype=i32)
    start = entry * page_len
    hit = (own_table[:, :, None] == page[None, None, :]) & (
        start[None, :, None] + within[None, None, :] < own_len[:, None, None]
    )
    valid = jnp.any(hit, axis=1)

    keys = kv_pool[0].reshape(positions, cols)
    values = kv_pool[1].reshape(positions, cols)
    head_of = jnp.arange(cols, dtype=i32) // HEAD_DIM
    head_mask = head_of[None, :] == jnp.arange(heads, dtype=i32)[:, None]
    spread_q = jnp.where(head_mask[:, None, :], query_own[None], 0).reshape(heads * rows, cols)
    scores = (
        lax.dot_general(spread_q, keys, (((1,), (1,)), ((), ())), preferred_element_type=f32) * scale
    ).reshape(heads, rows, positions)
    scores = jnp.where(valid[None], scores, -jnp.inf)
    self_score = (
        jnp.sum(
            (query_own.astype(f32) * key_own.astype(f32)).reshape(rows, heads, HEAD_DIM), axis=-1
        ).T
        * scale
    )
    top = jnp.maximum(jnp.max(scores, axis=2), self_score)
    weights = jnp.exp(scores - top[:, :, None])
    self_weight = jnp.exp(self_score - top)
    total = jnp.sum(weights, axis=2) + self_weight
    numer = jnp.dot(
        weights.astype(bf16).reshape(heads * rows, positions), values, preferred_element_type=f32
    ).reshape(heads, rows, cols)
    numer = numer + self_weight.astype(bf16).astype(f32)[:, :, None] * value_own.astype(f32)[None]
    attn = jnp.sum(
        jnp.where(head_mask[:, None, :], numer / total[:, :, None], 0.0), axis=0
    ).astype(bf16)

    extra = resid_own.astype(f32) + out_bias.astype(f32)[None, :]
    partial = jnp.dot(attn, out_weight, preferred_element_type=f32)
    place = (jnp.arange(n_tp, dtype=i32) == me_tp)[None, :, None]
    partial = (
        partial.reshape(rows, n_tp, cols) + jnp.where(place, extra[:, None, :], 0.0)
    ).reshape(rows, width)
    stream = sum_pairs(partial, "tp").astype(bf16)
    stream_f = stream.astype(f32)
    mean = jnp.mean(stream_f, axis=1, keepdims=True)
    var = jnp.mean((stream_f - mean) ** 2, axis=1, keepdims=True)
    inverse = lax.rsqrt(var + NORM_EPS)
    stream_own = lax.dynamic_slice_in_dim(stream, me_tp * cols, cols, axis=1)
    normed = (
        (stream_own.astype(f32) - mean) * inverse * norm_gain.astype(f32)[None, :]
        + norm_bias.astype(f32)[None, :]
    ).astype(bf16)

    normed_all = gather_rows(normed, "req")
    slot_of = owner * rows + rank
    wanted = slot_of[order[origin_ids]]
    place_hot = (wanted[:, None] == origin_ids[None, :]).astype(bf16)
    mine_hot = (wanted[:, None] == (me * rows + slots)[None, :]).astype(bf16)
    normed_out = jnp.dot(place_hot, normed_all, preferred_element_type=f32).astype(bf16)
    hidden = lax.dot_general(
        normed_out, up_weight_t, (((1,), (1,)), ((), ())), preferred_element_type=f32
    ).astype(bf16)
    summed = sum_pairs(hidden, "tp").astype(f32)
    activated = jax.nn.gelu(summed + up_bias.astype(f32)[None, :], approximate=False).astype(bf16)
    feed = jnp.dot(activated, down_weight, preferred_element_type=f32)
    feed = feed + jnp.dot(mine_hot, stream_own, preferred_element_type=f32)
    mixed = fold_rows(feed, "req")
    return (mixed + down_bias.astype(f32)[None, :]).astype(bf16)


def solution(mesh):
    pairs = mesh.shape["req"] == REQ and mesh.shape["tp"] == TP
    per_device = on_pairs if pairs else on_any_mesh
    in_specs = (
        P("req", "tp"),
        P("req", "tp"),
        P("req", "tp"),
        P("req", "tp"),
        P(),
        P(),
        P(),
        P(None, "req", None, "tp"),
        P("tp", None),
        P("tp"),
        P("tp"),
        P("tp"),
        P("req", "tp"),
        P("req"),
        P("req", "tp"),
        P("tp"),
        P(),
    )
    out_specs = P("req", "tp")
    return jax.shard_map(
        per_device, mesh=mesh, in_specs=in_specs, out_specs=out_specs, check_vma=False
    )
```

```python
import functools
import math

import jax
import jax.numpy as jnp
from jax import lax
from jax.experimental import pallas as pl
from jax.experimental.pallas import tpu as pltpu
from jax.sharding import PartitionSpec as P

HEAD_DIM = 128
NORM_EPS = 1e-05
PAIRWISE = 16
REQ, TP = 8, 4
WEIGHT_PARTS = 4
ATTENTION_ROOM = 52.2
ALL_ROOM = 58
F32, BF16, I32 = jnp.float32, jnp.bfloat16, jnp.int32
VMEM = pl.BlockSpec(memory_space=pltpu.VMEM)
HBM = pl.BlockSpec(memory_space=pltpu.HBM)


def iota(shape, dim):
    return lax.broadcasted_iota(I32, shape, dim)


def onto_mxu(a, b):
    return jnp.dot(a, b, preferred_element_type=F32)


def nt_dot(a, b):
    return lax.dot_general(a, b, (((1,), (1,)), ((), ())), preferred_element_type=F32)


def hot(condition):
    return jnp.where(condition, 1.0, 0.0).astype(BF16)


def pile(parts):
    height = sum(p.shape[0] for p in parts)
    at, piled = 0, 0
    for p in parts:
        around = ((at, height - at - p.shape[0]),) + ((0, 0),) * (p.ndim - 1)
        piled += jnp.pad(p, around)
        at += p.shape[0]
    return piled


def row(vectors, i, cols):
    return vectors[i * cols : (i + 1) * cols][None, :]


def pack_kernel(owner_in, query, key, value, resid, out, owner, q, k, v, r, sems):
    parts = ((owner_in, owner), (query, q), (key, k), (value, v), (resid, r))
    copies = [pltpu.make_async_copy(x, y, sems.at[i]) for i, (x, y) in enumerate(parts)]
    for copy in copies:
        copy.start()
    rows, cols = q.shape
    fields = 4
    count = REQ * rows
    shape = (REQ * fields, fields * rows)
    down, across = iota(shape, 0), iota(shape, 1)
    here = (count, fields * rows)
    of_mine = hot(iota(here, 0) == lax.axis_index("req") * rows + iota(here, 1) % rows)
    copies[0].wait()
    owner_of = onto_mxu(owner[...].astype(F32).astype(BF16), of_mine).astype(I32)
    pick = hot((down % fields == across // rows) & (owner_of == down // fields))
    for copy in copies[1:]:
        copy.wait()
    all_rows = jnp.concatenate([q[...], k[...], v[...], r[...]], axis=0)
    blocks = onto_mxu(pick, all_rows).astype(BF16)
    for d in range(REQ):
        block = blocks[d * fields : (d + 1) * fields]
        out[REQ - 1 - d, :fields, :] = block[:, : cols // 2]
        out[REQ - 1 - d, fields:, :] = block[:, cols // 2 :]


def index_kernel(place, numbers, pick, valid, arrange, arrange_own, *, page_len):
    owner, order, lengths = (numbers[i : i + 1, :] for i in range(3))
    table = numbers[8:, :]
    me = place[0:1, 0:1]
    count = owner.shape[1]
    rows = count // REQ
    square = (count, count)
    down, across = iota(square, 0), iota(square, 1)
    owner_row = owner
    same_place = down == across
    owner_col = jnp.sum(jnp.where(same_place, owner_row, 0), axis=1, keepdims=True)
    order_col = jnp.sum(jnp.where(same_place, order, 0), axis=1, keepdims=True)
    same_owner = owner_col == owner_row
    rank_row = jnp.sum(jnp.where(same_owner & (down < across), 1, 0), axis=0, keepdims=True)
    rank_col = jnp.sum(jnp.where(same_owner & (across < down), 1, 0), axis=1, keepdims=True)

    shape = pick.shape
    down_p, across_p = iota(shape, 0), iota(shape, 1)
    down_i = iota((shape[0], count), 0)
    mine = hot((owner_row == me) & (rank_row == down_i % rows))
    source = REQ - 1 - iota((count, shape[1]), 1) // (2 * rows)
    came = hot(iota((count, shape[1]), 0) // rows == source)
    from_there = onto_mxu(mine, came)
    pick[...] = hot((from_there > 0.5) & (down_p // rows == across_p % rows))

    shape = valid.shape
    slot = iota((shape[0], count), 0) % rows
    mine_v = hot((owner_row == me) & (rank_row == slot))
    table_v = nt_dot(mine_v, table.astype(F32).astype(BF16)).astype(I32)
    length_v = jnp.sum(jnp.where(mine_v > 0.5, lengths, 0), axis=1, keepdims=True)
    position = iota(shape, 1)
    page, within = position // page_len, position % page_len
    seen = jnp.zeros(shape, F32)
    for j in range(table.shape[0]):
        inside = (table_v[:, j : j + 1] == page) & (within + j * page_len < length_v)
        seen = jnp.where(inside, 1.0, seen)
    valid[...] = seen

    ordered = hot(order_col == across)
    holds = hot((owner_col == REQ - 1 - across // rows) & (rank_col == across % rows))
    arrange[...] = onto_mxu(ordered, holds).astype(BF16)
    here = hot((owner_col == me) & (rank_col == iota(arrange_own.shape, 1)))
    arrange_own[...] = onto_mxu(ordered, here).astype(BF16)


def attention_kernel(
    place, arrived, pick, valid, vectors, pool, weight_in, partial, weight, sems, *, rows
):
    deep = weight.shape[0] // WEIGHT_PARTS
    copies = []
    for i in range(WEIGHT_PARTS):
        part = pl.ds(i * deep, deep)
        copies.append(pltpu.make_async_copy(weight_in.at[part], weight.at[part], sems.at[i]))
    for copy in copies:
        copy.start()
    half = arrived.shape[2]
    cols = 2 * half
    heads = cols // HEAD_DIM
    scale = 1.0 / math.sqrt(HEAD_DIM)
    came = arrived[...].reshape(-1, half)
    which = (iota(pick.shape, 1) // rows) % 2
    chosen = pick[...].astype(F32)
    own = jnp.concatenate(
        [onto_mxu(jnp.where(which == i, chosen, 0.0).astype(BF16), came) for i in range(2)], axis=1
    )
    query, key, value, resid = (own[i * rows : (i + 1) * rows] for i in range(4))

    def tile(x):
        return jnp.concatenate([x] * heads, axis=0)

    shape = (heads * rows, cols)
    in_head = iota(shape, 0) // rows == iota(shape, 1) // HEAD_DIM
    wide = jnp.where(in_head, tile(query), 0.0)
    positions = valid.shape[1]
    self_score = jnp.sum(wide * tile(key), axis=1, keepdims=True) * scale
    scores = nt_dot(wide.astype(BF16), pool[0].reshape(positions, cols)) * scale
    scores = jnp.where(valid[...] > 0.5, scores, -jnp.inf)
    top = jnp.maximum(jnp.max(scores, axis=1, keepdims=True), self_score)
    weights = jnp.exp(scores - top)
    self_weight = jnp.exp(self_score - top)
    total = jnp.sum(weights, axis=1, keepdims=True) + self_weight
    numer = onto_mxu(weights.astype(BF16), pool[1].reshape(positions, cols))
    numer = numer + self_weight.astype(BF16).astype(F32) * tile(value)
    numer = jnp.where(in_head, numer / total, 0.0)
    attn = sum(numer[i * rows : (i + 1) * rows] for i in range(heads))
    attn = jnp.concatenate([attn, jnp.zeros_like(attn)], axis=0).astype(BF16)
    for copy in copies:
        copy.wait()
    projected = onto_mxu(attn, weight[...])[:rows]
    extra = resid + row(vectors, 0, cols)
    for t in range(TP):
        mine = jnp.where(place[1:2, 0:1] == t, extra, 0.0)
        partial[:, t * cols : (t + 1) * cols] = projected[:, t * cols : (t + 1) * cols] + mine


def norm_kernel(place, near, far, vectors, blocks, stream_own):
    mine = near[...].astype(BF16).astype(F32)
    stream = (mine + far[...].astype(F32)).astype(BF16).astype(F32)
    width = stream.shape[1]
    cols = width // TP
    mean = jnp.sum(stream, axis=1, keepdims=True) / width
    var = jnp.sum((stream - mean) ** 2, axis=1, keepdims=True) / width
    own = stream[:, :cols]
    for t in range(1, TP):
        own = jnp.where(place[1:2, 0:1] == t, stream[:, t * cols : (t + 1) * cols], own)
    stream_own[...] = own.astype(BF16)
    gain, bias = row(vectors, 1, cols), row(vectors, 2, cols)
    block = ((own - mean) * lax.rsqrt(var + NORM_EPS) * gain + bias).astype(BF16)
    for d in range(REQ):
        blocks[d] = block


def up_kernel(rows_in, arrange, weight, out):
    came = rows_in[...].reshape(-1, rows_in.shape[2])
    ordered = onto_mxu(arrange[...], came).astype(BF16)
    out[...] = nt_dot(ordered, weight[...]).astype(BF16)


def down_kernel(near, far, vectors, weight, arrange_own, stream_own, out):
    hidden = near[...].astype(F32) + far[...].astype(F32)
    hidden = hidden + vectors[vectors.shape[0] - hidden.shape[1] :][None, :]
    activated = (0.5 * hidden * (1.0 + lax.erf(hidden * math.sqrt(0.5)))).astype(BF16)
    feed = onto_mxu(activated, weight[...]) + onto_mxu(arrange_own[...], stream_own[...])
    rows = out.shape[1]
    for d in range(REQ):
        out[REQ - 1 - d] = feed[d * rows : (d + 1) * rows].astype(BF16)


def finish_kernel(pieces, vectors, out):
    cols = out.shape[1]
    out[...] = (jnp.sum(pieces[...].astype(F32), axis=0) + row(vectors, 3, cols)).astype(BF16)


def call(kernel, shapes, specs, args, scratch=(), room=16, **fixed):
    moved = sum(a.size * a.dtype.itemsize for a in args)
    return pl.pallas_call(
        functools.partial(kernel, **fixed) if fixed else kernel,
        out_shape=shapes,
        in_specs=specs,
        out_specs=[VMEM] * len(shapes),
        scratch_shapes=scratch,
        compiler_params=pltpu.CompilerParams(vmem_limit_bytes=int(room * 2**20)),
        cost_estimate=pl.CostEstimate(flops=0, bytes_accessed=moved, transcendentals=0),
    )(*args)


def trade(blocks):
    group = [list(reversed(range(REQ)))]
    return lax.all_to_all(blocks, "req", 0, 0, tiled=True, axis_index_groups=group)


def on_pairs(
    query,
    key_new,
    value_new,
    resid,
    lengths,
    owner,
    page_table,
    kv_pool,
    out_weight,
    out_bias,
    norm_gain,
    norm_bias,
    up_weight_t,
    up_bias,
    down_weight,
    down_bias,
    order,
):
    rows, cols = query.shape
    width = cols * TP
    pool_pages, page_len = kv_pool.shape[1], kv_pool.shape[2]
    positions = pool_pages * page_len
    heads = cols // HEAD_DIM
    count = owner.shape[0]
    hidden = up_bias.shape[0]

    def arr(shape, dtype=BF16):
        return jax.ShapeDtypeStruct(shape, dtype)

    position = jnp.stack([lax.axis_index("req"), lax.axis_index("tp")]).astype(I32)
    place = jnp.broadcast_to(position[:, None], (2, HEAD_DIM))

    (packed,) = call(
        pack_kernel,
        [arr((REQ, 8, cols // 2))],
        [HBM] * 5,
        [owner[None, :], query, key_new, value_new, resid],
        [pltpu.VMEM((1, count), I32)]
        + [pltpu.VMEM((rows, cols), BF16)] * 4
        + [pltpu.SemaphoreType.DMA((5,))],
        room=ALL_ROOM,
    )
    arrived = trade(packed)
    numbers = pile(
        [owner[None, :], order[None, :], lengths[None, :], jnp.zeros((5, count), I32), page_table.T]
    )
    vectors = pile([x.astype(F32) for x in (out_bias, norm_gain, norm_bias, down_bias, up_bias)])
    pick, valid, arrange, arrange_own = call(
        index_kernel,
        [
            arr((4 * rows, 2 * count)),
            arr((heads * rows, positions), F32),
            arr((count, count)),
            arr((count, rows)),
        ],
        [VMEM, VMEM],
        [place, numbers],
        page_len=page_len,
    )

    pool = jnp.where(position[0] >= 0, kv_pool, jnp.zeros_like(kv_pool))

    (partial,) = call(
        attention_kernel,
        [arr((rows, width), F32)],
        [VMEM] * 6 + [HBM],
        [place, arrived, pick, valid, vectors, pool, out_weight],
        [
            pltpu.VMEM(out_weight.shape, BF16),
            pltpu.SemaphoreType.DMA((WEIGHT_PARTS,)),
        ],
        room=ATTENTION_ROOM,
        rows=rows,
    )
    pair = partial + swap(partial, "tp", 1)
    blocks, stream_own = call(
        norm_kernel,
        [arr((REQ, rows, cols)), arr((rows, cols))],
        [VMEM] * 4,
        [place, pair, swap(pair.astype(BF16), "tp", 3), vectors],
    )

    (part,) = call(
        up_kernel,
        [arr((count, hidden))],
        [VMEM] * 3,
        [trade(blocks), arrange, up_weight_t],
    )
    part = (part.astype(F32) + swap(part, "tp", 1).astype(F32)).astype(BF16)
    (feed,) = call(
        down_kernel,
        [arr((REQ, rows, cols))],
        [VMEM] * 6,
        [part, swap(part, "tp", 3), vectors, down_weight, arrange_own, stream_own],
    )
    (out,) = call(finish_kernel, [arr((rows, cols))], [VMEM] * 2, [trade(feed), vectors])
    return out


def swap(x, axis, step):
    n = lax.axis_size(axis)
    return lax.ppermute(x, axis, [(i, i ^ step) for i in range(n)])


def origins(axis):
    n, me = lax.axis_size(axis), lax.axis_index(axis)
    if n > PAIRWISE:
        return jnp.arange(n, dtype=jnp.int32)
    offsets = [0]
    step = n // 2
    while step:
        offsets = offsets + [o ^ step for o in offsets]
        step //= 2
    return jnp.array(offsets, dtype=jnp.int32) ^ me


def gather_rows(x, axis):
    n = lax.axis_size(axis)
    if n > PAIRWISE:
        return lax.all_gather(x, axis, axis=0, tiled=True)
    step = n // 2
    while step:
        x = jnp.concatenate([x, swap(x, axis, step)], axis=0)
        step //= 2
    return x


def fold_rows(x, axis):
    n = lax.axis_size(axis)
    if n > PAIRWISE:
        return lax.psum_scatter(x, axis, scatter_dimension=0, tiled=True)
    step = 1
    while step < n:
        half = x.shape[0] // 2
        x = x[:half] + swap(x[half:], axis, step)
        step *= 2
    return x


def sum_pairs(x, axis):
    n = lax.axis_size(axis)
    step = 1
    while step < n:
        x = (x.astype(jnp.float32) + swap(x, axis, step).astype(jnp.float32)).astype(x.dtype)
        step *= 2
    return x


def on_any_mesh(
    query,
    key_new,
    value_new,
    resid,
    lengths,
    owner,
    page_table,
    kv_pool,
    out_weight,
    out_bias,
    norm_gain,
    norm_bias,
    up_weight_t,
    up_bias,
    down_weight,
    down_bias,
    order,
):
    f32, bf16, i32 = jnp.float32, jnp.bfloat16, jnp.int32
    n_req = lax.axis_size("req")
    n_tp = lax.axis_size("tp")
    me = lax.axis_index("req")
    me_tp = lax.axis_index("tp")
    rows, cols = query.shape
    width = cols * n_tp
    heads = cols // HEAD_DIM
    pool_pages, page_len = kv_pool.shape[1], kv_pool.shape[2]
    positions = pool_pages * page_len
    scale = 1.0 / math.sqrt(HEAD_DIM)

    origin = origins("req")
    packed = jnp.concatenate([query, key_new, value_new, resid], axis=1)
    arrived = gather_rows(packed, "req")

    same = owner[:, None] == owner[None, :]
    ids = jnp.arange(owner.shape[0], dtype=i32)
    rank = jnp.sum((same & (ids[None, :] < ids[:, None])).astype(i32), axis=1)
    slots = jnp.arange(rows, dtype=i32)
    mine = (owner == me)[None, :] & (rank[None, :] == slots[:, None])
    mine_i = mine.astype(i32)
    own_len = jnp.sum(mine_i * lengths[None, :], axis=1)
    own_table = jnp.sum(mine_i[:, :, None] * page_table[None], axis=1)
    origin_ids = (origin[:, None] * rows + slots[None, :]).reshape(-1)
    own_id = jnp.sum(mine_i * ids[None, :], axis=1)
    take_hot = (own_id[:, None] == origin_ids[None, :]).astype(bf16)
    own = jnp.dot(take_hot, arrived, preferred_element_type=f32).astype(bf16)
    query_own, key_own, value_own, resid_own = (own[:, i * cols : (i + 1) * cols] for i in range(4))

    pos = jnp.arange(positions, dtype=i32)
    page, within = pos // page_len, pos % page_len
    entry = jnp.arange(page_table.shape[1], dtype=i32)
    start = entry * page_len
    hit = (own_table[:, :, None] == page[None, None, :]) & (
        start[None, :, None] + within[None, None, :] < own_len[:, None, None]
    )
    valid = jnp.any(hit, axis=1)

    keys = kv_pool[0].reshape(positions, cols)
    values = kv_pool[1].reshape(positions, cols)
    head_of = jnp.arange(cols, dtype=i32) // HEAD_DIM
    head_mask = head_of[None, :] == jnp.arange(heads, dtype=i32)[:, None]
    spread_q = jnp.where(head_mask[:, None, :], query_own[None], 0).reshape(heads * rows, cols)
    scores = (
        lax.dot_general(spread_q, keys, (((1,), (1,)), ((), ())), preferred_element_type=f32) * scale
    ).reshape(heads, rows, positions)
    scores = jnp.where(valid[None], scores, -jnp.inf)
    self_score = (
        jnp.sum(
            (query_own.astype(f32) * key_own.astype(f32)).reshape(rows, heads, HEAD_DIM), axis=-1
        ).T
        * scale
    )
    top = jnp.maximum(jnp.max(scores, axis=2), self_score)
    weights = jnp.exp(scores - top[:, :, None])
    self_weight = jnp.exp(self_score - top)
    total = jnp.sum(weights, axis=2) + self_weight
    numer = jnp.dot(
        weights.astype(bf16).reshape(heads * rows, positions), values, preferred_element_type=f32
    ).reshape(heads, rows, cols)
    numer = numer + self_weight.astype(bf16).astype(f32)[:, :, None] * value_own.astype(f32)[None]
    attn = jnp.sum(
        jnp.where(head_mask[:, None, :], numer / total[:, :, None], 0.0), axis=0
    ).astype(bf16)

    extra = resid_own.astype(f32) + out_bias.astype(f32)[None, :]
    partial = jnp.dot(attn, out_weight, preferred_element_type=f32)
    place = (jnp.arange(n_tp, dtype=i32) == me_tp)[None, :, None]
    partial = (
        partial.reshape(rows, n_tp, cols) + jnp.where(place, extra[:, None, :], 0.0)
    ).reshape(rows, width)
    stream = sum_pairs(partial, "tp").astype(bf16)
    stream_f = stream.astype(f32)
    mean = jnp.mean(stream_f, axis=1, keepdims=True)
    var = jnp.mean((stream_f - mean) ** 2, axis=1, keepdims=True)
    inverse = lax.rsqrt(var + NORM_EPS)
    stream_own = lax.dynamic_slice_in_dim(stream, me_tp * cols, cols, axis=1)
    normed = (
        (stream_own.astype(f32) - mean) * inverse * norm_gain.astype(f32)[None, :]
        + norm_bias.astype(f32)[None, :]
    ).astype(bf16)

    normed_all = gather_rows(normed, "req")
    slot_of = owner * rows + rank
    wanted = slot_of[order[origin_ids]]
    place_hot = (wanted[:, None] == origin_ids[None, :]).astype(bf16)
    mine_hot = (wanted[:, None] == (me * rows + slots)[None, :]).astype(bf16)
    normed_out = jnp.dot(place_hot, normed_all, preferred_element_type=f32).astype(bf16)
    hidden = lax.dot_general(
        normed_out, up_weight_t, (((1,), (1,)), ((), ())), preferred_element_type=f32
    ).astype(bf16)
    summed = sum_pairs(hidden, "tp").astype(f32)
    activated = jax.nn.gelu(summed + up_bias.astype(f32)[None, :], approximate=False).astype(bf16)
    feed = jnp.dot(activated, down_weight, preferred_element_type=f32)
    feed = feed + jnp.dot(mine_hot, stream_own, preferred_element_type=f32)
    mixed = fold_rows(feed, "req")
    return (mixed + down_bias.astype(f32)[None, :]).astype(bf16)


def solution(mesh):
    pairs = mesh.shape["req"] == REQ and mesh.shape["tp"] == TP
    per_device = on_pairs if pairs else on_any_mesh
    in_specs = (
        P("req", "tp"),
        P("req", "tp"),
        P("req", "tp"),
        P("req", "tp"),
        P(),
        P(),
        P(),
        P(None, "req", None, "tp"),
        P("tp", None),
        P("tp"),
        P("tp"),
        P("tp"),
        P("req", "tp"),
        P("req"),
        P("req", "tp"),
        P("tp"),
        P(),
    )
    out_specs = P("req", "tp")
    return jax.shard_map(
        per_device, mesh=mesh, in_specs=in_specs, out_specs=out_specs, check_vma=False
    )
```

```python
import functools
import math

import jax
import jax.numpy as jnp
from jax import lax
from jax.experimental import pallas as pl
from jax.experimental.pallas import tpu as pltpu
from jax.sharding import PartitionSpec as P

HEAD_DIM = 128
NORM_EPS = 1e-05
PAIRWISE = 16
REQ, TP = 8, 4
ATTENTION_ROOM = 51.2
ALL_ROOM = 58
F32, BF16, I32 = jnp.float32, jnp.bfloat16, jnp.int32
VMEM = pl.BlockSpec(memory_space=pltpu.VMEM)
HBM = pl.BlockSpec(memory_space=pltpu.HBM)


def iota(shape, dim):
    return lax.broadcasted_iota(I32, shape, dim)


def onto_mxu(a, b):
    return jnp.dot(a, b, preferred_element_type=F32)


def nt_dot(a, b):
    return lax.dot_general(a, b, (((1,), (1,)), ((), ())), preferred_element_type=F32)


def hot(condition):
    return jnp.where(condition, 1.0, 0.0).astype(BF16)


def pile(parts):
    height = sum(p.shape[0] for p in parts)
    at, piled = 0, 0
    for p in parts:
        around = ((at, height - at - p.shape[0]),) + ((0, 0),) * (p.ndim - 1)
        piled += jnp.pad(p, around)
        at += p.shape[0]
    return piled


def row(vectors, i, cols):
    return vectors[i * cols : (i + 1) * cols][None, :]


def pack_kernel(owner_in, query, key, value, resid, out, owner, q, k, v, r, sems):
    parts = ((owner_in, owner), (query, q), (key, k), (value, v), (resid, r))
    copies = [pltpu.make_async_copy(x, y, sems.at[i]) for i, (x, y) in enumerate(parts)]
    for copy in copies:
        copy.start()
    rows, cols = q.shape
    fields = 4
    count = REQ * rows
    shape = (REQ * fields, fields * rows)
    down, across = iota(shape, 0), iota(shape, 1)
    here = (count, fields * rows)
    of_mine = hot(iota(here, 0) == lax.axis_index("req") * rows + iota(here, 1) % rows)
    copies[0].wait()
    owner_of = onto_mxu(owner[...].astype(F32).astype(BF16), of_mine).astype(I32)
    pick = hot((down % fields == across // rows) & (owner_of == down // fields))
    for copy in copies[1:]:
        copy.wait()
    all_rows = jnp.concatenate([q[...], k[...], v[...], r[...]], axis=0)
    blocks = onto_mxu(pick, all_rows).astype(BF16)
    for d in range(REQ):
        block = blocks[d * fields : (d + 1) * fields]
        out[REQ - 1 - d, :fields, :] = block[:, : cols // 2]
        out[REQ - 1 - d, fields:, :] = block[:, cols // 2 :]


def index_kernel(place, numbers, pick, valid, arrange, arrange_own, *, page_len):
    owner, order, lengths = (numbers[i : i + 1, :] for i in range(3))
    table = numbers[8:, :]
    me = place[0:1, 0:1]
    count = owner.shape[1]
    rows = count // REQ
    square = (count, count)
    down, across = iota(square, 0), iota(square, 1)
    owner_row = owner
    same_place = down == across
    owner_col = jnp.sum(jnp.where(same_place, owner_row, 0), axis=1, keepdims=True)
    order_col = jnp.sum(jnp.where(same_place, order, 0), axis=1, keepdims=True)
    same_owner = owner_col == owner_row
    rank_row = jnp.sum(jnp.where(same_owner & (down < across), 1, 0), axis=0, keepdims=True)
    rank_col = jnp.sum(jnp.where(same_owner & (across < down), 1, 0), axis=1, keepdims=True)

    shape = pick.shape
    down_p, across_p = iota(shape, 0), iota(shape, 1)
    down_i = iota((shape[0], count), 0)
    mine = hot((owner_row == me) & (rank_row == down_i % rows))
    source = REQ - 1 - iota((count, shape[1]), 1) // (2 * rows)
    came = hot(iota((count, shape[1]), 0) // rows == source)
    from_there = onto_mxu(mine, came)
    pick[...] = hot((from_there > 0.5) & (down_p // rows == across_p % rows))

    shape = valid.shape
    slot = iota((shape[0], count), 0) % rows
    mine_v = hot((owner_row == me) & (rank_row == slot))
    table_v = nt_dot(mine_v, table.astype(F32).astype(BF16)).astype(I32)
    length_v = jnp.sum(jnp.where(mine_v > 0.5, lengths, 0), axis=1, keepdims=True)
    position = iota(shape, 1)
    page, within = position // page_len, position % page_len
    seen = jnp.zeros(shape, F32)
    for j in range(table.shape[0]):
        inside = (table_v[:, j : j + 1] == page) & (within + j * page_len < length_v)
        seen = jnp.where(inside, 1.0, seen)
    valid[...] = seen

    ordered = hot(order_col == across)
    holds = hot((owner_col == REQ - 1 - across // rows) & (rank_col == across % rows))
    arrange[...] = onto_mxu(ordered, holds).astype(BF16)
    here = hot((owner_col == me) & (rank_col == iota(arrange_own.shape, 1)))
    arrange_own[...] = onto_mxu(ordered, here).astype(BF16)


def attention_kernel(
    place, arrived, pick, valid, vectors, pool, upper, weight, partial, rounded, lower, sem, *, rows
):
    deep = upper.shape[0]
    copy = pltpu.make_async_copy(weight.at[pl.ds(deep, deep)], lower, sem)
    copy.start()
    half = arrived.shape[2]
    cols = 2 * half
    heads = cols // HEAD_DIM
    scale = 1.0 / math.sqrt(HEAD_DIM)
    came = arrived[...].reshape(-1, half)
    which = (iota(pick.shape, 1) // rows) % 2
    chosen = pick[...].astype(F32)
    own = jnp.concatenate(
        [onto_mxu(jnp.where(which == i, chosen, 0.0).astype(BF16), came) for i in range(2)], axis=1
    )
    query, key, value, resid = (own[i * rows : (i + 1) * rows] for i in range(4))

    def tile(x):
        return jnp.concatenate([x] * heads, axis=0)

    shape = (heads * rows, cols)
    in_head = iota(shape, 0) // rows == iota(shape, 1) // HEAD_DIM
    wide = jnp.where(in_head, tile(query), 0.0)
    positions = valid.shape[1]
    self_score = jnp.sum(wide * tile(key), axis=1, keepdims=True) * scale
    scores = nt_dot(wide.astype(BF16), pool[0].reshape(positions, cols)) * scale
    scores = jnp.where(valid[...] > 0.5, scores, -jnp.inf)
    top = jnp.maximum(jnp.max(scores, axis=1, keepdims=True), self_score)
    weights = jnp.exp(scores - top)
    self_weight = jnp.exp(self_score - top)
    total = jnp.sum(weights, axis=1, keepdims=True) + self_weight
    numer = onto_mxu(weights.astype(BF16), pool[1].reshape(positions, cols))
    numer = numer + self_weight.astype(BF16).astype(F32) * tile(value)
    numer = jnp.where(in_head, numer / total, 0.0)
    attn = sum(numer[i * rows : (i + 1) * rows] for i in range(heads))
    attn = jnp.concatenate([attn, jnp.zeros_like(attn)], axis=0).astype(BF16)
    projected = onto_mxu(attn[:, :deep], upper[...])
    copy.wait()
    projected = (projected + onto_mxu(attn[:, deep:], lower[...]))[:rows]
    extra = resid + row(vectors, 0, cols)
    for t in range(TP):
        mine = jnp.where(place[1:2, 0:1] == t, extra, 0.0)
        whole = projected[:, t * cols : (t + 1) * cols] + mine
        partial[:, t * cols : (t + 1) * cols] = whole
        rounded[:, t * cols : (t + 1) * cols] = whole.astype(BF16)


def norm_kernel(place, own, sibling, far, far_sibling, vectors, blocks, stream_own):
    others = sibling[...].astype(F32) + far[...].astype(F32) + far_sibling[...].astype(F32)
    stream = (own[...] + others).astype(BF16).astype(F32)
    width = stream.shape[1]
    cols = width // TP
    mean = jnp.sum(stream, axis=1, keepdims=True) / width
    var = jnp.sum((stream - mean) ** 2, axis=1, keepdims=True) / width
    mine = stream[:, :cols]
    for t in range(1, TP):
        mine = jnp.where(place[1:2, 0:1] == t, stream[:, t * cols : (t + 1) * cols], mine)
    stream_own[...] = mine.astype(BF16)
    gain, bias = row(vectors, 1, cols), row(vectors, 2, cols)
    block = ((mine - mean) * lax.rsqrt(var + NORM_EPS) * gain + bias).astype(BF16)
    for d in range(REQ):
        blocks[d] = block


def up_kernel(rows_in, arrange, weight, out):
    came = rows_in[...].reshape(-1, rows_in.shape[2])
    ordered = onto_mxu(arrange[...], came).astype(BF16)
    out[...] = nt_dot(ordered, weight[...]).astype(BF16)


def down_kernel(near, far, vectors, weight, arrange_own, stream_own, out):
    hidden = near[...].astype(F32) + far[...].astype(F32)
    hidden = hidden + vectors[vectors.shape[0] - hidden.shape[1] :][None, :]
    activated = (0.5 * hidden * (1.0 + lax.erf(hidden * math.sqrt(0.5)))).astype(BF16)
    feed = onto_mxu(activated, weight[...]) + onto_mxu(arrange_own[...], stream_own[...])
    rows = out.shape[1]
    for d in range(REQ):
        out[REQ - 1 - d] = feed[d * rows : (d + 1) * rows].astype(BF16)


def finish_kernel(pieces, vectors, out):
    cols = out.shape[1]
    out[...] = (jnp.sum(pieces[...].astype(F32), axis=0) + row(vectors, 3, cols)).astype(BF16)


def call(kernel, shapes, specs, args, scratch=(), room=16, **fixed):
    moved = sum(a.size * a.dtype.itemsize for a in args)
    return pl.pallas_call(
        functools.partial(kernel, **fixed) if fixed else kernel,
        out_shape=shapes,
        in_specs=specs,
        out_specs=[VMEM] * len(shapes),
        scratch_shapes=scratch,
        compiler_params=pltpu.CompilerParams(vmem_limit_bytes=int(room * 2**20)),
        cost_estimate=pl.CostEstimate(flops=0, bytes_accessed=moved, transcendentals=0),
    )(*args)


def trade(blocks):
    group = [list(reversed(range(REQ)))]
    return lax.all_to_all(blocks, "req", 0, 0, tiled=True, axis_index_groups=group)


def on_pairs(
    query,
    key_new,
    value_new,
    resid,
    lengths,
    owner,
    page_table,
    kv_pool,
    out_weight,
    out_bias,
    norm_gain,
    norm_bias,
    up_weight_t,
    up_bias,
    down_weight,
    down_bias,
    order,
):
    rows, cols = query.shape
    width = cols * TP
    pool_pages, page_len = kv_pool.shape[1], kv_pool.shape[2]
    positions = pool_pages * page_len
    heads = cols // HEAD_DIM
    count = owner.shape[0]
    hidden = up_bias.shape[0]

    def arr(shape, dtype=BF16):
        return jax.ShapeDtypeStruct(shape, dtype)

    position = jnp.stack([lax.axis_index("req"), lax.axis_index("tp")]).astype(I32)
    place = jnp.broadcast_to(position[:, None], (2, HEAD_DIM))

    (packed,) = call(
        pack_kernel,
        [arr((REQ, 8, cols // 2))],
        [HBM] * 5,
        [owner[None, :], query, key_new, value_new, resid],
        [pltpu.VMEM((1, count), I32)]
        + [pltpu.VMEM((rows, cols), BF16)] * 4
        + [pltpu.SemaphoreType.DMA((5,))],
        room=ALL_ROOM,
    )
    arrived = trade(packed)
    numbers = pile(
        [owner[None, :], order[None, :], lengths[None, :], jnp.zeros((5, count), I32), page_table.T]
    )
    vectors = pile([x.astype(F32) for x in (out_bias, norm_gain, norm_bias, down_bias, up_bias)])
    pick, valid, arrange, arrange_own = call(
        index_kernel,
        [
            arr((4 * rows, 2 * count)),
            arr((heads * rows, positions), F32),
            arr((count, count)),
            arr((count, rows)),
        ],
        [VMEM, VMEM],
        [place, numbers],
        page_len=page_len,
    )

    here = position[0] >= 0
    pool = jnp.where(here, kv_pool, jnp.zeros_like(kv_pool))
    upper = out_weight[: cols // 2]
    upper = jnp.where(here, upper, jnp.zeros_like(upper))

    partial, rounded = call(
        attention_kernel,
        [arr((rows, width), F32), arr((rows, width))],
        [VMEM] * 7 + [HBM],
        [place, arrived, pick, valid, vectors, pool, upper, out_weight],
        [pltpu.VMEM(upper.shape, BF16), pltpu.SemaphoreType.DMA],
        room=ATTENTION_ROOM,
        rows=rows,
    )
    blocks, stream_own = call(
        norm_kernel,
        [arr((REQ, rows, cols)), arr((rows, cols))],
        [VMEM] * 6,
        [place, partial] + [swap(rounded, "tp", step) for step in (1, 2, 3)] + [vectors],
    )

    (part,) = call(
        up_kernel,
        [arr((count, hidden))],
        [VMEM] * 3,
        [trade(blocks), arrange, up_weight_t],
    )
    part = (part.astype(F32) + swap(part, "tp", 1).astype(F32)).astype(BF16)
    (feed,) = call(
        down_kernel,
        [arr((REQ, rows, cols))],
        [VMEM] * 6,
        [part, swap(part, "tp", 3), vectors, down_weight, arrange_own, stream_own],
    )
    (out,) = call(finish_kernel, [arr((rows, cols))], [VMEM] * 2, [trade(feed), vectors])
    return out


def swap(x, axis, step):
    n = lax.axis_size(axis)
    return lax.ppermute(x, axis, [(i, i ^ step) for i in range(n)])


def origins(axis):
    n, me = lax.axis_size(axis), lax.axis_index(axis)
    if n > PAIRWISE:
        return jnp.arange(n, dtype=jnp.int32)
    offsets = [0]
    step = n // 2
    while step:
        offsets = offsets + [o ^ step for o in offsets]
        step //= 2
    return jnp.array(offsets, dtype=jnp.int32) ^ me


def gather_rows(x, axis):
    n = lax.axis_size(axis)
    if n > PAIRWISE:
        return lax.all_gather(x, axis, axis=0, tiled=True)
    step = n // 2
    while step:
        x = jnp.concatenate([x, swap(x, axis, step)], axis=0)
        step //= 2
    return x


def fold_rows(x, axis):
    n = lax.axis_size(axis)
    if n > PAIRWISE:
        return lax.psum_scatter(x, axis, scatter_dimension=0, tiled=True)
    step = 1
    while step < n:
        half = x.shape[0] // 2
        x = x[:half] + swap(x[half:], axis, step)
        step *= 2
    return x


def sum_pairs(x, axis):
    n = lax.axis_size(axis)
    step = 1
    while step < n:
        x = (x.astype(jnp.float32) + swap(x, axis, step).astype(jnp.float32)).astype(x.dtype)
        step *= 2
    return x


def on_any_mesh(
    query,
    key_new,
    value_new,
    resid,
    lengths,
    owner,
    page_table,
    kv_pool,
    out_weight,
    out_bias,
    norm_gain,
    norm_bias,
    up_weight_t,
    up_bias,
    down_weight,
    down_bias,
    order,
):
    f32, bf16, i32 = jnp.float32, jnp.bfloat16, jnp.int32
    n_req = lax.axis_size("req")
    n_tp = lax.axis_size("tp")
    me = lax.axis_index("req")
    me_tp = lax.axis_index("tp")
    rows, cols = query.shape
    width = cols * n_tp
    heads = cols // HEAD_DIM
    pool_pages, page_len = kv_pool.shape[1], kv_pool.shape[2]
    positions = pool_pages * page_len
    scale = 1.0 / math.sqrt(HEAD_DIM)

    origin = origins("req")
    packed = jnp.concatenate([query, key_new, value_new, resid], axis=1)
    arrived = gather_rows(packed, "req")

    same = owner[:, None] == owner[None, :]
    ids = jnp.arange(owner.shape[0], dtype=i32)
    rank = jnp.sum((same & (ids[None, :] < ids[:, None])).astype(i32), axis=1)
    slots = jnp.arange(rows, dtype=i32)
    mine = (owner == me)[None, :] & (rank[None, :] == slots[:, None])
    mine_i = mine.astype(i32)
    own_len = jnp.sum(mine_i * lengths[None, :], axis=1)
    own_table = jnp.sum(mine_i[:, :, None] * page_table[None], axis=1)
    origin_ids = (origin[:, None] * rows + slots[None, :]).reshape(-1)
    own_id = jnp.sum(mine_i * ids[None, :], axis=1)
    take_hot = (own_id[:, None] == origin_ids[None, :]).astype(bf16)
    own = jnp.dot(take_hot, arrived, preferred_element_type=f32).astype(bf16)
    query_own, key_own, value_own, resid_own = (own[:, i * cols : (i + 1) * cols] for i in range(4))

    pos = jnp.arange(positions, dtype=i32)
    page, within = pos // page_len, pos % page_len
    entry = jnp.arange(page_table.shape[1], dtype=i32)
    start = entry * page_len
    hit = (own_table[:, :, None] == page[None, None, :]) & (
        start[None, :, None] + within[None, None, :] < own_len[:, None, None]
    )
    valid = jnp.any(hit, axis=1)

    keys = kv_pool[0].reshape(positions, cols)
    values = kv_pool[1].reshape(positions, cols)
    head_of = jnp.arange(cols, dtype=i32) // HEAD_DIM
    head_mask = head_of[None, :] == jnp.arange(heads, dtype=i32)[:, None]
    spread_q = jnp.where(head_mask[:, None, :], query_own[None], 0).reshape(heads * rows, cols)
    scores = (
        lax.dot_general(spread_q, keys, (((1,), (1,)), ((), ())), preferred_element_type=f32) * scale
    ).reshape(heads, rows, positions)
    scores = jnp.where(valid[None], scores, -jnp.inf)
    self_score = (
        jnp.sum(
            (query_own.astype(f32) * key_own.astype(f32)).reshape(rows, heads, HEAD_DIM), axis=-1
        ).T
        * scale
    )
    top = jnp.maximum(jnp.max(scores, axis=2), self_score)
    weights = jnp.exp(scores - top[:, :, None])
    self_weight = jnp.exp(self_score - top)
    total = jnp.sum(weights, axis=2) + self_weight
    numer = jnp.dot(
        weights.astype(bf16).reshape(heads * rows, positions), values, preferred_element_type=f32
    ).reshape(heads, rows, cols)
    numer = numer + self_weight.astype(bf16).astype(f32)[:, :, None] * value_own.astype(f32)[None]
    attn = jnp.sum(
        jnp.where(head_mask[:, None, :], numer / total[:, :, None], 0.0), axis=0
    ).astype(bf16)

    extra = resid_own.astype(f32) + out_bias.astype(f32)[None, :]
    partial = jnp.dot(attn, out_weight, preferred_element_type=f32)
    place = (jnp.arange(n_tp, dtype=i32) == me_tp)[None, :, None]
    partial = (
        partial.reshape(rows, n_tp, cols) + jnp.where(place, extra[:, None, :], 0.0)
    ).reshape(rows, width)
    stream = sum_pairs(partial, "tp").astype(bf16)
    stream_f = stream.astype(f32)
    mean = jnp.mean(stream_f, axis=1, keepdims=True)
    var = jnp.mean((stream_f - mean) ** 2, axis=1, keepdims=True)
    inverse = lax.rsqrt(var + NORM_EPS)
    stream_own = lax.dynamic_slice_in_dim(stream, me_tp * cols, cols, axis=1)
    normed = (
        (stream_own.astype(f32) - mean) * inverse * norm_gain.astype(f32)[None, :]
        + norm_bias.astype(f32)[None, :]
    ).astype(bf16)

    normed_all = gather_rows(normed, "req")
    slot_of = owner * rows + rank
    wanted = slot_of[order[origin_ids]]
    place_hot = (wanted[:, None] == origin_ids[None, :]).astype(bf16)
    mine_hot = (wanted[:, None] == (me * rows + slots)[None, :]).astype(bf16)
    normed_out = jnp.dot(place_hot, normed_all, preferred_element_type=f32).astype(bf16)
    hidden = lax.dot_general(
        normed_out, up_weight_t, (((1,), (1,)), ((), ())), preferred_element_type=f32
    ).astype(bf16)
    summed = sum_pairs(hidden, "tp").astype(f32)
    activated = jax.nn.gelu(summed + up_bias.astype(f32)[None, :], approximate=False).astype(bf16)
    feed = jnp.dot(activated, down_weight, preferred_element_type=f32)
    feed = feed + jnp.dot(mine_hot, stream_own, preferred_element_type=f32)
    mixed = fold_rows(feed, "req")
    return (mixed + down_bias.astype(f32)[None, :]).astype(bf16)


def solution(mesh):
    pairs = mesh.shape["req"] == REQ and mesh.shape["tp"] == TP
    per_device = on_pairs if pairs else on_any_mesh
    in_specs = (
        P("req", "tp"),
        P("req", "tp"),
        P("req", "tp"),
        P("req", "tp"),
        P(),
        P(),
        P(),
        P(None, "req", None, "tp"),
        P("tp", None),
        P("tp"),
        P("tp"),
        P("tp"),
        P("req", "tp"),
        P("req"),
        P("req", "tp"),
        P("tp"),
        P(),
    )
    out_specs = P("req", "tp")
    return jax.shard_map(
        per_device, mesh=mesh, in_specs=in_specs, out_specs=out_specs, check_vma=False
    )
```

```python
import functools
import math

import jax
import jax.numpy as jnp
from jax import lax
from jax.experimental import pallas as pl
from jax.experimental.pallas import tpu as pltpu
from jax.sharding import PartitionSpec as P

HEAD_DIM = 128
NORM_EPS = 1e-05
PAIRWISE = 16
REQ, TP = 8, 4
ATTENTION_ROOM = 51.2
ALL_ROOM = 58
F32, BF16, I32 = jnp.float32, jnp.bfloat16, jnp.int32
VMEM = pl.BlockSpec(memory_space=pltpu.VMEM)
HBM = pl.BlockSpec(memory_space=pltpu.HBM)

ENDS_FIRST = [3, 4, 2, 5, 1, 6, 0, 7]
LOW_FIRST = [7, 6, 5, 4, 3, 2, 1, 0]


def ends_first(place):
    return jnp.where(place % 2 == 0, 3 - place // 2, 4 + place // 2)


def iota(shape, dim):
    return lax.broadcasted_iota(I32, shape, dim)


def onto_mxu(a, b):
    return jnp.dot(a, b, preferred_element_type=F32)


def nt_dot(a, b):
    return lax.dot_general(a, b, (((1,), (1,)), ((), ())), preferred_element_type=F32)


def hot(condition):
    return jnp.where(condition, 1.0, 0.0).astype(BF16)


def pile(parts):
    height = sum(p.shape[0] for p in parts)
    at, piled = 0, 0
    for p in parts:
        around = ((at, height - at - p.shape[0]),) + ((0, 0),) * (p.ndim - 1)
        piled += jnp.pad(p, around)
        at += p.shape[0]
    return piled


def row(vectors, i, cols):
    return vectors[i * cols : (i + 1) * cols][None, :]


def pack_kernel(owner_in, query, key, value, resid, out, owner, q, k, v, r, sems):
    parts = ((owner_in, owner), (query, q), (key, k), (value, v), (resid, r))
    copies = [pltpu.make_async_copy(x, y, sems.at[i]) for i, (x, y) in enumerate(parts)]
    for copy in copies:
        copy.start()
    rows, cols = q.shape
    fields = 4
    count = REQ * rows
    shape = (REQ * fields, fields * rows)
    down, across = iota(shape, 0), iota(shape, 1)
    here = (count, fields * rows)
    of_mine = hot(iota(here, 0) == lax.axis_index("req") * rows + iota(here, 1) % rows)
    copies[0].wait()
    owner_of = onto_mxu(owner[...].astype(F32).astype(BF16), of_mine).astype(I32)
    pick = hot((down % fields == across // rows) & (owner_of == down // fields))
    for copy in copies[1:]:
        copy.wait()
    all_rows = jnp.concatenate([q[...], k[...], v[...], r[...]], axis=0)
    blocks = onto_mxu(pick, all_rows).astype(BF16)
    for d in range(REQ):
        block = blocks[d * fields : (d + 1) * fields]
        at = ENDS_FIRST.index(d)
        out[at, :fields, :] = block[:, : cols // 2]
        out[at, fields:, :] = block[:, cols // 2 :]


def index_kernel(place, numbers, pick, valid, arrange, arrange_own, *, page_len):
    owner, order, lengths = (numbers[i : i + 1, :] for i in range(3))
    table = numbers[8:, :]
    me = place[0:1, 0:1]
    count = owner.shape[1]
    rows = count // REQ
    square = (count, count)
    down, across = iota(square, 0), iota(square, 1)
    owner_row = owner
    same_place = down == across
    owner_col = jnp.sum(jnp.where(same_place, owner_row, 0), axis=1, keepdims=True)
    order_col = jnp.sum(jnp.where(same_place, order, 0), axis=1, keepdims=True)
    same_owner = owner_col == owner_row
    rank_row = jnp.sum(jnp.where(same_owner & (down < across), 1, 0), axis=0, keepdims=True)
    rank_col = jnp.sum(jnp.where(same_owner & (across < down), 1, 0), axis=1, keepdims=True)

    shape = pick.shape
    down_p, across_p = iota(shape, 0), iota(shape, 1)
    down_i = iota((shape[0], count), 0)
    mine = hot((owner_row == me) & (rank_row == down_i % rows))
    source = ends_first(iota((count, shape[1]), 1) // (2 * rows))
    came = hot(iota((count, shape[1]), 0) // rows == source)
    from_there = onto_mxu(mine, came)
    pick[...] = hot((from_there > 0.5) & (down_p // rows == across_p % rows))

    shape = valid.shape
    slot = iota((shape[0], count), 0) % rows
    mine_v = hot((owner_row == me) & (rank_row == slot))
    table_v = nt_dot(mine_v, table.astype(F32).astype(BF16)).astype(I32)
    length_v = jnp.sum(jnp.where(mine_v > 0.5, lengths, 0), axis=1, keepdims=True)
    position = iota(shape, 1)
    page, within = position // page_len, position % page_len
    seen = jnp.zeros(shape, F32)
    for j in range(table.shape[0]):
        inside = (table_v[:, j : j + 1] == page) & (within + j * page_len < length_v)
        seen = jnp.where(inside, 1.0, seen)
    valid[...] = seen

    ordered = hot(order_col == across)
    holds = hot((owner_col == ends_first(across // rows)) & (rank_col == across % rows))
    arrange[...] = onto_mxu(ordered, holds).astype(BF16)
    here = hot((owner_col == me) & (rank_col == iota(arrange_own.shape, 1)))
    arrange_own[...] = onto_mxu(ordered, here).astype(BF16)


def attention_kernel(
    place, arrived, pick, valid, vectors, pool, upper, weight, partial, rounded, lower, sem, *, rows
):
    deep = upper.shape[0]
    copy = pltpu.make_async_copy(weight.at[pl.ds(deep, deep)], lower, sem)
    copy.start()
    half = arrived.shape[2]
    cols = 2 * half
    heads = cols // HEAD_DIM
    scale = 1.0 / math.sqrt(HEAD_DIM)
    came = arrived[...].reshape(-1, half)
    which = (iota(pick.shape, 1) // rows) % 2
    chosen = pick[...].astype(F32)
    own = jnp.concatenate(
        [onto_mxu(jnp.where(which == i, chosen, 0.0).astype(BF16), came) for i in range(2)], axis=1
    )
    query, key, value, resid = (own[i * rows : (i + 1) * rows] for i in range(4))

    def tile(x):
        return jnp.concatenate([x] * heads, axis=0)

    shape = (heads * rows, cols)
    in_head = iota(shape, 0) // rows == iota(shape, 1) // HEAD_DIM
    wide = jnp.where(in_head, tile(query), 0.0)
    positions = valid.shape[1]
    self_score = jnp.sum(wide * tile(key), axis=1, keepdims=True) * scale
    scores = nt_dot(wide.astype(BF16), pool[0].reshape(positions, cols)) * scale
    scores = jnp.where(valid[...] > 0.5, scores, -jnp.inf)
    top = jnp.maximum(jnp.max(scores, axis=1, keepdims=True), self_score)
    weights = jnp.exp(scores - top)
    self_weight = jnp.exp(self_score - top)
    total = jnp.sum(weights, axis=1, keepdims=True) + self_weight
    numer = onto_mxu(weights.astype(BF16), pool[1].reshape(positions, cols))
    numer = numer + self_weight.astype(BF16).astype(F32) * tile(value)
    numer = jnp.where(in_head, numer / total, 0.0)
    attn = sum(numer[i * rows : (i + 1) * rows] for i in range(heads))
    attn = jnp.concatenate([attn, jnp.zeros_like(attn)], axis=0).astype(BF16)
    projected = onto_mxu(attn[:, :deep], upper[...])
    copy.wait()
    projected = (projected + onto_mxu(attn[:, deep:], lower[...]))[:rows]
    extra = resid + row(vectors, 0, cols)
    for t in range(TP):
        mine = jnp.where(place[1:2, 0:1] == t, extra, 0.0)
        whole = projected[:, t * cols : (t + 1) * cols] + mine
        partial[:, t * cols : (t + 1) * cols] = whole
        rounded[:, t * cols : (t + 1) * cols] = whole.astype(BF16)


def norm_kernel(place, own, sibling, far, far_sibling, vectors, blocks, stream_own):
    others = sibling[...].astype(F32) + far[...].astype(F32) + far_sibling[...].astype(F32)
    stream = (own[...] + others).astype(BF16).astype(F32)
    width = stream.shape[1]
    cols = width // TP
    mean = jnp.sum(stream, axis=1, keepdims=True) / width
    var = jnp.sum((stream - mean) ** 2, axis=1, keepdims=True) / width
    mine = stream[:, :cols]
    for t in range(1, TP):
        mine = jnp.where(place[1:2, 0:1] == t, stream[:, t * cols : (t + 1) * cols], mine)
    stream_own[...] = mine.astype(BF16)
    gain, bias = row(vectors, 1, cols), row(vectors, 2, cols)
    block = ((mine - mean) * lax.rsqrt(var + NORM_EPS) * gain + bias).astype(BF16)
    for d in range(REQ):
        blocks[d] = block


def up_kernel(rows_in, arrange, weight, out):
    came = rows_in[...].reshape(-1, rows_in.shape[2])
    ordered = onto_mxu(arrange[...], came).astype(BF16)
    out[...] = nt_dot(ordered, weight[...]).astype(BF16)


def down_kernel(near, far, vectors, weight, arrange_own, stream_own, out):
    hidden = near[...].astype(F32) + far[...].astype(F32)
    hidden = hidden + vectors[vectors.shape[0] - hidden.shape[1] :][None, :]
    activated = (0.5 * hidden * (1.0 + lax.erf(hidden * math.sqrt(0.5)))).astype(BF16)
    feed = onto_mxu(activated, weight[...]) + onto_mxu(arrange_own[...], stream_own[...])
    rows = out.shape[1]
    for d in range(REQ):
        out[LOW_FIRST.index(d)] = feed[d * rows : (d + 1) * rows].astype(BF16)


def finish_kernel(pieces, vectors, out):
    cols = out.shape[1]
    out[...] = (jnp.sum(pieces[...].astype(F32), axis=0) + row(vectors, 3, cols)).astype(BF16)


def call(kernel, shapes, specs, args, scratch=(), room=16, **fixed):
    moved = sum(a.size * a.dtype.itemsize for a in args)
    return pl.pallas_call(
        functools.partial(kernel, **fixed) if fixed else kernel,
        out_shape=shapes,
        in_specs=specs,
        out_specs=[VMEM] * len(shapes),
        scratch_shapes=scratch,
        compiler_params=pltpu.CompilerParams(vmem_limit_bytes=int(room * 2**20)),
        cost_estimate=pl.CostEstimate(flops=0, bytes_accessed=moved, transcendentals=0),
    )(*args)


def trade(blocks, group):
    return lax.all_to_all(blocks, "req", 0, 0, tiled=True, axis_index_groups=[group])


def on_pairs(
    query,
    key_new,
    value_new,
    resid,
    lengths,
    owner,
    page_table,
    kv_pool,
    out_weight,
    out_bias,
    norm_gain,
    norm_bias,
    up_weight_t,
    up_bias,
    down_weight,
    down_bias,
    order,
):
    rows, cols = query.shape
    width = cols * TP
    pool_pages, page_len = kv_pool.shape[1], kv_pool.shape[2]
    positions = pool_pages * page_len
    heads = cols // HEAD_DIM
    count = owner.shape[0]
    hidden = up_bias.shape[0]

    def arr(shape, dtype=BF16):
        return jax.ShapeDtypeStruct(shape, dtype)

    position = jnp.stack([lax.axis_index("req"), lax.axis_index("tp")]).astype(I32)
    place = jnp.broadcast_to(position[:, None], (2, HEAD_DIM))

    (packed,) = call(
        pack_kernel,
        [arr((REQ, 8, cols // 2))],
        [HBM] * 5,
        [owner[None, :], query, key_new, value_new, resid],
        [pltpu.VMEM((1, count), I32)]
        + [pltpu.VMEM((rows, cols), BF16)] * 4
        + [pltpu.SemaphoreType.DMA((5,))],
        room=ALL_ROOM,
    )
    arrived = trade(packed, ENDS_FIRST)
    numbers = pile(
        [owner[None, :], order[None, :], lengths[None, :], jnp.zeros((5, count), I32), page_table.T]
    )
    vectors = pile([x.astype(F32) for x in (out_bias, norm_gain, norm_bias, down_bias, up_bias)])
    pick, valid, arrange, arrange_own = call(
        index_kernel,
        [
            arr((4 * rows, 2 * count)),
            arr((heads * rows, positions), F32),
            arr((count, count)),
            arr((count, rows)),
        ],
        [VMEM, VMEM],
        [place, numbers],
        page_len=page_len,
    )

    here = position[0] >= 0
    pool = jnp.where(here, kv_pool, jnp.zeros_like(kv_pool))
    upper = out_weight[: cols // 2]
    upper = jnp.where(here, upper, jnp.zeros_like(upper))

    partial, rounded = call(
        attention_kernel,
        [arr((rows, width), F32), arr((rows, width))],
        [VMEM] * 7 + [HBM],
        [place, arrived, pick, valid, vectors, pool, upper, out_weight],
        [pltpu.VMEM(upper.shape, BF16), pltpu.SemaphoreType.DMA],
        room=ATTENTION_ROOM,
        rows=rows,
    )
    blocks, stream_own = call(
        norm_kernel,
        [arr((REQ, rows, cols)), arr((rows, cols))],
        [VMEM] * 6,
        [place, partial] + [swap(rounded, "tp", step) for step in (1, 2, 3)] + [vectors],
    )

    (part,) = call(
        up_kernel,
        [arr((count, hidden))],
        [VMEM] * 3,
        [trade(blocks, ENDS_FIRST), arrange, up_weight_t],
    )
    part = (part.astype(F32) + swap(part, "tp", 1).astype(F32)).astype(BF16)
    (feed,) = call(
        down_kernel,
        [arr((REQ, rows, cols))],
        [VMEM] * 6,
        [part, swap(part, "tp", 3), vectors, down_weight, arrange_own, stream_own],
    )
    (out,) = call(finish_kernel, [arr((rows, cols))], [VMEM] * 2, [trade(feed, LOW_FIRST), vectors])
    return out


def swap(x, axis, step):
    n = lax.axis_size(axis)
    return lax.ppermute(x, axis, [(i, i ^ step) for i in range(n)])


def origins(axis):
    n, me = lax.axis_size(axis), lax.axis_index(axis)
    if n > PAIRWISE:
        return jnp.arange(n, dtype=jnp.int32)
    offsets = [0]
    step = n // 2
    while step:
        offsets = offsets + [o ^ step for o in offsets]
        step //= 2
    return jnp.array(offsets, dtype=jnp.int32) ^ me


def gather_rows(x, axis):
    n = lax.axis_size(axis)
    if n > PAIRWISE:
        return lax.all_gather(x, axis, axis=0, tiled=True)
    step = n // 2
    while step:
        x = jnp.concatenate([x, swap(x, axis, step)], axis=0)
        step //= 2
    return x


def fold_rows(x, axis):
    n = lax.axis_size(axis)
    if n > PAIRWISE:
        return lax.psum_scatter(x, axis, scatter_dimension=0, tiled=True)
    step = 1
    while step < n:
        half = x.shape[0] // 2
        x = x[:half] + swap(x[half:], axis, step)
        step *= 2
    return x


def sum_pairs(x, axis):
    n = lax.axis_size(axis)
    step = 1
    while step < n:
        x = (x.astype(jnp.float32) + swap(x, axis, step).astype(jnp.float32)).astype(x.dtype)
        step *= 2
    return x


def on_any_mesh(
    query,
    key_new,
    value_new,
    resid,
    lengths,
    owner,
    page_table,
    kv_pool,
    out_weight,
    out_bias,
    norm_gain,
    norm_bias,
    up_weight_t,
    up_bias,
    down_weight,
    down_bias,
    order,
):
    f32, bf16, i32 = jnp.float32, jnp.bfloat16, jnp.int32
    n_req = lax.axis_size("req")
    n_tp = lax.axis_size("tp")
    me = lax.axis_index("req")
    me_tp = lax.axis_index("tp")
    rows, cols = query.shape
    width = cols * n_tp
    heads = cols // HEAD_DIM
    pool_pages, page_len = kv_pool.shape[1], kv_pool.shape[2]
    positions = pool_pages * page_len
    scale = 1.0 / math.sqrt(HEAD_DIM)

    origin = origins("req")
    packed = jnp.concatenate([query, key_new, value_new, resid], axis=1)
    arrived = gather_rows(packed, "req")

    same = owner[:, None] == owner[None, :]
    ids = jnp.arange(owner.shape[0], dtype=i32)
    rank = jnp.sum((same & (ids[None, :] < ids[:, None])).astype(i32), axis=1)
    slots = jnp.arange(rows, dtype=i32)
    mine = (owner == me)[None, :] & (rank[None, :] == slots[:, None])
    mine_i = mine.astype(i32)
    own_len = jnp.sum(mine_i * lengths[None, :], axis=1)
    own_table = jnp.sum(mine_i[:, :, None] * page_table[None], axis=1)
    origin_ids = (origin[:, None] * rows + slots[None, :]).reshape(-1)
    own_id = jnp.sum(mine_i * ids[None, :], axis=1)
    take_hot = (own_id[:, None] == origin_ids[None, :]).astype(bf16)
    own = jnp.dot(take_hot, arrived, preferred_element_type=f32).astype(bf16)
    query_own, key_own, value_own, resid_own = (own[:, i * cols : (i + 1) * cols] for i in range(4))

    pos = jnp.arange(positions, dtype=i32)
    page, within = pos // page_len, pos % page_len
    entry = jnp.arange(page_table.shape[1], dtype=i32)
    start = entry * page_len
    hit = (own_table[:, :, None] == page[None, None, :]) & (
        start[None, :, None] + within[None, None, :] < own_len[:, None, None]
    )
    valid = jnp.any(hit, axis=1)

    keys = kv_pool[0].reshape(positions, cols)
    values = kv_pool[1].reshape(positions, cols)
    head_of = jnp.arange(cols, dtype=i32) // HEAD_DIM
    head_mask = head_of[None, :] == jnp.arange(heads, dtype=i32)[:, None]
    spread_q = jnp.where(head_mask[:, None, :], query_own[None], 0).reshape(heads * rows, cols)
    scores = (
        lax.dot_general(spread_q, keys, (((1,), (1,)), ((), ())), preferred_element_type=f32) * scale
    ).reshape(heads, rows, positions)
    scores = jnp.where(valid[None], scores, -jnp.inf)
    self_score = (
        jnp.sum(
            (query_own.astype(f32) * key_own.astype(f32)).reshape(rows, heads, HEAD_DIM), axis=-1
        ).T
        * scale
    )
    top = jnp.maximum(jnp.max(scores, axis=2), self_score)
    weights = jnp.exp(scores - top[:, :, None])
    self_weight = jnp.exp(self_score - top)
    total = jnp.sum(weights, axis=2) + self_weight
    numer = jnp.dot(
        weights.astype(bf16).reshape(heads * rows, positions), values, preferred_element_type=f32
    ).reshape(heads, rows, cols)
    numer = numer + self_weight.astype(bf16).astype(f32)[:, :, None] * value_own.astype(f32)[None]
    attn = jnp.sum(
        jnp.where(head_mask[:, None, :], numer / total[:, :, None], 0.0), axis=0
    ).astype(bf16)

    extra = resid_own.astype(f32) + out_bias.astype(f32)[None, :]
    partial = jnp.dot(attn, out_weight, preferred_element_type=f32)
    place = (jnp.arange(n_tp, dtype=i32) == me_tp)[None, :, None]
    partial = (
        partial.reshape(rows, n_tp, cols) + jnp.where(place, extra[:, None, :], 0.0)
    ).reshape(rows, width)
    stream = sum_pairs(partial, "tp").astype(bf16)
    stream_f = stream.astype(f32)
    mean = jnp.mean(stream_f, axis=1, keepdims=True)
    var = jnp.mean((stream_f - mean) ** 2, axis=1, keepdims=True)
    inverse = lax.rsqrt(var + NORM_EPS)
    stream_own = lax.dynamic_slice_in_dim(stream, me_tp * cols, cols, axis=1)
    normed = (
        (stream_own.astype(f32) - mean) * inverse * norm_gain.astype(f32)[None, :]
        + norm_bias.astype(f32)[None, :]
    ).astype(bf16)

    normed_all = gather_rows(normed, "req")
    slot_of = owner * rows + rank
    wanted = slot_of[order[origin_ids]]
    place_hot = (wanted[:, None] == origin_ids[None, :]).astype(bf16)
    mine_hot = (wanted[:, None] == (me * rows + slots)[None, :]).astype(bf16)
    normed_out = jnp.dot(place_hot, normed_all, preferred_element_type=f32).astype(bf16)
    hidden = lax.dot_general(
        normed_out, up_weight_t, (((1,), (1,)), ((), ())), preferred_element_type=f32
    ).astype(bf16)
    summed = sum_pairs(hidden, "tp").astype(f32)
    activated = jax.nn.gelu(summed + up_bias.astype(f32)[None, :], approximate=False).astype(bf16)
    feed = jnp.dot(activated, down_weight, preferred_element_type=f32)
    feed = feed + jnp.dot(mine_hot, stream_own, preferred_element_type=f32)
    mixed = fold_rows(feed, "req")
    return (mixed + down_bias.astype(f32)[None, :]).astype(bf16)


def solution(mesh):
    pairs = mesh.shape["req"] == REQ and mesh.shape["tp"] == TP
    per_device = on_pairs if pairs else on_any_mesh
    in_specs = (
        P("req", "tp"),
        P("req", "tp"),
        P("req", "tp"),
        P("req", "tp"),
        P(),
        P(),
        P(),
        P(None, "req", None, "tp"),
        P("tp", None),
        P("tp"),
        P("tp"),
        P("tp"),
        P("req", "tp"),
        P("req"),
        P("req", "tp"),
        P("tp"),
        P(),
    )
    out_specs = P("req", "tp")
    return jax.shard_map(
        per_device, mesh=mesh, in_specs=in_specs, out_specs=out_specs, check_vma=False
    )
```

```python
import functools
import math

import jax
import jax.numpy as jnp
from jax import lax
from jax.experimental import pallas as pl
from jax.experimental.pallas import tpu as pltpu
from jax.sharding import PartitionSpec as P

HEAD_DIM = 128
NORM_EPS = 1e-05
PAIRWISE = 16
REQ, TP = 8, 4
ATTENTION_ROOM = 51.2
ALL_ROOM = 58
F32, BF16, I32 = jnp.float32, jnp.bfloat16, jnp.int32
VMEM = pl.BlockSpec(memory_space=pltpu.VMEM)
HBM = pl.BlockSpec(memory_space=pltpu.HBM)

RING = [0, 1, 3, 5, 7, 6, 4, 2]


def on_ring(place):
    return jnp.where(place < 5, jnp.maximum(2 * place - 1, 0), 16 - 2 * place)


def iota(shape, dim):
    return lax.broadcasted_iota(I32, shape, dim)


def onto_mxu(a, b):
    return jnp.dot(a, b, preferred_element_type=F32)


def nt_dot(a, b):
    return lax.dot_general(a, b, (((1,), (1,)), ((), ())), preferred_element_type=F32)


def hot(condition):
    return jnp.where(condition, 1.0, 0.0).astype(BF16)


def pile(parts):
    height = sum(p.shape[0] for p in parts)
    at, piled = 0, 0
    for p in parts:
        around = ((at, height - at - p.shape[0]),) + ((0, 0),) * (p.ndim - 1)
        piled += jnp.pad(p, around)
        at += p.shape[0]
    return piled


def row(vectors, i, cols):
    return vectors[i * cols : (i + 1) * cols][None, :]


def pack_kernel(owner_in, query, key, value, resid, out, owner, q, k, v, r, sems):
    parts = ((owner_in, owner), (query, q), (key, k), (value, v), (resid, r))
    copies = [pltpu.make_async_copy(x, y, sems.at[i]) for i, (x, y) in enumerate(parts)]
    for copy in copies:
        copy.start()
    rows, cols = q.shape
    fields = 4
    count = REQ * rows
    shape = (REQ * fields, fields * rows)
    down, across = iota(shape, 0), iota(shape, 1)
    here = (count, fields * rows)
    of_mine = hot(iota(here, 0) == lax.axis_index("req") * rows + iota(here, 1) % rows)
    copies[0].wait()
    owner_of = onto_mxu(owner[...].astype(F32).astype(BF16), of_mine).astype(I32)
    pick = hot((down % fields == across // rows) & (owner_of == down // fields))
    for copy in copies[1:]:
        copy.wait()
    all_rows = jnp.concatenate([q[...], k[...], v[...], r[...]], axis=0)
    blocks = onto_mxu(pick, all_rows).astype(BF16)
    for d in range(REQ):
        block = blocks[d * fields : (d + 1) * fields]
        at = RING.index(d)
        out[at, :fields, :] = block[:, : cols // 2]
        out[at, fields:, :] = block[:, cols // 2 :]


def index_kernel(place, numbers, pick, valid, arrange, arrange_own, *, page_len):
    owner, order, lengths = (numbers[i : i + 1, :] for i in range(3))
    table = numbers[8:, :]
    me = place[0:1, 0:1]
    count = owner.shape[1]
    rows = count // REQ
    square = (count, count)
    down, across = iota(square, 0), iota(square, 1)
    owner_row = owner
    same_place = down == across
    owner_col = jnp.sum(jnp.where(same_place, owner_row, 0), axis=1, keepdims=True)
    order_col = jnp.sum(jnp.where(same_place, order, 0), axis=1, keepdims=True)
    same_owner = owner_col == owner_row
    rank_row = jnp.sum(jnp.where(same_owner & (down < across), 1, 0), axis=0, keepdims=True)
    rank_col = jnp.sum(jnp.where(same_owner & (across < down), 1, 0), axis=1, keepdims=True)

    shape = pick.shape
    down_p, across_p = iota(shape, 0), iota(shape, 1)
    down_i = iota((shape[0], count), 0)
    mine = hot((owner_row == me) & (rank_row == down_i % rows))
    source = on_ring(iota((count, shape[1]), 1) // (2 * rows))
    came = hot(iota((count, shape[1]), 0) // rows == source)
    from_there = onto_mxu(mine, came)
    pick[...] = hot((from_there > 0.5) & (down_p // rows == across_p % rows))

    shape = valid.shape
    slot = iota((shape[0], count), 0) % rows
    mine_v = hot((owner_row == me) & (rank_row == slot))
    table_v = nt_dot(mine_v, table.astype(F32).astype(BF16)).astype(I32)
    length_v = jnp.sum(jnp.where(mine_v > 0.5, lengths, 0), axis=1, keepdims=True)
    position = iota(shape, 1)
    page, within = position // page_len, position % page_len
    seen = jnp.zeros(shape, F32)
    for j in range(table.shape[0]):
        inside = (table_v[:, j : j + 1] == page) & (within + j * page_len < length_v)
        seen = jnp.where(inside, 1.0, seen)
    valid[...] = seen

    ordered = hot(order_col == across)
    holds = hot((owner_col == on_ring(across // rows)) & (rank_col == across % rows))
    arrange[...] = onto_mxu(ordered, holds).astype(BF16)
    here = hot((owner_col == me) & (rank_col == iota(arrange_own.shape, 1)))
    arrange_own[...] = onto_mxu(ordered, here).astype(BF16)


def attention_kernel(
    place, arrived, pick, valid, vectors, pool, upper, weight, partial, rounded, lower, sem, *, rows
):
    deep = upper.shape[0]
    copy = pltpu.make_async_copy(weight.at[pl.ds(deep, deep)], lower, sem)
    copy.start()
    half = arrived.shape[2]
    cols = 2 * half
    heads = cols // HEAD_DIM
    scale = 1.0 / math.sqrt(HEAD_DIM)
    came = arrived[...].reshape(-1, half)
    which = (iota(pick.shape, 1) // rows) % 2
    chosen = pick[...].astype(F32)
    own = jnp.concatenate(
        [onto_mxu(jnp.where(which == i, chosen, 0.0).astype(BF16), came) for i in range(2)], axis=1
    )
    query, key, value, resid = (own[i * rows : (i + 1) * rows] for i in range(4))

    def tile(x):
        return jnp.concatenate([x] * heads, axis=0)

    shape = (heads * rows, cols)
    in_head = iota(shape, 0) // rows == iota(shape, 1) // HEAD_DIM
    wide = jnp.where(in_head, tile(query), 0.0)
    positions = valid.shape[1]
    self_score = jnp.sum(wide * tile(key), axis=1, keepdims=True) * scale
    scores = nt_dot(wide.astype(BF16), pool[0].reshape(positions, cols)) * scale
    scores = jnp.where(valid[...] > 0.5, scores, -jnp.inf)
    top = jnp.maximum(jnp.max(scores, axis=1, keepdims=True), self_score)
    weights = jnp.exp(scores - top)
    self_weight = jnp.exp(self_score - top)
    total = jnp.sum(weights, axis=1, keepdims=True) + self_weight
    numer = onto_mxu(weights.astype(BF16), pool[1].reshape(positions, cols))
    numer = numer + self_weight.astype(BF16).astype(F32) * tile(value)
    numer = jnp.where(in_head, numer / total, 0.0)
    attn = sum(numer[i * rows : (i + 1) * rows] for i in range(heads))
    attn = jnp.concatenate([attn, jnp.zeros_like(attn)], axis=0).astype(BF16)
    projected = onto_mxu(attn[:, :deep], upper[...])
    copy.wait()
    projected = (projected + onto_mxu(attn[:, deep:], lower[...]))[:rows]
    extra = resid + row(vectors, 0, cols)
    for t in range(TP):
        mine = jnp.where(place[1:2, 0:1] == t, extra, 0.0)
        whole = projected[:, t * cols : (t + 1) * cols] + mine
        partial[:, t * cols : (t + 1) * cols] = whole
        rounded[:, t * cols : (t + 1) * cols] = whole.astype(BF16)


def norm_kernel(place, own, sibling, far, far_sibling, vectors, blocks, stream_own):
    others = sibling[...].astype(F32) + far[...].astype(F32) + far_sibling[...].astype(F32)
    stream = (own[...] + others).astype(BF16).astype(F32)
    width = stream.shape[1]
    cols = width // TP
    mean = jnp.sum(stream, axis=1, keepdims=True) / width
    var = jnp.sum((stream - mean) ** 2, axis=1, keepdims=True) / width
    mine = stream[:, :cols]
    for t in range(1, TP):
        mine = jnp.where(place[1:2, 0:1] == t, stream[:, t * cols : (t + 1) * cols], mine)
    stream_own[...] = mine.astype(BF16)
    gain, bias = row(vectors, 1, cols), row(vectors, 2, cols)
    block = ((mine - mean) * lax.rsqrt(var + NORM_EPS) * gain + bias).astype(BF16)
    for d in range(REQ):
        blocks[d] = block


def up_kernel(rows_in, arrange, weight, out):
    came = rows_in[...].reshape(-1, rows_in.shape[2])
    ordered = onto_mxu(arrange[...], came).astype(BF16)
    out[...] = nt_dot(ordered, weight[...]).astype(BF16)


def down_kernel(near, far, vectors, weight, arrange_own, stream_own, out):
    hidden = near[...].astype(F32) + far[...].astype(F32)
    hidden = hidden + vectors[vectors.shape[0] - hidden.shape[1] :][None, :]
    activated = (0.5 * hidden * (1.0 + lax.erf(hidden * math.sqrt(0.5)))).astype(BF16)
    feed = onto_mxu(activated, weight[...]) + onto_mxu(arrange_own[...], stream_own[...])
    rows = out.shape[1]
    for d in range(REQ):
        out[RING.index(d)] = feed[d * rows : (d + 1) * rows].astype(BF16)


def finish_kernel(pieces, vectors, out):
    cols = out.shape[1]
    out[...] = (jnp.sum(pieces[...].astype(F32), axis=0) + row(vectors, 3, cols)).astype(BF16)


def call(kernel, shapes, specs, args, scratch=(), room=16, **fixed):
    moved = sum(a.size * a.dtype.itemsize for a in args)
    return pl.pallas_call(
        functools.partial(kernel, **fixed) if fixed else kernel,
        out_shape=shapes,
        in_specs=specs,
        out_specs=[VMEM] * len(shapes),
        scratch_shapes=scratch,
        compiler_params=pltpu.CompilerParams(vmem_limit_bytes=int(room * 2**20)),
        cost_estimate=pl.CostEstimate(flops=0, bytes_accessed=moved, transcendentals=0),
    )(*args)


def trade(blocks):
    return lax.all_to_all(blocks, "req", 0, 0, tiled=True, axis_index_groups=[RING])


def on_pairs(
    query,
    key_new,
    value_new,
    resid,
    lengths,
    owner,
    page_table,
    kv_pool,
    out_weight,
    out_bias,
    norm_gain,
    norm_bias,
    up_weight_t,
    up_bias,
    down_weight,
    down_bias,
    order,
):
    rows, cols = query.shape
    width = cols * TP
    pool_pages, page_len = kv_pool.shape[1], kv_pool.shape[2]
    positions = pool_pages * page_len
    heads = cols // HEAD_DIM
    count = owner.shape[0]
    hidden = up_bias.shape[0]

    def arr(shape, dtype=BF16):
        return jax.ShapeDtypeStruct(shape, dtype)

    position = jnp.stack([lax.axis_index("req"), lax.axis_index("tp")]).astype(I32)
    place = jnp.broadcast_to(position[:, None], (2, HEAD_DIM))

    (packed,) = call(
        pack_kernel,
        [arr((REQ, 8, cols // 2))],
        [HBM] * 5,
        [owner[None, :], query, key_new, value_new, resid],
        [pltpu.VMEM((1, count), I32)]
        + [pltpu.VMEM((rows, cols), BF16)] * 4
        + [pltpu.SemaphoreType.DMA((5,))],
        room=ALL_ROOM,
    )
    arrived = trade(packed)
    numbers = pile(
        [owner[None, :], order[None, :], lengths[None, :], jnp.zeros((5, count), I32), page_table.T]
    )
    vectors = pile([x.astype(F32) for x in (out_bias, norm_gain, norm_bias, down_bias, up_bias)])
    pick, valid, arrange, arrange_own = call(
        index_kernel,
        [
            arr((4 * rows, 2 * count)),
            arr((heads * rows, positions), F32),
            arr((count, count)),
            arr((count, rows)),
        ],
        [VMEM, VMEM],
        [place, numbers],
        page_len=page_len,
    )

    here = position[0] >= 0
    pool = jnp.where(here, kv_pool, jnp.zeros_like(kv_pool))
    upper = out_weight[: cols // 2]
    upper = jnp.where(here, upper, jnp.zeros_like(upper))

    partial, rounded = call(
        attention_kernel,
        [arr((rows, width), F32), arr((rows, width))],
        [VMEM] * 7 + [HBM],
        [place, arrived, pick, valid, vectors, pool, upper, out_weight],
        [pltpu.VMEM(upper.shape, BF16), pltpu.SemaphoreType.DMA],
        room=ATTENTION_ROOM,
        rows=rows,
    )
    blocks, stream_own = call(
        norm_kernel,
        [arr((REQ, rows, cols)), arr((rows, cols))],
        [VMEM] * 6,
        [place, partial] + [swap(rounded, "tp", step) for step in (1, 2, 3)] + [vectors],
    )

    (part,) = call(
        up_kernel,
        [arr((count, hidden))],
        [VMEM] * 3,
        [trade(blocks), arrange, up_weight_t],
    )
    part = (part.astype(F32) + swap(part, "tp", 1).astype(F32)).astype(BF16)
    (feed,) = call(
        down_kernel,
        [arr((REQ, rows, cols))],
        [VMEM] * 6,
        [part, swap(part, "tp", 3), vectors, down_weight, arrange_own, stream_own],
    )
    (out,) = call(finish_kernel, [arr((rows, cols))], [VMEM] * 2, [trade(feed), vectors])
    return out


def swap(x, axis, step):
    n = lax.axis_size(axis)
    return lax.ppermute(x, axis, [(i, i ^ step) for i in range(n)])


def origins(axis):
    n, me = lax.axis_size(axis), lax.axis_index(axis)
    if n > PAIRWISE:
        return jnp.arange(n, dtype=jnp.int32)
    offsets = [0]
    step = n // 2
    while step:
        offsets = offsets + [o ^ step for o in offsets]
        step //= 2
    return jnp.array(offsets, dtype=jnp.int32) ^ me


def gather_rows(x, axis):
    n = lax.axis_size(axis)
    if n > PAIRWISE:
        return lax.all_gather(x, axis, axis=0, tiled=True)
    step = n // 2
    while step:
        x = jnp.concatenate([x, swap(x, axis, step)], axis=0)
        step //= 2
    return x


def fold_rows(x, axis):
    n = lax.axis_size(axis)
    if n > PAIRWISE:
        return lax.psum_scatter(x, axis, scatter_dimension=0, tiled=True)
    step = 1
    while step < n:
        half = x.shape[0] // 2
        x = x[:half] + swap(x[half:], axis, step)
        step *= 2
    return x


def sum_pairs(x, axis):
    n = lax.axis_size(axis)
    step = 1
    while step < n:
        x = (x.astype(jnp.float32) + swap(x, axis, step).astype(jnp.float32)).astype(x.dtype)
        step *= 2
    return x


def on_any_mesh(
    query,
    key_new,
    value_new,
    resid,
    lengths,
    owner,
    page_table,
    kv_pool,
    out_weight,
    out_bias,
    norm_gain,
    norm_bias,
    up_weight_t,
    up_bias,
    down_weight,
    down_bias,
    order,
):
    f32, bf16, i32 = jnp.float32, jnp.bfloat16, jnp.int32
    n_req = lax.axis_size("req")
    n_tp = lax.axis_size("tp")
    me = lax.axis_index("req")
    me_tp = lax.axis_index("tp")
    rows, cols = query.shape
    width = cols * n_tp
    heads = cols // HEAD_DIM
    pool_pages, page_len = kv_pool.shape[1], kv_pool.shape[2]
    positions = pool_pages * page_len
    scale = 1.0 / math.sqrt(HEAD_DIM)

    origin = origins("req")
    packed = jnp.concatenate([query, key_new, value_new, resid], axis=1)
    arrived = gather_rows(packed, "req")

    same = owner[:, None] == owner[None, :]
    ids = jnp.arange(owner.shape[0], dtype=i32)
    rank = jnp.sum((same & (ids[None, :] < ids[:, None])).astype(i32), axis=1)
    slots = jnp.arange(rows, dtype=i32)
    mine = (owner == me)[None, :] & (rank[None, :] == slots[:, None])
    mine_i = mine.astype(i32)
    own_len = jnp.sum(mine_i * lengths[None, :], axis=1)
    own_table = jnp.sum(mine_i[:, :, None] * page_table[None], axis=1)
    origin_ids = (origin[:, None] * rows + slots[None, :]).reshape(-1)
    own_id = jnp.sum(mine_i * ids[None, :], axis=1)
    take_hot = (own_id[:, None] == origin_ids[None, :]).astype(bf16)
    own = jnp.dot(take_hot, arrived, preferred_element_type=f32).astype(bf16)
    query_own, key_own, value_own, resid_own = (own[:, i * cols : (i + 1) * cols] for i in range(4))

    pos = jnp.arange(positions, dtype=i32)
    page, within = pos // page_len, pos % page_len
    entry = jnp.arange(page_table.shape[1], dtype=i32)
    start = entry * page_len
    hit = (own_table[:, :, None] == page[None, None, :]) & (
        start[None, :, None] + within[None, None, :] < own_len[:, None, None]
    )
    valid = jnp.any(hit, axis=1)

    keys = kv_pool[0].reshape(positions, cols)
    values = kv_pool[1].reshape(positions, cols)
    head_of = jnp.arange(cols, dtype=i32) // HEAD_DIM
    head_mask = head_of[None, :] == jnp.arange(heads, dtype=i32)[:, None]
    spread_q = jnp.where(head_mask[:, None, :], query_own[None], 0).reshape(heads * rows, cols)
    scores = (
        lax.dot_general(spread_q, keys, (((1,), (1,)), ((), ())), preferred_element_type=f32) * scale
    ).reshape(heads, rows, positions)
    scores = jnp.where(valid[None], scores, -jnp.inf)
    self_score = (
        jnp.sum(
            (query_own.astype(f32) * key_own.astype(f32)).reshape(rows, heads, HEAD_DIM), axis=-1
        ).T
        * scale
    )
    top = jnp.maximum(jnp.max(scores, axis=2), self_score)
    weights = jnp.exp(scores - top[:, :, None])
    self_weight = jnp.exp(self_score - top)
    total = jnp.sum(weights, axis=2) + self_weight
    numer = jnp.dot(
        weights.astype(bf16).reshape(heads * rows, positions), values, preferred_element_type=f32
    ).reshape(heads, rows, cols)
    numer = numer + self_weight.astype(bf16).astype(f32)[:, :, None] * value_own.astype(f32)[None]
    attn = jnp.sum(
        jnp.where(head_mask[:, None, :], numer / total[:, :, None], 0.0), axis=0
    ).astype(bf16)

    extra = resid_own.astype(f32) + out_bias.astype(f32)[None, :]
    partial = jnp.dot(attn, out_weight, preferred_element_type=f32)
    place = (jnp.arange(n_tp, dtype=i32) == me_tp)[None, :, None]
    partial = (
        partial.reshape(rows, n_tp, cols) + jnp.where(place, extra[:, None, :], 0.0)
    ).reshape(rows, width)
    stream = sum_pairs(partial, "tp").astype(bf16)
    stream_f = stream.astype(f32)
    mean = jnp.mean(stream_f, axis=1, keepdims=True)
    var = jnp.mean((stream_f - mean) ** 2, axis=1, keepdims=True)
    inverse = lax.rsqrt(var + NORM_EPS)
    stream_own = lax.dynamic_slice_in_dim(stream, me_tp * cols, cols, axis=1)
    normed = (
        (stream_own.astype(f32) - mean) * inverse * norm_gain.astype(f32)[None, :]
        + norm_bias.astype(f32)[None, :]
    ).astype(bf16)

    normed_all = gather_rows(normed, "req")
    slot_of = owner * rows + rank
    wanted = slot_of[order[origin_ids]]
    place_hot = (wanted[:, None] == origin_ids[None, :]).astype(bf16)
    mine_hot = (wanted[:, None] == (me * rows + slots)[None, :]).astype(bf16)
    normed_out = jnp.dot(place_hot, normed_all, preferred_element_type=f32).astype(bf16)
    hidden = lax.dot_general(
        normed_out, up_weight_t, (((1,), (1,)), ((), ())), preferred_element_type=f32
    ).astype(bf16)
    summed = sum_pairs(hidden, "tp").astype(f32)
    activated = jax.nn.gelu(summed + up_bias.astype(f32)[None, :], approximate=False).astype(bf16)
    feed = jnp.dot(activated, down_weight, preferred_element_type=f32)
    feed = feed + jnp.dot(mine_hot, stream_own, preferred_element_type=f32)
    mixed = fold_rows(feed, "req")
    return (mixed + down_bias.astype(f32)[None, :]).astype(bf16)


def solution(mesh):
    pairs = mesh.shape["req"] == REQ and mesh.shape["tp"] == TP
    per_device = on_pairs if pairs else on_any_mesh
    in_specs = (
        P("req", "tp"),
        P("req", "tp"),
        P("req", "tp"),
        P("req", "tp"),
        P(),
        P(),
        P(),
        P(None, "req", None, "tp"),
        P("tp", None),
        P("tp"),
        P("tp"),
        P("tp"),
        P("req", "tp"),
        P("req"),
        P("req", "tp"),
        P("tp"),
        P(),
    )
    out_specs = P("req", "tp")
    return jax.shard_map(
        per_device, mesh=mesh, in_specs=in_specs, out_specs=out_specs, check_vma=False
    )
```

```python
import functools
import math

import jax
import jax.numpy as jnp
from jax import lax
from jax.experimental import pallas as pl
from jax.experimental.pallas import tpu as pltpu
from jax.sharding import PartitionSpec as P

HEAD_DIM = 128
NORM_EPS = 1e-05
PAIRWISE = 16
REQ, TP = 8, 4
ATTENTION_ROOM = 51.2
ALL_ROOM = 58
F32, BF16, I32 = jnp.float32, jnp.bfloat16, jnp.int32
VMEM = pl.BlockSpec(memory_space=pltpu.VMEM)
HBM = pl.BlockSpec(memory_space=pltpu.HBM)

ENDS_FIRST = [4, 3, 5, 2, 6, 1, 7, 0]
LOW_FIRST = [7, 6, 5, 4, 3, 2, 1, 0]


def ends_first(place):
    return jnp.where(place % 2 == 0, 4 + place // 2, 3 - place // 2)


def iota(shape, dim):
    return lax.broadcasted_iota(I32, shape, dim)


def onto_mxu(a, b):
    return jnp.dot(a, b, preferred_element_type=F32)


def nt_dot(a, b):
    return lax.dot_general(a, b, (((1,), (1,)), ((), ())), preferred_element_type=F32)


def hot(condition):
    return jnp.where(condition, 1.0, 0.0).astype(BF16)


def pile(parts):
    height = sum(p.shape[0] for p in parts)
    at, piled = 0, 0
    for p in parts:
        around = ((at, height - at - p.shape[0]),) + ((0, 0),) * (p.ndim - 1)
        piled += jnp.pad(p, around)
        at += p.shape[0]
    return piled


def row(vectors, i, cols):
    return vectors[i * cols : (i + 1) * cols][None, :]


def pack_kernel(owner_in, query, key, value, resid, out, owner, q, k, v, r, sems):
    parts = ((owner_in, owner), (query, q), (key, k), (value, v), (resid, r))
    copies = [pltpu.make_async_copy(x, y, sems.at[i]) for i, (x, y) in enumerate(parts)]
    for copy in copies:
        copy.start()
    rows, cols = q.shape
    fields = 4
    count = REQ * rows
    shape = (REQ * fields, fields * rows)
    down, across = iota(shape, 0), iota(shape, 1)
    here = (count, fields * rows)
    of_mine = hot(iota(here, 0) == lax.axis_index("req") * rows + iota(here, 1) % rows)
    copies[0].wait()
    owner_of = onto_mxu(owner[...].astype(F32).astype(BF16), of_mine).astype(I32)
    pick = hot((down % fields == across // rows) & (owner_of == down // fields))
    for copy in copies[1:]:
        copy.wait()
    all_rows = jnp.concatenate([q[...], k[...], v[...], r[...]], axis=0)
    blocks = onto_mxu(pick, all_rows).astype(BF16)
    for d in range(REQ):
        block = blocks[d * fields : (d + 1) * fields]
        at = ENDS_FIRST.index(d)
        out[at, :fields, :] = block[:, : cols // 2]
        out[at, fields:, :] = block[:, cols // 2 :]


def index_kernel(place, numbers, pick, valid, arrange, arrange_own, *, page_len):
    owner, order, lengths = (numbers[i : i + 1, :] for i in range(3))
    table = numbers[8:, :]
    me = place[0:1, 0:1]
    count = owner.shape[1]
    rows = count // REQ
    square = (count, count)
    down, across = iota(square, 0), iota(square, 1)
    owner_row = owner
    same_place = down == across
    owner_col = jnp.sum(jnp.where(same_place, owner_row, 0), axis=1, keepdims=True)
    order_col = jnp.sum(jnp.where(same_place, order, 0), axis=1, keepdims=True)
    same_owner = owner_col == owner_row
    rank_row = jnp.sum(jnp.where(same_owner & (down < across), 1, 0), axis=0, keepdims=True)
    rank_col = jnp.sum(jnp.where(same_owner & (across < down), 1, 0), axis=1, keepdims=True)

    shape = pick.shape
    down_p, across_p = iota(shape, 0), iota(shape, 1)
    down_i = iota((shape[0], count), 0)
    mine = hot((owner_row == me) & (rank_row == down_i % rows))
    source = ends_first(iota((count, shape[1]), 1) // (2 * rows))
    came = hot(iota((count, shape[1]), 0) // rows == source)
    from_there = onto_mxu(mine, came)
    pick[...] = hot((from_there > 0.5) & (down_p // rows == across_p % rows))

    shape = valid.shape
    slot = iota((shape[0], count), 0) % rows
    mine_v = hot((owner_row == me) & (rank_row == slot))
    table_v = nt_dot(mine_v, table.astype(F32).astype(BF16)).astype(I32)
    length_v = jnp.sum(jnp.where(mine_v > 0.5, lengths, 0), axis=1, keepdims=True)
    position = iota(shape, 1)
    page, within = position // page_len, position % page_len
    seen = jnp.zeros(shape, F32)
    for j in range(table.shape[0]):
        inside = (table_v[:, j : j + 1] == page) & (within + j * page_len < length_v)
        seen = jnp.where(inside, 1.0, seen)
    valid[...] = seen

    ordered = hot(order_col == across)
    holds = hot((owner_col == ends_first(across // rows)) & (rank_col == across % rows))
    arrange[...] = onto_mxu(ordered, holds).astype(BF16)
    here = hot((owner_col == me) & (rank_col == iota(arrange_own.shape, 1)))
    arrange_own[...] = onto_mxu(ordered, here).astype(BF16)


def attention_kernel(
    place, arrived, pick, valid, vectors, pool, upper, weight, partial, rounded, lower, sem, *, rows
):
    deep = upper.shape[0]
    copy = pltpu.make_async_copy(weight.at[pl.ds(deep, deep)], lower, sem)
    copy.start()
    half = arrived.shape[2]
    cols = 2 * half
    heads = cols // HEAD_DIM
    scale = 1.0 / math.sqrt(HEAD_DIM)
    came = arrived[...].reshape(-1, half)
    which = (iota(pick.shape, 1) // rows) % 2
    chosen = pick[...].astype(F32)
    own = jnp.concatenate(
        [onto_mxu(jnp.where(which == i, chosen, 0.0).astype(BF16), came) for i in range(2)], axis=1
    )
    query, key, value, resid = (own[i * rows : (i + 1) * rows] for i in range(4))

    def tile(x):
        return jnp.concatenate([x] * heads, axis=0)

    shape = (heads * rows, cols)
    in_head = iota(shape, 0) // rows == iota(shape, 1) // HEAD_DIM
    wide = jnp.where(in_head, tile(query), 0.0)
    positions = valid.shape[1]
    self_score = jnp.sum(wide * tile(key), axis=1, keepdims=True) * scale
    scores = nt_dot(wide.astype(BF16), pool[0].reshape(positions, cols)) * scale
    scores = jnp.where(valid[...] > 0.5, scores, -jnp.inf)
    top = jnp.maximum(jnp.max(scores, axis=1, keepdims=True), self_score)
    weights = jnp.exp(scores - top)
    self_weight = jnp.exp(self_score - top)
    total = jnp.sum(weights, axis=1, keepdims=True) + self_weight
    numer = onto_mxu(weights.astype(BF16), pool[1].reshape(positions, cols))
    numer = numer + self_weight.astype(BF16).astype(F32) * tile(value)
    numer = jnp.where(in_head, numer / total, 0.0)
    attn = sum(numer[i * rows : (i + 1) * rows] for i in range(heads))
    attn = jnp.concatenate([attn, jnp.zeros_like(attn)], axis=0).astype(BF16)
    projected = onto_mxu(attn[:, :deep], upper[...])
    copy.wait()
    projected = (projected + onto_mxu(attn[:, deep:], lower[...]))[:rows]
    extra = resid + row(vectors, 0, cols)
    for t in range(TP):
        mine = jnp.where(place[1:2, 0:1] == t, extra, 0.0)
        whole = projected[:, t * cols : (t + 1) * cols] + mine
        partial[:, t * cols : (t + 1) * cols] = whole
        rounded[:, t * cols : (t + 1) * cols] = whole.astype(BF16)


def norm_kernel(place, own, sibling, far, far_sibling, vectors, blocks, stream_own):
    others = sibling[...].astype(F32) + far[...].astype(F32) + far_sibling[...].astype(F32)
    stream = (own[...] + others).astype(BF16).astype(F32)
    width = stream.shape[1]
    cols = width // TP
    mean = jnp.sum(stream, axis=1, keepdims=True) / width
    var = jnp.sum((stream - mean) ** 2, axis=1, keepdims=True) / width
    mine = stream[:, :cols]
    for t in range(1, TP):
        mine = jnp.where(place[1:2, 0:1] == t, stream[:, t * cols : (t + 1) * cols], mine)
    stream_own[...] = mine.astype(BF16)
    gain, bias = row(vectors, 1, cols), row(vectors, 2, cols)
    block = ((mine - mean) * lax.rsqrt(var + NORM_EPS) * gain + bias).astype(BF16)
    for d in range(REQ):
        blocks[d] = block


def up_kernel(rows_in, arrange, weight, out):
    came = rows_in[...].reshape(-1, rows_in.shape[2])
    ordered = onto_mxu(arrange[...], came).astype(BF16)
    out[...] = nt_dot(ordered, weight[...]).astype(BF16)


def down_kernel(near, far, vectors, weight, arrange_own, stream_own, out):
    hidden = near[...].astype(F32) + far[...].astype(F32)
    hidden = hidden + vectors[vectors.shape[0] - hidden.shape[1] :][None, :]
    activated = (0.5 * hidden * (1.0 + lax.erf(hidden * math.sqrt(0.5)))).astype(BF16)
    feed = onto_mxu(activated, weight[...]) + onto_mxu(arrange_own[...], stream_own[...])
    rows = out.shape[1]
    for d in range(REQ):
        out[LOW_FIRST.index(d)] = feed[d * rows : (d + 1) * rows].astype(BF16)


def finish_kernel(pieces, vectors, out):
    cols = out.shape[1]
    out[...] = (jnp.sum(pieces[...].astype(F32), axis=0) + row(vectors, 3, cols)).astype(BF16)


def call(kernel, shapes, specs, args, scratch=(), room=16, **fixed):
    moved = sum(a.size * a.dtype.itemsize for a in args)
    return pl.pallas_call(
        functools.partial(kernel, **fixed) if fixed else kernel,
        out_shape=shapes,
        in_specs=specs,
        out_specs=[VMEM] * len(shapes),
        scratch_shapes=scratch,
        compiler_params=pltpu.CompilerParams(vmem_limit_bytes=int(room * 2**20)),
        cost_estimate=pl.CostEstimate(flops=0, bytes_accessed=moved, transcendentals=0),
    )(*args)


def trade(blocks, group):
    return lax.all_to_all(blocks, "req", 0, 0, tiled=True, axis_index_groups=[group])


def on_pairs(
    query,
    key_new,
    value_new,
    resid,
    lengths,
    owner,
    page_table,
    kv_pool,
    out_weight,
    out_bias,
    norm_gain,
    norm_bias,
    up_weight_t,
    up_bias,
    down_weight,
    down_bias,
    order,
):
    rows, cols = query.shape
    width = cols * TP
    pool_pages, page_len = kv_pool.shape[1], kv_pool.shape[2]
    positions = pool_pages * page_len
    heads = cols // HEAD_DIM
    count = owner.shape[0]
    hidden = up_bias.shape[0]

    def arr(shape, dtype=BF16):
        return jax.ShapeDtypeStruct(shape, dtype)

    position = jnp.stack([lax.axis_index("req"), lax.axis_index("tp")]).astype(I32)
    place = jnp.broadcast_to(position[:, None], (2, HEAD_DIM))

    (packed,) = call(
        pack_kernel,
        [arr((REQ, 8, cols // 2))],
        [HBM] * 5,
        [owner[None, :], query, key_new, value_new, resid],
        [pltpu.VMEM((1, count), I32)]
        + [pltpu.VMEM((rows, cols), BF16)] * 4
        + [pltpu.SemaphoreType.DMA((5,))],
        room=ALL_ROOM,
    )
    arrived = trade(packed, ENDS_FIRST)
    numbers = pile(
        [owner[None, :], order[None, :], lengths[None, :], jnp.zeros((5, count), I32), page_table.T]
    )
    vectors = pile([x.astype(F32) for x in (out_bias, norm_gain, norm_bias, down_bias, up_bias)])
    pick, valid, arrange, arrange_own = call(
        index_kernel,
        [
            arr((4 * rows, 2 * count)),
            arr((heads * rows, positions), F32),
            arr((count, count)),
            arr((count, rows)),
        ],
        [VMEM, VMEM],
        [place, numbers],
        page_len=page_len,
    )

    here = position[0] >= 0
    pool = jnp.where(here, kv_pool, jnp.zeros_like(kv_pool))
    upper = out_weight[: cols // 2]
    upper = jnp.where(here, upper, jnp.zeros_like(upper))

    partial, rounded = call(
        attention_kernel,
        [arr((rows, width), F32), arr((rows, width))],
        [VMEM] * 7 + [HBM],
        [place, arrived, pick, valid, vectors, pool, upper, out_weight],
        [pltpu.VMEM(upper.shape, BF16), pltpu.SemaphoreType.DMA],
        room=ATTENTION_ROOM,
        rows=rows,
    )
    blocks, stream_own = call(
        norm_kernel,
        [arr((REQ, rows, cols)), arr((rows, cols))],
        [VMEM] * 6,
        [place, partial] + [swap(rounded, "tp", step) for step in (1, 2, 3)] + [vectors],
    )

    (part,) = call(
        up_kernel,
        [arr((count, hidden))],
        [VMEM] * 3,
        [trade(blocks, ENDS_FIRST), arrange, up_weight_t],
    )
    part = (part.astype(F32) + swap(part, "tp", 1).astype(F32)).astype(BF16)
    (feed,) = call(
        down_kernel,
        [arr((REQ, rows, cols))],
        [VMEM] * 6,
        [part, swap(part, "tp", 3), vectors, down_weight, arrange_own, stream_own],
    )
    (out,) = call(finish_kernel, [arr((rows, cols))], [VMEM] * 2, [trade(feed, LOW_FIRST), vectors])
    return out


def swap(x, axis, step):
    n = lax.axis_size(axis)
    return lax.ppermute(x, axis, [(i, i ^ step) for i in range(n)])


def origins(axis):
    n, me = lax.axis_size(axis), lax.axis_index(axis)
    if n > PAIRWISE:
        return jnp.arange(n, dtype=jnp.int32)
    offsets = [0]
    step = n // 2
    while step:
        offsets = offsets + [o ^ step for o in offsets]
        step //= 2
    return jnp.array(offsets, dtype=jnp.int32) ^ me


def gather_rows(x, axis):
    n = lax.axis_size(axis)
    if n > PAIRWISE:
        return lax.all_gather(x, axis, axis=0, tiled=True)
    step = n // 2
    while step:
        x = jnp.concatenate([x, swap(x, axis, step)], axis=0)
        step //= 2
    return x


def fold_rows(x, axis):
    n = lax.axis_size(axis)
    if n > PAIRWISE:
        return lax.psum_scatter(x, axis, scatter_dimension=0, tiled=True)
    step = 1
    while step < n:
        half = x.shape[0] // 2
        x = x[:half] + swap(x[half:], axis, step)
        step *= 2
    return x


def sum_pairs(x, axis):
    n = lax.axis_size(axis)
    step = 1
    while step < n:
        x = (x.astype(jnp.float32) + swap(x, axis, step).astype(jnp.float32)).astype(x.dtype)
        step *= 2
    return x


def on_any_mesh(
    query,
    key_new,
    value_new,
    resid,
    lengths,
    owner,
    page_table,
    kv_pool,
    out_weight,
    out_bias,
    norm_gain,
    norm_bias,
    up_weight_t,
    up_bias,
    down_weight,
    down_bias,
    order,
):
    f32, bf16, i32 = jnp.float32, jnp.bfloat16, jnp.int32
    n_req = lax.axis_size("req")
    n_tp = lax.axis_size("tp")
    me = lax.axis_index("req")
    me_tp = lax.axis_index("tp")
    rows, cols = query.shape
    width = cols * n_tp
    heads = cols // HEAD_DIM
    pool_pages, page_len = kv_pool.shape[1], kv_pool.shape[2]
    positions = pool_pages * page_len
    scale = 1.0 / math.sqrt(HEAD_DIM)

    origin = origins("req")
    packed = jnp.concatenate([query, key_new, value_new, resid], axis=1)
    arrived = gather_rows(packed, "req")

    same = owner[:, None] == owner[None, :]
    ids = jnp.arange(owner.shape[0], dtype=i32)
    rank = jnp.sum((same & (ids[None, :] < ids[:, None])).astype(i32), axis=1)
    slots = jnp.arange(rows, dtype=i32)
    mine = (owner == me)[None, :] & (rank[None, :] == slots[:, None])
    mine_i = mine.astype(i32)
    own_len = jnp.sum(mine_i * lengths[None, :], axis=1)
    own_table = jnp.sum(mine_i[:, :, None] * page_table[None], axis=1)
    origin_ids = (origin[:, None] * rows + slots[None, :]).reshape(-1)
    own_id = jnp.sum(mine_i * ids[None, :], axis=1)
    take_hot = (own_id[:, None] == origin_ids[None, :]).astype(bf16)
    own = jnp.dot(take_hot, arrived, preferred_element_type=f32).astype(bf16)
    query_own, key_own, value_own, resid_own = (own[:, i * cols : (i + 1) * cols] for i in range(4))

    pos = jnp.arange(positions, dtype=i32)
    page, within = pos // page_len, pos % page_len
    entry = jnp.arange(page_table.shape[1], dtype=i32)
    start = entry * page_len
    hit = (own_table[:, :, None] == page[None, None, :]) & (
        start[None, :, None] + within[None, None, :] < own_len[:, None, None]
    )
    valid = jnp.any(hit, axis=1)

    keys = kv_pool[0].reshape(positions, cols)
    values = kv_pool[1].reshape(positions, cols)
    head_of = jnp.arange(cols, dtype=i32) // HEAD_DIM
    head_mask = head_of[None, :] == jnp.arange(heads, dtype=i32)[:, None]
    spread_q = jnp.where(head_mask[:, None, :], query_own[None], 0).reshape(heads * rows, cols)
    scores = (
        lax.dot_general(spread_q, keys, (((1,), (1,)), ((), ())), preferred_element_type=f32) * scale
    ).reshape(heads, rows, positions)
    scores = jnp.where(valid[None], scores, -jnp.inf)
    self_score = (
        jnp.sum(
            (query_own.astype(f32) * key_own.astype(f32)).reshape(rows, heads, HEAD_DIM), axis=-1
        ).T
        * scale
    )
    top = jnp.maximum(jnp.max(scores, axis=2), self_score)
    weights = jnp.exp(scores - top[:, :, None])
    self_weight = jnp.exp(self_score - top)
    total = jnp.sum(weights, axis=2) + self_weight
    numer = jnp.dot(
        weights.astype(bf16).reshape(heads * rows, positions), values, preferred_element_type=f32
    ).reshape(heads, rows, cols)
    numer = numer + self_weight.astype(bf16).astype(f32)[:, :, None] * value_own.astype(f32)[None]
    attn = jnp.sum(
        jnp.where(head_mask[:, None, :], numer / total[:, :, None], 0.0), axis=0
    ).astype(bf16)

    extra = resid_own.astype(f32) + out_bias.astype(f32)[None, :]
    partial = jnp.dot(attn, out_weight, preferred_element_type=f32)
    place = (jnp.arange(n_tp, dtype=i32) == me_tp)[None, :, None]
    partial = (
        partial.reshape(rows, n_tp, cols) + jnp.where(place, extra[:, None, :], 0.0)
    ).reshape(rows, width)
    stream = sum_pairs(partial, "tp").astype(bf16)
    stream_f = stream.astype(f32)
    mean = jnp.mean(stream_f, axis=1, keepdims=True)
    var = jnp.mean((stream_f - mean) ** 2, axis=1, keepdims=True)
    inverse = lax.rsqrt(var + NORM_EPS)
    stream_own = lax.dynamic_slice_in_dim(stream, me_tp * cols, cols, axis=1)
    normed = (
        (stream_own.astype(f32) - mean) * inverse * norm_gain.astype(f32)[None, :]
        + norm_bias.astype(f32)[None, :]
    ).astype(bf16)

    normed_all = gather_rows(normed, "req")
    slot_of = owner * rows + rank
    wanted = slot_of[order[origin_ids]]
    place_hot = (wanted[:, None] == origin_ids[None, :]).astype(bf16)
    mine_hot = (wanted[:, None] == (me * rows + slots)[None, :]).astype(bf16)
    normed_out = jnp.dot(place_hot, normed_all, preferred_element_type=f32).astype(bf16)
    hidden = lax.dot_general(
        normed_out, up_weight_t, (((1,), (1,)), ((), ())), preferred_element_type=f32
    ).astype(bf16)
    summed = sum_pairs(hidden, "tp").astype(f32)
    activated = jax.nn.gelu(summed + up_bias.astype(f32)[None, :], approximate=False).astype(bf16)
    feed = jnp.dot(activated, down_weight, preferred_element_type=f32)
    feed = feed + jnp.dot(mine_hot, stream_own, preferred_element_type=f32)
    mixed = fold_rows(feed, "req")
    return (mixed + down_bias.astype(f32)[None, :]).astype(bf16)


def solution(mesh):
    pairs = mesh.shape["req"] == REQ and mesh.shape["tp"] == TP
    per_device = on_pairs if pairs else on_any_mesh
    in_specs = (
        P("req", "tp"),
        P("req", "tp"),
        P("req", "tp"),
        P("req", "tp"),
        P(),
        P(),
        P(),
        P(None, "req", None, "tp"),
        P("tp", None),
        P("tp"),
        P("tp"),
        P("tp"),
        P("req", "tp"),
        P("req"),
        P("req", "tp"),
        P("tp"),
        P(),
    )
    out_specs = P("req", "tp")
    return jax.shard_map(
        per_device, mesh=mesh, in_specs=in_specs, out_specs=out_specs, check_vma=False
    )
```

```python
import functools
import math

import jax
import jax.numpy as jnp
from jax import lax
from jax.experimental import pallas as pl
from jax.experimental.pallas import tpu as pltpu
from jax.sharding import PartitionSpec as P

HEAD_DIM = 128
NORM_EPS = 1e-05
PAIRWISE = 16
REQ, TP = 8, 4
ATTENTION_ROOM = 51.2
ALL_ROOM = 58
F32, BF16, I32 = jnp.float32, jnp.bfloat16, jnp.int32
VMEM = pl.BlockSpec(memory_space=pltpu.VMEM)
HBM = pl.BlockSpec(memory_space=pltpu.HBM)

ENDS_FIRST = [3, 4, 2, 5, 1, 6, 0, 7]
LOW_FIRST = [7, 6, 5, 4, 3, 2, 1, 0]


def ends_first(place):
    return jnp.where(place % 2 == 0, 3 - place // 2, 4 + place // 2)


def iota(shape, dim):
    return lax.broadcasted_iota(I32, shape, dim)


def onto_mxu(a, b):
    return jnp.dot(a, b, preferred_element_type=F32)


def nt_dot(a, b):
    return lax.dot_general(a, b, (((1,), (1,)), ((), ())), preferred_element_type=F32)


def hot(condition):
    return jnp.where(condition, 1.0, 0.0).astype(BF16)


def pile(parts):
    height = sum(p.shape[0] for p in parts)
    at, piled = 0, 0
    for p in parts:
        around = ((at, height - at - p.shape[0]),) + ((0, 0),) * (p.ndim - 1)
        piled += jnp.pad(p, around)
        at += p.shape[0]
    return piled


def row(vectors, i, cols):
    return vectors[i * cols : (i + 1) * cols][None, :]


def pack_kernel(owner_in, query, key, value, resid, out, owner, q, k, v, r, sems):
    parts = ((owner_in, owner), (query, q), (key, k), (value, v), (resid, r))
    copies = [pltpu.make_async_copy(x, y, sems.at[i]) for i, (x, y) in enumerate(parts)]
    for copy in copies:
        copy.start()
    rows, cols = q.shape
    fields = 4
    count = REQ * rows
    shape = (REQ * fields, fields * rows)
    down, across = iota(shape, 0), iota(shape, 1)
    here = (count, fields * rows)
    of_mine = hot(iota(here, 0) == lax.axis_index("req") * rows + iota(here, 1) % rows)
    copies[0].wait()
    owner_of = onto_mxu(owner[...].astype(F32).astype(BF16), of_mine).astype(I32)
    pick = hot((down % fields == across // rows) & (owner_of == down // fields))
    for copy in copies[1:]:
        copy.wait()
    all_rows = jnp.concatenate([q[...], k[...], v[...], r[...]], axis=0)
    blocks = onto_mxu(pick, all_rows).astype(BF16)
    for d in range(REQ):
        block = blocks[d * fields : (d + 1) * fields]
        at = ENDS_FIRST.index(d)
        out[at, :fields, :] = block[:, : cols // 2]
        out[at, fields:, :] = block[:, cols // 2 :]


def index_kernel(place, numbers, pick, valid, arrange, arrange_own, *, page_len):
    owner, order, lengths = (numbers[i : i + 1, :] for i in range(3))
    table = numbers[8:, :]
    me = place[0:1, 0:1]
    count = owner.shape[1]
    rows = count // REQ
    square = (count, count)
    down, across = iota(square, 0), iota(square, 1)
    owner_row = owner
    same_place = down == across
    owner_col = jnp.sum(jnp.where(same_place, owner_row, 0), axis=1, keepdims=True)
    order_col = jnp.sum(jnp.where(same_place, order, 0), axis=1, keepdims=True)
    same_owner = owner_col == owner_row
    rank_row = jnp.sum(jnp.where(same_owner & (down < across), 1, 0), axis=0, keepdims=True)
    rank_col = jnp.sum(jnp.where(same_owner & (across < down), 1, 0), axis=1, keepdims=True)

    shape = pick.shape
    down_p, across_p = iota(shape, 0), iota(shape, 1)
    down_i = iota((shape[0], count), 0)
    mine = hot((owner_row == me) & (rank_row == down_i % rows))
    source = ends_first(iota((count, shape[1]), 1) // (2 * rows))
    came = hot(iota((count, shape[1]), 0) // rows == source)
    from_there = onto_mxu(mine, came)
    pick[...] = hot((from_there > 0.5) & (down_p // rows == across_p % rows))

    shape = valid.shape
    slot = iota((shape[0], count), 0) % rows
    mine_v = hot((owner_row == me) & (rank_row == slot))
    table_v = nt_dot(mine_v, table.astype(F32).astype(BF16)).astype(I32)
    length_v = jnp.sum(jnp.where(mine_v > 0.5, lengths, 0), axis=1, keepdims=True)
    position = iota(shape, 1)
    page, within = position // page_len, position % page_len
    seen = jnp.zeros(shape, F32)
    for j in range(table.shape[0]):
        inside = (table_v[:, j : j + 1] == page) & (within + j * page_len < length_v)
        seen = jnp.where(inside, 1.0, seen)
    valid[...] = seen

    ordered = hot(order_col == across)
    across_a = iota(arrange.shape, 1)
    held_by = ends_first(across_a // (2 * rows))
    holds = hot((owner_col == held_by) & (rank_col == across_a % rows))
    arrange[...] = onto_mxu(ordered, holds).astype(BF16)
    here = hot((owner_col == me) & (rank_col == iota(arrange_own.shape, 1)))
    arrange_own[...] = onto_mxu(ordered, here).astype(BF16)


def attention_kernel(
    place, arrived, pick, valid, vectors, pool, upper, weight,
    partial, rounded, near, lower, sem, *, rows
):
    deep = upper.shape[0]
    copy = pltpu.make_async_copy(weight.at[pl.ds(deep, deep)], lower, sem)
    copy.start()
    half = arrived.shape[2]
    cols = 2 * half
    heads = cols // HEAD_DIM
    scale = 1.0 / math.sqrt(HEAD_DIM)
    came = arrived[...].reshape(-1, half)
    which = (iota(pick.shape, 1) // rows) % 2
    chosen = pick[...].astype(F32)
    own = jnp.concatenate(
        [onto_mxu(jnp.where(which == i, chosen, 0.0).astype(BF16), came) for i in range(2)], axis=1
    )
    query, key, value, resid = (own[i * rows : (i + 1) * rows] for i in range(4))

    def tile(x):
        return jnp.concatenate([x] * heads, axis=0)

    shape = (heads * rows, cols)
    in_head = iota(shape, 0) // rows == iota(shape, 1) // HEAD_DIM
    wide = jnp.where(in_head, tile(query), 0.0)
    positions = valid.shape[1]
    self_score = jnp.sum(wide * tile(key), axis=1, keepdims=True) * scale
    scores = nt_dot(wide.astype(BF16), pool[0].reshape(positions, cols)) * scale
    scores = jnp.where(valid[...] > 0.5, scores, -jnp.inf)
    top = jnp.maximum(jnp.max(scores, axis=1, keepdims=True), self_score)
    weights = jnp.exp(scores - top)
    self_weight = jnp.exp(self_score - top)
    total = jnp.sum(weights, axis=1, keepdims=True) + self_weight
    numer = onto_mxu(weights.astype(BF16), pool[1].reshape(positions, cols))
    numer = numer + self_weight.astype(BF16).astype(F32) * tile(value)
    numer = jnp.where(in_head, numer / total, 0.0)
    attn = sum(numer[i * rows : (i + 1) * rows] for i in range(heads))
    attn = jnp.concatenate([attn, jnp.zeros_like(attn)], axis=0).astype(BF16)
    projected = onto_mxu(attn[:, :deep], upper[...])
    copy.wait()
    projected = (projected + onto_mxu(attn[:, deep:], lower[...]))[:rows]
    extra = resid + row(vectors, 0, cols)
    for t in range(TP):
        mine = jnp.where(place[1:2, 0:1] == t, extra, 0.0)
        whole = projected[:, t * cols : (t + 1) * cols] + mine
        partial[:, t * cols : (t + 1) * cols] = whole
        rounded[:, t * cols : (t + 1) * cols] = whole.astype(BF16)
        near[:rows, t * cols : (t + 1) * cols] = whole.astype(BF16)
    for i in (1, 2):
        near[rows : 2 * rows, (i - 1) * cols : i * cols] = jnp.broadcast_to(
            row(vectors, i, cols), (rows, cols)
        ).astype(BF16)


def norm_kernel(place, own, sibling, far, far_sibling, vectors, blocks, stream_own):
    rows = own.shape[0]
    others = sibling[:rows, :].astype(F32) + far[...].astype(F32) + far_sibling[...].astype(F32)
    stream = (own[...] + others).astype(BF16).astype(F32)
    width = stream.shape[1]
    cols = width // TP
    mean = jnp.sum(stream, axis=1, keepdims=True) / width
    var = jnp.sum((stream - mean) ** 2, axis=1, keepdims=True) / width
    inverse = lax.rsqrt(var + NORM_EPS)
    me = place[1:2, 0:1]
    chip = jnp.where(me // 2 == 0, stream[:, : 2 * cols], stream[:, 2 * cols :])
    core = me % 2
    halves = []
    for half in range(2):
        gain, bias = (
            jnp.where(
                core == half,
                row(vectors, i, cols),
                sibling[rows : rows + 1, (i - 1) * cols : i * cols].astype(F32),
            )
            for i in (1, 2)
        )
        part = chip[:, half * cols : (half + 1) * cols]
        halves.append((part - mean) * inverse * gain + bias)
    stream_own[...] = jnp.where(core == 0, chip[:, :cols], chip[:, cols:]).astype(BF16)
    block = jnp.concatenate(halves, axis=0).astype(BF16)
    for d in range(REQ):
        blocks[d] = block


def up_kernel(place, rows_in, arrange, weight, other, out, *, rows):
    came = rows_in[...].reshape(-1, rows_in.shape[2])
    which = (iota(arrange.shape, 1) // rows) % 2
    chosen = arrange[...].astype(F32)
    core = place[1:2, 0:1] % 2

    def ordered(half):
        return onto_mxu(jnp.where(which == half, chosen, 0.0).astype(BF16), came).astype(BF16)

    hidden = nt_dot(ordered(core), weight[...]) + nt_dot(ordered(1 - core), other[...])
    out[...] = hidden.astype(BF16)


def down_kernel(near, far, vectors, weight, arrange_own, stream_own, out):
    hidden = near[...].astype(F32) + far[...].astype(F32)
    hidden = hidden + vectors[vectors.shape[0] - hidden.shape[1] :][None, :]
    activated = (0.5 * hidden * (1.0 + lax.erf(hidden * math.sqrt(0.5)))).astype(BF16)
    feed = onto_mxu(activated, weight[...]) + onto_mxu(arrange_own[...], stream_own[...])
    rows = out.shape[1]
    for d in range(REQ):
        out[LOW_FIRST.index(d)] = feed[d * rows : (d + 1) * rows].astype(BF16)


def finish_kernel(pieces, vectors, out):
    cols = out.shape[1]
    out[...] = (jnp.sum(pieces[...].astype(F32), axis=0) + row(vectors, 3, cols)).astype(BF16)


def call(kernel, shapes, specs, args, scratch=(), room=16, **fixed):
    moved = sum(a.size * a.dtype.itemsize for a in args)
    return pl.pallas_call(
        functools.partial(kernel, **fixed) if fixed else kernel,
        out_shape=shapes,
        in_specs=specs,
        out_specs=[VMEM] * len(shapes),
        scratch_shapes=scratch,
        compiler_params=pltpu.CompilerParams(vmem_limit_bytes=int(room * 2**20)),
        cost_estimate=pl.CostEstimate(flops=0, bytes_accessed=moved, transcendentals=0),
    )(*args)


def trade(blocks, group):
    return lax.all_to_all(blocks, "req", 0, 0, tiled=True, axis_index_groups=[group])


def on_pairs(
    query,
    key_new,
    value_new,
    resid,
    lengths,
    owner,
    page_table,
    kv_pool,
    out_weight,
    out_bias,
    norm_gain,
    norm_bias,
    up_weight_t,
    up_bias,
    down_weight,
    down_bias,
    order,
):
    rows, cols = query.shape
    width = cols * TP
    pool_pages, page_len = kv_pool.shape[1], kv_pool.shape[2]
    positions = pool_pages * page_len
    heads = cols // HEAD_DIM
    count = owner.shape[0]
    hidden = up_bias.shape[0]

    def arr(shape, dtype=BF16):
        return jax.ShapeDtypeStruct(shape, dtype)

    position = jnp.stack([lax.axis_index("req"), lax.axis_index("tp")]).astype(I32)
    place = jnp.broadcast_to(position[:, None], (2, HEAD_DIM))

    (packed,) = call(
        pack_kernel,
        [arr((REQ, 8, cols // 2))],
        [HBM] * 5,
        [owner[None, :], query, key_new, value_new, resid],
        [pltpu.VMEM((1, count), I32)]
        + [pltpu.VMEM((rows, cols), BF16)] * 4
        + [pltpu.SemaphoreType.DMA((5,))],
        room=ALL_ROOM,
    )
    up_other = swap(up_weight_t, "tp", 1)
    arrived = trade(packed, ENDS_FIRST)
    numbers = pile(
        [owner[None, :], order[None, :], lengths[None, :], jnp.zeros((5, count), I32), page_table.T]
    )
    vectors = pile([x.astype(F32) for x in (out_bias, norm_gain, norm_bias, down_bias, up_bias)])
    pick, valid, arrange, arrange_own = call(
        index_kernel,
        [
            arr((4 * rows, 2 * count)),
            arr((heads * rows, positions), F32),
            arr((count, 2 * count)),
            arr((count, rows)),
        ],
        [VMEM, VMEM],
        [place, numbers],
        page_len=page_len,
    )

    here = position[0] >= 0
    pool = jnp.where(here, kv_pool, jnp.zeros_like(kv_pool))
    upper = out_weight[: cols // 2]
    upper = jnp.where(here, upper, jnp.zeros_like(upper))

    partial, rounded, near = call(
        attention_kernel,
        [arr((rows, width), F32), arr((rows, width)), arr((2 * rows, width))],
        [VMEM] * 7 + [HBM],
        [place, arrived, pick, valid, vectors, pool, upper, out_weight],
        [pltpu.VMEM(upper.shape, BF16), pltpu.SemaphoreType.DMA],
        room=ATTENTION_ROOM,
        rows=rows,
    )
    blocks, stream_own = call(
        norm_kernel,
        [arr((REQ, 2 * rows, cols)), arr((rows, cols))],
        [VMEM] * 6,
        [place, partial, swap(near, "tp", 1)]
        + [swap(rounded, "tp", step) for step in (2, 3)]
        + [vectors],
    )

    (part,) = call(
        up_kernel,
        [arr((count, hidden))],
        [VMEM] * 5,
        [place, trade(blocks, ENDS_FIRST), arrange, up_weight_t, up_other],
        rows=rows,
    )
    (feed,) = call(
        down_kernel,
        [arr((REQ, rows, cols))],
        [VMEM] * 6,
        [part, swap(part, "tp", 3), vectors, down_weight, arrange_own, stream_own],
    )
    (out,) = call(finish_kernel, [arr((rows, cols))], [VMEM] * 2, [trade(feed, LOW_FIRST), vectors])
    return out


def swap(x, axis, step):
    n = lax.axis_size(axis)
    return lax.ppermute(x, axis, [(i, i ^ step) for i in range(n)])


def origins(axis):
    n, me = lax.axis_size(axis), lax.axis_index(axis)
    if n > PAIRWISE:
        return jnp.arange(n, dtype=jnp.int32)
    offsets = [0]
    step = n // 2
    while step:
        offsets = offsets + [o ^ step for o in offsets]
        step //= 2
    return jnp.array(offsets, dtype=jnp.int32) ^ me


def gather_rows(x, axis):
    n = lax.axis_size(axis)
    if n > PAIRWISE:
        return lax.all_gather(x, axis, axis=0, tiled=True)
    step = n // 2
    while step:
        x = jnp.concatenate([x, swap(x, axis, step)], axis=0)
        step //= 2
    return x


def fold_rows(x, axis):
    n = lax.axis_size(axis)
    if n > PAIRWISE:
        return lax.psum_scatter(x, axis, scatter_dimension=0, tiled=True)
    step = 1
    while step < n:
        half = x.shape[0] // 2
        x = x[:half] + swap(x[half:], axis, step)
        step *= 2
    return x


def sum_pairs(x, axis):
    n = lax.axis_size(axis)
    step = 1
    while step < n:
        x = (x.astype(jnp.float32) + swap(x, axis, step).astype(jnp.float32)).astype(x.dtype)
        step *= 2
    return x


def on_any_mesh(
    query,
    key_new,
    value_new,
    resid,
    lengths,
    owner,
    page_table,
    kv_pool,
    out_weight,
    out_bias,
    norm_gain,
    norm_bias,
    up_weight_t,
    up_bias,
    down_weight,
    down_bias,
    order,
):
    f32, bf16, i32 = jnp.float32, jnp.bfloat16, jnp.int32
    n_req = lax.axis_size("req")
    n_tp = lax.axis_size("tp")
    me = lax.axis_index("req")
    me_tp = lax.axis_index("tp")
    rows, cols = query.shape
    width = cols * n_tp
    heads = cols // HEAD_DIM
    pool_pages, page_len = kv_pool.shape[1], kv_pool.shape[2]
    positions = pool_pages * page_len
    scale = 1.0 / math.sqrt(HEAD_DIM)

    origin = origins("req")
    packed = jnp.concatenate([query, key_new, value_new, resid], axis=1)
    arrived = gather_rows(packed, "req")

    same = owner[:, None] == owner[None, :]
    ids = jnp.arange(owner.shape[0], dtype=i32)
    rank = jnp.sum((same & (ids[None, :] < ids[:, None])).astype(i32), axis=1)
    slots = jnp.arange(rows, dtype=i32)
    mine = (owner == me)[None, :] & (rank[None, :] == slots[:, None])
    mine_i = mine.astype(i32)
    own_len = jnp.sum(mine_i * lengths[None, :], axis=1)
    own_table = jnp.sum(mine_i[:, :, None] * page_table[None], axis=1)
    origin_ids = (origin[:, None] * rows + slots[None, :]).reshape(-1)
    own_id = jnp.sum(mine_i * ids[None, :], axis=1)
    take_hot = (own_id[:, None] == origin_ids[None, :]).astype(bf16)
    own = jnp.dot(take_hot, arrived, preferred_element_type=f32).astype(bf16)
    query_own, key_own, value_own, resid_own = (own[:, i * cols : (i + 1) * cols] for i in range(4))

    pos = jnp.arange(positions, dtype=i32)
    page, within = pos // page_len, pos % page_len
    entry = jnp.arange(page_table.shape[1], dtype=i32)
    start = entry * page_len
    hit = (own_table[:, :, None] == page[None, None, :]) & (
        start[None, :, None] + within[None, None, :] < own_len[:, None, None]
    )
    valid = jnp.any(hit, axis=1)

    keys = kv_pool[0].reshape(positions, cols)
    values = kv_pool[1].reshape(positions, cols)
    head_of = jnp.arange(cols, dtype=i32) // HEAD_DIM
    head_mask = head_of[None, :] == jnp.arange(heads, dtype=i32)[:, None]
    spread_q = jnp.where(head_mask[:, None, :], query_own[None], 0).reshape(heads * rows, cols)
    scores = (
        lax.dot_general(spread_q, keys, (((1,), (1,)), ((), ())), preferred_element_type=f32) * scale
    ).reshape(heads, rows, positions)
    scores = jnp.where(valid[None], scores, -jnp.inf)
    self_score = (
        jnp.sum(
            (query_own.astype(f32) * key_own.astype(f32)).reshape(rows, heads, HEAD_DIM), axis=-1
        ).T
        * scale
    )
    top = jnp.maximum(jnp.max(scores, axis=2), self_score)
    weights = jnp.exp(scores - top[:, :, None])
    self_weight = jnp.exp(self_score - top)
    total = jnp.sum(weights, axis=2) + self_weight
    numer = jnp.dot(
        weights.astype(bf16).reshape(heads * rows, positions), values, preferred_element_type=f32
    ).reshape(heads, rows, cols)
    numer = numer + self_weight.astype(bf16).astype(f32)[:, :, None] * value_own.astype(f32)[None]
    attn = jnp.sum(
        jnp.where(head_mask[:, None, :], numer / total[:, :, None], 0.0), axis=0
    ).astype(bf16)

    extra = resid_own.astype(f32) + out_bias.astype(f32)[None, :]
    partial = jnp.dot(attn, out_weight, preferred_element_type=f32)
    place = (jnp.arange(n_tp, dtype=i32) == me_tp)[None, :, None]
    partial = (
        partial.reshape(rows, n_tp, cols) + jnp.where(place, extra[:, None, :], 0.0)
    ).reshape(rows, width)
    stream = sum_pairs(partial, "tp").astype(bf16)
    stream_f = stream.astype(f32)
    mean = jnp.mean(stream_f, axis=1, keepdims=True)
    var = jnp.mean((stream_f - mean) ** 2, axis=1, keepdims=True)
    inverse = lax.rsqrt(var + NORM_EPS)
    stream_own = lax.dynamic_slice_in_dim(stream, me_tp * cols, cols, axis=1)
    normed = (
        (stream_own.astype(f32) - mean) * inverse * norm_gain.astype(f32)[None, :]
        + norm_bias.astype(f32)[None, :]
    ).astype(bf16)

    normed_all = gather_rows(normed, "req")
    slot_of = owner * rows + rank
    wanted = slot_of[order[origin_ids]]
    place_hot = (wanted[:, None] == origin_ids[None, :]).astype(bf16)
    mine_hot = (wanted[:, None] == (me * rows + slots)[None, :]).astype(bf16)
    normed_out = jnp.dot(place_hot, normed_all, preferred_element_type=f32).astype(bf16)
    hidden = lax.dot_general(
        normed_out, up_weight_t, (((1,), (1,)), ((), ())), preferred_element_type=f32
    ).astype(bf16)
    summed = sum_pairs(hidden, "tp").astype(f32)
    activated = jax.nn.gelu(summed + up_bias.astype(f32)[None, :], approximate=False).astype(bf16)
    feed = jnp.dot(activated, down_weight, preferred_element_type=f32)
    feed = feed + jnp.dot(mine_hot, stream_own, preferred_element_type=f32)
    mixed = fold_rows(feed, "req")
    return (mixed + down_bias.astype(f32)[None, :]).astype(bf16)


def solution(mesh):
    pairs = mesh.shape["req"] == REQ and mesh.shape["tp"] == TP
    per_device = on_pairs if pairs else on_any_mesh
    in_specs = (
        P("req", "tp"),
        P("req", "tp"),
        P("req", "tp"),
        P("req", "tp"),
        P(),
        P(),
        P(),
        P(None, "req", None, "tp"),
        P("tp", None),
        P("tp"),
        P("tp"),
        P("tp"),
        P("req", "tp"),
        P("req"),
        P("req", "tp"),
        P("tp"),
        P(),
    )
    out_specs = P("req", "tp")
    return jax.shard_map(
        per_device, mesh=mesh, in_specs=in_specs, out_specs=out_specs, check_vma=False
    )
```

```python
import functools
import math

import jax
import jax.numpy as jnp
from jax import lax
from jax.experimental import pallas as pl
from jax.experimental.pallas import tpu as pltpu
from jax.sharding import PartitionSpec as P

HEAD_DIM = 128
NORM_EPS = 1e-05
PAIRWISE = 16
REQ, TP = 8, 4
ATTENTION_ROOM = 51.2
ALL_ROOM = 58
F32, BF16, I32 = jnp.float32, jnp.bfloat16, jnp.int32
VMEM = pl.BlockSpec(memory_space=pltpu.VMEM)
HBM = pl.BlockSpec(memory_space=pltpu.HBM)

FIRST_ORDER = [3, 5, 2, 4, 1, 7, 0, 6]
MIDDLE_ORDER = [3, 4, 1, 6, 2, 5, 0, 7]
LAST_ORDER = [4, 3, 5, 2, 6, 1, 7, 0]


def pick_from(order, place):
    found = jnp.zeros_like(place)
    for i, index in enumerate(order):
        found = jnp.where(place == i, index, found)
    return found


def iota(shape, dim):
    return lax.broadcasted_iota(I32, shape, dim)


def onto_mxu(a, b):
    return jnp.dot(a, b, preferred_element_type=F32)


def nt_dot(a, b):
    return lax.dot_general(a, b, (((1,), (1,)), ((), ())), preferred_element_type=F32)


def hot(condition):
    return jnp.where(condition, 1.0, 0.0).astype(BF16)


def pile(parts):
    height = sum(p.shape[0] for p in parts)
    at, piled = 0, 0
    for p in parts:
        around = ((at, height - at - p.shape[0]),) + ((0, 0),) * (p.ndim - 1)
        piled += jnp.pad(p, around)
        at += p.shape[0]
    return piled


def row(vectors, i, cols):
    return vectors[i * cols : (i + 1) * cols][None, :]


def pack_kernel(owner_in, query, key, value, resid, out, owner, q, k, v, r, sems):
    parts = ((owner_in, owner), (query, q), (key, k), (value, v), (resid, r))
    copies = [pltpu.make_async_copy(x, y, sems.at[i]) for i, (x, y) in enumerate(parts)]
    for copy in copies:
        copy.start()
    rows, cols = q.shape
    fields = 4
    count = REQ * rows
    shape = (REQ * fields, fields * rows)
    down, across = iota(shape, 0), iota(shape, 1)
    here = (count, fields * rows)
    of_mine = hot(iota(here, 0) == lax.axis_index("req") * rows + iota(here, 1) % rows)
    copies[0].wait()
    owner_of = onto_mxu(owner[...].astype(F32).astype(BF16), of_mine).astype(I32)
    pick = hot((down % fields == across // rows) & (owner_of == down // fields))
    for copy in copies[1:]:
        copy.wait()
    all_rows = jnp.concatenate([q[...], k[...], v[...], r[...]], axis=0)
    blocks = onto_mxu(pick, all_rows).astype(BF16)
    for d in range(REQ):
        block = blocks[d * fields : (d + 1) * fields]
        at = FIRST_ORDER.index(d)
        out[at, :fields, :] = block[:, : cols // 2]
        out[at, fields:, :] = block[:, cols // 2 :]


def index_kernel(place, numbers, pick, valid, arrange, arrange_own, *, page_len):
    owner, order, lengths = (numbers[i : i + 1, :] for i in range(3))
    table = numbers[8:, :]
    me = place[0:1, 0:1]
    count = owner.shape[1]
    rows = count // REQ
    square = (count, count)
    down, across = iota(square, 0), iota(square, 1)
    owner_row = owner
    same_place = down == across
    owner_col = jnp.sum(jnp.where(same_place, owner_row, 0), axis=1, keepdims=True)
    order_col = jnp.sum(jnp.where(same_place, order, 0), axis=1, keepdims=True)
    same_owner = owner_col == owner_row
    rank_row = jnp.sum(jnp.where(same_owner & (down < across), 1, 0), axis=0, keepdims=True)
    rank_col = jnp.sum(jnp.where(same_owner & (across < down), 1, 0), axis=1, keepdims=True)

    shape = pick.shape
    down_p, across_p = iota(shape, 0), iota(shape, 1)
    down_i = iota((shape[0], count), 0)
    mine = hot((owner_row == me) & (rank_row == down_i % rows))
    source = pick_from(FIRST_ORDER, iota((count, shape[1]), 1) // (2 * rows))
    came = hot(iota((count, shape[1]), 0) // rows == source)
    from_there = onto_mxu(mine, came)
    pick[...] = hot((from_there > 0.5) & (down_p // rows == across_p % rows))

    shape = valid.shape
    slot = iota((shape[0], count), 0) % rows
    mine_v = hot((owner_row == me) & (rank_row == slot))
    table_v = nt_dot(mine_v, table.astype(F32).astype(BF16)).astype(I32)
    length_v = jnp.sum(jnp.where(mine_v > 0.5, lengths, 0), axis=1, keepdims=True)
    position = iota(shape, 1)
    page, within = position // page_len, position % page_len
    seen = jnp.zeros(shape, F32)
    for j in range(table.shape[0]):
        inside = (table_v[:, j : j + 1] == page) & (within + j * page_len < length_v)
        seen = jnp.where(inside, 1.0, seen)
    valid[...] = seen

    ordered = hot(order_col == across)
    holds = hot((owner_col == pick_from(MIDDLE_ORDER, across // rows)) & (rank_col == across % rows))
    arrange[...] = onto_mxu(ordered, holds).astype(BF16)
    here = hot((owner_col == me) & (rank_col == iota(arrange_own.shape, 1)))
    arrange_own[...] = onto_mxu(ordered, here).astype(BF16)


def attention_kernel(
    place, arrived, pick, valid, vectors, pool, upper, weight, partial, rounded, lower, sem, *, rows
):
    deep = upper.shape[0]
    copy = pltpu.make_async_copy(weight.at[pl.ds(deep, deep)], lower, sem)
    copy.start()
    half = arrived.shape[2]
    cols = 2 * half
    heads = cols // HEAD_DIM
    scale = 1.0 / math.sqrt(HEAD_DIM)
    came = arrived[...].reshape(-1, half)
    which = (iota(pick.shape, 1) // rows) % 2
    chosen = pick[...].astype(F32)
    own = jnp.concatenate(
        [onto_mxu(jnp.where(which == i, chosen, 0.0).astype(BF16), came) for i in range(2)], axis=1
    )
    query, key, value, resid = (own[i * rows : (i + 1) * rows] for i in range(4))

    def tile(x):
        return jnp.concatenate([x] * heads, axis=0)

    shape = (heads * rows, cols)
    in_head = iota(shape, 0) // rows == iota(shape, 1) // HEAD_DIM
    wide = jnp.where(in_head, tile(query), 0.0)
    positions = valid.shape[1]
    self_score = jnp.sum(wide * tile(key), axis=1, keepdims=True) * scale
    scores = nt_dot(wide.astype(BF16), pool[0].reshape(positions, cols)) * scale
    scores = jnp.where(valid[...] > 0.5, scores, -jnp.inf)
    top = jnp.maximum(jnp.max(scores, axis=1, keepdims=True), self_score)
    weights = jnp.exp(scores - top)
    self_weight = jnp.exp(self_score - top)
    total = jnp.sum(weights, axis=1, keepdims=True) + self_weight
    numer = onto_mxu(weights.astype(BF16), pool[1].reshape(positions, cols))
    numer = numer + self_weight.astype(BF16).astype(F32) * tile(value)
    numer = jnp.where(in_head, numer / total, 0.0)
    attn = sum(numer[i * rows : (i + 1) * rows] for i in range(heads))
    attn = jnp.concatenate([attn, jnp.zeros_like(attn)], axis=0).astype(BF16)
    projected = onto_mxu(attn[:, :deep], upper[...])
    copy.wait()
    projected = (projected + onto_mxu(attn[:, deep:], lower[...]))[:rows]
    extra = resid + row(vectors, 0, cols)
    for t in range(TP):
        mine = jnp.where(place[1:2, 0:1] == t, extra, 0.0)
        whole = projected[:, t * cols : (t + 1) * cols] + mine
        partial[:, t * cols : (t + 1) * cols] = whole
        rounded[:, t * cols : (t + 1) * cols] = whole.astype(BF16)


def norm_kernel(place, own, sibling, far, far_sibling, vectors, blocks, stream_own):
    others = sibling[...].astype(F32) + far[...].astype(F32) + far_sibling[...].astype(F32)
    stream = (own[...] + others).astype(BF16).astype(F32)
    width = stream.shape[1]
    cols = width // TP
    mean = jnp.sum(stream, axis=1, keepdims=True) / width
    var = jnp.sum((stream - mean) ** 2, axis=1, keepdims=True) / width
    mine = stream[:, :cols]
    for t in range(1, TP):
        mine = jnp.where(place[1:2, 0:1] == t, stream[:, t * cols : (t + 1) * cols], mine)
    stream_own[...] = mine.astype(BF16)
    gain, bias = row(vectors, 1, cols), row(vectors, 2, cols)
    block = ((mine - mean) * lax.rsqrt(var + NORM_EPS) * gain + bias).astype(BF16)
    for d in range(REQ):
        blocks[d] = block


def up_kernel(rows_in, arrange, weight, out):
    came = rows_in[...].reshape(-1, rows_in.shape[2])
    ordered = onto_mxu(arrange[...], came).astype(BF16)
    out[...] = nt_dot(ordered, weight[...]).astype(BF16)


def down_kernel(near, far, vectors, weight, arrange_own, stream_own, out):
    hidden = near[...].astype(F32) + far[...].astype(F32)
    hidden = hidden + vectors[vectors.shape[0] - hidden.shape[1] :][None, :]
    activated = (0.5 * hidden * (1.0 + lax.erf(hidden * math.sqrt(0.5)))).astype(BF16)
    feed = onto_mxu(activated, weight[...]) + onto_mxu(arrange_own[...], stream_own[...])
    rows = out.shape[1]
    for d in range(REQ):
        out[LAST_ORDER.index(d)] = feed[d * rows : (d + 1) * rows].astype(BF16)


def finish_kernel(pieces, vectors, out):
    cols = out.shape[1]
    out[...] = (jnp.sum(pieces[...].astype(F32), axis=0) + row(vectors, 3, cols)).astype(BF16)


def call(kernel, shapes, specs, args, scratch=(), room=16, **fixed):
    moved = sum(a.size * a.dtype.itemsize for a in args)
    return pl.pallas_call(
        functools.partial(kernel, **fixed) if fixed else kernel,
        out_shape=shapes,
        in_specs=specs,
        out_specs=[VMEM] * len(shapes),
        scratch_shapes=scratch,
        compiler_params=pltpu.CompilerParams(vmem_limit_bytes=int(room * 2**20)),
        cost_estimate=pl.CostEstimate(flops=0, bytes_accessed=moved, transcendentals=0),
    )(*args)


def trade(blocks, group):
    return lax.all_to_all(blocks, "req", 0, 0, tiled=True, axis_index_groups=[group])


def on_pairs(
    query,
    key_new,
    value_new,
    resid,
    lengths,
    owner,
    page_table,
    kv_pool,
    out_weight,
    out_bias,
    norm_gain,
    norm_bias,
    up_weight_t,
    up_bias,
    down_weight,
    down_bias,
    order,
):
    rows, cols = query.shape
    width = cols * TP
    pool_pages, page_len = kv_pool.shape[1], kv_pool.shape[2]
    positions = pool_pages * page_len
    heads = cols // HEAD_DIM
    count = owner.shape[0]
    hidden = up_bias.shape[0]

    def arr(shape, dtype=BF16):
        return jax.ShapeDtypeStruct(shape, dtype)

    position = jnp.stack([lax.axis_index("req"), lax.axis_index("tp")]).astype(I32)
    place = jnp.broadcast_to(position[:, None], (2, HEAD_DIM))

    (packed,) = call(
        pack_kernel,
        [arr((REQ, 8, cols // 2))],
        [HBM] * 5,
        [owner[None, :], query, key_new, value_new, resid],
        [pltpu.VMEM((1, count), I32)]
        + [pltpu.VMEM((rows, cols), BF16)] * 4
        + [pltpu.SemaphoreType.DMA((5,))],
        room=ALL_ROOM,
    )
    arrived = trade(packed, FIRST_ORDER)
    numbers = pile(
        [owner[None, :], order[None, :], lengths[None, :], jnp.zeros((5, count), I32), page_table.T]
    )
    vectors = pile([x.astype(F32) for x in (out_bias, norm_gain, norm_bias, down_bias, up_bias)])
    pick, valid, arrange, arrange_own = call(
        index_kernel,
        [
            arr((4 * rows, 2 * count)),
            arr((heads * rows, positions), F32),
            arr((count, count)),
            arr((count, rows)),
        ],
        [VMEM, VMEM],
        [place, numbers],
        page_len=page_len,
    )

    here = position[0] >= 0
    pool = jnp.where(here, kv_pool, jnp.zeros_like(kv_pool))
    upper = out_weight[: cols // 2]
    upper = jnp.where(here, upper, jnp.zeros_like(upper))

    partial, rounded = call(
        attention_kernel,
        [arr((rows, width), F32), arr((rows, width))],
        [VMEM] * 7 + [HBM],
        [place, arrived, pick, valid, vectors, pool, upper, out_weight],
        [pltpu.VMEM(upper.shape, BF16), pltpu.SemaphoreType.DMA],
        room=ATTENTION_ROOM,
        rows=rows,
    )
    blocks, stream_own = call(
        norm_kernel,
        [arr((REQ, rows, cols)), arr((rows, cols))],
        [VMEM] * 6,
        [place, partial] + [swap(rounded, "tp", step) for step in (1, 2, 3)] + [vectors],
    )

    (part,) = call(
        up_kernel,
        [arr((count, hidden))],
        [VMEM] * 3,
        [trade(blocks, MIDDLE_ORDER), arrange, up_weight_t],
    )
    part = (part.astype(F32) + swap(part, "tp", 1).astype(F32)).astype(BF16)
    (feed,) = call(
        down_kernel,
        [arr((REQ, rows, cols))],
        [VMEM] * 6,
        [part, swap(part, "tp", 3), vectors, down_weight, arrange_own, stream_own],
    )
    (out,) = call(finish_kernel, [arr((rows, cols))], [VMEM] * 2, [trade(feed, LAST_ORDER), vectors])
    return out


def swap(x, axis, step):
    n = lax.axis_size(axis)
    return lax.ppermute(x, axis, [(i, i ^ step) for i in range(n)])


def origins(axis):
    n, me = lax.axis_size(axis), lax.axis_index(axis)
    if n > PAIRWISE:
        return jnp.arange(n, dtype=jnp.int32)
    offsets = [0]
    step = n // 2
    while step:
        offsets = offsets + [o ^ step for o in offsets]
        step //= 2
    return jnp.array(offsets, dtype=jnp.int32) ^ me


def gather_rows(x, axis):
    n = lax.axis_size(axis)
    if n > PAIRWISE:
        return lax.all_gather(x, axis, axis=0, tiled=True)
    step = n // 2
    while step:
        x = jnp.concatenate([x, swap(x, axis, step)], axis=0)
        step //= 2
    return x


def fold_rows(x, axis):
    n = lax.axis_size(axis)
    if n > PAIRWISE:
        return lax.psum_scatter(x, axis, scatter_dimension=0, tiled=True)
    step = 1
    while step < n:
        half = x.shape[0] // 2
        x = x[:half] + swap(x[half:], axis, step)
        step *= 2
    return x


def sum_pairs(x, axis):
    n = lax.axis_size(axis)
    step = 1
    while step < n:
        x = (x.astype(jnp.float32) + swap(x, axis, step).astype(jnp.float32)).astype(x.dtype)
        step *= 2
    return x


def on_any_mesh(
    query,
    key_new,
    value_new,
    resid,
    lengths,
    owner,
    page_table,
    kv_pool,
    out_weight,
    out_bias,
    norm_gain,
    norm_bias,
    up_weight_t,
    up_bias,
    down_weight,
    down_bias,
    order,
):
    f32, bf16, i32 = jnp.float32, jnp.bfloat16, jnp.int32
    n_req = lax.axis_size("req")
    n_tp = lax.axis_size("tp")
    me = lax.axis_index("req")
    me_tp = lax.axis_index("tp")
    rows, cols = query.shape
    width = cols * n_tp
    heads = cols // HEAD_DIM
    pool_pages, page_len = kv_pool.shape[1], kv_pool.shape[2]
    positions = pool_pages * page_len
    scale = 1.0 / math.sqrt(HEAD_DIM)

    origin = origins("req")
    packed = jnp.concatenate([query, key_new, value_new, resid], axis=1)
    arrived = gather_rows(packed, "req")

    same = owner[:, None] == owner[None, :]
    ids = jnp.arange(owner.shape[0], dtype=i32)
    rank = jnp.sum((same & (ids[None, :] < ids[:, None])).astype(i32), axis=1)
    slots = jnp.arange(rows, dtype=i32)
    mine = (owner == me)[None, :] & (rank[None, :] == slots[:, None])
    mine_i = mine.astype(i32)
    own_len = jnp.sum(mine_i * lengths[None, :], axis=1)
    own_table = jnp.sum(mine_i[:, :, None] * page_table[None], axis=1)
    origin_ids = (origin[:, None] * rows + slots[None, :]).reshape(-1)
    own_id = jnp.sum(mine_i * ids[None, :], axis=1)
    take_hot = (own_id[:, None] == origin_ids[None, :]).astype(bf16)
    own = jnp.dot(take_hot, arrived, preferred_element_type=f32).astype(bf16)
    query_own, key_own, value_own, resid_own = (own[:, i * cols : (i + 1) * cols] for i in range(4))

    pos = jnp.arange(positions, dtype=i32)
    page, within = pos // page_len, pos % page_len
    entry = jnp.arange(page_table.shape[1], dtype=i32)
    start = entry * page_len
    hit = (own_table[:, :, None] == page[None, None, :]) & (
        start[None, :, None] + within[None, None, :] < own_len[:, None, None]
    )
    valid = jnp.any(hit, axis=1)

    keys = kv_pool[0].reshape(positions, cols)
    values = kv_pool[1].reshape(positions, cols)
    head_of = jnp.arange(cols, dtype=i32) // HEAD_DIM
    head_mask = head_of[None, :] == jnp.arange(heads, dtype=i32)[:, None]
    spread_q = jnp.where(head_mask[:, None, :], query_own[None], 0).reshape(heads * rows, cols)
    scores = (
        lax.dot_general(spread_q, keys, (((1,), (1,)), ((), ())), preferred_element_type=f32) * scale
    ).reshape(heads, rows, positions)
    scores = jnp.where(valid[None], scores, -jnp.inf)
    self_score = (
        jnp.sum(
            (query_own.astype(f32) * key_own.astype(f32)).reshape(rows, heads, HEAD_DIM), axis=-1
        ).T
        * scale
    )
    top = jnp.maximum(jnp.max(scores, axis=2), self_score)
    weights = jnp.exp(scores - top[:, :, None])
    self_weight = jnp.exp(self_score - top)
    total = jnp.sum(weights, axis=2) + self_weight
    numer = jnp.dot(
        weights.astype(bf16).reshape(heads * rows, positions), values, preferred_element_type=f32
    ).reshape(heads, rows, cols)
    numer = numer + self_weight.astype(bf16).astype(f32)[:, :, None] * value_own.astype(f32)[None]
    attn = jnp.sum(
        jnp.where(head_mask[:, None, :], numer / total[:, :, None], 0.0), axis=0
    ).astype(bf16)

    extra = resid_own.astype(f32) + out_bias.astype(f32)[None, :]
    partial = jnp.dot(attn, out_weight, preferred_element_type=f32)
    place = (jnp.arange(n_tp, dtype=i32) == me_tp)[None, :, None]
    partial = (
        partial.reshape(rows, n_tp, cols) + jnp.where(place, extra[:, None, :], 0.0)
    ).reshape(rows, width)
    stream = sum_pairs(partial, "tp").astype(bf16)
    stream_f = stream.astype(f32)
    mean = jnp.mean(stream_f, axis=1, keepdims=True)
    var = jnp.mean((stream_f - mean) ** 2, axis=1, keepdims=True)
    inverse = lax.rsqrt(var + NORM_EPS)
    stream_own = lax.dynamic_slice_in_dim(stream, me_tp * cols, cols, axis=1)
    normed = (
        (stream_own.astype(f32) - mean) * inverse * norm_gain.astype(f32)[None, :]
        + norm_bias.astype(f32)[None, :]
    ).astype(bf16)

    normed_all = gather_rows(normed, "req")
    slot_of = owner * rows + rank
    wanted = slot_of[order[origin_ids]]
    place_hot = (wanted[:, None] == origin_ids[None, :]).astype(bf16)
    mine_hot = (wanted[:, None] == (me * rows + slots)[None, :]).astype(bf16)
    normed_out = jnp.dot(place_hot, normed_all, preferred_element_type=f32).astype(bf16)
    hidden = lax.dot_general(
        normed_out, up_weight_t, (((1,), (1,)), ((), ())), preferred_element_type=f32
    ).astype(bf16)
    summed = sum_pairs(hidden, "tp").astype(f32)
    activated = jax.nn.gelu(summed + up_bias.astype(f32)[None, :], approximate=False).astype(bf16)
    feed = jnp.dot(activated, down_weight, preferred_element_type=f32)
    feed = feed + jnp.dot(mine_hot, stream_own, preferred_element_type=f32)
    mixed = fold_rows(feed, "req")
    return (mixed + down_bias.astype(f32)[None, :]).astype(bf16)


def solution(mesh):
    pairs = mesh.shape["req"] == REQ and mesh.shape["tp"] == TP
    per_device = on_pairs if pairs else on_any_mesh
    in_specs = (
        P("req", "tp"),
        P("req", "tp"),
        P("req", "tp"),
        P("req", "tp"),
        P(),
        P(),
        P(),
        P(None, "req", None, "tp"),
        P("tp", None),
        P("tp"),
        P("tp"),
        P("tp"),
        P("req", "tp"),
        P("req"),
        P("req", "tp"),
        P("tp"),
        P(),
    )
    out_specs = P("req", "tp")
    return jax.shard_map(
        per_device, mesh=mesh, in_specs=in_specs, out_specs=out_specs, check_vma=False
    )
```

```python
import functools
import math

import jax
import jax.numpy as jnp
from jax import lax
from jax.experimental import pallas as pl
from jax.experimental.pallas import tpu as pltpu
from jax.sharding import PartitionSpec as P

HEAD_DIM = 128
NORM_EPS = 1e-05
PAIRWISE = 16
REQ, TP = 8, 4
ATTENTION_ROOM = 51.2
ALL_ROOM = 58
F32, BF16, I32 = jnp.float32, jnp.bfloat16, jnp.int32
VMEM = pl.BlockSpec(memory_space=pltpu.VMEM)
HBM = pl.BlockSpec(memory_space=pltpu.HBM)

FIRST_ORDER = [3, 5, 2, 4, 1, 7, 0, 6]
MIDDLE_ORDER = [3, 4, 1, 6, 2, 5, 0, 7]
LAST_ORDER = [7, 6, 5, 4, 3, 2, 1, 0]


def pick_from(order, place):
    found = jnp.zeros_like(place)
    for i, index in enumerate(order):
        found = jnp.where(place == i, index, found)
    return found


def iota(shape, dim):
    return lax.broadcasted_iota(I32, shape, dim)


def onto_mxu(a, b):
    return jnp.dot(a, b, preferred_element_type=F32)


def nt_dot(a, b):
    return lax.dot_general(a, b, (((1,), (1,)), ((), ())), preferred_element_type=F32)


def hot(condition):
    return jnp.where(condition, 1.0, 0.0).astype(BF16)


def pile(parts):
    height = sum(p.shape[0] for p in parts)
    at, piled = 0, 0
    for p in parts:
        around = ((at, height - at - p.shape[0]),) + ((0, 0),) * (p.ndim - 1)
        piled += jnp.pad(p, around)
        at += p.shape[0]
    return piled


def row(vectors, i, cols):
    return vectors[i * cols : (i + 1) * cols][None, :]


def pack_kernel(owner_in, query, key, value, resid, out, owner, q, k, v, r, sems):
    parts = ((owner_in, owner), (query, q), (key, k), (value, v), (resid, r))
    copies = [pltpu.make_async_copy(x, y, sems.at[i]) for i, (x, y) in enumerate(parts)]
    for copy in copies:
        copy.start()
    rows, cols = q.shape
    fields = 4
    count = REQ * rows
    shape = (REQ * fields, fields * rows)
    down, across = iota(shape, 0), iota(shape, 1)
    here = (count, fields * rows)
    of_mine = hot(iota(here, 0) == lax.axis_index("req") * rows + iota(here, 1) % rows)
    copies[0].wait()
    owner_of = onto_mxu(owner[...].astype(F32).astype(BF16), of_mine).astype(I32)
    pick = hot((down % fields == across // rows) & (owner_of == down // fields))
    for copy in copies[1:]:
        copy.wait()
    all_rows = jnp.concatenate([q[...], k[...], v[...], r[...]], axis=0)
    blocks = onto_mxu(pick, all_rows).astype(BF16)
    for d in range(REQ):
        block = blocks[d * fields : (d + 1) * fields]
        at = FIRST_ORDER.index(d)
        out[at, :fields, :] = block[:, : cols // 2]
        out[at, fields:, :] = block[:, cols // 2 :]


def index_kernel(place, numbers, pick, valid, arrange, arrange_own, *, page_len, heads):
    owner, order, lengths = (numbers[i : i + 1, :] for i in range(3))
    table = numbers[8:, :]
    me = place[0:1, 0:1]
    count = owner.shape[1]
    rows = count // REQ
    square = (count, count)
    down, across = iota(square, 0), iota(square, 1)
    owner_row = owner
    same_place = down == across
    owner_col = jnp.sum(jnp.where(same_place, owner_row, 0), axis=1, keepdims=True)
    order_col = jnp.sum(jnp.where(same_place, order, 0), axis=1, keepdims=True)
    same_owner = owner_col == owner_row
    rank_row = jnp.sum(jnp.where(same_owner & (down < across), 1, 0), axis=0, keepdims=True)
    rank_col = jnp.sum(jnp.where(same_owner & (across < down), 1, 0), axis=1, keepdims=True)

    shape = pick.shape
    down_p, across_p = iota(shape, 0), iota(shape, 1)
    down_i = iota((shape[0], count), 0)
    mine = hot((owner_row == me) & (rank_row == down_i % rows))
    source = pick_from(FIRST_ORDER, iota((count, shape[1]), 1) // (2 * rows))
    came = hot(iota((count, shape[1]), 0) // rows == source)
    from_there = onto_mxu(mine, came)
    field = jnp.minimum(down_p // (heads * rows), 3)
    pick[...] = hot((from_there > 0.5) & (field == across_p % rows))

    shape = valid.shape
    slot = iota((shape[0], count), 0) % rows
    mine_v = hot((owner_row == me) & (rank_row == slot))
    table_v = nt_dot(mine_v, table.astype(F32).astype(BF16)).astype(I32)
    length_v = jnp.sum(jnp.where(mine_v > 0.5, lengths, 0), axis=1, keepdims=True)
    position = iota(shape, 1)
    page, within = position // page_len, position % page_len
    seen = jnp.zeros(shape, F32)
    for j in range(table.shape[0]):
        inside = (table_v[:, j : j + 1] == page) & (within + j * page_len < length_v)
        seen = jnp.where(inside, 1.0, seen)
    valid[...] = seen

    ordered = hot(order_col == across)
    holds = hot((owner_col == pick_from(MIDDLE_ORDER, across // rows)) & (rank_col == across % rows))
    arrange[...] = onto_mxu(ordered, holds).astype(BF16)
    here = hot((owner_col == me) & (rank_col == iota(arrange_own.shape, 1)))
    arrange_own[...] = onto_mxu(ordered, here).astype(BF16)


def attention_kernel(
    place, arrived, pick, valid, vectors, pool, upper, weight, partial, rounded, lower, sem, *, rows
):
    deep = upper.shape[0]
    copy = pltpu.make_async_copy(weight.at[pl.ds(deep, deep)], lower, sem)
    copy.start()
    half = arrived.shape[2]
    cols = 2 * half
    heads = cols // HEAD_DIM
    scale = 1.0 / math.sqrt(HEAD_DIM)
    came = arrived[...].reshape(-1, half)
    which = (iota(pick.shape, 1) // rows) % 2
    chosen = pick[...].astype(F32)
    own = jnp.concatenate(
        [onto_mxu(jnp.where(which == i, chosen, 0.0).astype(BF16), came) for i in range(2)], axis=1
    )
    each = heads * rows
    query, key, value = (own[i * each : (i + 1) * each] for i in range(3))
    resid = own[3 * each : 3 * each + rows]
    shape = (each, cols)
    in_head = iota(shape, 0) // rows == iota(shape, 1) // HEAD_DIM
    wide = jnp.where(in_head, query, 0.0)
    positions = valid.shape[1]
    self_score = jnp.sum(wide * key, axis=1, keepdims=True) * scale
    scores = nt_dot(wide.astype(BF16), pool[0].reshape(positions, cols)) * scale
    scores = jnp.where(valid[...] > 0.5, scores, -jnp.inf)
    top = jnp.maximum(jnp.max(scores, axis=1, keepdims=True), self_score)
    weights = jnp.exp(scores - top)
    self_weight = jnp.exp(self_score - top)
    total = jnp.sum(weights, axis=1, keepdims=True) + self_weight
    numer = onto_mxu(weights.astype(BF16), pool[1].reshape(positions, cols))
    numer = numer + self_weight.astype(BF16).astype(F32) * value
    numer = jnp.where(in_head, numer / total, 0.0)
    attn = sum(numer[i * rows : (i + 1) * rows] for i in range(heads))
    attn = jnp.concatenate([attn, jnp.zeros_like(attn)], axis=0).astype(BF16)
    projected = onto_mxu(attn[:, :deep], upper[...])
    copy.wait()
    projected = (projected + onto_mxu(attn[:, deep:], lower[...]))[:rows]
    extra = resid + row(vectors, 0, cols)
    for t in range(TP):
        mine = jnp.where(place[1:2, 0:1] == t, extra, 0.0)
        whole = projected[:, t * cols : (t + 1) * cols] + mine
        partial[:, t * cols : (t + 1) * cols] = whole
        rounded[:, t * cols : (t + 1) * cols] = whole.astype(BF16)


def norm_kernel(place, own, sibling, far, far_sibling, vectors, blocks, stream_own):
    others = sibling[...].astype(F32) + far[...].astype(F32) + far_sibling[...].astype(F32)
    stream = (own[...] + others).astype(BF16).astype(F32)
    width = stream.shape[1]
    cols = width // TP
    mean = jnp.sum(stream, axis=1, keepdims=True) / width
    var = jnp.sum((stream - mean) ** 2, axis=1, keepdims=True) / width
    mine = stream[:, :cols]
    for t in range(1, TP):
        mine = jnp.where(place[1:2, 0:1] == t, stream[:, t * cols : (t + 1) * cols], mine)
    stream_own[...] = mine.astype(BF16)
    gain, bias = row(vectors, 1, cols), row(vectors, 2, cols)
    block = ((mine - mean) * lax.rsqrt(var + NORM_EPS) * gain + bias).astype(BF16)
    for d in range(REQ):
        blocks[d] = block


def up_kernel(rows_in, arrange, weight, out):
    came = rows_in[...].reshape(-1, rows_in.shape[2])
    ordered = onto_mxu(arrange[...], came).astype(BF16)
    out[...] = nt_dot(ordered, weight[...]).astype(BF16)


def down_kernel(near, far, vectors, weight, arrange_own, stream_own, out):
    hidden = near[...].astype(F32) + far[...].astype(F32)
    hidden = hidden + vectors[vectors.shape[0] - hidden.shape[1] :][None, :]
    activated = (0.5 * hidden * (1.0 + lax.erf(hidden * math.sqrt(0.5)))).astype(BF16)
    feed = onto_mxu(activated, weight[...]) + onto_mxu(arrange_own[...], stream_own[...])
    rows = out.shape[1]
    for d in range(REQ):
        out[LAST_ORDER.index(d)] = feed[d * rows : (d + 1) * rows].astype(BF16)


def finish_kernel(pieces, vectors, out):
    cols = out.shape[1]
    out[...] = (jnp.sum(pieces[...].astype(F32), axis=0) + row(vectors, 3, cols)).astype(BF16)


def call(kernel, shapes, specs, args, scratch=(), room=16, **fixed):
    moved = sum(a.size * a.dtype.itemsize for a in args)
    return pl.pallas_call(
        functools.partial(kernel, **fixed) if fixed else kernel,
        out_shape=shapes,
        in_specs=specs,
        out_specs=[VMEM] * len(shapes),
        scratch_shapes=scratch,
        compiler_params=pltpu.CompilerParams(vmem_limit_bytes=int(room * 2**20)),
        cost_estimate=pl.CostEstimate(flops=0, bytes_accessed=moved, transcendentals=0),
    )(*args)


def trade(blocks, group):
    return lax.all_to_all(blocks, "req", 0, 0, tiled=True, axis_index_groups=[group])


def on_pairs(
    query,
    key_new,
    value_new,
    resid,
    lengths,
    owner,
    page_table,
    kv_pool,
    out_weight,
    out_bias,
    norm_gain,
    norm_bias,
    up_weight_t,
    up_bias,
    down_weight,
    down_bias,
    order,
):
    rows, cols = query.shape
    width = cols * TP
    pool_pages, page_len = kv_pool.shape[1], kv_pool.shape[2]
    positions = pool_pages * page_len
    heads = cols // HEAD_DIM
    count = owner.shape[0]
    hidden = up_bias.shape[0]

    def arr(shape, dtype=BF16):
        return jax.ShapeDtypeStruct(shape, dtype)

    position = jnp.stack([lax.axis_index("req"), lax.axis_index("tp")]).astype(I32)
    place = jnp.broadcast_to(position[:, None], (2, HEAD_DIM))

    (packed,) = call(
        pack_kernel,
        [arr((REQ, 8, cols // 2))],
        [HBM] * 5,
        [owner[None, :], query, key_new, value_new, resid],
        [pltpu.VMEM((1, count), I32)]
        + [pltpu.VMEM((rows, cols), BF16)] * 4
        + [pltpu.SemaphoreType.DMA((5,))],
        room=ALL_ROOM,
    )
    arrived = trade(packed, FIRST_ORDER)
    numbers = pile(
        [owner[None, :], order[None, :], lengths[None, :], jnp.zeros((5, count), I32), page_table.T]
    )
    vectors = pile([x.astype(F32) for x in (out_bias, norm_gain, norm_bias, down_bias, up_bias)])
    pick, valid, arrange, arrange_own = call(
        index_kernel,
        [
            arr((3 * heads * rows + 2 * rows, 2 * count)),
            arr((heads * rows, positions), F32),
            arr((count, count)),
            arr((count, rows)),
        ],
        [VMEM, VMEM],
        [place, numbers],
        page_len=page_len,
        heads=heads,
    )

    here = position[0] >= 0
    pool = jnp.where(here, kv_pool, jnp.zeros_like(kv_pool))
    upper = out_weight[: cols // 2]
    upper = jnp.where(here, upper, jnp.zeros_like(upper))

    partial, rounded = call(
        attention_kernel,
        [arr((rows, width), F32), arr((rows, width))],
        [VMEM] * 7 + [HBM],
        [place, arrived, pick, valid, vectors, pool, upper, out_weight],
        [pltpu.VMEM(upper.shape, BF16), pltpu.SemaphoreType.DMA],
        room=ATTENTION_ROOM,
        rows=rows,
    )
    blocks, stream_own = call(
        norm_kernel,
        [arr((REQ, rows, cols)), arr((rows, cols))],
        [VMEM] * 6,
        [place, partial] + [swap(rounded, "tp", step) for step in (1, 2, 3)] + [vectors],
    )

    (part,) = call(
        up_kernel,
        [arr((count, hidden))],
        [VMEM] * 3,
        [trade(blocks, MIDDLE_ORDER), arrange, up_weight_t],
    )
    part = (part.astype(F32) + swap(part, "tp", 1).astype(F32)).astype(BF16)
    (feed,) = call(
        down_kernel,
        [arr((REQ, rows, cols))],
        [VMEM] * 6,
        [part, swap(part, "tp", 3), vectors, down_weight, arrange_own, stream_own],
    )
    (out,) = call(finish_kernel, [arr((rows, cols))], [VMEM] * 2, [trade(feed, LAST_ORDER), vectors])
    return out


def swap(x, axis, step):
    n = lax.axis_size(axis)
    return lax.ppermute(x, axis, [(i, i ^ step) for i in range(n)])


def origins(axis):
    n, me = lax.axis_size(axis), lax.axis_index(axis)
    if n > PAIRWISE:
        return jnp.arange(n, dtype=jnp.int32)
    offsets = [0]
    step = n // 2
    while step:
        offsets = offsets + [o ^ step for o in offsets]
        step //= 2
    return jnp.array(offsets, dtype=jnp.int32) ^ me


def gather_rows(x, axis):
    n = lax.axis_size(axis)
    if n > PAIRWISE:
        return lax.all_gather(x, axis, axis=0, tiled=True)
    step = n // 2
    while step:
        x = jnp.concatenate([x, swap(x, axis, step)], axis=0)
        step //= 2
    return x


def fold_rows(x, axis):
    n = lax.axis_size(axis)
    if n > PAIRWISE:
        return lax.psum_scatter(x, axis, scatter_dimension=0, tiled=True)
    step = 1
    while step < n:
        half = x.shape[0] // 2
        x = x[:half] + swap(x[half:], axis, step)
        step *= 2
    return x


def sum_pairs(x, axis):
    n = lax.axis_size(axis)
    step = 1
    while step < n:
        x = (x.astype(jnp.float32) + swap(x, axis, step).astype(jnp.float32)).astype(x.dtype)
        step *= 2
    return x


def on_any_mesh(
    query,
    key_new,
    value_new,
    resid,
    lengths,
    owner,
    page_table,
    kv_pool,
    out_weight,
    out_bias,
    norm_gain,
    norm_bias,
    up_weight_t,
    up_bias,
    down_weight,
    down_bias,
    order,
):
    f32, bf16, i32 = jnp.float32, jnp.bfloat16, jnp.int32
    n_req = lax.axis_size("req")
    n_tp = lax.axis_size("tp")
    me = lax.axis_index("req")
    me_tp = lax.axis_index("tp")
    rows, cols = query.shape
    width = cols * n_tp
    heads = cols // HEAD_DIM
    pool_pages, page_len = kv_pool.shape[1], kv_pool.shape[2]
    positions = pool_pages * page_len
    scale = 1.0 / math.sqrt(HEAD_DIM)

    origin = origins("req")
    packed = jnp.concatenate([query, key_new, value_new, resid], axis=1)
    arrived = gather_rows(packed, "req")

    same = owner[:, None] == owner[None, :]
    ids = jnp.arange(owner.shape[0], dtype=i32)
    rank = jnp.sum((same & (ids[None, :] < ids[:, None])).astype(i32), axis=1)
    slots = jnp.arange(rows, dtype=i32)
    mine = (owner == me)[None, :] & (rank[None, :] == slots[:, None])
    mine_i = mine.astype(i32)
    own_len = jnp.sum(mine_i * lengths[None, :], axis=1)
    own_table = jnp.sum(mine_i[:, :, None] * page_table[None], axis=1)
    origin_ids = (origin[:, None] * rows + slots[None, :]).reshape(-1)
    own_id = jnp.sum(mine_i * ids[None, :], axis=1)
    take_hot = (own_id[:, None] == origin_ids[None, :]).astype(bf16)
    own = jnp.dot(take_hot, arrived, preferred_element_type=f32).astype(bf16)
    query_own, key_own, value_own, resid_own = (own[:, i * cols : (i + 1) * cols] for i in range(4))

    pos = jnp.arange(positions, dtype=i32)
    page, within = pos // page_len, pos % page_len
    entry = jnp.arange(page_table.shape[1], dtype=i32)
    start = entry * page_len
    hit = (own_table[:, :, None] == page[None, None, :]) & (
        start[None, :, None] + within[None, None, :] < own_len[:, None, None]
    )
    valid = jnp.any(hit, axis=1)

    keys = kv_pool[0].reshape(positions, cols)
    values = kv_pool[1].reshape(positions, cols)
    head_of = jnp.arange(cols, dtype=i32) // HEAD_DIM
    head_mask = head_of[None, :] == jnp.arange(heads, dtype=i32)[:, None]
    spread_q = jnp.where(head_mask[:, None, :], query_own[None], 0).reshape(heads * rows, cols)
    scores = (
        lax.dot_general(spread_q, keys, (((1,), (1,)), ((), ())), preferred_element_type=f32) * scale
    ).reshape(heads, rows, positions)
    scores = jnp.where(valid[None], scores, -jnp.inf)
    self_score = (
        jnp.sum(
            (query_own.astype(f32) * key_own.astype(f32)).reshape(rows, heads, HEAD_DIM), axis=-1
        ).T
        * scale
    )
    top = jnp.maximum(jnp.max(scores, axis=2), self_score)
    weights = jnp.exp(scores - top[:, :, None])
    self_weight = jnp.exp(self_score - top)
    total = jnp.sum(weights, axis=2) + self_weight
    numer = jnp.dot(
        weights.astype(bf16).reshape(heads * rows, positions), values, preferred_element_type=f32
    ).reshape(heads, rows, cols)
    numer = numer + self_weight.astype(bf16).astype(f32)[:, :, None] * value_own.astype(f32)[None]
    attn = jnp.sum(
        jnp.where(head_mask[:, None, :], numer / total[:, :, None], 0.0), axis=0
    ).astype(bf16)

    extra = resid_own.astype(f32) + out_bias.astype(f32)[None, :]
    partial = jnp.dot(attn, out_weight, preferred_element_type=f32)
    place = (jnp.arange(n_tp, dtype=i32) == me_tp)[None, :, None]
    partial = (
        partial.reshape(rows, n_tp, cols) + jnp.where(place, extra[:, None, :], 0.0)
    ).reshape(rows, width)
    stream = sum_pairs(partial, "tp").astype(bf16)
    stream_f = stream.astype(f32)
    mean = jnp.mean(stream_f, axis=1, keepdims=True)
    var = jnp.mean((stream_f - mean) ** 2, axis=1, keepdims=True)
    inverse = lax.rsqrt(var + NORM_EPS)
    stream_own = lax.dynamic_slice_in_dim(stream, me_tp * cols, cols, axis=1)
    normed = (
        (stream_own.astype(f32) - mean) * inverse * norm_gain.astype(f32)[None, :]
        + norm_bias.astype(f32)[None, :]
    ).astype(bf16)

    normed_all = gather_rows(normed, "req")
    slot_of = owner * rows + rank
    wanted = slot_of[order[origin_ids]]
    place_hot = (wanted[:, None] == origin_ids[None, :]).astype(bf16)
    mine_hot = (wanted[:, None] == (me * rows + slots)[None, :]).astype(bf16)
    normed_out = jnp.dot(place_hot, normed_all, preferred_element_type=f32).astype(bf16)
    hidden = lax.dot_general(
        normed_out, up_weight_t, (((1,), (1,)), ((), ())), preferred_element_type=f32
    ).astype(bf16)
    summed = sum_pairs(hidden, "tp").astype(f32)
    activated = jax.nn.gelu(summed + up_bias.astype(f32)[None, :], approximate=False).astype(bf16)
    feed = jnp.dot(activated, down_weight, preferred_element_type=f32)
    feed = feed + jnp.dot(mine_hot, stream_own, preferred_element_type=f32)
    mixed = fold_rows(feed, "req")
    return (mixed + down_bias.astype(f32)[None, :]).astype(bf16)


def solution(mesh):
    pairs = mesh.shape["req"] == REQ and mesh.shape["tp"] == TP
    per_device = on_pairs if pairs else on_any_mesh
    in_specs = (
        P("req", "tp"),
        P("req", "tp"),
        P("req", "tp"),
        P("req", "tp"),
        P(),
        P(),
        P(),
        P(None, "req", None, "tp"),
        P("tp", None),
        P("tp"),
        P("tp"),
        P("tp"),
        P("req", "tp"),
        P("req"),
        P("req", "tp"),
        P("tp"),
        P(),
    )
    out_specs = P("req", "tp")
    return jax.shard_map(
        per_device, mesh=mesh, in_specs=in_specs, out_specs=out_specs, check_vma=False
    )
```

```python
import functools
import math

import jax
import jax.numpy as jnp
from jax import lax
from jax.experimental import pallas as pl
from jax.experimental.pallas import tpu as pltpu
from jax.sharding import PartitionSpec as P

HEAD_DIM = 128
NORM_EPS = 1e-05
PAIRWISE = 16
REQ, TP = 8, 4
ATTENTION_ROOM = 50.6
ALL_ROOM = 58
F32, BF16, I32 = jnp.float32, jnp.bfloat16, jnp.int32
VMEM = pl.BlockSpec(memory_space=pltpu.VMEM)
HBM = pl.BlockSpec(memory_space=pltpu.HBM)

FIRST_ORDER = [2, 4, 0, 6, 3, 5, 1, 7]
MIDDLE_ORDER = [1, 4, 3, 6, 0, 5, 2, 7]
LAST_ORDER = [7, 6, 5, 4, 3, 2, 1, 0]


def pick_from(order, place):
    found = jnp.zeros_like(place)
    for i, index in enumerate(order):
        found = jnp.where(place == i, index, found)
    return found


def iota(shape, dim):
    return lax.broadcasted_iota(I32, shape, dim)


def onto_mxu(a, b):
    return jnp.dot(a, b, preferred_element_type=F32)


def nt_dot(a, b):
    return lax.dot_general(a, b, (((1,), (1,)), ((), ())), preferred_element_type=F32)


def hot(condition):
    return jnp.where(condition, 1.0, 0.0).astype(BF16)


def pile(parts):
    height = sum(p.shape[0] for p in parts)
    at, piled = 0, 0
    for p in parts:
        around = ((at, height - at - p.shape[0]),) + ((0, 0),) * (p.ndim - 1)
        piled += jnp.pad(p, around)
        at += p.shape[0]
    return piled


def row(vectors, i, cols):
    return vectors[i * cols : (i + 1) * cols][None, :]


def pack_kernel(owner_in, query, key, value, resid, out, owner, q, k, v, r, sems):
    parts = ((owner_in, owner), (query, q), (key, k), (value, v), (resid, r))
    copies = [pltpu.make_async_copy(x, y, sems.at[i]) for i, (x, y) in enumerate(parts)]
    for copy in copies:
        copy.start()
    rows, cols = q.shape
    fields = 4
    count = REQ * rows
    shape = (REQ * fields, fields * rows)
    down, across = iota(shape, 0), iota(shape, 1)
    here = (count, fields * rows)
    of_mine = hot(iota(here, 0) == lax.axis_index("req") * rows + iota(here, 1) % rows)
    copies[0].wait()
    owner_of = onto_mxu(owner[...].astype(F32).astype(BF16), of_mine).astype(I32)
    pick = hot((down % fields == across // rows) & (owner_of == down // fields))
    for copy in copies[1:]:
        copy.wait()
    all_rows = jnp.concatenate([q[...], k[...], v[...], r[...]], axis=0)
    blocks = onto_mxu(pick, all_rows).astype(BF16)
    for d in range(REQ):
        block = blocks[d * fields : (d + 1) * fields]
        at = FIRST_ORDER.index(d)
        out[at, :fields, :] = block[:, : cols // 2]
        out[at, fields:, :] = block[:, cols // 2 :]


def index_kernel(place, numbers, pick, valid, arrange, arrange_own, *, page_len, heads):
    owner, order, lengths = (numbers[i : i + 1, :] for i in range(3))
    table = numbers[8:, :]
    me = place[0:1, 0:1]
    count = owner.shape[1]
    rows = count // REQ
    square = (count, count)
    down, across = iota(square, 0), iota(square, 1)
    owner_row = owner
    same_place = down == across
    owner_col = jnp.sum(jnp.where(same_place, owner_row, 0), axis=1, keepdims=True)
    order_col = jnp.sum(jnp.where(same_place, order, 0), axis=1, keepdims=True)
    same_owner = owner_col == owner_row
    rank_row = jnp.sum(jnp.where(same_owner & (down < across), 1, 0), axis=0, keepdims=True)
    rank_col = jnp.sum(jnp.where(same_owner & (across < down), 1, 0), axis=1, keepdims=True)

    shape = pick.shape
    down_p, across_p = iota(shape, 0), iota(shape, 1)
    down_i = iota((shape[0], count), 0)
    mine = hot((owner_row == me) & (rank_row == down_i % rows))
    source = pick_from(FIRST_ORDER, iota((count, shape[1]), 1) // (2 * rows))
    came = hot(iota((count, shape[1]), 0) // rows == source)
    from_there = onto_mxu(mine, came)
    field = jnp.minimum(down_p // (heads * rows), 3)
    pick[...] = hot((from_there > 0.5) & (field == across_p % rows))

    shape = valid.shape
    slot = iota((shape[0], count), 0) % rows
    mine_v = hot((owner_row == me) & (rank_row == slot))
    table_v = nt_dot(mine_v, table.astype(F32).astype(BF16)).astype(I32)
    length_v = jnp.sum(jnp.where(mine_v > 0.5, lengths, 0), axis=1, keepdims=True)
    position = iota(shape, 1)
    page, within = position // page_len, position % page_len
    seen = jnp.zeros(shape, F32)
    for j in range(table.shape[0]):
        inside = (table_v[:, j : j + 1] == page) & (within + j * page_len < length_v)
        seen = jnp.where(inside, 1.0, seen)
    valid[...] = seen

    ordered = hot(order_col == across)
    holds = hot((owner_col == pick_from(MIDDLE_ORDER, across // rows)) & (rank_col == across % rows))
    arrange[...] = onto_mxu(ordered, holds).astype(BF16)
    here = hot((owner_col == me) & (rank_col == iota(arrange_own.shape, 1)))
    arrange_own[...] = onto_mxu(ordered, here).astype(BF16)


def attention_kernel(
    place, arrived, pick, valid, vectors, pool, upper, weight, partial, rounded, lower, sem, *, rows
):
    deep = upper.shape[0]
    copy = pltpu.make_async_copy(weight.at[pl.ds(deep, lower.shape[0])], lower, sem)
    copy.start()
    half = arrived.shape[2]
    cols = 2 * half
    heads = cols // HEAD_DIM
    scale = 1.0 / math.sqrt(HEAD_DIM)
    came = arrived[...].reshape(-1, half)
    which = (iota(pick.shape, 1) // rows) % 2
    chosen = pick[...].astype(F32)
    own = jnp.concatenate(
        [onto_mxu(jnp.where(which == i, chosen, 0.0).astype(BF16), came) for i in range(2)], axis=1
    )
    each = heads * rows
    query, key, value = (own[i * each : (i + 1) * each] for i in range(3))
    resid = own[3 * each : 3 * each + rows]
    shape = (each, cols)
    in_head = iota(shape, 0) // rows == iota(shape, 1) // HEAD_DIM
    wide = jnp.where(in_head, query, 0.0)
    positions = valid.shape[1]
    self_score = jnp.sum(wide * key, axis=1, keepdims=True) * scale
    scores = nt_dot(wide.astype(BF16), pool[0].reshape(positions, cols)) * scale
    scores = jnp.where(valid[...] > 0.5, scores, -jnp.inf)
    top = jnp.maximum(jnp.max(scores, axis=1, keepdims=True), self_score)
    weights = jnp.exp(scores - top)
    self_weight = jnp.exp(self_score - top)
    total = jnp.sum(weights, axis=1, keepdims=True) + self_weight
    numer = onto_mxu(weights.astype(BF16), pool[1].reshape(positions, cols))
    numer = numer + self_weight.astype(BF16).astype(F32) * value
    numer = jnp.where(in_head, numer / total, 0.0)
    attn = sum(numer[i * rows : (i + 1) * rows] for i in range(heads))
    attn = jnp.concatenate([attn, jnp.zeros_like(attn)], axis=0).astype(BF16)
    projected = onto_mxu(attn[:, :deep], upper[...])
    copy.wait()
    projected = (projected + onto_mxu(attn[:, deep:], lower[...]))[:rows]
    extra = resid + row(vectors, 0, cols)
    for t in range(TP):
        mine = jnp.where(place[1:2, 0:1] == t, extra, 0.0)
        whole = projected[:, t * cols : (t + 1) * cols] + mine
        partial[:, t * cols : (t + 1) * cols] = whole
        rounded[:, t * cols : (t + 1) * cols] = whole.astype(BF16)


def norm_kernel(place, own, sibling, far, far_sibling, vectors, blocks, stream_own):
    others = sibling[...].astype(F32) + far[...].astype(F32) + far_sibling[...].astype(F32)
    stream = (own[...] + others).astype(BF16).astype(F32)
    width = stream.shape[1]
    cols = width // TP
    mean = jnp.sum(stream, axis=1, keepdims=True) / width
    var = jnp.sum((stream - mean) ** 2, axis=1, keepdims=True) / width
    mine = stream[:, :cols]
    for t in range(1, TP):
        mine = jnp.where(place[1:2, 0:1] == t, stream[:, t * cols : (t + 1) * cols], mine)
    stream_own[...] = mine.astype(BF16)
    gain, bias = row(vectors, 1, cols), row(vectors, 2, cols)
    block = ((mine - mean) * lax.rsqrt(var + NORM_EPS) * gain + bias).astype(BF16)
    for d in range(REQ):
        blocks[d] = block


def up_kernel(rows_in, arrange, weight, out):
    came = rows_in[...].reshape(-1, rows_in.shape[2])
    ordered = onto_mxu(arrange[...], came).astype(BF16)
    out[...] = nt_dot(ordered, weight[...]).astype(BF16)


def down_kernel(near, far, vectors, weight, arrange_own, stream_own, out):
    hidden = near[...].astype(F32) + far[...].astype(F32)
    hidden = hidden + vectors[vectors.shape[0] - hidden.shape[1] :][None, :]
    activated = (0.5 * hidden * (1.0 + lax.erf(hidden * math.sqrt(0.5)))).astype(BF16)
    feed = onto_mxu(activated, weight[...]) + onto_mxu(arrange_own[...], stream_own[...])
    rows = out.shape[1]
    for d in range(REQ):
        out[LAST_ORDER.index(d)] = feed[d * rows : (d + 1) * rows].astype(BF16)


def finish_kernel(pieces, vectors, out):
    cols = out.shape[1]
    out[...] = (jnp.sum(pieces[...].astype(F32), axis=0) + row(vectors, 3, cols)).astype(BF16)


def call(kernel, shapes, specs, args, scratch=(), room=16, **fixed):
    moved = sum(a.size * a.dtype.itemsize for a in args)
    return pl.pallas_call(
        functools.partial(kernel, **fixed) if fixed else kernel,
        out_shape=shapes,
        in_specs=specs,
        out_specs=[VMEM] * len(shapes),
        scratch_shapes=scratch,
        compiler_params=pltpu.CompilerParams(vmem_limit_bytes=int(room * 2**20)),
        cost_estimate=pl.CostEstimate(flops=0, bytes_accessed=moved, transcendentals=0),
    )(*args)


def trade(blocks, group):
    return lax.all_to_all(blocks, "req", 0, 0, tiled=True, axis_index_groups=[group])


def on_pairs(
    query,
    key_new,
    value_new,
    resid,
    lengths,
    owner,
    page_table,
    kv_pool,
    out_weight,
    out_bias,
    norm_gain,
    norm_bias,
    up_weight_t,
    up_bias,
    down_weight,
    down_bias,
    order,
):
    rows, cols = query.shape
    width = cols * TP
    pool_pages, page_len = kv_pool.shape[1], kv_pool.shape[2]
    positions = pool_pages * page_len
    heads = cols // HEAD_DIM
    count = owner.shape[0]
    hidden = up_bias.shape[0]

    def arr(shape, dtype=BF16):
        return jax.ShapeDtypeStruct(shape, dtype)

    position = jnp.stack([lax.axis_index("req"), lax.axis_index("tp")]).astype(I32)
    place = jnp.broadcast_to(position[:, None], (2, HEAD_DIM))

    (packed,) = call(
        pack_kernel,
        [arr((REQ, 8, cols // 2))],
        [HBM] * 5,
        [owner[None, :], query, key_new, value_new, resid],
        [pltpu.VMEM((1, count), I32)]
        + [pltpu.VMEM((rows, cols), BF16)] * 4
        + [pltpu.SemaphoreType.DMA((5,))],
        room=ALL_ROOM,
    )
    arrived = trade(packed, FIRST_ORDER)
    numbers = pile(
        [owner[None, :], order[None, :], lengths[None, :], jnp.zeros((5, count), I32), page_table.T]
    )
    vectors = pile([x.astype(F32) for x in (out_bias, norm_gain, norm_bias, down_bias, up_bias)])
    pick, valid, arrange, arrange_own = call(
        index_kernel,
        [
            arr((3 * heads * rows + 2 * rows, 2 * count)),
            arr((heads * rows, positions), F32),
            arr((count, count)),
            arr((count, rows)),
        ],
        [VMEM, VMEM],
        [place, numbers],
        page_len=page_len,
        heads=heads,
    )

    here = position[0] >= 0
    pool = jnp.where(here, kv_pool, jnp.zeros_like(kv_pool))
    upper = out_weight[: 3 * cols // 4]
    upper = jnp.where(here, upper, jnp.zeros_like(upper))

    partial, rounded = call(
        attention_kernel,
        [arr((rows, width), F32), arr((rows, width))],
        [VMEM] * 7 + [HBM],
        [place, arrived, pick, valid, vectors, pool, upper, out_weight],
        [pltpu.VMEM((cols - upper.shape[0], width), BF16), pltpu.SemaphoreType.DMA],
        room=ATTENTION_ROOM,
        rows=rows,
    )
    blocks, stream_own = call(
        norm_kernel,
        [arr((REQ, rows, cols)), arr((rows, cols))],
        [VMEM] * 6,
        [place, partial] + [swap(rounded, "tp", step) for step in (1, 2, 3)] + [vectors],
    )

    (part,) = call(
        up_kernel,
        [arr((count, hidden))],
        [VMEM] * 3,
        [trade(blocks, MIDDLE_ORDER), arrange, up_weight_t],
    )
    part = (part.astype(F32) + swap(part, "tp", 1).astype(F32)).astype(BF16)
    (feed,) = call(
        down_kernel,
        [arr((REQ, rows, cols))],
        [VMEM] * 6,
        [part, swap(part, "tp", 3), vectors, down_weight, arrange_own, stream_own],
    )
    (out,) = call(finish_kernel, [arr((rows, cols))], [VMEM] * 2, [trade(feed, LAST_ORDER), vectors])
    return out


def swap(x, axis, step):
    n = lax.axis_size(axis)
    return lax.ppermute(x, axis, [(i, i ^ step) for i in range(n)])


def origins(axis):
    n, me = lax.axis_size(axis), lax.axis_index(axis)
    if n > PAIRWISE:
        return jnp.arange(n, dtype=jnp.int32)
    offsets = [0]
    step = n // 2
    while step:
        offsets = offsets + [o ^ step for o in offsets]
        step //= 2
    return jnp.array(offsets, dtype=jnp.int32) ^ me


def gather_rows(x, axis):
    n = lax.axis_size(axis)
    if n > PAIRWISE:
        return lax.all_gather(x, axis, axis=0, tiled=True)
    step = n // 2
    while step:
        x = jnp.concatenate([x, swap(x, axis, step)], axis=0)
        step //= 2
    return x


def fold_rows(x, axis):
    n = lax.axis_size(axis)
    if n > PAIRWISE:
        return lax.psum_scatter(x, axis, scatter_dimension=0, tiled=True)
    step = 1
    while step < n:
        half = x.shape[0] // 2
        x = x[:half] + swap(x[half:], axis, step)
        step *= 2
    return x


def sum_pairs(x, axis):
    n = lax.axis_size(axis)
    step = 1
    while step < n:
        x = (x.astype(jnp.float32) + swap(x, axis, step).astype(jnp.float32)).astype(x.dtype)
        step *= 2
    return x


def on_any_mesh(
    query,
    key_new,
    value_new,
    resid,
    lengths,
    owner,
    page_table,
    kv_pool,
    out_weight,
    out_bias,
    norm_gain,
    norm_bias,
    up_weight_t,
    up_bias,
    down_weight,
    down_bias,
    order,
):
    f32, bf16, i32 = jnp.float32, jnp.bfloat16, jnp.int32
    n_req = lax.axis_size("req")
    n_tp = lax.axis_size("tp")
    me = lax.axis_index("req")
    me_tp = lax.axis_index("tp")
    rows, cols = query.shape
    width = cols * n_tp
    heads = cols // HEAD_DIM
    pool_pages, page_len = kv_pool.shape[1], kv_pool.shape[2]
    positions = pool_pages * page_len
    scale = 1.0 / math.sqrt(HEAD_DIM)

    origin = origins("req")
    packed = jnp.concatenate([query, key_new, value_new, resid], axis=1)
    arrived = gather_rows(packed, "req")

    same = owner[:, None] == owner[None, :]
    ids = jnp.arange(owner.shape[0], dtype=i32)
    rank = jnp.sum((same & (ids[None, :] < ids[:, None])).astype(i32), axis=1)
    slots = jnp.arange(rows, dtype=i32)
    mine = (owner == me)[None, :] & (rank[None, :] == slots[:, None])
    mine_i = mine.astype(i32)
    own_len = jnp.sum(mine_i * lengths[None, :], axis=1)
    own_table = jnp.sum(mine_i[:, :, None] * page_table[None], axis=1)
    origin_ids = (origin[:, None] * rows + slots[None, :]).reshape(-1)
    own_id = jnp.sum(mine_i * ids[None, :], axis=1)
    take_hot = (own_id[:, None] == origin_ids[None, :]).astype(bf16)
    own = jnp.dot(take_hot, arrived, preferred_element_type=f32).astype(bf16)
    query_own, key_own, value_own, resid_own = (own[:, i * cols : (i + 1) * cols] for i in range(4))

    pos = jnp.arange(positions, dtype=i32)
    page, within = pos // page_len, pos % page_len
    entry = jnp.arange(page_table.shape[1], dtype=i32)
    start = entry * page_len
    hit = (own_table[:, :, None] == page[None, None, :]) & (
        start[None, :, None] + within[None, None, :] < own_len[:, None, None]
    )
    valid = jnp.any(hit, axis=1)

    keys = kv_pool[0].reshape(positions, cols)
    values = kv_pool[1].reshape(positions, cols)
    head_of = jnp.arange(cols, dtype=i32) // HEAD_DIM
    head_mask = head_of[None, :] == jnp.arange(heads, dtype=i32)[:, None]
    spread_q = jnp.where(head_mask[:, None, :], query_own[None], 0).reshape(heads * rows, cols)
    scores = (
        lax.dot_general(spread_q, keys, (((1,), (1,)), ((), ())), preferred_element_type=f32) * scale
    ).reshape(heads, rows, positions)
    scores = jnp.where(valid[None], scores, -jnp.inf)
    self_score = (
        jnp.sum(
            (query_own.astype(f32) * key_own.astype(f32)).reshape(rows, heads, HEAD_DIM), axis=-1
        ).T
        * scale
    )
    top = jnp.maximum(jnp.max(scores, axis=2), self_score)
    weights = jnp.exp(scores - top[:, :, None])
    self_weight = jnp.exp(self_score - top)
    total = jnp.sum(weights, axis=2) + self_weight
    numer = jnp.dot(
        weights.astype(bf16).reshape(heads * rows, positions), values, preferred_element_type=f32
    ).reshape(heads, rows, cols)
    numer = numer + self_weight.astype(bf16).astype(f32)[:, :, None] * value_own.astype(f32)[None]
    attn = jnp.sum(
        jnp.where(head_mask[:, None, :], numer / total[:, :, None], 0.0), axis=0
    ).astype(bf16)

    extra = resid_own.astype(f32) + out_bias.astype(f32)[None, :]
    partial = jnp.dot(attn, out_weight, preferred_element_type=f32)
    place = (jnp.arange(n_tp, dtype=i32) == me_tp)[None, :, None]
    partial = (
        partial.reshape(rows, n_tp, cols) + jnp.where(place, extra[:, None, :], 0.0)
    ).reshape(rows, width)
    stream = sum_pairs(partial, "tp").astype(bf16)
    stream_f = stream.astype(f32)
    mean = jnp.mean(stream_f, axis=1, keepdims=True)
    var = jnp.mean((stream_f - mean) ** 2, axis=1, keepdims=True)
    inverse = lax.rsqrt(var + NORM_EPS)
    stream_own = lax.dynamic_slice_in_dim(stream, me_tp * cols, cols, axis=1)
    normed = (
        (stream_own.astype(f32) - mean) * inverse * norm_gain.astype(f32)[None, :]
        + norm_bias.astype(f32)[None, :]
    ).astype(bf16)

    normed_all = gather_rows(normed, "req")
    slot_of = owner * rows + rank
    wanted = slot_of[order[origin_ids]]
    place_hot = (wanted[:, None] == origin_ids[None, :]).astype(bf16)
    mine_hot = (wanted[:, None] == (me * rows + slots)[None, :]).astype(bf16)
    normed_out = jnp.dot(place_hot, normed_all, preferred_element_type=f32).astype(bf16)
    hidden = lax.dot_general(
        normed_out, up_weight_t, (((1,), (1,)), ((), ())), preferred_element_type=f32
    ).astype(bf16)
    summed = sum_pairs(hidden, "tp").astype(f32)
    activated = jax.nn.gelu(summed + up_bias.astype(f32)[None, :], approximate=False).astype(bf16)
    feed = jnp.dot(activated, down_weight, preferred_element_type=f32)
    feed = feed + jnp.dot(mine_hot, stream_own, preferred_element_type=f32)
    mixed = fold_rows(feed, "req")
    return (mixed + down_bias.astype(f32)[None, :]).astype(bf16)


def solution(mesh):
    pairs = mesh.shape["req"] == REQ and mesh.shape["tp"] == TP
    per_device = on_pairs if pairs else on_any_mesh
    in_specs = (
        P("req", "tp"),
        P("req", "tp"),
        P("req", "tp"),
        P("req", "tp"),
        P(),
        P(),
        P(),
        P(None, "req", None, "tp"),
        P("tp", None),
        P("tp"),
        P("tp"),
        P("tp"),
        P("req", "tp"),
        P("req"),
        P("req", "tp"),
        P("tp"),
        P(),
    )
    out_specs = P("req", "tp")
    return jax.shard_map(
        per_device, mesh=mesh, in_specs=in_specs, out_specs=out_specs, check_vma=False
    )
```

```python
import functools
import math

import jax
import jax.numpy as jnp
from jax import lax
from jax.experimental import pallas as pl
from jax.experimental.pallas import tpu as pltpu
from jax.sharding import PartitionSpec as P

HEAD_DIM = 128
NORM_EPS = 1e-05
PAIRWISE = 16
REQ, TP = 8, 4
ATTENTION_ROOM = 50.6
ALL_ROOM = 58
F32, BF16, I32 = jnp.float32, jnp.bfloat16, jnp.int32
VMEM = pl.BlockSpec(memory_space=pltpu.VMEM)
HBM = pl.BlockSpec(memory_space=pltpu.HBM)

ORDER = [3, 4, 1, 6, 2, 5, 0, 7]


def index_at(place):
    found = jnp.zeros_like(place)
    for i, index in enumerate(ORDER):
        found = jnp.where(place == i, index, found)
    return found


def iota(shape, dim):
    return lax.broadcasted_iota(I32, shape, dim)


def onto_mxu(a, b):
    return jnp.dot(a, b, preferred_element_type=F32)


def nt_dot(a, b):
    return lax.dot_general(a, b, (((1,), (1,)), ((), ())), preferred_element_type=F32)


def hot(condition):
    return jnp.where(condition, 1.0, 0.0).astype(BF16)


def pile(parts):
    height = sum(p.shape[0] for p in parts)
    at, piled = 0, 0
    for p in parts:
        around = ((at, height - at - p.shape[0]),) + ((0, 0),) * (p.ndim - 1)
        piled += jnp.pad(p, around)
        at += p.shape[0]
    return piled


def row(vectors, i, cols):
    return vectors[i * cols : (i + 1) * cols][None, :]


def pack_kernel(owner_in, query, key, value, resid, out, owner, q, k, v, r, sems):
    parts = ((owner_in, owner), (query, q), (key, k), (value, v), (resid, r))
    copies = [pltpu.make_async_copy(x, y, sems.at[i]) for i, (x, y) in enumerate(parts)]
    for copy in copies:
        copy.start()
    rows, cols = q.shape
    fields = 4
    count = REQ * rows
    shape = (REQ * fields, fields * rows)
    down, across = iota(shape, 0), iota(shape, 1)
    here = (count, fields * rows)
    of_mine = hot(iota(here, 0) == lax.axis_index("req") * rows + iota(here, 1) % rows)
    copies[0].wait()
    owner_of = onto_mxu(owner[...].astype(F32).astype(BF16), of_mine).astype(I32)
    pick = hot((down % fields == across // rows) & (owner_of == down // fields))
    for copy in copies[1:]:
        copy.wait()
    all_rows = jnp.concatenate([q[...], k[...], v[...], r[...]], axis=0)
    blocks = onto_mxu(pick, all_rows).astype(BF16)
    for d in range(REQ):
        block = blocks[d * fields : (d + 1) * fields]
        at = ORDER.index(d)
        out[at, :fields, :] = block[:, : cols // 2]
        out[at, fields:, :] = block[:, cols // 2 :]


def index_kernel(place, numbers, pick, valid, arrange, arrange_own, *, page_len, heads):
    owner, order, lengths = (numbers[i : i + 1, :] for i in range(3))
    table = numbers[8:, :]
    me = place[0:1, 0:1]
    count = owner.shape[1]
    rows = count // REQ
    square = (count, count)
    down, across = iota(square, 0), iota(square, 1)
    owner_row = owner
    same_place = down == across
    owner_col = jnp.sum(jnp.where(same_place, owner_row, 0), axis=1, keepdims=True)
    order_col = jnp.sum(jnp.where(same_place, order, 0), axis=1, keepdims=True)
    same_owner = owner_col == owner_row
    rank_row = jnp.sum(jnp.where(same_owner & (down < across), 1, 0), axis=0, keepdims=True)
    rank_col = jnp.sum(jnp.where(same_owner & (across < down), 1, 0), axis=1, keepdims=True)

    shape = pick.shape
    down_p, across_p = iota(shape, 0), iota(shape, 1)
    down_i = iota((shape[0], count), 0)
    mine = hot((owner_row == me) & (rank_row == down_i % rows))
    source = index_at(iota((count, shape[1]), 1) // (2 * rows))
    came = hot(iota((count, shape[1]), 0) // rows == source)
    from_there = onto_mxu(mine, came)
    field = jnp.minimum(down_p // (heads * rows), 3)
    pick[...] = hot((from_there > 0.5) & (field == across_p % rows))

    shape = valid.shape
    slot = iota((shape[0], count), 0) % rows
    mine_v = hot((owner_row == me) & (rank_row == slot))
    table_v = nt_dot(mine_v, table.astype(F32).astype(BF16)).astype(I32)
    length_v = jnp.sum(jnp.where(mine_v > 0.5, lengths, 0), axis=1, keepdims=True)
    position = iota(shape, 1)
    page, within = position // page_len, position % page_len
    seen = jnp.zeros(shape, F32)
    for j in range(table.shape[0]):
        inside = (table_v[:, j : j + 1] == page) & (within + j * page_len < length_v)
        seen = jnp.where(inside, 1.0, seen)
    valid[...] = seen

    ordered = hot(order_col == across)
    holds = hot((owner_col == index_at(across // rows)) & (rank_col == across % rows))
    arrange[...] = onto_mxu(ordered, holds).astype(BF16)
    here = hot((owner_col == me) & (rank_col == iota(arrange_own.shape, 1)))
    arrange_own[...] = onto_mxu(ordered, here).astype(BF16)


def attention_kernel(
    place, arrived, pick, valid, vectors, pool, upper, weight, partial, rounded, lower, sem, *, rows
):
    deep = upper.shape[0]
    copy = pltpu.make_async_copy(weight.at[pl.ds(deep, lower.shape[0])], lower, sem)
    copy.start()
    half = arrived.shape[2]
    cols = 2 * half
    heads = cols // HEAD_DIM
    scale = 1.0 / math.sqrt(HEAD_DIM)
    came = arrived[...].reshape(-1, half)
    which = (iota(pick.shape, 1) // rows) % 2
    chosen = pick[...].astype(F32)
    own = jnp.concatenate(
        [onto_mxu(jnp.where(which == i, chosen, 0.0).astype(BF16), came) for i in range(2)], axis=1
    )
    each = heads * rows
    query, key, value = (own[i * each : (i + 1) * each] for i in range(3))
    resid = own[3 * each : 3 * each + rows]
    shape = (each, cols)
    in_head = iota(shape, 0) // rows == iota(shape, 1) // HEAD_DIM
    wide = jnp.where(in_head, query, 0.0)
    positions = valid.shape[1]
    self_score = jnp.sum(wide * key, axis=1, keepdims=True) * scale
    scores = nt_dot(wide.astype(BF16), pool[0].reshape(positions, cols)) * scale
    scores = jnp.where(valid[...] > 0.5, scores, -jnp.inf)
    top = jnp.maximum(jnp.max(scores, axis=1, keepdims=True), self_score)
    weights = jnp.exp(scores - top)
    self_weight = jnp.exp(self_score - top)
    total = jnp.sum(weights, axis=1, keepdims=True) + self_weight
    numer = onto_mxu(weights.astype(BF16), pool[1].reshape(positions, cols))
    numer = numer + self_weight.astype(BF16).astype(F32) * value
    numer = jnp.where(in_head, numer / total, 0.0)
    attn = sum(numer[i * rows : (i + 1) * rows] for i in range(heads))
    attn = jnp.concatenate([attn, jnp.zeros_like(attn)], axis=0).astype(BF16)
    projected = onto_mxu(attn[:, :deep], upper[...])
    copy.wait()
    projected = (projected + onto_mxu(attn[:, deep:], lower[...]))[:rows]
    extra = resid + row(vectors, 0, cols)
    for t in range(TP):
        mine = jnp.where(place[1:2, 0:1] == t, extra, 0.0)
        whole = projected[:, t * cols : (t + 1) * cols] + mine
        partial[:, t * cols : (t + 1) * cols] = whole
        rounded[:, t * cols : (t + 1) * cols] = whole.astype(BF16)


def norm_kernel(place, own, sibling, far, far_sibling, vectors, blocks, stream_own):
    others = sibling[...].astype(F32) + far[...].astype(F32) + far_sibling[...].astype(F32)
    stream = (own[...] + others).astype(BF16).astype(F32)
    width = stream.shape[1]
    cols = width // TP
    mean = jnp.sum(stream, axis=1, keepdims=True) / width
    var = jnp.sum((stream - mean) ** 2, axis=1, keepdims=True) / width
    mine = stream[:, :cols]
    for t in range(1, TP):
        mine = jnp.where(place[1:2, 0:1] == t, stream[:, t * cols : (t + 1) * cols], mine)
    stream_own[...] = mine.astype(BF16)
    gain, bias = row(vectors, 1, cols), row(vectors, 2, cols)
    block = ((mine - mean) * lax.rsqrt(var + NORM_EPS) * gain + bias).astype(BF16)
    for d in range(REQ):
        blocks[d] = block


def up_kernel(rows_in, arrange, weight, out):
    came = rows_in[...].reshape(-1, rows_in.shape[2])
    ordered = onto_mxu(arrange[...], came).astype(BF16)
    out[...] = nt_dot(ordered, weight[...]).astype(BF16)


def down_kernel(near, far, vectors, weight, arrange_own, stream_own, out):
    hidden = near[...].astype(F32) + far[...].astype(F32)
    hidden = hidden + vectors[vectors.shape[0] - hidden.shape[1] :][None, :]
    activated = (0.5 * hidden * (1.0 + lax.erf(hidden * math.sqrt(0.5)))).astype(BF16)
    feed = onto_mxu(activated, weight[...]) + onto_mxu(arrange_own[...], stream_own[...])
    rows = out.shape[1]
    for d in range(REQ):
        out[ORDER.index(d)] = feed[d * rows : (d + 1) * rows].astype(BF16)


def finish_kernel(pieces, vectors, out):
    cols = out.shape[1]
    out[...] = (jnp.sum(pieces[...].astype(F32), axis=0) + row(vectors, 3, cols)).astype(BF16)


def call(kernel, shapes, specs, args, scratch=(), room=16, **fixed):
    moved = sum(a.size * a.dtype.itemsize for a in args)
    return pl.pallas_call(
        functools.partial(kernel, **fixed) if fixed else kernel,
        out_shape=shapes,
        in_specs=specs,
        out_specs=[VMEM] * len(shapes),
        scratch_shapes=scratch,
        compiler_params=pltpu.CompilerParams(vmem_limit_bytes=int(room * 2**20)),
        cost_estimate=pl.CostEstimate(flops=0, bytes_accessed=moved, transcendentals=0),
    )(*args)


def trade(blocks):
    return lax.all_to_all(blocks, "req", 0, 0, tiled=True, axis_index_groups=[ORDER])


def on_pairs(
    query,
    key_new,
    value_new,
    resid,
    lengths,
    owner,
    page_table,
    kv_pool,
    out_weight,
    out_bias,
    norm_gain,
    norm_bias,
    up_weight_t,
    up_bias,
    down_weight,
    down_bias,
    order,
):
    rows, cols = query.shape
    width = cols * TP
    pool_pages, page_len = kv_pool.shape[1], kv_pool.shape[2]
    positions = pool_pages * page_len
    heads = cols // HEAD_DIM
    count = owner.shape[0]
    hidden = up_bias.shape[0]

    def arr(shape, dtype=BF16):
        return jax.ShapeDtypeStruct(shape, dtype)

    position = jnp.stack([lax.axis_index("req"), lax.axis_index("tp")]).astype(I32)
    place = jnp.broadcast_to(position[:, None], (2, HEAD_DIM))

    (packed,) = call(
        pack_kernel,
        [arr((REQ, 8, cols // 2))],
        [HBM] * 5,
        [owner[None, :], query, key_new, value_new, resid],
        [pltpu.VMEM((1, count), I32)]
        + [pltpu.VMEM((rows, cols), BF16)] * 4
        + [pltpu.SemaphoreType.DMA((5,))],
        room=ALL_ROOM,
    )
    arrived = trade(packed)
    numbers = pile(
        [owner[None, :], order[None, :], lengths[None, :], jnp.zeros((5, count), I32), page_table.T]
    )
    vectors = pile([x.astype(F32) for x in (out_bias, norm_gain, norm_bias, down_bias, up_bias)])
    pick, valid, arrange, arrange_own = call(
        index_kernel,
        [
            arr((3 * heads * rows + 2 * rows, 2 * count)),
            arr((heads * rows, positions), F32),
            arr((count, count)),
            arr((count, rows)),
        ],
        [VMEM, VMEM],
        [place, numbers],
        page_len=page_len,
        heads=heads,
    )

    here = position[0] >= 0
    pool = jnp.where(here, kv_pool, jnp.zeros_like(kv_pool))
    upper = out_weight[: 3 * cols // 4]
    upper = jnp.where(here, upper, jnp.zeros_like(upper))

    partial, rounded = call(
        attention_kernel,
        [arr((rows, width), F32), arr((rows, width))],
        [VMEM] * 7 + [HBM],
        [place, arrived, pick, valid, vectors, pool, upper, out_weight],
        [pltpu.VMEM((cols - upper.shape[0], width), BF16), pltpu.SemaphoreType.DMA],
        room=ATTENTION_ROOM,
        rows=rows,
    )
    blocks, stream_own = call(
        norm_kernel,
        [arr((REQ, rows, cols)), arr((rows, cols))],
        [VMEM] * 6,
        [place, partial] + [swap(rounded, "tp", step) for step in (1, 2, 3)] + [vectors],
    )

    (part,) = call(
        up_kernel,
        [arr((count, hidden))],
        [VMEM] * 3,
        [trade(blocks), arrange, up_weight_t],
    )
    part = (part.astype(F32) + swap(part, "tp", 1).astype(F32)).astype(BF16)
    (feed,) = call(
        down_kernel,
        [arr((REQ, rows, cols))],
        [VMEM] * 6,
        [part, swap(part, "tp", 3), vectors, down_weight, arrange_own, stream_own],
    )
    (out,) = call(finish_kernel, [arr((rows, cols))], [VMEM] * 2, [trade(feed), vectors])
    return out


def swap(x, axis, step):
    n = lax.axis_size(axis)
    return lax.ppermute(x, axis, [(i, i ^ step) for i in range(n)])


def origins(axis):
    n, me = lax.axis_size(axis), lax.axis_index(axis)
    if n > PAIRWISE:
        return jnp.arange(n, dtype=jnp.int32)
    offsets = [0]
    step = n // 2
    while step:
        offsets = offsets + [o ^ step for o in offsets]
        step //= 2
    return jnp.array(offsets, dtype=jnp.int32) ^ me


def gather_rows(x, axis):
    n = lax.axis_size(axis)
    if n > PAIRWISE:
        return lax.all_gather(x, axis, axis=0, tiled=True)
    step = n // 2
    while step:
        x = jnp.concatenate([x, swap(x, axis, step)], axis=0)
        step //= 2
    return x


def fold_rows(x, axis):
    n = lax.axis_size(axis)
    if n > PAIRWISE:
        return lax.psum_scatter(x, axis, scatter_dimension=0, tiled=True)
    step = 1
    while step < n:
        half = x.shape[0] // 2
        x = x[:half] + swap(x[half:], axis, step)
        step *= 2
    return x


def sum_pairs(x, axis):
    n = lax.axis_size(axis)
    step = 1
    while step < n:
        x = (x.astype(jnp.float32) + swap(x, axis, step).astype(jnp.float32)).astype(x.dtype)
        step *= 2
    return x


def on_any_mesh(
    query,
    key_new,
    value_new,
    resid,
    lengths,
    owner,
    page_table,
    kv_pool,
    out_weight,
    out_bias,
    norm_gain,
    norm_bias,
    up_weight_t,
    up_bias,
    down_weight,
    down_bias,
    order,
):
    f32, bf16, i32 = jnp.float32, jnp.bfloat16, jnp.int32
    n_req = lax.axis_size("req")
    n_tp = lax.axis_size("tp")
    me = lax.axis_index("req")
    me_tp = lax.axis_index("tp")
    rows, cols = query.shape
    width = cols * n_tp
    heads = cols // HEAD_DIM
    pool_pages, page_len = kv_pool.shape[1], kv_pool.shape[2]
    positions = pool_pages * page_len
    scale = 1.0 / math.sqrt(HEAD_DIM)

    origin = origins("req")
    packed = jnp.concatenate([query, key_new, value_new, resid], axis=1)
    arrived = gather_rows(packed, "req")

    same = owner[:, None] == owner[None, :]
    ids = jnp.arange(owner.shape[0], dtype=i32)
    rank = jnp.sum((same & (ids[None, :] < ids[:, None])).astype(i32), axis=1)
    slots = jnp.arange(rows, dtype=i32)
    mine = (owner == me)[None, :] & (rank[None, :] == slots[:, None])
    mine_i = mine.astype(i32)
    own_len = jnp.sum(mine_i * lengths[None, :], axis=1)
    own_table = jnp.sum(mine_i[:, :, None] * page_table[None], axis=1)
    origin_ids = (origin[:, None] * rows + slots[None, :]).reshape(-1)
    own_id = jnp.sum(mine_i * ids[None, :], axis=1)
    take_hot = (own_id[:, None] == origin_ids[None, :]).astype(bf16)
    own = jnp.dot(take_hot, arrived, preferred_element_type=f32).astype(bf16)
    query_own, key_own, value_own, resid_own = (own[:, i * cols : (i + 1) * cols] for i in range(4))

    pos = jnp.arange(positions, dtype=i32)
    page, within = pos // page_len, pos % page_len
    entry = jnp.arange(page_table.shape[1], dtype=i32)
    start = entry * page_len
    hit = (own_table[:, :, None] == page[None, None, :]) & (
        start[None, :, None] + within[None, None, :] < own_len[:, None, None]
    )
    valid = jnp.any(hit, axis=1)

    keys = kv_pool[0].reshape(positions, cols)
    values = kv_pool[1].reshape(positions, cols)
    head_of = jnp.arange(cols, dtype=i32) // HEAD_DIM
    head_mask = head_of[None, :] == jnp.arange(heads, dtype=i32)[:, None]
    spread_q = jnp.where(head_mask[:, None, :], query_own[None], 0).reshape(heads * rows, cols)
    scores = (
        lax.dot_general(spread_q, keys, (((1,), (1,)), ((), ())), preferred_element_type=f32) * scale
    ).reshape(heads, rows, positions)
    scores = jnp.where(valid[None], scores, -jnp.inf)
    self_score = (
        jnp.sum(
            (query_own.astype(f32) * key_own.astype(f32)).reshape(rows, heads, HEAD_DIM), axis=-1
        ).T
        * scale
    )
    top = jnp.maximum(jnp.max(scores, axis=2), self_score)
    weights = jnp.exp(scores - top[:, :, None])
    self_weight = jnp.exp(self_score - top)
    total = jnp.sum(weights, axis=2) + self_weight
    numer = jnp.dot(
        weights.astype(bf16).reshape(heads * rows, positions), values, preferred_element_type=f32
    ).reshape(heads, rows, cols)
    numer = numer + self_weight.astype(bf16).astype(f32)[:, :, None] * value_own.astype(f32)[None]
    attn = jnp.sum(
        jnp.where(head_mask[:, None, :], numer / total[:, :, None], 0.0), axis=0
    ).astype(bf16)

    extra = resid_own.astype(f32) + out_bias.astype(f32)[None, :]
    partial = jnp.dot(attn, out_weight, preferred_element_type=f32)
    place = (jnp.arange(n_tp, dtype=i32) == me_tp)[None, :, None]
    partial = (
        partial.reshape(rows, n_tp, cols) + jnp.where(place, extra[:, None, :], 0.0)
    ).reshape(rows, width)
    stream = sum_pairs(partial, "tp").astype(bf16)
    stream_f = stream.astype(f32)
    mean = jnp.mean(stream_f, axis=1, keepdims=True)
    var = jnp.mean((stream_f - mean) ** 2, axis=1, keepdims=True)
    inverse = lax.rsqrt(var + NORM_EPS)
    stream_own = lax.dynamic_slice_in_dim(stream, me_tp * cols, cols, axis=1)
    normed = (
        (stream_own.astype(f32) - mean) * inverse * norm_gain.astype(f32)[None, :]
        + norm_bias.astype(f32)[None, :]
    ).astype(bf16)

    normed_all = gather_rows(normed, "req")
    slot_of = owner * rows + rank
    wanted = slot_of[order[origin_ids]]
    place_hot = (wanted[:, None] == origin_ids[None, :]).astype(bf16)
    mine_hot = (wanted[:, None] == (me * rows + slots)[None, :]).astype(bf16)
    normed_out = jnp.dot(place_hot, normed_all, preferred_element_type=f32).astype(bf16)
    hidden = lax.dot_general(
        normed_out, up_weight_t, (((1,), (1,)), ((), ())), preferred_element_type=f32
    ).astype(bf16)
    summed = sum_pairs(hidden, "tp").astype(f32)
    activated = jax.nn.gelu(summed + up_bias.astype(f32)[None, :], approximate=False).astype(bf16)
    feed = jnp.dot(activated, down_weight, preferred_element_type=f32)
    feed = feed + jnp.dot(mine_hot, stream_own, preferred_element_type=f32)
    mixed = fold_rows(feed, "req")
    return (mixed + down_bias.astype(f32)[None, :]).astype(bf16)


def solution(mesh):
    pairs = mesh.shape["req"] == REQ and mesh.shape["tp"] == TP
    per_device = on_pairs if pairs else on_any_mesh
    in_specs = (
        P("req", "tp"),
        P("req", "tp"),
        P("req", "tp"),
        P("req", "tp"),
        P(),
        P(),
        P(),
        P(None, "req", None, "tp"),
        P("tp", None),
        P("tp"),
        P("tp"),
        P("tp"),
        P("req", "tp"),
        P("req"),
        P("req", "tp"),
        P("tp"),
        P(),
    )
    out_specs = P("req", "tp")
    return jax.shard_map(
        per_device, mesh=mesh, in_specs=in_specs, out_specs=out_specs, check_vma=False
    )
```

```python
import functools
import math

import jax
import jax.numpy as jnp
from jax import lax
from jax.experimental import pallas as pl
from jax.experimental.pallas import tpu as pltpu
from jax.sharding import PartitionSpec as P

HEAD_DIM = 128
NORM_EPS = 1e-05
PAIRWISE = 16
REQ, TP = 8, 4
ATTENTION_ROOM = 50.6
ALL_ROOM = 58
F32, BF16, I32 = jnp.float32, jnp.bfloat16, jnp.int32
VMEM = pl.BlockSpec(memory_space=pltpu.VMEM)
HBM = pl.BlockSpec(memory_space=pltpu.HBM)

FIRST_ORDER = [3, 5, 2, 4, 1, 7, 0, 6]
MIDDLE_ORDER = [3, 4, 1, 6, 2, 5, 0, 7]
LAST_ORDER = [7, 6, 5, 4, 3, 2, 1, 0]


def pick_from(order, place):
    found = jnp.zeros_like(place)
    for i, index in enumerate(order):
        found = jnp.where(place == i, index, found)
    return found


def iota(shape, dim):
    return lax.broadcasted_iota(I32, shape, dim)


def onto_mxu(a, b):
    return jnp.dot(a, b, preferred_element_type=F32)


def nt_dot(a, b):
    return lax.dot_general(a, b, (((1,), (1,)), ((), ())), preferred_element_type=F32)


def hot(condition):
    return jnp.where(condition, 1.0, 0.0).astype(BF16)


def pile(parts):
    height = sum(p.shape[0] for p in parts)
    at, piled = 0, 0
    for p in parts:
        around = ((at, height - at - p.shape[0]),) + ((0, 0),) * (p.ndim - 1)
        piled += jnp.pad(p, around)
        at += p.shape[0]
    return piled


def row(vectors, i, cols):
    return vectors[i * cols : (i + 1) * cols][None, :]


def pack_kernel(owner_in, query, key, value, resid, out, owner, q, k, v, r, sems):
    parts = ((owner_in, owner), (query, q), (key, k), (value, v), (resid, r))
    copies = [pltpu.make_async_copy(x, y, sems.at[i]) for i, (x, y) in enumerate(parts)]
    for copy in copies:
        copy.start()
    rows, cols = q.shape
    fields = 4
    count = REQ * rows
    shape = (REQ * fields, fields * rows)
    down, across = iota(shape, 0), iota(shape, 1)
    here = (count, fields * rows)
    of_mine = hot(iota(here, 0) == lax.axis_index("req") * rows + iota(here, 1) % rows)
    copies[0].wait()
    owner_of = onto_mxu(owner[...].astype(F32).astype(BF16), of_mine).astype(I32)
    pick = hot((down % fields == across // rows) & (owner_of == down // fields))
    for copy in copies[1:]:
        copy.wait()
    all_rows = jnp.concatenate([q[...], k[...], v[...], r[...]], axis=0)
    blocks = onto_mxu(pick, all_rows).astype(BF16)
    for d in range(REQ):
        block = blocks[d * fields : (d + 1) * fields]
        at = FIRST_ORDER.index(d)
        out[at, :fields, :] = block[:, : cols // 2]
        out[at, fields:, :] = block[:, cols // 2 :]


def index_kernel(place, numbers, pick, valid, arrange, arrange_own, *, page_len, heads):
    owner, order, lengths = (numbers[i : i + 1, :] for i in range(3))
    table = numbers[8:, :]
    me = place[0:1, 0:1]
    count = owner.shape[1]
    rows = count // REQ
    square = (count, count)
    down, across = iota(square, 0), iota(square, 1)
    owner_row = owner
    same_place = down == across
    owner_col = jnp.sum(jnp.where(same_place, owner_row, 0), axis=1, keepdims=True)
    order_col = jnp.sum(jnp.where(same_place, order, 0), axis=1, keepdims=True)
    same_owner = owner_col == owner_row
    rank_row = jnp.sum(jnp.where(same_owner & (down < across), 1, 0), axis=0, keepdims=True)
    rank_col = jnp.sum(jnp.where(same_owner & (across < down), 1, 0), axis=1, keepdims=True)

    shape = pick.shape
    down_p, across_p = iota(shape, 0), iota(shape, 1)
    down_i = iota((shape[0], count), 0)
    mine = hot((owner_row == me) & (rank_row == down_i % rows))
    source = pick_from(FIRST_ORDER, iota((count, shape[1]), 1) // (2 * rows))
    came = hot(iota((count, shape[1]), 0) // rows == source)
    from_there = onto_mxu(mine, came)
    field = jnp.minimum(down_p // (heads * rows), 3)
    pick[...] = hot((from_there > 0.5) & (field == across_p % rows))

    shape = valid.shape
    slot = iota((shape[0], count), 0) % rows
    mine_v = hot((owner_row == me) & (rank_row == slot))
    table_v = nt_dot(mine_v, table.astype(F32).astype(BF16)).astype(I32)
    length_v = jnp.sum(jnp.where(mine_v > 0.5, lengths, 0), axis=1, keepdims=True)
    position = iota(shape, 1)
    page, within = position // page_len, position % page_len
    seen = jnp.zeros(shape, F32)
    for j in range(table.shape[0]):
        inside = (table_v[:, j : j + 1] == page) & (within + j * page_len < length_v)
        seen = jnp.where(inside, 1.0, seen)
    valid[...] = seen

    ordered = hot(order_col == across)
    holds = hot((owner_col == pick_from(MIDDLE_ORDER, across // rows)) & (rank_col == across % rows))
    arrange[...] = onto_mxu(ordered, holds).astype(BF16)
    here = hot((owner_col == me) & (rank_col == iota(arrange_own.shape, 1)))
    arrange_own[...] = onto_mxu(ordered, here).astype(BF16)


def attention_kernel(
    place, arrived, pick, valid, vectors, pool, upper, weight, partial, rounded, lower, sem, *, rows
):
    deep = upper.shape[0]
    copy = pltpu.make_async_copy(weight.at[pl.ds(deep, lower.shape[0])], lower, sem)
    copy.start()
    half = arrived.shape[2]
    cols = 2 * half
    heads = cols // HEAD_DIM
    scale = 1.0 / math.sqrt(HEAD_DIM)
    came = arrived[...].reshape(-1, half)
    which = (iota(pick.shape, 1) // rows) % 2
    chosen = pick[...].astype(F32)
    own = jnp.concatenate(
        [onto_mxu(jnp.where(which == i, chosen, 0.0).astype(BF16), came) for i in range(2)], axis=1
    )
    each = heads * rows
    query, key, value = (own[i * each : (i + 1) * each] for i in range(3))
    resid = own[3 * each : 3 * each + rows]
    shape = (each, cols)
    in_head = iota(shape, 0) // rows == iota(shape, 1) // HEAD_DIM
    wide = jnp.where(in_head, query, 0.0)
    positions = valid.shape[1]
    self_score = jnp.sum(wide * key, axis=1, keepdims=True) * scale
    scores = nt_dot(wide.astype(BF16), pool[0].reshape(positions, cols)) * scale
    scores = jnp.where(valid[...] > 0.5, scores, -jnp.inf)
    top = jnp.maximum(jnp.max(scores, axis=1, keepdims=True), self_score)
    weights = jnp.exp(scores - top)
    self_weight = jnp.exp(self_score - top)
    total = jnp.sum(weights, axis=1, keepdims=True) + self_weight
    numer = onto_mxu(weights.astype(BF16), pool[1].reshape(positions, cols))
    numer = numer + self_weight.astype(BF16).astype(F32) * value
    numer = jnp.where(in_head, numer / total, 0.0)
    attn = sum(numer[i * rows : (i + 1) * rows] for i in range(heads))
    attn = jnp.concatenate([attn, jnp.zeros_like(attn)], axis=0).astype(BF16)
    projected = onto_mxu(attn[:, :deep], upper[...])
    copy.wait()
    projected = (projected + onto_mxu(attn[:, deep:], lower[...]))[:rows]
    extra = resid + row(vectors, 0, cols)
    for t in range(TP):
        mine = jnp.where(place[1:2, 0:1] == t, extra, 0.0)
        whole = projected[:, t * cols : (t + 1) * cols] + mine
        partial[:, t * cols : (t + 1) * cols] = whole
        rounded[:, t * cols : (t + 1) * cols] = whole.astype(BF16)


def norm_kernel(place, own, sibling, far, far_sibling, vectors, blocks, stream_own):
    others = sibling[...].astype(F32) + far[...].astype(F32) + far_sibling[...].astype(F32)
    stream = (own[...] + others).astype(BF16).astype(F32)
    width = stream.shape[1]
    cols = width // TP
    mean = jnp.sum(stream, axis=1, keepdims=True) / width
    var = jnp.sum((stream - mean) ** 2, axis=1, keepdims=True) / width
    mine = stream[:, :cols]
    for t in range(1, TP):
        mine = jnp.where(place[1:2, 0:1] == t, stream[:, t * cols : (t + 1) * cols], mine)
    stream_own[...] = mine.astype(BF16)
    gain, bias = row(vectors, 1, cols), row(vectors, 2, cols)
    block = ((mine - mean) * lax.rsqrt(var + NORM_EPS) * gain + bias).astype(BF16)
    for d in range(REQ):
        blocks[d] = block


def up_kernel(rows_in, arrange, weight, out):
    came = rows_in[...].reshape(-1, rows_in.shape[2])
    ordered = onto_mxu(arrange[...], came).astype(BF16)
    out[...] = nt_dot(ordered, weight[...]).astype(BF16)


def down_kernel(near, far, vectors, weight, arrange_own, stream_own, out):
    hidden = near[...].astype(F32) + far[...].astype(F32)
    hidden = hidden + vectors[vectors.shape[0] - hidden.shape[1] :][None, :]
    activated = (0.5 * hidden * (1.0 + lax.erf(hidden * math.sqrt(0.5)))).astype(BF16)
    feed = onto_mxu(activated, weight[...]) + onto_mxu(arrange_own[...], stream_own[...])
    rows = out.shape[1]
    for d in range(REQ):
        out[LAST_ORDER.index(d)] = feed[d * rows : (d + 1) * rows].astype(BF16)


def finish_kernel(pieces, vectors, out):
    cols = out.shape[1]
    out[...] = (jnp.sum(pieces[...].astype(F32), axis=0) + row(vectors, 3, cols)).astype(BF16)


def call(kernel, shapes, specs, args, scratch=(), room=16, **fixed):
    moved = sum(a.size * a.dtype.itemsize for a in args)
    return pl.pallas_call(
        functools.partial(kernel, **fixed) if fixed else kernel,
        out_shape=shapes,
        in_specs=specs,
        out_specs=[VMEM] * len(shapes),
        scratch_shapes=scratch,
        compiler_params=pltpu.CompilerParams(vmem_limit_bytes=int(room * 2**20)),
        cost_estimate=pl.CostEstimate(flops=0, bytes_accessed=moved, transcendentals=0),
    )(*args)


def trade(blocks, group):
    return lax.all_to_all(blocks, "req", 0, 0, tiled=True, axis_index_groups=[group])


def on_pairs(
    query,
    key_new,
    value_new,
    resid,
    lengths,
    owner,
    page_table,
    kv_pool,
    out_weight,
    out_bias,
    norm_gain,
    norm_bias,
    up_weight_t,
    up_bias,
    down_weight,
    down_bias,
    order,
):
    rows, cols = query.shape
    width = cols * TP
    pool_pages, page_len = kv_pool.shape[1], kv_pool.shape[2]
    positions = pool_pages * page_len
    heads = cols // HEAD_DIM
    count = owner.shape[0]
    hidden = up_bias.shape[0]

    def arr(shape, dtype=BF16):
        return jax.ShapeDtypeStruct(shape, dtype)

    position = jnp.stack([lax.axis_index("req"), lax.axis_index("tp")]).astype(I32)
    place = jnp.broadcast_to(position[:, None], (2, HEAD_DIM))

    (packed,) = call(
        pack_kernel,
        [arr((REQ, 8, cols // 2))],
        [HBM] * 5,
        [owner[None, :], query, key_new, value_new, resid],
        [pltpu.VMEM((1, count), I32)]
        + [pltpu.VMEM((rows, cols), BF16)] * 4
        + [pltpu.SemaphoreType.DMA((5,))],
        room=ALL_ROOM,
    )
    arrived = trade(packed, FIRST_ORDER)
    numbers = pile(
        [owner[None, :], order[None, :], lengths[None, :], jnp.zeros((5, count), I32), page_table.T]
    )
    vectors = pile([x.astype(F32) for x in (out_bias, norm_gain, norm_bias, down_bias, up_bias)])
    pick, valid, arrange, arrange_own = call(
        index_kernel,
        [
            arr((3 * heads * rows + 2 * rows, 2 * count)),
            arr((heads * rows, positions), F32),
            arr((count, count)),
            arr((count, rows)),
        ],
        [VMEM, VMEM],
        [place, numbers],
        page_len=page_len,
        heads=heads,
    )

    here = position[0] >= 0
    pool = jnp.where(here, kv_pool, jnp.zeros_like(kv_pool))
    upper = out_weight[: 3 * cols // 4]
    upper = jnp.where(here, upper, jnp.zeros_like(upper))

    partial, rounded = call(
        attention_kernel,
        [arr((rows, width), F32), arr((rows, width))],
        [VMEM] * 7 + [HBM],
        [place, arrived, pick, valid, vectors, pool, upper, out_weight],
        [pltpu.VMEM((cols - upper.shape[0], width), BF16), pltpu.SemaphoreType.DMA],
        room=ATTENTION_ROOM,
        rows=rows,
    )
    blocks, stream_own = call(
        norm_kernel,
        [arr((REQ, rows, cols)), arr((rows, cols))],
        [VMEM] * 6,
        [place, partial] + [swap(rounded, "tp", step) for step in (1, 2, 3)] + [vectors],
    )

    (part,) = call(
        up_kernel,
        [arr((count, hidden))],
        [VMEM] * 3,
        [trade(blocks, MIDDLE_ORDER), arrange, up_weight_t],
    )
    part = (part.astype(F32) + swap(part, "tp", 1).astype(F32)).astype(BF16)
    (feed,) = call(
        down_kernel,
        [arr((REQ, rows, cols))],
        [VMEM] * 6,
        [part, swap(part, "tp", 3), vectors, down_weight, arrange_own, stream_own],
    )
    (out,) = call(finish_kernel, [arr((rows, cols))], [VMEM] * 2, [trade(feed, LAST_ORDER), vectors])
    return out


def swap(x, axis, step):
    n = lax.axis_size(axis)
    return lax.ppermute(x, axis, [(i, i ^ step) for i in range(n)])


def origins(axis):
    n, me = lax.axis_size(axis), lax.axis_index(axis)
    if n > PAIRWISE:
        return jnp.arange(n, dtype=jnp.int32)
    offsets = [0]
    step = n // 2
    while step:
        offsets = offsets + [o ^ step for o in offsets]
        step //= 2
    return jnp.array(offsets, dtype=jnp.int32) ^ me


def gather_rows(x, axis):
    n = lax.axis_size(axis)
    if n > PAIRWISE:
        return lax.all_gather(x, axis, axis=0, tiled=True)
    step = n // 2
    while step:
        x = jnp.concatenate([x, swap(x, axis, step)], axis=0)
        step //= 2
    return x


def fold_rows(x, axis):
    n = lax.axis_size(axis)
    if n > PAIRWISE:
        return lax.psum_scatter(x, axis, scatter_dimension=0, tiled=True)
    step = 1
    while step < n:
        half = x.shape[0] // 2
        x = x[:half] + swap(x[half:], axis, step)
        step *= 2
    return x


def sum_pairs(x, axis):
    n = lax.axis_size(axis)
    step = 1
    while step < n:
        x = (x.astype(jnp.float32) + swap(x, axis, step).astype(jnp.float32)).astype(x.dtype)
        step *= 2
    return x


def on_any_mesh(
    query,
    key_new,
    value_new,
    resid,
    lengths,
    owner,
    page_table,
    kv_pool,
    out_weight,
    out_bias,
    norm_gain,
    norm_bias,
    up_weight_t,
    up_bias,
    down_weight,
    down_bias,
    order,
):
    f32, bf16, i32 = jnp.float32, jnp.bfloat16, jnp.int32
    n_req = lax.axis_size("req")
    n_tp = lax.axis_size("tp")
    me = lax.axis_index("req")
    me_tp = lax.axis_index("tp")
    rows, cols = query.shape
    width = cols * n_tp
    heads = cols // HEAD_DIM
    pool_pages, page_len = kv_pool.shape[1], kv_pool.shape[2]
    positions = pool_pages * page_len
    scale = 1.0 / math.sqrt(HEAD_DIM)

    origin = origins("req")
    packed = jnp.concatenate([query, key_new, value_new, resid], axis=1)
    arrived = gather_rows(packed, "req")

    same = owner[:, None] == owner[None, :]
    ids = jnp.arange(owner.shape[0], dtype=i32)
    rank = jnp.sum((same & (ids[None, :] < ids[:, None])).astype(i32), axis=1)
    slots = jnp.arange(rows, dtype=i32)
    mine = (owner == me)[None, :] & (rank[None, :] == slots[:, None])
    mine_i = mine.astype(i32)
    own_len = jnp.sum(mine_i * lengths[None, :], axis=1)
    own_table = jnp.sum(mine_i[:, :, None] * page_table[None], axis=1)
    origin_ids = (origin[:, None] * rows + slots[None, :]).reshape(-1)
    own_id = jnp.sum(mine_i * ids[None, :], axis=1)
    take_hot = (own_id[:, None] == origin_ids[None, :]).astype(bf16)
    own = jnp.dot(take_hot, arrived, preferred_element_type=f32).astype(bf16)
    query_own, key_own, value_own, resid_own = (own[:, i * cols : (i + 1) * cols] for i in range(4))

    pos = jnp.arange(positions, dtype=i32)
    page, within = pos // page_len, pos % page_len
    entry = jnp.arange(page_table.shape[1], dtype=i32)
    start = entry * page_len
    hit = (own_table[:, :, None] == page[None, None, :]) & (
        start[None, :, None] + within[None, None, :] < own_len[:, None, None]
    )
    valid = jnp.any(hit, axis=1)

    keys = kv_pool[0].reshape(positions, cols)
    values = kv_pool[1].reshape(positions, cols)
    head_of = jnp.arange(cols, dtype=i32) // HEAD_DIM
    head_mask = head_of[None, :] == jnp.arange(heads, dtype=i32)[:, None]
    spread_q = jnp.where(head_mask[:, None, :], query_own[None], 0).reshape(heads * rows, cols)
    scores = (
        lax.dot_general(spread_q, keys, (((1,), (1,)), ((), ())), preferred_element_type=f32) * scale
    ).reshape(heads, rows, positions)
    scores = jnp.where(valid[None], scores, -jnp.inf)
    self_score = (
        jnp.sum(
            (query_own.astype(f32) * key_own.astype(f32)).reshape(rows, heads, HEAD_DIM), axis=-1
        ).T
        * scale
    )
    top = jnp.maximum(jnp.max(scores, axis=2), self_score)
    weights = jnp.exp(scores - top[:, :, None])
    self_weight = jnp.exp(self_score - top)
    total = jnp.sum(weights, axis=2) + self_weight
    numer = jnp.dot(
        weights.astype(bf16).reshape(heads * rows, positions), values, preferred_element_type=f32
    ).reshape(heads, rows, cols)
    numer = numer + self_weight.astype(bf16).astype(f32)[:, :, None] * value_own.astype(f32)[None]
    attn = jnp.sum(
        jnp.where(head_mask[:, None, :], numer / total[:, :, None], 0.0), axis=0
    ).astype(bf16)

    extra = resid_own.astype(f32) + out_bias.astype(f32)[None, :]
    partial = jnp.dot(attn, out_weight, preferred_element_type=f32)
    place = (jnp.arange(n_tp, dtype=i32) == me_tp)[None, :, None]
    partial = (
        partial.reshape(rows, n_tp, cols) + jnp.where(place, extra[:, None, :], 0.0)
    ).reshape(rows, width)
    stream = sum_pairs(partial, "tp").astype(bf16)
    stream_f = stream.astype(f32)
    mean = jnp.mean(stream_f, axis=1, keepdims=True)
    var = jnp.mean((stream_f - mean) ** 2, axis=1, keepdims=True)
    inverse = lax.rsqrt(var + NORM_EPS)
    stream_own = lax.dynamic_slice_in_dim(stream, me_tp * cols, cols, axis=1)
    normed = (
        (stream_own.astype(f32) - mean) * inverse * norm_gain.astype(f32)[None, :]
        + norm_bias.astype(f32)[None, :]
    ).astype(bf16)

    normed_all = gather_rows(normed, "req")
    slot_of = owner * rows + rank
    wanted = slot_of[order[origin_ids]]
    place_hot = (wanted[:, None] == origin_ids[None, :]).astype(bf16)
    mine_hot = (wanted[:, None] == (me * rows + slots)[None, :]).astype(bf16)
    normed_out = jnp.dot(place_hot, normed_all, preferred_element_type=f32).astype(bf16)
    hidden = lax.dot_general(
        normed_out, up_weight_t, (((1,), (1,)), ((), ())), preferred_element_type=f32
    ).astype(bf16)
    summed = sum_pairs(hidden, "tp").astype(f32)
    activated = jax.nn.gelu(summed + up_bias.astype(f32)[None, :], approximate=False).astype(bf16)
    feed = jnp.dot(activated, down_weight, preferred_element_type=f32)
    feed = feed + jnp.dot(mine_hot, stream_own, preferred_element_type=f32)
    mixed = fold_rows(feed, "req")
    return (mixed + down_bias.astype(f32)[None, :]).astype(bf16)


def solution(mesh):
    pairs = mesh.shape["req"] == REQ and mesh.shape["tp"] == TP
    per_device = on_pairs if pairs else on_any_mesh
    in_specs = (
        P("req", "tp"),
        P("req", "tp"),
        P("req", "tp"),
        P("req", "tp"),
        P(),
        P(),
        P(),
        P(None, "req", None, "tp"),
        P("tp", None),
        P("tp"),
        P("tp"),
        P("tp"),
        P("req", "tp"),
        P("req"),
        P("req", "tp"),
        P("tp"),
        P(),
    )
    out_specs = P("req", "tp")
    return jax.shard_map(
        per_device, mesh=mesh, in_specs=in_specs, out_specs=out_specs, check_vma=False
    )
```

```python
import functools
import math

import jax
import jax.numpy as jnp
from jax import lax
from jax.experimental import pallas as pl
from jax.experimental.pallas import tpu as pltpu
from jax.sharding import PartitionSpec as P

HEAD_DIM = 128
NORM_EPS = 1e-05
PAIRWISE = 16
REQ, TP = 8, 4
ATTENTION_ROOM = 50.6
ALL_ROOM = 58
F32, BF16, I32 = jnp.float32, jnp.bfloat16, jnp.int32
VMEM = pl.BlockSpec(memory_space=pltpu.VMEM)
HBM = pl.BlockSpec(memory_space=pltpu.HBM)

ORDER = [3, 4, 1, 6, 2, 5, 0, 7]


def index_at(place):
    found = jnp.zeros_like(place)
    for i, index in enumerate(ORDER):
        found = jnp.where(place == i, index, found)
    return found


def iota(shape, dim):
    return lax.broadcasted_iota(I32, shape, dim)


def onto_mxu(a, b):
    return jnp.dot(a, b, preferred_element_type=F32)


def nt_dot(a, b):
    return lax.dot_general(a, b, (((1,), (1,)), ((), ())), preferred_element_type=F32)


def hot(condition):
    return jnp.where(condition, 1.0, 0.0).astype(BF16)


def pile(parts):
    height = sum(p.shape[0] for p in parts)
    at, piled = 0, 0
    for p in parts:
        around = ((at, height - at - p.shape[0]),) + ((0, 0),) * (p.ndim - 1)
        piled += jnp.pad(p, around)
        at += p.shape[0]
    return piled


def row(vectors, i, cols):
    return vectors[i * cols : (i + 1) * cols][None, :]


def pack_kernel(owner_in, query, key, value, resid, out, owner, q, k, v, r, sems):
    parts = ((owner_in, owner), (query, q), (key, k), (value, v), (resid, r))
    copies = [pltpu.make_async_copy(x, y, sems.at[i]) for i, (x, y) in enumerate(parts)]
    for copy in copies:
        copy.start()
    rows, cols = q.shape
    fields = 4
    count = REQ * rows
    shape = (REQ * fields, fields * rows)
    down, across = iota(shape, 0), iota(shape, 1)
    here = (count, fields * rows)
    of_mine = hot(iota(here, 0) == lax.axis_index("req") * rows + iota(here, 1) % rows)
    copies[0].wait()
    owner_of = onto_mxu(owner[...].astype(F32).astype(BF16), of_mine).astype(I32)
    pick = hot((down % fields == across // rows) & (owner_of == down // fields))
    for copy in copies[1:]:
        copy.wait()
    all_rows = jnp.concatenate([q[...], k[...], v[...], r[...]], axis=0)
    blocks = onto_mxu(pick, all_rows).astype(BF16)
    for d in range(REQ):
        block = blocks[d * fields : (d + 1) * fields]
        at = ORDER.index(d)
        out[at, :fields, :] = block[:, : cols // 2]
        out[at, fields:, :] = block[:, cols // 2 :]


def index_kernel(place, numbers, pick, valid, arrange, arrange_own, *, page_len, heads):
    owner, order, lengths = (numbers[i : i + 1, :] for i in range(3))
    table = numbers[8:, :]
    me = place[0:1, 0:1]
    count = owner.shape[1]
    rows = count // REQ
    square = (count, count)
    down, across = iota(square, 0), iota(square, 1)
    owner_row = owner
    same_place = down == across
    owner_col = jnp.sum(jnp.where(same_place, owner_row, 0), axis=1, keepdims=True)
    order_col = jnp.sum(jnp.where(same_place, order, 0), axis=1, keepdims=True)
    same_owner = owner_col == owner_row
    rank_row = jnp.sum(jnp.where(same_owner & (down < across), 1, 0), axis=0, keepdims=True)
    rank_col = jnp.sum(jnp.where(same_owner & (across < down), 1, 0), axis=1, keepdims=True)

    shape = pick.shape
    down_p, across_p = iota(shape, 0), iota(shape, 1)
    down_i = iota((shape[0], count), 0)
    mine = hot((owner_row == me) & (rank_row == down_i % rows))
    source = index_at(iota((count, shape[1]), 1) // (2 * rows))
    came = hot(iota((count, shape[1]), 0) // rows == source)
    from_there = onto_mxu(mine, came)
    field = jnp.minimum(down_p // (heads * rows), 3)
    pick[...] = hot((from_there > 0.5) & (field == across_p % rows))

    shape = valid.shape
    slot = iota((shape[0], count), 0) % rows
    mine_v = hot((owner_row == me) & (rank_row == slot))
    table_v = nt_dot(mine_v, table.astype(F32).astype(BF16)).astype(I32)
    length_v = jnp.sum(jnp.where(mine_v > 0.5, lengths, 0), axis=1, keepdims=True)
    position = iota(shape, 1)
    page, within = position // page_len, position % page_len
    seen = jnp.zeros(shape, F32)
    for j in range(table.shape[0]):
        inside = (table_v[:, j : j + 1] == page) & (within + j * page_len < length_v)
        seen = jnp.where(inside, 1.0, seen)
    valid[...] = seen

    ordered = hot(order_col == across)
    holds = hot((owner_col == index_at(across // rows)) & (rank_col == across % rows))
    arrange[...] = onto_mxu(ordered, holds).astype(BF16)
    here = hot((owner_col == me) & (rank_col == iota(arrange_own.shape, 1)))
    arrange_own[...] = onto_mxu(ordered, here).astype(BF16)


def attention_kernel(
    place, arrived, pick, valid, vectors, pool, upper, weight, partial, rounded, lower, sem, *, rows
):
    deep = upper.shape[0]
    copy = pltpu.make_async_copy(weight.at[pl.ds(deep, lower.shape[0])], lower, sem)
    copy.start()
    half = arrived.shape[2]
    cols = 2 * half
    heads = cols // HEAD_DIM
    scale = 1.0 / math.sqrt(HEAD_DIM)
    came = arrived[...].reshape(-1, half)
    which = (iota(pick.shape, 1) // rows) % 2
    chosen = pick[...].astype(F32)
    own = jnp.concatenate(
        [onto_mxu(jnp.where(which == i, chosen, 0.0).astype(BF16), came) for i in range(2)], axis=1
    )
    each = heads * rows
    query, key, value = (own[i * each : (i + 1) * each] for i in range(3))
    resid = own[3 * each : 3 * each + rows]
    shape = (each, cols)
    in_head = iota(shape, 0) // rows == iota(shape, 1) // HEAD_DIM
    wide = jnp.where(in_head, query, 0.0)
    positions = valid.shape[1]
    self_score = jnp.sum(wide * key, axis=1, keepdims=True) * scale
    scores = nt_dot(wide.astype(BF16), pool[0].reshape(positions, cols)) * scale
    scores = jnp.where(valid[...] > 0.5, scores, -jnp.inf)
    top = jnp.maximum(jnp.max(scores, axis=1, keepdims=True), self_score)
    weights = jnp.exp(scores - top)
    self_weight = jnp.exp(self_score - top)
    total = jnp.sum(weights, axis=1, keepdims=True) + self_weight
    numer = onto_mxu(weights.astype(BF16), pool[1].reshape(positions, cols))
    numer = numer + self_weight.astype(BF16).astype(F32) * value
    numer = jnp.where(in_head, numer / total, 0.0)
    attn = sum(numer[i * rows : (i + 1) * rows] for i in range(heads))
    attn = jnp.concatenate([attn, jnp.zeros_like(attn)], axis=0).astype(BF16)
    projected = onto_mxu(attn[:, :deep], upper[...])
    copy.wait()
    projected = (projected + onto_mxu(attn[:, deep:], lower[...]))[:rows]
    extra = resid + row(vectors, 0, cols)
    for t in range(TP):
        mine = jnp.where(place[1:2, 0:1] == t, extra, 0.0)
        whole = projected[:, t * cols : (t + 1) * cols] + mine
        partial[:, t * cols : (t + 1) * cols] = whole
        rounded[:, t * cols : (t + 1) * cols] = whole.astype(BF16)


def norm_kernel(place, own, sibling, far, far_sibling, vectors, blocks, stream_own):
    others = sibling[...].astype(F32) + far[...].astype(F32) + far_sibling[...].astype(F32)
    stream = (own[...] + others).astype(BF16).astype(F32)
    width = stream.shape[1]
    cols = width // TP
    mean = jnp.sum(stream, axis=1, keepdims=True) / width
    var = jnp.sum((stream - mean) ** 2, axis=1, keepdims=True) / width
    mine = stream[:, :cols]
    for t in range(1, TP):
        mine = jnp.where(place[1:2, 0:1] == t, stream[:, t * cols : (t + 1) * cols], mine)
    stream_own[...] = mine.astype(BF16)
    gain, bias = row(vectors, 1, cols), row(vectors, 2, cols)
    block = ((mine - mean) * lax.rsqrt(var + NORM_EPS) * gain + bias).astype(BF16)
    for d in range(REQ):
        blocks[d] = block


def up_kernel(rows_in, arrange, weight, out):
    came = rows_in[...].reshape(-1, rows_in.shape[2])
    ordered = onto_mxu(arrange[...], came).astype(BF16)
    out[...] = nt_dot(ordered, weight[...]).astype(BF16)


def down_kernel(part, near, far, far_near, vectors, weight, arrange_own, stream_own, out):
    hidden = part[...].astype(F32) + near[...].astype(F32)
    hidden = hidden + (far[...].astype(F32) + far_near[...].astype(F32))
    hidden = hidden + vectors[vectors.shape[0] - hidden.shape[1] :][None, :]
    activated = (0.5 * hidden * (1.0 + lax.erf(hidden * math.sqrt(0.5)))).astype(BF16)
    feed = onto_mxu(activated, weight[...]) + onto_mxu(arrange_own[...], stream_own[...])
    rows = out.shape[1]
    for d in range(REQ):
        out[ORDER.index(d)] = feed[d * rows : (d + 1) * rows].astype(BF16)


def finish_kernel(pieces, vectors, out):
    cols = out.shape[1]
    out[...] = (jnp.sum(pieces[...].astype(F32), axis=0) + row(vectors, 3, cols)).astype(BF16)


def call(kernel, shapes, specs, args, scratch=(), room=16, **fixed):
    moved = sum(a.size * a.dtype.itemsize for a in args)
    return pl.pallas_call(
        functools.partial(kernel, **fixed) if fixed else kernel,
        out_shape=shapes,
        in_specs=specs,
        out_specs=[VMEM] * len(shapes),
        scratch_shapes=scratch,
        compiler_params=pltpu.CompilerParams(vmem_limit_bytes=int(room * 2**20)),
        cost_estimate=pl.CostEstimate(flops=0, bytes_accessed=moved, transcendentals=0),
    )(*args)


def trade(blocks):
    return lax.all_to_all(blocks, "req", 0, 0, tiled=True, axis_index_groups=[ORDER])


def on_pairs(
    query,
    key_new,
    value_new,
    resid,
    lengths,
    owner,
    page_table,
    kv_pool,
    out_weight,
    out_bias,
    norm_gain,
    norm_bias,
    up_weight_t,
    up_bias,
    down_weight,
    down_bias,
    order,
):
    rows, cols = query.shape
    width = cols * TP
    pool_pages, page_len = kv_pool.shape[1], kv_pool.shape[2]
    positions = pool_pages * page_len
    heads = cols // HEAD_DIM
    count = owner.shape[0]
    hidden = up_bias.shape[0]

    def arr(shape, dtype=BF16):
        return jax.ShapeDtypeStruct(shape, dtype)

    position = jnp.stack([lax.axis_index("req"), lax.axis_index("tp")]).astype(I32)
    place = jnp.broadcast_to(position[:, None], (2, HEAD_DIM))

    (packed,) = call(
        pack_kernel,
        [arr((REQ, 8, cols // 2))],
        [HBM] * 5,
        [owner[None, :], query, key_new, value_new, resid],
        [pltpu.VMEM((1, count), I32)]
        + [pltpu.VMEM((rows, cols), BF16)] * 4
        + [pltpu.SemaphoreType.DMA((5,))],
        room=ALL_ROOM,
    )
    arrived = trade(packed)
    numbers = pile(
        [owner[None, :], order[None, :], lengths[None, :], jnp.zeros((5, count), I32), page_table.T]
    )
    vectors = pile([x.astype(F32) for x in (out_bias, norm_gain, norm_bias, down_bias, up_bias)])
    pick, valid, arrange, arrange_own = call(
        index_kernel,
        [
            arr((3 * heads * rows + 2 * rows, 2 * count)),
            arr((heads * rows, positions), F32),
            arr((count, count)),
            arr((count, rows)),
        ],
        [VMEM, VMEM],
        [place, numbers],
        page_len=page_len,
        heads=heads,
    )

    here = position[0] >= 0
    pool = jnp.where(here, kv_pool, jnp.zeros_like(kv_pool))
    upper = out_weight[: 3 * cols // 4]
    upper = jnp.where(here, upper, jnp.zeros_like(upper))

    partial, rounded = call(
        attention_kernel,
        [arr((rows, width), F32), arr((rows, width))],
        [VMEM] * 7 + [HBM],
        [place, arrived, pick, valid, vectors, pool, upper, out_weight],
        [pltpu.VMEM((cols - upper.shape[0], width), BF16), pltpu.SemaphoreType.DMA],
        room=ATTENTION_ROOM,
        rows=rows,
    )
    blocks, stream_own = call(
        norm_kernel,
        [arr((REQ, rows, cols)), arr((rows, cols))],
        [VMEM] * 6,
        [place, partial] + [swap(rounded, "tp", step) for step in (1, 2, 3)] + [vectors],
    )

    (part,) = call(
        up_kernel,
        [arr((count, hidden))],
        [VMEM] * 3,
        [trade(blocks), arrange, up_weight_t],
    )
    (feed,) = call(
        down_kernel,
        [arr((REQ, rows, cols))],
        [VMEM] * 8,
        [part]
        + [swap(part, "tp", step) for step in (1, 2, 3)]
        + [vectors, down_weight, arrange_own, stream_own],
    )
    (out,) = call(finish_kernel, [arr((rows, cols))], [VMEM] * 2, [trade(feed), vectors])
    return out


def swap(x, axis, step):
    n = lax.axis_size(axis)
    return lax.ppermute(x, axis, [(i, i ^ step) for i in range(n)])


def origins(axis):
    n, me = lax.axis_size(axis), lax.axis_index(axis)
    if n > PAIRWISE:
        return jnp.arange(n, dtype=jnp.int32)
    offsets = [0]
    step = n // 2
    while step:
        offsets = offsets + [o ^ step for o in offsets]
        step //= 2
    return jnp.array(offsets, dtype=jnp.int32) ^ me


def gather_rows(x, axis):
    n = lax.axis_size(axis)
    if n > PAIRWISE:
        return lax.all_gather(x, axis, axis=0, tiled=True)
    step = n // 2
    while step:
        x = jnp.concatenate([x, swap(x, axis, step)], axis=0)
        step //= 2
    return x


def fold_rows(x, axis):
    n = lax.axis_size(axis)
    if n > PAIRWISE:
        return lax.psum_scatter(x, axis, scatter_dimension=0, tiled=True)
    step = 1
    while step < n:
        half = x.shape[0] // 2
        x = x[:half] + swap(x[half:], axis, step)
        step *= 2
    return x


def sum_pairs(x, axis):
    n = lax.axis_size(axis)
    step = 1
    while step < n:
        x = (x.astype(jnp.float32) + swap(x, axis, step).astype(jnp.float32)).astype(x.dtype)
        step *= 2
    return x


def on_any_mesh(
    query,
    key_new,
    value_new,
    resid,
    lengths,
    owner,
    page_table,
    kv_pool,
    out_weight,
    out_bias,
    norm_gain,
    norm_bias,
    up_weight_t,
    up_bias,
    down_weight,
    down_bias,
    order,
):
    f32, bf16, i32 = jnp.float32, jnp.bfloat16, jnp.int32
    n_req = lax.axis_size("req")
    n_tp = lax.axis_size("tp")
    me = lax.axis_index("req")
    me_tp = lax.axis_index("tp")
    rows, cols = query.shape
    width = cols * n_tp
    heads = cols // HEAD_DIM
    pool_pages, page_len = kv_pool.shape[1], kv_pool.shape[2]
    positions = pool_pages * page_len
    scale = 1.0 / math.sqrt(HEAD_DIM)

    origin = origins("req")
    packed = jnp.concatenate([query, key_new, value_new, resid], axis=1)
    arrived = gather_rows(packed, "req")

    same = owner[:, None] == owner[None, :]
    ids = jnp.arange(owner.shape[0], dtype=i32)
    rank = jnp.sum((same & (ids[None, :] < ids[:, None])).astype(i32), axis=1)
    slots = jnp.arange(rows, dtype=i32)
    mine = (owner == me)[None, :] & (rank[None, :] == slots[:, None])
    mine_i = mine.astype(i32)
    own_len = jnp.sum(mine_i * lengths[None, :], axis=1)
    own_table = jnp.sum(mine_i[:, :, None] * page_table[None], axis=1)
    origin_ids = (origin[:, None] * rows + slots[None, :]).reshape(-1)
    own_id = jnp.sum(mine_i * ids[None, :], axis=1)
    take_hot = (own_id[:, None] == origin_ids[None, :]).astype(bf16)
    own = jnp.dot(take_hot, arrived, preferred_element_type=f32).astype(bf16)
    query_own, key_own, value_own, resid_own = (own[:, i * cols : (i + 1) * cols] for i in range(4))

    pos = jnp.arange(positions, dtype=i32)
    page, within = pos // page_len, pos % page_len
    entry = jnp.arange(page_table.shape[1], dtype=i32)
    start = entry * page_len
    hit = (own_table[:, :, None] == page[None, None, :]) & (
        start[None, :, None] + within[None, None, :] < own_len[:, None, None]
    )
    valid = jnp.any(hit, axis=1)

    keys = kv_pool[0].reshape(positions, cols)
    values = kv_pool[1].reshape(positions, cols)
    head_of = jnp.arange(cols, dtype=i32) // HEAD_DIM
    head_mask = head_of[None, :] == jnp.arange(heads, dtype=i32)[:, None]
    spread_q = jnp.where(head_mask[:, None, :], query_own[None], 0).reshape(heads * rows, cols)
    scores = (
        lax.dot_general(spread_q, keys, (((1,), (1,)), ((), ())), preferred_element_type=f32) * scale
    ).reshape(heads, rows, positions)
    scores = jnp.where(valid[None], scores, -jnp.inf)
    self_score = (
        jnp.sum(
            (query_own.astype(f32) * key_own.astype(f32)).reshape(rows, heads, HEAD_DIM), axis=-1
        ).T
        * scale
    )
    top = jnp.maximum(jnp.max(scores, axis=2), self_score)
    weights = jnp.exp(scores - top[:, :, None])
    self_weight = jnp.exp(self_score - top)
    total = jnp.sum(weights, axis=2) + self_weight
    numer = jnp.dot(
        weights.astype(bf16).reshape(heads * rows, positions), values, preferred_element_type=f32
    ).reshape(heads, rows, cols)
    numer = numer + self_weight.astype(bf16).astype(f32)[:, :, None] * value_own.astype(f32)[None]
    attn = jnp.sum(
        jnp.where(head_mask[:, None, :], numer / total[:, :, None], 0.0), axis=0
    ).astype(bf16)

    extra = resid_own.astype(f32) + out_bias.astype(f32)[None, :]
    partial = jnp.dot(attn, out_weight, preferred_element_type=f32)
    place = (jnp.arange(n_tp, dtype=i32) == me_tp)[None, :, None]
    partial = (
        partial.reshape(rows, n_tp, cols) + jnp.where(place, extra[:, None, :], 0.0)
    ).reshape(rows, width)
    stream = sum_pairs(partial, "tp").astype(bf16)
    stream_f = stream.astype(f32)
    mean = jnp.mean(stream_f, axis=1, keepdims=True)
    var = jnp.mean((stream_f - mean) ** 2, axis=1, keepdims=True)
    inverse = lax.rsqrt(var + NORM_EPS)
    stream_own = lax.dynamic_slice_in_dim(stream, me_tp * cols, cols, axis=1)
    normed = (
        (stream_own.astype(f32) - mean) * inverse * norm_gain.astype(f32)[None, :]
        + norm_bias.astype(f32)[None, :]
    ).astype(bf16)

    normed_all = gather_rows(normed, "req")
    slot_of = owner * rows + rank
    wanted = slot_of[order[origin_ids]]
    place_hot = (wanted[:, None] == origin_ids[None, :]).astype(bf16)
    mine_hot = (wanted[:, None] == (me * rows + slots)[None, :]).astype(bf16)
    normed_out = jnp.dot(place_hot, normed_all, preferred_element_type=f32).astype(bf16)
    hidden = lax.dot_general(
        normed_out, up_weight_t, (((1,), (1,)), ((), ())), preferred_element_type=f32
    ).astype(bf16)
    summed = sum_pairs(hidden, "tp").astype(f32)
    activated = jax.nn.gelu(summed + up_bias.astype(f32)[None, :], approximate=False).astype(bf16)
    feed = jnp.dot(activated, down_weight, preferred_element_type=f32)
    feed = feed + jnp.dot(mine_hot, stream_own, preferred_element_type=f32)
    mixed = fold_rows(feed, "req")
    return (mixed + down_bias.astype(f32)[None, :]).astype(bf16)


def solution(mesh):
    pairs = mesh.shape["req"] == REQ and mesh.shape["tp"] == TP
    per_device = on_pairs if pairs else on_any_mesh
    in_specs = (
        P("req", "tp"),
        P("req", "tp"),
        P("req", "tp"),
        P("req", "tp"),
        P(),
        P(),
        P(),
        P(None, "req", None, "tp"),
        P("tp", None),
        P("tp"),
        P("tp"),
        P("tp"),
        P("req", "tp"),
        P("req"),
        P("req", "tp"),
        P("tp"),
        P(),
    )
    out_specs = P("req", "tp")
    return jax.shard_map(
        per_device, mesh=mesh, in_specs=in_specs, out_specs=out_specs, check_vma=False
    )
```

```python
import functools
import math

import jax
import jax.numpy as jnp
from jax import lax
from jax.experimental import pallas as pl
from jax.experimental.pallas import tpu as pltpu
from jax.sharding import PartitionSpec as P

HEAD_DIM = 128
NORM_EPS = 1e-05
PAIRWISE = 16
REQ, TP = 8, 4
ATTENTION_ROOM = 51.2
ALL_ROOM = 58
F32, BF16, I32 = jnp.float32, jnp.bfloat16, jnp.int32
VMEM = pl.BlockSpec(memory_space=pltpu.VMEM)
HBM = pl.BlockSpec(memory_space=pltpu.HBM)

FIRST_ORDER = [3, 5, 2, 4, 1, 7, 0, 6]
MIDDLE_ORDER = [3, 4, 1, 6, 2, 5, 0, 7]
LAST_ORDER = [7, 6, 5, 4, 3, 2, 1, 0]


def pick_from(order, place):
    found = jnp.zeros_like(place)
    for i, index in enumerate(order):
        found = jnp.where(place == i, index, found)
    return found


def iota(shape, dim):
    return lax.broadcasted_iota(I32, shape, dim)


def onto_mxu(a, b):
    return jnp.dot(a, b, preferred_element_type=F32)


def nt_dot(a, b):
    return lax.dot_general(a, b, (((1,), (1,)), ((), ())), preferred_element_type=F32)


def hot(condition):
    return jnp.where(condition, 1.0, 0.0).astype(BF16)


def pile(parts):
    height = sum(p.shape[0] for p in parts)
    at, piled = 0, 0
    for p in parts:
        around = ((at, height - at - p.shape[0]),) + ((0, 0),) * (p.ndim - 1)
        piled += jnp.pad(p, around)
        at += p.shape[0]
    return piled


def row(vectors, i, cols):
    return vectors[i * cols : (i + 1) * cols][None, :]


def pack_kernel(owner_in, query, key, value, resid, out, owner, q, k, v, r, sems):
    parts = ((owner_in, owner), (query, q), (key, k), (value, v), (resid, r))
    copies = [pltpu.make_async_copy(x, y, sems.at[i]) for i, (x, y) in enumerate(parts)]
    for copy in copies:
        copy.start()
    rows, cols = q.shape
    fields = 4
    shape = (REQ * fields, fields * rows)
    down, across = iota(shape, 0), iota(shape, 1)
    me = lax.axis_index("req")
    copies[0].wait()
    owner_of = jnp.full(shape, owner[me * rows], I32)
    for i in range(1, rows):
        owner_of = jnp.where(across % rows == i, owner[me * rows + i], owner_of)
    pick = hot((down % fields == across // rows) & (owner_of == down // fields))
    for copy in copies[1:]:
        copy.wait()
    all_rows = jnp.concatenate([q[...], k[...], v[...], r[...]], axis=0)
    blocks = onto_mxu(pick, all_rows).astype(BF16)
    for d in range(REQ):
        block = blocks[d * fields : (d + 1) * fields]
        at = FIRST_ORDER.index(d)
        out[at, :fields, :] = block[:, : cols // 2]
        out[at, fields:, :] = block[:, cols // 2 :]


def index_kernel(place, numbers, pick, valid, arrange, arrange_own, *, page_len, heads):
    owner, order, lengths = (numbers[i : i + 1, :] for i in range(3))
    table = numbers[8:, :]
    me = place[0:1, 0:1]
    count = owner.shape[1]
    rows = count // REQ
    square = (count, count)
    down, across = iota(square, 0), iota(square, 1)
    owner_row = owner
    same_place = down == across
    owner_col = jnp.sum(jnp.where(same_place, owner_row, 0), axis=1, keepdims=True)
    order_col = jnp.sum(jnp.where(same_place, order, 0), axis=1, keepdims=True)
    same_owner = owner_col == owner_row
    rank_row = jnp.sum(jnp.where(same_owner & (down < across), 1, 0), axis=0, keepdims=True)
    rank_col = jnp.sum(jnp.where(same_owner & (across < down), 1, 0), axis=1, keepdims=True)

    shape = pick.shape
    down_p, across_p = iota(shape, 0), iota(shape, 1)
    down_i = iota((shape[0], count), 0)
    mine = hot((owner_row == me) & (rank_row == down_i % rows))
    source = pick_from(FIRST_ORDER, iota((count, shape[1]), 1) // (2 * rows))
    came = hot(iota((count, shape[1]), 0) // rows == source)
    from_there = onto_mxu(mine, came)
    field = jnp.minimum(down_p // (heads * rows), 3)
    pick[...] = hot((from_there > 0.5) & (field == across_p % rows))

    shape = valid.shape
    slot = iota((shape[0], count), 0) % rows
    mine_v = hot((owner_row == me) & (rank_row == slot))
    table_v = nt_dot(mine_v, table.astype(F32).astype(BF16)).astype(I32)
    length_v = jnp.sum(jnp.where(mine_v > 0.5, lengths, 0), axis=1, keepdims=True)
    position = iota(shape, 1)
    page, within = position // page_len, position % page_len
    seen = jnp.zeros(shape, F32)
    for j in range(table.shape[0]):
        inside = (table_v[:, j : j + 1] == page) & (within + j * page_len < length_v)
        seen = jnp.where(inside, 1.0, seen)
    valid[...] = seen

    ordered = hot(order_col == across)
    holds = hot((owner_col == pick_from(MIDDLE_ORDER, across // rows)) & (rank_col == across % rows))
    arrange[...] = onto_mxu(ordered, holds).astype(BF16)
    here = hot((owner_col == me) & (rank_col == iota(arrange_own.shape, 1)))
    arrange_own[...] = onto_mxu(ordered, here).astype(BF16)


def attention_kernel(
    place, arrived, pick, valid, vectors, pool, upper, weight, partial, rounded, lower, sem, *, rows
):
    deep = upper.shape[0]
    copy = pltpu.make_async_copy(weight.at[pl.ds(deep, deep)], lower, sem)
    copy.start()
    half = arrived.shape[2]
    cols = 2 * half
    heads = cols // HEAD_DIM
    scale = 1.0 / math.sqrt(HEAD_DIM)
    came = arrived[...].reshape(-1, half)
    which = (iota(pick.shape, 1) // rows) % 2
    chosen = pick[...].astype(F32)
    own = jnp.concatenate(
        [onto_mxu(jnp.where(which == i, chosen, 0.0).astype(BF16), came) for i in range(2)], axis=1
    )
    each = heads * rows
    query, key, value = (own[i * each : (i + 1) * each] for i in range(3))
    resid = own[3 * each : 3 * each + rows]
    shape = (each, cols)
    in_head = iota(shape, 0) // rows == iota(shape, 1) // HEAD_DIM
    wide = jnp.where(in_head, query, 0.0)
    positions = valid.shape[1]
    self_score = jnp.sum(wide * key, axis=1, keepdims=True) * scale
    scores = nt_dot(wide.astype(BF16), pool[0].reshape(positions, cols)) * scale
    scores = jnp.where(valid[...] > 0.5, scores, -jnp.inf)
    top = jnp.maximum(jnp.max(scores, axis=1, keepdims=True), self_score)
    weights = jnp.exp(scores - top)
    self_weight = jnp.exp(self_score - top)
    total = jnp.sum(weights, axis=1, keepdims=True) + self_weight
    numer = onto_mxu(weights.astype(BF16), pool[1].reshape(positions, cols))
    numer = numer + self_weight.astype(BF16).astype(F32) * value
    numer = jnp.where(in_head, numer / total, 0.0)
    attn = sum(numer[i * rows : (i + 1) * rows] for i in range(heads))
    attn = jnp.concatenate([attn, jnp.zeros_like(attn)], axis=0).astype(BF16)
    projected = onto_mxu(attn[:, :deep], upper[...])
    copy.wait()
    projected = (projected + onto_mxu(attn[:, deep:], lower[...]))[:rows]
    extra = resid + row(vectors, 0, cols)
    for t in range(TP):
        mine = jnp.where(place[1:2, 0:1] == t, extra, 0.0)
        whole = projected[:, t * cols : (t + 1) * cols] + mine
        partial[:, t * cols : (t + 1) * cols] = whole
        rounded[:, t * cols : (t + 1) * cols] = whole.astype(BF16)


def norm_kernel(place, own, sibling, far, far_sibling, vectors, blocks, stream_own):
    others = sibling[...].astype(F32) + far[...].astype(F32) + far_sibling[...].astype(F32)
    stream = (own[...] + others).astype(BF16).astype(F32)
    width = stream.shape[1]
    cols = width // TP
    mean = jnp.sum(stream, axis=1, keepdims=True) / width
    var = jnp.sum((stream - mean) ** 2, axis=1, keepdims=True) / width
    mine = stream[:, :cols]
    for t in range(1, TP):
        mine = jnp.where(place[1:2, 0:1] == t, stream[:, t * cols : (t + 1) * cols], mine)
    stream_own[...] = mine.astype(BF16)
    gain, bias = row(vectors, 1, cols), row(vectors, 2, cols)
    block = ((mine - mean) * lax.rsqrt(var + NORM_EPS) * gain + bias).astype(BF16)
    for d in range(REQ):
        blocks[d] = block


def up_kernel(rows_in, arrange, weight, out):
    came = rows_in[...].reshape(-1, rows_in.shape[2])
    ordered = onto_mxu(arrange[...], came).astype(BF16)
    out[...] = nt_dot(ordered, weight[...]).astype(BF16)


def down_kernel(near, far, vectors, weight, arrange_own, stream_own, out):
    hidden = near[...].astype(F32) + far[...].astype(F32)
    hidden = hidden + vectors[vectors.shape[0] - hidden.shape[1] :][None, :]
    activated = (0.5 * hidden * (1.0 + lax.erf(hidden * math.sqrt(0.5)))).astype(BF16)
    feed = onto_mxu(activated, weight[...]) + onto_mxu(arrange_own[...], stream_own[...])
    rows = out.shape[1]
    for d in range(REQ):
        out[LAST_ORDER.index(d)] = feed[d * rows : (d + 1) * rows].astype(BF16)


def finish_kernel(pieces, vectors, out):
    cols = out.shape[1]
    out[...] = (jnp.sum(pieces[...].astype(F32), axis=0) + row(vectors, 3, cols)).astype(BF16)


def call(kernel, shapes, specs, args, scratch=(), room=16, **fixed):
    moved = sum(a.size * a.dtype.itemsize for a in args)
    return pl.pallas_call(
        functools.partial(kernel, **fixed) if fixed else kernel,
        out_shape=shapes,
        in_specs=specs,
        out_specs=[VMEM] * len(shapes),
        scratch_shapes=scratch,
        compiler_params=pltpu.CompilerParams(vmem_limit_bytes=int(room * 2**20)),
        cost_estimate=pl.CostEstimate(flops=0, bytes_accessed=moved, transcendentals=0),
    )(*args)


def trade(blocks, group):
    return lax.all_to_all(blocks, "req", 0, 0, tiled=True, axis_index_groups=[group])


def on_pairs(
    query,
    key_new,
    value_new,
    resid,
    lengths,
    owner,
    page_table,
    kv_pool,
    out_weight,
    out_bias,
    norm_gain,
    norm_bias,
    up_weight_t,
    up_bias,
    down_weight,
    down_bias,
    order,
):
    rows, cols = query.shape
    width = cols * TP
    pool_pages, page_len = kv_pool.shape[1], kv_pool.shape[2]
    positions = pool_pages * page_len
    heads = cols // HEAD_DIM
    count = owner.shape[0]
    hidden = up_bias.shape[0]

    def arr(shape, dtype=BF16):
        return jax.ShapeDtypeStruct(shape, dtype)

    position = jnp.stack([lax.axis_index("req"), lax.axis_index("tp")]).astype(I32)
    place = jnp.broadcast_to(position[:, None], (2, HEAD_DIM))

    (packed,) = call(
        pack_kernel,
        [arr((REQ, 8, cols // 2))],
        [HBM] * 5,
        [owner, query, key_new, value_new, resid],
        [pltpu.SMEM((count,), I32)]
        + [pltpu.VMEM((rows, cols), BF16)] * 4
        + [pltpu.SemaphoreType.DMA((5,))],
        room=ALL_ROOM,
    )
    arrived = trade(packed, FIRST_ORDER)
    numbers = pile(
        [owner[None, :], order[None, :], lengths[None, :], jnp.zeros((5, count), I32), page_table.T]
    )
    vectors = pile([x.astype(F32) for x in (out_bias, norm_gain, norm_bias, down_bias, up_bias)])
    pick, valid, arrange, arrange_own = call(
        index_kernel,
        [
            arr((3 * heads * rows + 2 * rows, 2 * count)),
            arr((heads * rows, positions), F32),
            arr((count, count)),
            arr((count, rows)),
        ],
        [VMEM, VMEM],
        [place, numbers],
        page_len=page_len,
        heads=heads,
    )

    here = position[0] >= 0
    pool = jnp.where(here, kv_pool, jnp.zeros_like(kv_pool))
    upper = out_weight[: cols // 2]
    upper = jnp.where(here, upper, jnp.zeros_like(upper))

    partial, rounded = call(
        attention_kernel,
        [arr((rows, width), F32), arr((rows, width))],
        [VMEM] * 7 + [HBM],
        [place, arrived, pick, valid, vectors, pool, upper, out_weight],
        [pltpu.VMEM(upper.shape, BF16), pltpu.SemaphoreType.DMA],
        room=ATTENTION_ROOM,
        rows=rows,
    )
    blocks, stream_own = call(
        norm_kernel,
        [arr((REQ, rows, cols)), arr((rows, cols))],
        [VMEM] * 6,
        [place, partial] + [swap(rounded, "tp", step) for step in (1, 2, 3)] + [vectors],
    )

    (part,) = call(
        up_kernel,
        [arr((count, hidden))],
        [VMEM] * 3,
        [trade(blocks, MIDDLE_ORDER), arrange, up_weight_t],
    )
    part = (part.astype(F32) + swap(part, "tp", 1).astype(F32)).astype(BF16)
    (feed,) = call(
        down_kernel,
        [arr((REQ, rows, cols))],
        [VMEM] * 6,
        [part, swap(part, "tp", 3), vectors, down_weight, arrange_own, stream_own],
    )
    (out,) = call(finish_kernel, [arr((rows, cols))], [VMEM] * 2, [trade(feed, LAST_ORDER), vectors])
    return out


def swap(x, axis, step):
    n = lax.axis_size(axis)
    return lax.ppermute(x, axis, [(i, i ^ step) for i in range(n)])


def origins(axis):
    n, me = lax.axis_size(axis), lax.axis_index(axis)
    if n > PAIRWISE:
        return jnp.arange(n, dtype=jnp.int32)
    offsets = [0]
    step = n // 2
    while step:
        offsets = offsets + [o ^ step for o in offsets]
        step //= 2
    return jnp.array(offsets, dtype=jnp.int32) ^ me


def gather_rows(x, axis):
    n = lax.axis_size(axis)
    if n > PAIRWISE:
        return lax.all_gather(x, axis, axis=0, tiled=True)
    step = n // 2
    while step:
        x = jnp.concatenate([x, swap(x, axis, step)], axis=0)
        step //= 2
    return x


def fold_rows(x, axis):
    n = lax.axis_size(axis)
    if n > PAIRWISE:
        return lax.psum_scatter(x, axis, scatter_dimension=0, tiled=True)
    step = 1
    while step < n:
        half = x.shape[0] // 2
        x = x[:half] + swap(x[half:], axis, step)
        step *= 2
    return x


def sum_pairs(x, axis):
    n = lax.axis_size(axis)
    step = 1
    while step < n:
        x = (x.astype(jnp.float32) + swap(x, axis, step).astype(jnp.float32)).astype(x.dtype)
        step *= 2
    return x


def on_any_mesh(
    query,
    key_new,
    value_new,
    resid,
    lengths,
    owner,
    page_table,
    kv_pool,
    out_weight,
    out_bias,
    norm_gain,
    norm_bias,
    up_weight_t,
    up_bias,
    down_weight,
    down_bias,
    order,
):
    f32, bf16, i32 = jnp.float32, jnp.bfloat16, jnp.int32
    n_req = lax.axis_size("req")
    n_tp = lax.axis_size("tp")
    me = lax.axis_index("req")
    me_tp = lax.axis_index("tp")
    rows, cols = query.shape
    width = cols * n_tp
    heads = cols // HEAD_DIM
    pool_pages, page_len = kv_pool.shape[1], kv_pool.shape[2]
    positions = pool_pages * page_len
    scale = 1.0 / math.sqrt(HEAD_DIM)

    origin = origins("req")
    packed = jnp.concatenate([query, key_new, value_new, resid], axis=1)
    arrived = gather_rows(packed, "req")

    same = owner[:, None] == owner[None, :]
    ids = jnp.arange(owner.shape[0], dtype=i32)
    rank = jnp.sum((same & (ids[None, :] < ids[:, None])).astype(i32), axis=1)
    slots = jnp.arange(rows, dtype=i32)
    mine = (owner == me)[None, :] & (rank[None, :] == slots[:, None])
    mine_i = mine.astype(i32)
    own_len = jnp.sum(mine_i * lengths[None, :], axis=1)
    own_table = jnp.sum(mine_i[:, :, None] * page_table[None], axis=1)
    origin_ids = (origin[:, None] * rows + slots[None, :]).reshape(-1)
    own_id = jnp.sum(mine_i * ids[None, :], axis=1)
    take_hot = (own_id[:, None] == origin_ids[None, :]).astype(bf16)
    own = jnp.dot(take_hot, arrived, preferred_element_type=f32).astype(bf16)
    query_own, key_own, value_own, resid_own = (own[:, i * cols : (i + 1) * cols] for i in range(4))

    pos = jnp.arange(positions, dtype=i32)
    page, within = pos // page_len, pos % page_len
    entry = jnp.arange(page_table.shape[1], dtype=i32)
    start = entry * page_len
    hit = (own_table[:, :, None] == page[None, None, :]) & (
        start[None, :, None] + within[None, None, :] < own_len[:, None, None]
    )
    valid = jnp.any(hit, axis=1)

    keys = kv_pool[0].reshape(positions, cols)
    values = kv_pool[1].reshape(positions, cols)
    head_of = jnp.arange(cols, dtype=i32) // HEAD_DIM
    head_mask = head_of[None, :] == jnp.arange(heads, dtype=i32)[:, None]
    spread_q = jnp.where(head_mask[:, None, :], query_own[None], 0).reshape(heads * rows, cols)
    scores = (
        lax.dot_general(spread_q, keys, (((1,), (1,)), ((), ())), preferred_element_type=f32) * scale
    ).reshape(heads, rows, positions)
    scores = jnp.where(valid[None], scores, -jnp.inf)
    self_score = (
        jnp.sum(
            (query_own.astype(f32) * key_own.astype(f32)).reshape(rows, heads, HEAD_DIM), axis=-1
        ).T
        * scale
    )
    top = jnp.maximum(jnp.max(scores, axis=2), self_score)
    weights = jnp.exp(scores - top[:, :, None])
    self_weight = jnp.exp(self_score - top)
    total = jnp.sum(weights, axis=2) + self_weight
    numer = jnp.dot(
        weights.astype(bf16).reshape(heads * rows, positions), values, preferred_element_type=f32
    ).reshape(heads, rows, cols)
    numer = numer + self_weight.astype(bf16).astype(f32)[:, :, None] * value_own.astype(f32)[None]
    attn = jnp.sum(
        jnp.where(head_mask[:, None, :], numer / total[:, :, None], 0.0), axis=0
    ).astype(bf16)

    extra = resid_own.astype(f32) + out_bias.astype(f32)[None, :]
    partial = jnp.dot(attn, out_weight, preferred_element_type=f32)
    place = (jnp.arange(n_tp, dtype=i32) == me_tp)[None, :, None]
    partial = (
        partial.reshape(rows, n_tp, cols) + jnp.where(place, extra[:, None, :], 0.0)
    ).reshape(rows, width)
    stream = sum_pairs(partial, "tp").astype(bf16)
    stream_f = stream.astype(f32)
    mean = jnp.mean(stream_f, axis=1, keepdims=True)
    var = jnp.mean((stream_f - mean) ** 2, axis=1, keepdims=True)
    inverse = lax.rsqrt(var + NORM_EPS)
    stream_own = lax.dynamic_slice_in_dim(stream, me_tp * cols, cols, axis=1)
    normed = (
        (stream_own.astype(f32) - mean) * inverse * norm_gain.astype(f32)[None, :]
        + norm_bias.astype(f32)[None, :]
    ).astype(bf16)

    normed_all = gather_rows(normed, "req")
    slot_of = owner * rows + rank
    wanted = slot_of[order[origin_ids]]
    place_hot = (wanted[:, None] == origin_ids[None, :]).astype(bf16)
    mine_hot = (wanted[:, None] == (me * rows + slots)[None, :]).astype(bf16)
    normed_out = jnp.dot(place_hot, normed_all, preferred_element_type=f32).astype(bf16)
    hidden = lax.dot_general(
        normed_out, up_weight_t, (((1,), (1,)), ((), ())), preferred_element_type=f32
    ).astype(bf16)
    summed = sum_pairs(hidden, "tp").astype(f32)
    activated = jax.nn.gelu(summed + up_bias.astype(f32)[None, :], approximate=False).astype(bf16)
    feed = jnp.dot(activated, down_weight, preferred_element_type=f32)
    feed = feed + jnp.dot(mine_hot, stream_own, preferred_element_type=f32)
    mixed = fold_rows(feed, "req")
    return (mixed + down_bias.astype(f32)[None, :]).astype(bf16)


def solution(mesh):
    pairs = mesh.shape["req"] == REQ and mesh.shape["tp"] == TP
    per_device = on_pairs if pairs else on_any_mesh
    in_specs = (
        P("req", "tp"),
        P("req", "tp"),
        P("req", "tp"),
        P("req", "tp"),
        P(),
        P(),
        P(),
        P(None, "req", None, "tp"),
        P("tp", None),
        P("tp"),
        P("tp"),
        P("tp"),
        P("req", "tp"),
        P("req"),
        P("req", "tp"),
        P("tp"),
        P(),
    )
    out_specs = P("req", "tp")
    return jax.shard_map(
        per_device, mesh=mesh, in_specs=in_specs, out_specs=out_specs, check_vma=False
    )
```

```python
import functools
import math

import jax
import jax.numpy as jnp
from jax import lax
from jax.experimental import pallas as pl
from jax.experimental.pallas import tpu as pltpu
from jax.sharding import PartitionSpec as P

HEAD_DIM = 128
NORM_EPS = 1e-05
PAIRWISE = 16
REQ, TP = 8, 4
ATTENTION_ROOM = 50.6
ALL_ROOM = 58
F32, BF16, I32 = jnp.float32, jnp.bfloat16, jnp.int32
VMEM = pl.BlockSpec(memory_space=pltpu.VMEM)
HBM = pl.BlockSpec(memory_space=pltpu.HBM)

FIRST_ORDER = [3, 5, 2, 4, 1, 7, 0, 6]
MIDDLE_ORDER = [3, 4, 1, 6, 2, 5, 0, 7]
LAST_ORDER = [7, 6, 5, 4, 3, 2, 1, 0]


def pick_from(order, place):
    found = jnp.zeros_like(place)
    for i, index in enumerate(order):
        found = jnp.where(place == i, index, found)
    return found


def iota(shape, dim):
    return lax.broadcasted_iota(I32, shape, dim)


def onto_mxu(a, b):
    return jnp.dot(a, b, preferred_element_type=F32)


def nt_dot(a, b):
    return lax.dot_general(a, b, (((1,), (1,)), ((), ())), preferred_element_type=F32)


def hot(condition):
    return jnp.where(condition, 1.0, 0.0).astype(BF16)


def pile(parts):
    height = sum(p.shape[0] for p in parts)
    at, piled = 0, 0
    for p in parts:
        around = ((at, height - at - p.shape[0]),) + ((0, 0),) * (p.ndim - 1)
        piled += jnp.pad(p, around)
        at += p.shape[0]
    return piled


def row(vectors, i, cols):
    return vectors[i * cols : (i + 1) * cols][None, :]


def pack_kernel(owner_in, query, key, value, resid, out, owner, q, k, v, r, sems):
    parts = ((owner_in, owner), (query, q), (key, k), (value, v), (resid, r))
    copies = [pltpu.make_async_copy(x, y, sems.at[i]) for i, (x, y) in enumerate(parts)]
    for copy in copies:
        copy.start()
    rows, cols = q.shape
    fields = 4
    shape = (REQ * fields, fields * rows)
    down, across = iota(shape, 0), iota(shape, 1)
    me = lax.axis_index("req")
    copies[0].wait()
    owner_of = jnp.full(shape, owner[me * rows], I32)
    for i in range(1, rows):
        owner_of = jnp.where(across % rows == i, owner[me * rows + i], owner_of)
    pick = hot((down % fields == across // rows) & (owner_of == down // fields))
    for copy in copies[1:]:
        copy.wait()
    all_rows = jnp.concatenate([q[...], k[...], v[...], r[...]], axis=0)
    blocks = onto_mxu(pick, all_rows).astype(BF16)
    for d in range(REQ):
        block = blocks[d * fields : (d + 1) * fields]
        at = FIRST_ORDER.index(d)
        out[at, :fields, :] = block[:, : cols // 2]
        out[at, fields:, :] = block[:, cols // 2 :]


def index_kernel(place, numbers, pick, valid, arrange, arrange_own, *, page_len, heads):
    owner, order, lengths = (numbers[i : i + 1, :] for i in range(3))
    table = numbers[8:, :]
    me = place[0:1, 0:1]
    count = owner.shape[1]
    rows = count // REQ
    square = (count, count)
    down, across = iota(square, 0), iota(square, 1)
    owner_row = owner
    same_place = down == across
    owner_col = jnp.sum(jnp.where(same_place, owner_row, 0), axis=1, keepdims=True)
    order_col = jnp.sum(jnp.where(same_place, order, 0), axis=1, keepdims=True)
    same_owner = owner_col == owner_row
    rank_row = jnp.sum(jnp.where(same_owner & (down < across), 1, 0), axis=0, keepdims=True)
    rank_col = jnp.sum(jnp.where(same_owner & (across < down), 1, 0), axis=1, keepdims=True)

    shape = pick.shape
    down_p, across_p = iota(shape, 0), iota(shape, 1)
    down_i = iota((shape[0], count), 0)
    mine = hot((owner_row == me) & (rank_row == down_i % rows))
    source = pick_from(FIRST_ORDER, iota((count, shape[1]), 1) // (2 * rows))
    came = hot(iota((count, shape[1]), 0) // rows == source)
    from_there = onto_mxu(mine, came)
    field = jnp.minimum(down_p // (heads * rows), 3)
    pick[...] = hot((from_there > 0.5) & (field == across_p % rows))

    shape = valid.shape
    slot = iota((shape[0], count), 0) % rows
    mine_v = hot((owner_row == me) & (rank_row == slot))
    table_v = nt_dot(mine_v, table.astype(F32).astype(BF16)).astype(I32)
    length_v = jnp.sum(jnp.where(mine_v > 0.5, lengths, 0), axis=1, keepdims=True)
    position = iota(shape, 1)
    page, within = position // page_len, position % page_len
    seen = jnp.zeros(shape, F32)
    for j in range(table.shape[0]):
        inside = (table_v[:, j : j + 1] == page) & (within + j * page_len < length_v)
        seen = jnp.where(inside, 1.0, seen)
    valid[...] = seen

    ordered = hot(order_col == across)
    holds = hot((owner_col == pick_from(MIDDLE_ORDER, across // rows)) & (rank_col == across % rows))
    arrange[...] = onto_mxu(ordered, holds).astype(BF16)
    here = hot((owner_col == me) & (rank_col == iota(arrange_own.shape, 1)))
    arrange_own[...] = onto_mxu(ordered, here).astype(BF16)


def attention_kernel(
    place, arrived, pick, valid, vectors, pool, upper, weight, partial, rounded, lower, sem, *, rows
):
    deep = upper.shape[0]
    copy = pltpu.make_async_copy(weight.at[pl.ds(deep, lower.shape[0])], lower, sem)
    copy.start()
    half = arrived.shape[2]
    cols = 2 * half
    heads = cols // HEAD_DIM
    scale = 1.0 / math.sqrt(HEAD_DIM)
    came = arrived[...].reshape(-1, half)
    which = (iota(pick.shape, 1) // rows) % 2
    chosen = pick[...].astype(F32)
    own = jnp.concatenate(
        [onto_mxu(jnp.where(which == i, chosen, 0.0).astype(BF16), came) for i in range(2)], axis=1
    )
    each = heads * rows
    query, key, value = (own[i * each : (i + 1) * each] for i in range(3))
    resid = own[3 * each : 3 * each + rows]
    shape = (each, cols)
    in_head = iota(shape, 0) // rows == iota(shape, 1) // HEAD_DIM
    wide = jnp.where(in_head, query, 0.0)
    positions = valid.shape[1]
    self_score = jnp.sum(wide * key, axis=1, keepdims=True) * scale
    scores = nt_dot(wide.astype(BF16), pool[0].reshape(positions, cols)) * scale
    scores = jnp.where(valid[...] > 0.5, scores, -jnp.inf)
    top = jnp.maximum(jnp.max(scores, axis=1, keepdims=True), self_score)
    weights = jnp.exp(scores - top)
    self_weight = jnp.exp(self_score - top)
    total = jnp.sum(weights, axis=1, keepdims=True) + self_weight
    numer = onto_mxu(weights.astype(BF16), pool[1].reshape(positions, cols))
    numer = numer + self_weight.astype(BF16).astype(F32) * value
    numer = jnp.where(in_head, numer / total, 0.0)
    attn = sum(numer[i * rows : (i + 1) * rows] for i in range(heads))
    attn = jnp.concatenate([attn, jnp.zeros_like(attn)], axis=0).astype(BF16)
    projected = onto_mxu(attn[:, :deep], upper[...])
    copy.wait()
    projected = (projected + onto_mxu(attn[:, deep:], lower[...]))[:rows]
    extra = resid + row(vectors, 0, cols)
    for t in range(TP):
        mine = jnp.where(place[1:2, 0:1] == t, extra, 0.0)
        whole = projected[:, t * cols : (t + 1) * cols] + mine
        partial[:, t * cols : (t + 1) * cols] = whole
        rounded[:, t * cols : (t + 1) * cols] = whole.astype(BF16)


def norm_kernel(place, own, sibling, far, far_sibling, vectors, blocks, stream_own):
    others = sibling[...].astype(F32) + far[...].astype(F32) + far_sibling[...].astype(F32)
    stream = (own[...] + others).astype(BF16).astype(F32)
    width = stream.shape[1]
    cols = width // TP
    mean = jnp.sum(stream, axis=1, keepdims=True) / width
    var = jnp.sum((stream - mean) ** 2, axis=1, keepdims=True) / width
    mine = stream[:, :cols]
    for t in range(1, TP):
        mine = jnp.where(place[1:2, 0:1] == t, stream[:, t * cols : (t + 1) * cols], mine)
    stream_own[...] = mine.astype(BF16)
    gain, bias = row(vectors, 1, cols), row(vectors, 2, cols)
    block = ((mine - mean) * lax.rsqrt(var + NORM_EPS) * gain + bias).astype(BF16)
    for d in range(REQ):
        blocks[d] = block


def up_kernel(rows_in, arrange, weight, out):
    came = rows_in[...].reshape(-1, rows_in.shape[2])
    ordered = onto_mxu(arrange[...], came).astype(BF16)
    out[...] = nt_dot(ordered, weight[...]).astype(BF16)


def down_kernel(near, far, vectors, weight, arrange_own, stream_own, out):
    hidden = near[...].astype(F32) + far[...].astype(F32)
    hidden = hidden + vectors[vectors.shape[0] - hidden.shape[1] :][None, :]
    activated = (0.5 * hidden * (1.0 + lax.erf(hidden * math.sqrt(0.5)))).astype(BF16)
    feed = onto_mxu(activated, weight[...]) + onto_mxu(arrange_own[...], stream_own[...])
    rows = out.shape[1]
    for d in range(REQ):
        out[LAST_ORDER.index(d)] = feed[d * rows : (d + 1) * rows].astype(BF16)


def finish_kernel(pieces, vectors, out):
    cols = out.shape[1]
    out[...] = (jnp.sum(pieces[...].astype(F32), axis=0) + row(vectors, 3, cols)).astype(BF16)


def call(kernel, shapes, specs, args, scratch=(), room=16, **fixed):
    moved = sum(a.size * a.dtype.itemsize for a in args)
    return pl.pallas_call(
        functools.partial(kernel, **fixed) if fixed else kernel,
        out_shape=shapes,
        in_specs=specs,
        out_specs=[VMEM] * len(shapes),
        scratch_shapes=scratch,
        compiler_params=pltpu.CompilerParams(vmem_limit_bytes=int(room * 2**20)),
        cost_estimate=pl.CostEstimate(flops=0, bytes_accessed=moved, transcendentals=0),
    )(*args)


def trade(blocks, group):
    return lax.all_to_all(blocks, "req", 0, 0, tiled=True, axis_index_groups=[group])


def on_pairs(
    query,
    key_new,
    value_new,
    resid,
    lengths,
    owner,
    page_table,
    kv_pool,
    out_weight,
    out_bias,
    norm_gain,
    norm_bias,
    up_weight_t,
    up_bias,
    down_weight,
    down_bias,
    order,
):
    rows, cols = query.shape
    width = cols * TP
    pool_pages, page_len = kv_pool.shape[1], kv_pool.shape[2]
    positions = pool_pages * page_len
    heads = cols // HEAD_DIM
    count = owner.shape[0]
    hidden = up_bias.shape[0]

    def arr(shape, dtype=BF16):
        return jax.ShapeDtypeStruct(shape, dtype)

    position = jnp.stack([lax.axis_index("req"), lax.axis_index("tp")]).astype(I32)
    place = jnp.broadcast_to(position[:, None], (2, HEAD_DIM))

    (packed,) = call(
        pack_kernel,
        [arr((REQ, 8, cols // 2))],
        [HBM] * 5,
        [owner, query, key_new, value_new, resid],
        [pltpu.SMEM((count,), I32)]
        + [pltpu.VMEM((rows, cols), BF16)] * 4
        + [pltpu.SemaphoreType.DMA((5,))],
        room=ALL_ROOM,
    )
    arrived = trade(packed, FIRST_ORDER)
    numbers = pile(
        [owner[None, :], order[None, :], lengths[None, :], jnp.zeros((5, count), I32), page_table.T]
    )
    vectors = pile([x.astype(F32) for x in (out_bias, norm_gain, norm_bias, down_bias, up_bias)])
    pick, valid, arrange, arrange_own = call(
        index_kernel,
        [
            arr((3 * heads * rows + 2 * rows, 2 * count)),
            arr((heads * rows, positions), F32),
            arr((count, count)),
            arr((count, rows)),
        ],
        [VMEM, VMEM],
        [place, numbers],
        page_len=page_len,
        heads=heads,
    )

    here = position[0] >= 0
    pool = jnp.where(here, kv_pool, jnp.zeros_like(kv_pool))
    upper = out_weight[: 3 * cols // 4]
    upper = jnp.where(here, upper, jnp.zeros_like(upper))

    partial, rounded = call(
        attention_kernel,
        [arr((rows, width), F32), arr((rows, width))],
        [VMEM] * 7 + [HBM],
        [place, arrived, pick, valid, vectors, pool, upper, out_weight],
        [pltpu.VMEM((cols - upper.shape[0], width), BF16), pltpu.SemaphoreType.DMA],
        room=ATTENTION_ROOM,
        rows=rows,
    )
    blocks, stream_own = call(
        norm_kernel,
        [arr((REQ, rows, cols)), arr((rows, cols))],
        [VMEM] * 6,
        [place, partial] + [swap(rounded, "tp", step) for step in (1, 2, 3)] + [vectors],
    )

    (part,) = call(
        up_kernel,
        [arr((count, hidden))],
        [VMEM] * 3,
        [trade(blocks, MIDDLE_ORDER), arrange, up_weight_t],
    )
    part = (part.astype(F32) + swap(part, "tp", 1).astype(F32)).astype(BF16)
    (feed,) = call(
        down_kernel,
        [arr((REQ, rows, cols))],
        [VMEM] * 6,
        [part, swap(part, "tp", 3), vectors, down_weight, arrange_own, stream_own],
    )
    (out,) = call(finish_kernel, [arr((rows, cols))], [VMEM] * 2, [trade(feed, LAST_ORDER), vectors])
    return out


def swap(x, axis, step):
    n = lax.axis_size(axis)
    return lax.ppermute(x, axis, [(i, i ^ step) for i in range(n)])


def origins(axis):
    n, me = lax.axis_size(axis), lax.axis_index(axis)
    if n > PAIRWISE:
        return jnp.arange(n, dtype=jnp.int32)
    offsets = [0]
    step = n // 2
    while step:
        offsets = offsets + [o ^ step for o in offsets]
        step //= 2
    return jnp.array(offsets, dtype=jnp.int32) ^ me


def gather_rows(x, axis):
    n = lax.axis_size(axis)
    if n > PAIRWISE:
        return lax.all_gather(x, axis, axis=0, tiled=True)
    step = n // 2
    while step:
        x = jnp.concatenate([x, swap(x, axis, step)], axis=0)
        step //= 2
    return x


def fold_rows(x, axis):
    n = lax.axis_size(axis)
    if n > PAIRWISE:
        return lax.psum_scatter(x, axis, scatter_dimension=0, tiled=True)
    step = 1
    while step < n:
        half = x.shape[0] // 2
        x = x[:half] + swap(x[half:], axis, step)
        step *= 2
    return x


def sum_pairs(x, axis):
    n = lax.axis_size(axis)
    step = 1
    while step < n:
        x = (x.astype(jnp.float32) + swap(x, axis, step).astype(jnp.float32)).astype(x.dtype)
        step *= 2
    return x


def on_any_mesh(
    query,
    key_new,
    value_new,
    resid,
    lengths,
    owner,
    page_table,
    kv_pool,
    out_weight,
    out_bias,
    norm_gain,
    norm_bias,
    up_weight_t,
    up_bias,
    down_weight,
    down_bias,
    order,
):
    f32, bf16, i32 = jnp.float32, jnp.bfloat16, jnp.int32
    n_req = lax.axis_size("req")
    n_tp = lax.axis_size("tp")
    me = lax.axis_index("req")
    me_tp = lax.axis_index("tp")
    rows, cols = query.shape
    width = cols * n_tp
    heads = cols // HEAD_DIM
    pool_pages, page_len = kv_pool.shape[1], kv_pool.shape[2]
    positions = pool_pages * page_len
    scale = 1.0 / math.sqrt(HEAD_DIM)

    origin = origins("req")
    packed = jnp.concatenate([query, key_new, value_new, resid], axis=1)
    arrived = gather_rows(packed, "req")

    same = owner[:, None] == owner[None, :]
    ids = jnp.arange(owner.shape[0], dtype=i32)
    rank = jnp.sum((same & (ids[None, :] < ids[:, None])).astype(i32), axis=1)
    slots = jnp.arange(rows, dtype=i32)
    mine = (owner == me)[None, :] & (rank[None, :] == slots[:, None])
    mine_i = mine.astype(i32)
    own_len = jnp.sum(mine_i * lengths[None, :], axis=1)
    own_table = jnp.sum(mine_i[:, :, None] * page_table[None], axis=1)
    origin_ids = (origin[:, None] * rows + slots[None, :]).reshape(-1)
    own_id = jnp.sum(mine_i * ids[None, :], axis=1)
    take_hot = (own_id[:, None] == origin_ids[None, :]).astype(bf16)
    own = jnp.dot(take_hot, arrived, preferred_element_type=f32).astype(bf16)
    query_own, key_own, value_own, resid_own = (own[:, i * cols : (i + 1) * cols] for i in range(4))

    pos = jnp.arange(positions, dtype=i32)
    page, within = pos // page_len, pos % page_len
    entry = jnp.arange(page_table.shape[1], dtype=i32)
    start = entry * page_len
    hit = (own_table[:, :, None] == page[None, None, :]) & (
        start[None, :, None] + within[None, None, :] < own_len[:, None, None]
    )
    valid = jnp.any(hit, axis=1)

    keys = kv_pool[0].reshape(positions, cols)
    values = kv_pool[1].reshape(positions, cols)
    head_of = jnp.arange(cols, dtype=i32) // HEAD_DIM
    head_mask = head_of[None, :] == jnp.arange(heads, dtype=i32)[:, None]
    spread_q = jnp.where(head_mask[:, None, :], query_own[None], 0).reshape(heads * rows, cols)
    scores = (
        lax.dot_general(spread_q, keys, (((1,), (1,)), ((), ())), preferred_element_type=f32) * scale
    ).reshape(heads, rows, positions)
    scores = jnp.where(valid[None], scores, -jnp.inf)
    self_score = (
        jnp.sum(
            (query_own.astype(f32) * key_own.astype(f32)).reshape(rows, heads, HEAD_DIM), axis=-1
        ).T
        * scale
    )
    top = jnp.maximum(jnp.max(scores, axis=2), self_score)
    weights = jnp.exp(scores - top[:, :, None])
    self_weight = jnp.exp(self_score - top)
    total = jnp.sum(weights, axis=2) + self_weight
    numer = jnp.dot(
        weights.astype(bf16).reshape(heads * rows, positions), values, preferred_element_type=f32
    ).reshape(heads, rows, cols)
    numer = numer + self_weight.astype(bf16).astype(f32)[:, :, None] * value_own.astype(f32)[None]
    attn = jnp.sum(
        jnp.where(head_mask[:, None, :], numer / total[:, :, None], 0.0), axis=0
    ).astype(bf16)

    extra = resid_own.astype(f32) + out_bias.astype(f32)[None, :]
    partial = jnp.dot(attn, out_weight, preferred_element_type=f32)
    place = (jnp.arange(n_tp, dtype=i32) == me_tp)[None, :, None]
    partial = (
        partial.reshape(rows, n_tp, cols) + jnp.where(place, extra[:, None, :], 0.0)
    ).reshape(rows, width)
    stream = sum_pairs(partial, "tp").astype(bf16)
    stream_f = stream.astype(f32)
    mean = jnp.mean(stream_f, axis=1, keepdims=True)
    var = jnp.mean((stream_f - mean) ** 2, axis=1, keepdims=True)
    inverse = lax.rsqrt(var + NORM_EPS)
    stream_own = lax.dynamic_slice_in_dim(stream, me_tp * cols, cols, axis=1)
    normed = (
        (stream_own.astype(f32) - mean) * inverse * norm_gain.astype(f32)[None, :]
        + norm_bias.astype(f32)[None, :]
    ).astype(bf16)

    normed_all = gather_rows(normed, "req")
    slot_of = owner * rows + rank
    wanted = slot_of[order[origin_ids]]
    place_hot = (wanted[:, None] == origin_ids[None, :]).astype(bf16)
    mine_hot = (wanted[:, None] == (me * rows + slots)[None, :]).astype(bf16)
    normed_out = jnp.dot(place_hot, normed_all, preferred_element_type=f32).astype(bf16)
    hidden = lax.dot_general(
        normed_out, up_weight_t, (((1,), (1,)), ((), ())), preferred_element_type=f32
    ).astype(bf16)
    summed = sum_pairs(hidden, "tp").astype(f32)
    activated = jax.nn.gelu(summed + up_bias.astype(f32)[None, :], approximate=False).astype(bf16)
    feed = jnp.dot(activated, down_weight, preferred_element_type=f32)
    feed = feed + jnp.dot(mine_hot, stream_own, preferred_element_type=f32)
    mixed = fold_rows(feed, "req")
    return (mixed + down_bias.astype(f32)[None, :]).astype(bf16)


def solution(mesh):
    pairs = mesh.shape["req"] == REQ and mesh.shape["tp"] == TP
    per_device = on_pairs if pairs else on_any_mesh
    in_specs = (
        P("req", "tp"),
        P("req", "tp"),
        P("req", "tp"),
        P("req", "tp"),
        P(),
        P(),
        P(),
        P(None, "req", None, "tp"),
        P("tp", None),
        P("tp"),
        P("tp"),
        P("tp"),
        P("req", "tp"),
        P("req"),
        P("req", "tp"),
        P("tp"),
        P(),
    )
    out_specs = P("req", "tp")
    return jax.shard_map(
        per_device, mesh=mesh, in_specs=in_specs, out_specs=out_specs, check_vma=False
    )
```

```python
import functools
import math

import jax
import jax.numpy as jnp
from jax import lax
from jax.experimental import pallas as pl
from jax.experimental.pallas import tpu as pltpu
from jax.sharding import PartitionSpec as P

HEAD_DIM = 128
NORM_EPS = 1e-05
PAIRWISE = 16
REQ, TP = 8, 4
ATTENTION_ROOM = 51.2
ALL_ROOM = 58
F32, BF16, I32 = jnp.float32, jnp.bfloat16, jnp.int32
VMEM = pl.BlockSpec(memory_space=pltpu.VMEM)
HBM = pl.BlockSpec(memory_space=pltpu.HBM)

FIRST_ORDER = [4, 2, 5, 3, 6, 0, 7, 1]
MIDDLE_ORDER = [4, 3, 6, 1, 5, 2, 7, 0]
LAST_ORDER = [7, 6, 5, 4, 3, 2, 1, 0]


def pick_from(order, place):
    found = jnp.zeros_like(place)
    for i, index in enumerate(order):
        found = jnp.where(place == i, index, found)
    return found


def iota(shape, dim):
    return lax.broadcasted_iota(I32, shape, dim)


def onto_mxu(a, b):
    return jnp.dot(a, b, preferred_element_type=F32)


def nt_dot(a, b):
    return lax.dot_general(a, b, (((1,), (1,)), ((), ())), preferred_element_type=F32)


def hot(condition):
    return jnp.where(condition, 1.0, 0.0).astype(BF16)


def pile(parts):
    height = sum(p.shape[0] for p in parts)
    at, piled = 0, 0
    for p in parts:
        around = ((at, height - at - p.shape[0]),) + ((0, 0),) * (p.ndim - 1)
        piled += jnp.pad(p, around)
        at += p.shape[0]
    return piled


def row(vectors, i, cols):
    return vectors[i * cols : (i + 1) * cols][None, :]


def pack_kernel(owner_in, query, key, value, resid, out, owner, q, k, v, r, sems):
    parts = ((owner_in, owner), (query, q), (key, k), (value, v), (resid, r))
    copies = [pltpu.make_async_copy(x, y, sems.at[i]) for i, (x, y) in enumerate(parts)]
    for copy in copies:
        copy.start()
    rows, cols = q.shape
    fields = 4
    shape = (REQ * fields, fields * rows)
    down, across = iota(shape, 0), iota(shape, 1)
    me = lax.axis_index("req")
    copies[0].wait()
    owner_of = jnp.full(shape, owner[me * rows], I32)
    for i in range(1, rows):
        owner_of = jnp.where(across % rows == i, owner[me * rows + i], owner_of)
    pick = hot((down % fields == across // rows) & (owner_of == down // fields))
    for copy in copies[1:]:
        copy.wait()
    all_rows = jnp.concatenate([q[...], k[...], v[...], r[...]], axis=0)
    blocks = onto_mxu(pick, all_rows).astype(BF16)
    for d in range(REQ):
        block = blocks[d * fields : (d + 1) * fields]
        at = FIRST_ORDER.index(d)
        out[at, :fields, :] = block[:, : cols // 2]
        out[at, fields:, :] = block[:, cols // 2 :]


def index_kernel(place, numbers, pick, valid, arrange, arrange_own, *, page_len, heads):
    owner, order, lengths = (numbers[i : i + 1, :] for i in range(3))
    table = numbers[8:, :]
    me = place[0:1, 0:1]
    count = owner.shape[1]
    rows = count // REQ
    square = (count, count)
    down, across = iota(square, 0), iota(square, 1)
    owner_row = owner
    same_place = down == across
    owner_col = jnp.sum(jnp.where(same_place, owner_row, 0), axis=1, keepdims=True)
    order_col = jnp.sum(jnp.where(same_place, order, 0), axis=1, keepdims=True)
    same_owner = owner_col == owner_row
    rank_row = jnp.sum(jnp.where(same_owner & (down < across), 1, 0), axis=0, keepdims=True)
    rank_col = jnp.sum(jnp.where(same_owner & (across < down), 1, 0), axis=1, keepdims=True)

    shape = pick.shape
    down_p, across_p = iota(shape, 0), iota(shape, 1)
    down_i = iota((shape[0], count), 0)
    mine = hot((owner_row == me) & (rank_row == down_i % rows))
    source = pick_from(FIRST_ORDER, iota((count, shape[1]), 1) // (2 * rows))
    came = hot(iota((count, shape[1]), 0) // rows == source)
    from_there = onto_mxu(mine, came)
    field = jnp.minimum(down_p // (heads * rows), 3)
    pick[...] = hot((from_there > 0.5) & (field == across_p % rows))

    shape = valid.shape
    slot = iota((shape[0], count), 0) % rows
    mine_v = hot((owner_row == me) & (rank_row == slot))
    table_v = nt_dot(mine_v, table.astype(F32).astype(BF16)).astype(I32)
    length_v = jnp.sum(jnp.where(mine_v > 0.5, lengths, 0), axis=1, keepdims=True)
    position = iota(shape, 1)
    page, within = position // page_len, position % page_len
    seen = jnp.zeros(shape, F32)
    for j in range(table.shape[0]):
        inside = (table_v[:, j : j + 1] == page) & (within + j * page_len < length_v)
        seen = jnp.where(inside, 1.0, seen)
    valid[...] = seen

    ordered = hot(order_col == across)
    holds = hot((owner_col == pick_from(MIDDLE_ORDER, across // rows)) & (rank_col == across % rows))
    arrange[...] = onto_mxu(ordered, holds).astype(BF16)
    here = hot((owner_col == me) & (rank_col == iota(arrange_own.shape, 1)))
    arrange_own[...] = onto_mxu(ordered, here).astype(BF16)


def attention_kernel(
    place, arrived, pick, valid, vectors, pool, upper, weight, partial, rounded, lower, sem, *, rows
):
    deep = upper.shape[0]
    copy = pltpu.make_async_copy(weight.at[pl.ds(deep, deep)], lower, sem)
    copy.start()
    half = arrived.shape[2]
    cols = 2 * half
    heads = cols // HEAD_DIM
    scale = 1.0 / math.sqrt(HEAD_DIM)
    came = arrived[...].reshape(-1, half)
    which = (iota(pick.shape, 1) // rows) % 2
    chosen = pick[...].astype(F32)
    own = jnp.concatenate(
        [onto_mxu(jnp.where(which == i, chosen, 0.0).astype(BF16), came) for i in range(2)], axis=1
    )
    each = heads * rows
    query, key, value = (own[i * each : (i + 1) * each] for i in range(3))
    resid = own[3 * each : 3 * each + rows]
    shape = (each, cols)
    in_head = iota(shape, 0) // rows == iota(shape, 1) // HEAD_DIM
    wide = jnp.where(in_head, query, 0.0)
    positions = valid.shape[1]
    self_score = jnp.sum(wide * key, axis=1, keepdims=True) * scale
    scores = nt_dot(wide.astype(BF16), pool[0].reshape(positions, cols)) * scale
    scores = jnp.where(valid[...] > 0.5, scores, -jnp.inf)
    top = jnp.maximum(jnp.max(scores, axis=1, keepdims=True), self_score)
    weights = jnp.exp(scores - top)
    self_weight = jnp.exp(self_score - top)
    total = jnp.sum(weights, axis=1, keepdims=True) + self_weight
    numer = onto_mxu(weights.astype(BF16), pool[1].reshape(positions, cols))
    numer = numer + self_weight.astype(BF16).astype(F32) * value
    numer = jnp.where(in_head, numer / total, 0.0)
    attn = sum(numer[i * rows : (i + 1) * rows] for i in range(heads))
    attn = jnp.concatenate([attn, jnp.zeros_like(attn)], axis=0).astype(BF16)
    projected = onto_mxu(attn[:, :deep], upper[...])
    copy.wait()
    projected = (projected + onto_mxu(attn[:, deep:], lower[...]))[:rows]
    extra = resid + row(vectors, 0, cols)
    for t in range(TP):
        mine = jnp.where(place[1:2, 0:1] == t, extra, 0.0)
        whole = projected[:, t * cols : (t + 1) * cols] + mine
        partial[:, t * cols : (t + 1) * cols] = whole
        rounded[:, t * cols : (t + 1) * cols] = whole.astype(BF16)


def norm_kernel(place, own, sibling, far, far_sibling, vectors, blocks, stream_own):
    others = sibling[...].astype(F32) + far[...].astype(F32) + far_sibling[...].astype(F32)
    stream = (own[...] + others).astype(BF16).astype(F32)
    width = stream.shape[1]
    cols = width // TP
    mean = jnp.sum(stream, axis=1, keepdims=True) / width
    var = jnp.sum((stream - mean) ** 2, axis=1, keepdims=True) / width
    mine = stream[:, :cols]
    for t in range(1, TP):
        mine = jnp.where(place[1:2, 0:1] == t, stream[:, t * cols : (t + 1) * cols], mine)
    stream_own[...] = mine.astype(BF16)
    gain, bias = row(vectors, 1, cols), row(vectors, 2, cols)
    block = ((mine - mean) * lax.rsqrt(var + NORM_EPS) * gain + bias).astype(BF16)
    for d in range(REQ):
        blocks[d] = block


def up_kernel(rows_in, arrange, weight, out):
    came = rows_in[...].reshape(-1, rows_in.shape[2])
    ordered = onto_mxu(arrange[...], came).astype(BF16)
    out[...] = nt_dot(ordered, weight[...]).astype(BF16)


def down_kernel(near, far, vectors, weight, arrange_own, stream_own, out):
    hidden = near[...].astype(F32) + far[...].astype(F32)
    hidden = hidden + vectors[vectors.shape[0] - hidden.shape[1] :][None, :]
    activated = (0.5 * hidden * (1.0 + lax.erf(hidden * math.sqrt(0.5)))).astype(BF16)
    feed = onto_mxu(activated, weight[...]) + onto_mxu(arrange_own[...], stream_own[...])
    rows = out.shape[1]
    for d in range(REQ):
        out[LAST_ORDER.index(d)] = feed[d * rows : (d + 1) * rows].astype(BF16)


def finish_kernel(pieces, vectors, out):
    cols = out.shape[1]
    out[...] = (jnp.sum(pieces[...].astype(F32), axis=0) + row(vectors, 3, cols)).astype(BF16)


def call(kernel, shapes, specs, args, scratch=(), room=16, **fixed):
    moved = sum(a.size * a.dtype.itemsize for a in args)
    return pl.pallas_call(
        functools.partial(kernel, **fixed) if fixed else kernel,
        out_shape=shapes,
        in_specs=specs,
        out_specs=[VMEM] * len(shapes),
        scratch_shapes=scratch,
        compiler_params=pltpu.CompilerParams(vmem_limit_bytes=int(room * 2**20)),
        cost_estimate=pl.CostEstimate(flops=0, bytes_accessed=moved, transcendentals=0),
    )(*args)


def trade(blocks, group):
    return lax.all_to_all(blocks, "req", 0, 0, tiled=True, axis_index_groups=[group])


def on_pairs(
    query,
    key_new,
    value_new,
    resid,
    lengths,
    owner,
    page_table,
    kv_pool,
    out_weight,
    out_bias,
    norm_gain,
    norm_bias,
    up_weight_t,
    up_bias,
    down_weight,
    down_bias,
    order,
):
    rows, cols = query.shape
    width = cols * TP
    pool_pages, page_len = kv_pool.shape[1], kv_pool.shape[2]
    positions = pool_pages * page_len
    heads = cols // HEAD_DIM
    count = owner.shape[0]
    hidden = up_bias.shape[0]

    def arr(shape, dtype=BF16):
        return jax.ShapeDtypeStruct(shape, dtype)

    position = jnp.stack([lax.axis_index("req"), lax.axis_index("tp")]).astype(I32)
    place = jnp.broadcast_to(position[:, None], (2, HEAD_DIM))

    (packed,) = call(
        pack_kernel,
        [arr((REQ, 8, cols // 2))],
        [HBM] * 5,
        [owner, query, key_new, value_new, resid],
        [pltpu.SMEM((count,), I32)]
        + [pltpu.VMEM((rows, cols), BF16)] * 4
        + [pltpu.SemaphoreType.DMA((5,))],
        room=ALL_ROOM,
    )
    arrived = trade(packed, FIRST_ORDER)
    numbers = pile(
        [owner[None, :], order[None, :], lengths[None, :], jnp.zeros((5, count), I32), page_table.T]
    )
    vectors = pile([x.astype(F32) for x in (out_bias, norm_gain, norm_bias, down_bias, up_bias)])
    pick, valid, arrange, arrange_own = call(
        index_kernel,
        [
            arr((3 * heads * rows + 2 * rows, 2 * count)),
            arr((heads * rows, positions), F32),
            arr((count, count)),
            arr((count, rows)),
        ],
        [VMEM, VMEM],
        [place, numbers],
        page_len=page_len,
        heads=heads,
    )

    here = position[0] >= 0
    pool = jnp.where(here, kv_pool, jnp.zeros_like(kv_pool))
    upper = out_weight[: cols // 2]
    upper = jnp.where(here, upper, jnp.zeros_like(upper))

    partial, rounded = call(
        attention_kernel,
        [arr((rows, width), F32), arr((rows, width))],
        [VMEM] * 7 + [HBM],
        [place, arrived, pick, valid, vectors, pool, upper, out_weight],
        [pltpu.VMEM(upper.shape, BF16), pltpu.SemaphoreType.DMA],
        room=ATTENTION_ROOM,
        rows=rows,
    )
    blocks, stream_own = call(
        norm_kernel,
        [arr((REQ, rows, cols)), arr((rows, cols))],
        [VMEM] * 6,
        [place, partial] + [swap(rounded, "tp", step) for step in (1, 2, 3)] + [vectors],
    )

    (part,) = call(
        up_kernel,
        [arr((count, hidden))],
        [VMEM] * 3,
        [trade(blocks, MIDDLE_ORDER), arrange, up_weight_t],
    )
    part = (part.astype(F32) + swap(part, "tp", 1).astype(F32)).astype(BF16)
    (feed,) = call(
        down_kernel,
        [arr((REQ, rows, cols))],
        [VMEM] * 6,
        [part, swap(part, "tp", 3), vectors, down_weight, arrange_own, stream_own],
    )
    (out,) = call(finish_kernel, [arr((rows, cols))], [VMEM] * 2, [trade(feed, LAST_ORDER), vectors])
    return out


def swap(x, axis, step):
    n = lax.axis_size(axis)
    return lax.ppermute(x, axis, [(i, i ^ step) for i in range(n)])


def origins(axis):
    n, me = lax.axis_size(axis), lax.axis_index(axis)
    if n > PAIRWISE:
        return jnp.arange(n, dtype=jnp.int32)
    offsets = [0]
    step = n // 2
    while step:
        offsets = offsets + [o ^ step for o in offsets]
        step //= 2
    return jnp.array(offsets, dtype=jnp.int32) ^ me


def gather_rows(x, axis):
    n = lax.axis_size(axis)
    if n > PAIRWISE:
        return lax.all_gather(x, axis, axis=0, tiled=True)
    step = n // 2
    while step:
        x = jnp.concatenate([x, swap(x, axis, step)], axis=0)
        step //= 2
    return x


def fold_rows(x, axis):
    n = lax.axis_size(axis)
    if n > PAIRWISE:
        return lax.psum_scatter(x, axis, scatter_dimension=0, tiled=True)
    step = 1
    while step < n:
        half = x.shape[0] // 2
        x = x[:half] + swap(x[half:], axis, step)
        step *= 2
    return x


def sum_pairs(x, axis):
    n = lax.axis_size(axis)
    step = 1
    while step < n:
        x = (x.astype(jnp.float32) + swap(x, axis, step).astype(jnp.float32)).astype(x.dtype)
        step *= 2
    return x


def on_any_mesh(
    query,
    key_new,
    value_new,
    resid,
    lengths,
    owner,
    page_table,
    kv_pool,
    out_weight,
    out_bias,
    norm_gain,
    norm_bias,
    up_weight_t,
    up_bias,
    down_weight,
    down_bias,
    order,
):
    f32, bf16, i32 = jnp.float32, jnp.bfloat16, jnp.int32
    n_req = lax.axis_size("req")
    n_tp = lax.axis_size("tp")
    me = lax.axis_index("req")
    me_tp = lax.axis_index("tp")
    rows, cols = query.shape
    width = cols * n_tp
    heads = cols // HEAD_DIM
    pool_pages, page_len = kv_pool.shape[1], kv_pool.shape[2]
    positions = pool_pages * page_len
    scale = 1.0 / math.sqrt(HEAD_DIM)

    origin = origins("req")
    packed = jnp.concatenate([query, key_new, value_new, resid], axis=1)
    arrived = gather_rows(packed, "req")

    same = owner[:, None] == owner[None, :]
    ids = jnp.arange(owner.shape[0], dtype=i32)
    rank = jnp.sum((same & (ids[None, :] < ids[:, None])).astype(i32), axis=1)
    slots = jnp.arange(rows, dtype=i32)
    mine = (owner == me)[None, :] & (rank[None, :] == slots[:, None])
    mine_i = mine.astype(i32)
    own_len = jnp.sum(mine_i * lengths[None, :], axis=1)
    own_table = jnp.sum(mine_i[:, :, None] * page_table[None], axis=1)
    origin_ids = (origin[:, None] * rows + slots[None, :]).reshape(-1)
    own_id = jnp.sum(mine_i * ids[None, :], axis=1)
    take_hot = (own_id[:, None] == origin_ids[None, :]).astype(bf16)
    own = jnp.dot(take_hot, arrived, preferred_element_type=f32).astype(bf16)
    query_own, key_own, value_own, resid_own = (own[:, i * cols : (i + 1) * cols] for i in range(4))

    pos = jnp.arange(positions, dtype=i32)
    page, within = pos // page_len, pos % page_len
    entry = jnp.arange(page_table.shape[1], dtype=i32)
    start = entry * page_len
    hit = (own_table[:, :, None] == page[None, None, :]) & (
        start[None, :, None] + within[None, None, :] < own_len[:, None, None]
    )
    valid = jnp.any(hit, axis=1)

    keys = kv_pool[0].reshape(positions, cols)
    values = kv_pool[1].reshape(positions, cols)
    head_of = jnp.arange(cols, dtype=i32) // HEAD_DIM
    head_mask = head_of[None, :] == jnp.arange(heads, dtype=i32)[:, None]
    spread_q = jnp.where(head_mask[:, None, :], query_own[None], 0).reshape(heads * rows, cols)
    scores = (
        lax.dot_general(spread_q, keys, (((1,), (1,)), ((), ())), preferred_element_type=f32) * scale
    ).reshape(heads, rows, positions)
    scores = jnp.where(valid[None], scores, -jnp.inf)
    self_score = (
        jnp.sum(
            (query_own.astype(f32) * key_own.astype(f32)).reshape(rows, heads, HEAD_DIM), axis=-1
        ).T
        * scale
    )
    top = jnp.maximum(jnp.max(scores, axis=2), self_score)
    weights = jnp.exp(scores - top[:, :, None])
    self_weight = jnp.exp(self_score - top)
    total = jnp.sum(weights, axis=2) + self_weight
    numer = jnp.dot(
        weights.astype(bf16).reshape(heads * rows, positions), values, preferred_element_type=f32
    ).reshape(heads, rows, cols)
    numer = numer + self_weight.astype(bf16).astype(f32)[:, :, None] * value_own.astype(f32)[None]
    attn = jnp.sum(
        jnp.where(head_mask[:, None, :], numer / total[:, :, None], 0.0), axis=0
    ).astype(bf16)

    extra = resid_own.astype(f32) + out_bias.astype(f32)[None, :]
    partial = jnp.dot(attn, out_weight, preferred_element_type=f32)
    place = (jnp.arange(n_tp, dtype=i32) == me_tp)[None, :, None]
    partial = (
        partial.reshape(rows, n_tp, cols) + jnp.where(place, extra[:, None, :], 0.0)
    ).reshape(rows, width)
    stream = sum_pairs(partial, "tp").astype(bf16)
    stream_f = stream.astype(f32)
    mean = jnp.mean(stream_f, axis=1, keepdims=True)
    var = jnp.mean((stream_f - mean) ** 2, axis=1, keepdims=True)
    inverse = lax.rsqrt(var + NORM_EPS)
    stream_own = lax.dynamic_slice_in_dim(stream, me_tp * cols, cols, axis=1)
    normed = (
        (stream_own.astype(f32) - mean) * inverse * norm_gain.astype(f32)[None, :]
        + norm_bias.astype(f32)[None, :]
    ).astype(bf16)

    normed_all = gather_rows(normed, "req")
    slot_of = owner * rows + rank
    wanted = slot_of[order[origin_ids]]
    place_hot = (wanted[:, None] == origin_ids[None, :]).astype(bf16)
    mine_hot = (wanted[:, None] == (me * rows + slots)[None, :]).astype(bf16)
    normed_out = jnp.dot(place_hot, normed_all, preferred_element_type=f32).astype(bf16)
    hidden = lax.dot_general(
        normed_out, up_weight_t, (((1,), (1,)), ((), ())), preferred_element_type=f32
    ).astype(bf16)
    summed = sum_pairs(hidden, "tp").astype(f32)
    activated = jax.nn.gelu(summed + up_bias.astype(f32)[None, :], approximate=False).astype(bf16)
    feed = jnp.dot(activated, down_weight, preferred_element_type=f32)
    feed = feed + jnp.dot(mine_hot, stream_own, preferred_element_type=f32)
    mixed = fold_rows(feed, "req")
    return (mixed + down_bias.astype(f32)[None, :]).astype(bf16)


def solution(mesh):
    pairs = mesh.shape["req"] == REQ and mesh.shape["tp"] == TP
    per_device = on_pairs if pairs else on_any_mesh
    in_specs = (
        P("req", "tp"),
        P("req", "tp"),
        P("req", "tp"),
        P("req", "tp"),
        P(),
        P(),
        P(),
        P(None, "req", None, "tp"),
        P("tp", None),
        P("tp"),
        P("tp"),
        P("tp"),
        P("req", "tp"),
        P("req"),
        P("req", "tp"),
        P("tp"),
        P(),
    )
    out_specs = P("req", "tp")
    return jax.shard_map(
        per_device, mesh=mesh, in_specs=in_specs, out_specs=out_specs, check_vma=False
    )
```
